32 devices in a mesh: var: 4 (over z), samp: 8 (over y, x, core).
Axes of the slice: x: 2, y: 2, z: 4, core: 2. Of those that a mesh axis runs over, the one named last changes fastest.
Arguments:
- genotypes: int32 [3072, 24576], P('var', 'samp'), may hold values from 0 to 2, as said below
- called: int32 [3072, 24576], P('var', 'samp'), may hold values from 0 to 1
- dosage: int32 [24576, 1024], P(('samp', 'var')), may hold values from 0 to 200
- sample_order: int32 [32, 768], P(('samp', 'var')), may hold values from 0 to 767, each once within a row
- noise_ratio: float32 [16], replicated, may hold values from 0.5 to 4
- solution: float32 [24576, 16], P(('samp', 'var')), may hold values from -13 to 13
- residual: float32 [24576, 16], P(('samp', 'var')), may hold values from -13 to 13
- direction: float32 [24576, 16], P(('samp', 'var')), may hold values from -13 to 13
Outputs:
- solution_new: float32 [24576, 16], P(('samp', 'var'))
- residual_new: float32 [24576, 16], P(('samp', 'var'))
- direction_new: float32 [24576, 16], P(('samp', 'var'))
- scores: float32 [1024, 16], P(('var', 'samp'))
The draws below stay inside these ranges and needn't reach their ends.
Inputs may be any that keep to these rules, and one draw needn't show every extreme that they name: `genotypes`: where called is 1, the count of one allele. `sample_order`: each row lists 0 to 767 once.
All inputs are finite; a program needn't handle non-finite values.
Results may differ from the reference program's by a relative error of at most 0.023.
Values may be sent and summed in bfloat16 or wider, within the bound.
No kernel may reach another device: no remote copies, remote signals or barrier semaphores. Data moves between devices by JAX's collectives and lax.ppermute only.
A program may use at most 128 MiB of HBM per device.

```python
import math
import jax
import jax.numpy as jnp
from jax import lax

VARIANTS = 3072
IMPUTED = 1024
RHS = 16
SAMPLES = 24576
QUARTER = 768
BLOCKS = 32


def allele_pair(key, limit):
    key_first, key_second = jax.random.split(key, 2)
    first = jnp.where(jax.random.randint(key_first, (VARIANTS, SAMPLES), 0, 1000) < limit, 1, 0)
    second = jnp.where(jax.random.randint(key_second, (VARIANTS, SAMPLES), 0, 1000) < limit, 1, 0)
    return (first + second).astype(jnp.int32)


def trend_place(key):
    sample = jnp.arange(SAMPLES, dtype=jnp.int32)[None, :]
    flipped = jax.random.randint(key, (VARIANTS, 1), 0, 2)
    return jnp.where(flipped == 1, SAMPLES - 1 - sample, sample)


def draw_genotypes(key, part):
    key_base, key_codes, key_sign = jax.random.split(jax.random.fold_in(key, 17), 3)
    base = jax.random.randint(key_base, (VARIANTS, 1), 40, 241)
    place = trend_place(key_sign)
    limit = base * (SAMPLES + 3 * place) // SAMPLES
    return allele_pair(key_codes, limit)


def draw_called(key, part):
    key_mask, key_sign = jax.random.split(jax.random.fold_in(key, 29), 2)
    place = trend_place(key_sign)
    limit = 300 + 600 * place // SAMPLES
    drawn = jax.random.randint(key_mask, (VARIANTS, SAMPLES), 0, 1000)
    return jnp.where(drawn < limit, 1, 0).astype(jnp.int32)


def draw_dosage(key, part):
    key_ceiling, key_value = jax.random.split(jax.random.fold_in(key, 41), 2)
    ceiling = jax.random.randint(key_ceiling, (1, IMPUTED), 50, 68)
    sample = jnp.arange(SAMPLES, dtype=jnp.int32)[:, None]
    top = jnp.minimum(ceiling * (SAMPLES + 3 * sample) // SAMPLES, 200)
    return jax.random.randint(key_value, (SAMPLES, IMPUTED), 0, top + 1).astype(jnp.int32)


def vector_draw(key, salt):
    key_row, key_col, key_noise = jax.random.split(jax.random.fold_in(key, salt), 3)
    rows = jnp.arange(SAMPLES, dtype=jnp.float32)[:, None] / SAMPLES
    row_scale = jnp.exp(jax.random.uniform(key_row, (SAMPLES, 1), minval=0.0, maxval=math.log(10.0)))
    col_scale = jnp.exp(jax.random.uniform(key_col, (1, RHS), minval=0.0, maxval=math.log(10.0)))
    values = jnp.clip(jax.random.normal(key_noise, (SAMPLES, RHS)), -4.0, 4.0)
    rise = jnp.sqrt(1.0 + 2.0 * rows)
    return jnp.clip(0.1 * values * row_scale * col_scale * rise, -12.5, 12.5).astype(jnp.float32)


def draw_solution(key, part):
    return vector_draw(key, 101)


def draw_residual(key, part):
    return vector_draw(key, 202)


def draw_direction(key, part):
    return vector_draw(key, 303)


def setup_inputs(seed: int = 0) -> dict:
    arg_keys = jax.random.split(jax.random.key(seed), 9)
    return {
        "genotypes": draw_genotypes(jax.random.fold_in(arg_keys[8], 71), 0),
        "called": draw_called(jax.random.fold_in(arg_keys[8], 71), 0),
        "dosage": draw_dosage(jax.random.fold_in(arg_keys[8], 71), 0),
        "sample_order": jax.vmap(lambda own: jax.random.permutation(own, QUARTER))(jax.random.split(arg_keys[3], BLOCKS)).reshape((BLOCKS, QUARTER)).astype(jnp.int32),
        "noise_ratio": jnp.clip(jnp.exp(jax.random.uniform(arg_keys[4], (RHS,), jnp.float32, math.log(0.5), math.log(4.0))), 0.5, 4.0),
        "solution": draw_solution(jax.random.fold_in(arg_keys[8], 71), 0),
        "residual": draw_residual(jax.random.fold_in(arg_keys[8], 71), 0),
        "direction": draw_direction(jax.random.fold_in(arg_keys[8], 71), 0),
    }


def widen(values):
    return lax.optimization_barrier(values.astype(jnp.bfloat16)).astype(jnp.float32)

def product(matrix, vectors):
    return jnp.dot(matrix, vectors, preferred_element_type=jnp.float32, precision=lax.Precision.HIGHEST)

def reference(genotypes, called, dosage, sample_order, noise_ratio, solution, residual, direction):
    pieces = 4
    block_width = VARIANTS // pieces
    direction_b = widen(direction)
    frequencies = []
    spreads = []
    loadings = []
    for position in range(pieces):
        first_row = position * block_width
        codes_block = genotypes[first_row:first_row + block_width]
        called_block = called[first_row:first_row + block_width]
        coded = codes_block * called_block
        called_count = lax.optimization_barrier(jnp.sum(called_block, axis=1)).astype(jnp.float32)
        allele_sum = lax.optimization_barrier(jnp.sum(coded, axis=1)).astype(jnp.float32)
        frequency = (allele_sum + 1.0) / (2.0 * called_count + 2.0)
        spread = jnp.sqrt(2.0 * frequency * (1.0 - frequency))
        raw_proj = product(coded.astype(jnp.float32), direction_b)
        called_proj = product(called_block.astype(jnp.float32), direction_b)
        loading = (raw_proj - 2.0 * frequency[:, None] * called_proj) / spread[:, None]
        frequencies.append(frequency)
        spreads.append(spread)
        loadings.append(loading)
    back = jnp.zeros(direction.shape, jnp.float32)
    for position in range(pieces):
        first_row = position * block_width
        codes_block = genotypes[first_row:first_row + block_width]
        called_block = called[first_row:first_row + block_width]
        coded = (codes_block * called_block).astype(jnp.float32)
        scaled_a = widen(loadings[position] / spreads[position][:, None])
        scaled_b = widen(2.0 * frequencies[position][:, None] * loadings[position] / spreads[position][:, None])
        back = back + product(coded.T, scaled_a) - product(called_block.astype(jnp.float32).T, scaled_b)
    applied = noise_ratio[None, :] * direction + back / VARIANTS
    res_norm = lax.optimization_barrier(jnp.sum(residual * residual, axis=0))
    curvature = lax.optimization_barrier(jnp.sum(direction * applied, axis=0))
    step_size = res_norm / (curvature + 1e-06)
    solution_new = solution + step_size[None, :] * direction
    residual_new = residual - step_size[None, :] * applied
    res_new_norm = lax.optimization_barrier(jnp.sum(residual_new * residual_new, axis=0))
    direction_new = residual_new + (res_new_norm / (res_norm + 1e-06))[None, :] * direction
    rows = (jnp.arange(BLOCKS, dtype=jnp.int32)[:, None] * QUARTER + sample_order.astype(jnp.int32)).reshape(-1)
    picked = widen(jnp.take(solution_new, rows, axis=0))
    dosage_sum = lax.optimization_barrier(jnp.sum(dosage, axis=0)).astype(jnp.float32)
    cross_sum = product(dosage.astype(jnp.float32).T, picked)
    sol_sum = lax.optimization_barrier(jnp.sum(solution_new, axis=0))
    sol_square = lax.optimization_barrier(jnp.sum(solution_new * solution_new, axis=0))
    dose_freq = (dosage_sum / 100.0 + 1.0) / (2.0 * SAMPLES + 2.0)
    dose_spread = jnp.sqrt(2.0 * dose_freq * (1.0 - dose_freq))
    scale_norm = math.sqrt(SAMPLES) * jnp.sqrt(sol_square / SAMPLES + 1e-06)
    scores = (cross_sum / 100.0 - 2.0 * dose_freq[:, None] * sol_sum[None, :]) / (dose_spread[:, None] * scale_norm[None, :])
    return (solution_new, residual_new, direction_new, scores)
```

```python
import math

import jax
import jax.numpy as jnp
from jax import lax
from jax.sharding import PartitionSpec as P

BF16 = jnp.bfloat16
F32 = jnp.float32


def swap(values, axis, distance):
    size = lax.axis_size(axis)
    return lax.ppermute(values, axis, [(i, i ^ distance) for i in range(size)])


def sum_over(values, axis, stages):
    for distances in stages:
        total = values
        for arrived in [swap(values, axis, distance) for distance in distances]:
            total = total + arrived
        values = total
    return values


def stages_of(size, radices):
    stages = []
    step = 1
    while step < size:
        radix = min(radices[min(len(stages), len(radices) - 1)], size // step)
        stages.append([step * k for k in range(1, radix)])
        step *= radix
    return stages


def split2(values):
    high = lax.reduce_precision(values, 8, 7)
    return high.astype(BF16), (values - high).astype(BF16)


def body(genotypes, called, dosage, sample_order, noise_ratio, solution, residual, direction):
    var = lax.axis_index("var")
    samp = lax.axis_index("samp")
    n_var = lax.axis_size("var")
    n_samp = lax.axis_size("samp")
    own, rhs = direction.shape
    variants = genotypes.shape[0] * n_var
    samples = own * n_samp * n_var
    imputed = dosage.shape[1]
    var_all = list(range(1, n_var))
    samp_stages = stages_of(n_samp, [2, 4])

    direction_t = direction.T
    residual_t = residual.T
    solution_t = solution.T

    direction_b = direction_t.astype(BF16)
    pieces = jnp.stack([direction_b] + [swap(direction_b, "var", k) for k in var_all])
    piece = jnp.concatenate(
        [lax.dynamic_index_in_dim(pieces, p ^ var, keepdims=False) for p in range(n_var)], axis=1
    )

    coded = genotypes * called
    coded_b = coded.astype(BF16)
    called_b = called.astype(BF16)
    allele_part = jnp.sum(coded, axis=1).astype(F32)
    called_part = jnp.sum(called, axis=1).astype(F32)

    order_row = sample_order[0]
    both = jnp.concatenate([solution_t, direction_t], axis=0)
    picked = jnp.take(both, order_row, axis=1)
    picked_high, picked_low = split2(picked)
    dosage_b = dosage.astype(BF16)
    stack = jnp.concatenate([picked_high, picked_low, jnp.ones((16, own), BF16)], axis=0)
    cross = jnp.dot(stack, dosage_b, preferred_element_type=F32)
    cross = jnp.concatenate([cross[: 2 * rhs] + cross[2 * rhs : 4 * rhs], cross[4 * rhs : 4 * rhs + 8]])

    sums = jnp.concatenate(
        [
            jnp.sum(residual_t * residual_t, axis=1),
            jnp.sum(direction_t * direction_t, axis=1),
            jnp.sum(solution_t, axis=1),
            jnp.sum(solution_t * solution_t, axis=1),
            jnp.sum(solution_t * direction_t, axis=1),
            jnp.sum(direction_t, axis=1),
        ]
    )
    rows = genotypes.shape[0]
    extra = jnp.zeros((6, rows), F32).at[0, : 6 * rhs].set(sums)

    nt = (((1,), (1,)), ((), ()))
    raw_part = lax.dot_general(piece, coded_b, nt, preferred_element_type=F32)
    called_proj_part = lax.dot_general(piece, called_b, nt, preferred_element_type=F32)
    message = jnp.concatenate([raw_part, called_proj_part, allele_part[None], called_part[None], extra])
    total = sum_over(message, "samp", samp_stages)
    raw_proj = total[:rhs]
    called_proj = total[rhs : 2 * rhs]
    allele_sum = total[2 * rhs]
    called_count = total[2 * rhs + 1]
    sums = total[2 * rhs + 2, : 6 * rhs]

    frequency = (allele_sum + 1.0) / (2.0 * called_count + 2.0)
    spread = jnp.sqrt(2.0 * frequency * (1.0 - frequency))
    loading = (raw_proj - 2.0 * frequency * called_proj) / spread
    scaled = loading / spread
    scaled_a = scaled.astype(BF16)
    scaled_b = (2.0 * frequency * scaled).astype(BF16)

    small = jnp.concatenate([sums, jnp.sum(loading * loading, axis=1)])
    small = sum_over(small, "var", [var_all])

    term = jnp.dot(scaled_a, coded_b, preferred_element_type=F32)
    term = term - jnp.dot(scaled_b, called_b, preferred_element_type=F32)
    term = (term / variants).astype(BF16)
    term = term.reshape(rhs, n_var, own)
    take = lambda p: lax.dynamic_index_in_dim(term, p, axis=1, keepdims=False)
    back = take(var).astype(F32)
    for arrived in [swap(take(var ^ k), "var", k) for k in var_all]:
        back = back + arrived.astype(F32)

    res_norm, dir_norm, sol_one, sol_two, sol_dir, dir_one, load_square = small.reshape(7, rhs)
    applied = noise_ratio[:, None] * direction_t + back
    curvature = noise_ratio * dir_norm + load_square / variants
    step_size = res_norm / (curvature + 1e-06)
    solution_new = solution_t + step_size[:, None] * direction_t
    residual_new = residual_t - step_size[:, None] * applied
    res_new_norm = jnp.sum(residual_new * residual_new, axis=1)
    res_new_norm = sum_over(res_new_norm, "samp", [list(range(1, n_samp))] if n_samp <= 8 else samp_stages)
    res_new_norm = sum_over(res_new_norm, "var", [var_all])
    direction_new = residual_new + (res_new_norm / (res_norm + 1e-06))[:, None] * direction_t

    wide = imputed // n_var
    cross = cross.reshape(cross.shape[0], n_var, wide)
    take_cross = lambda p: lax.dynamic_index_in_dim(cross, p, axis=1, keepdims=False)
    mine = take_cross(var)
    for arrived in [swap(take_cross(var ^ k), "var", k) for k in var_all]:
        mine = mine + arrived
    mine = sum_over(mine, "samp", samp_stages)
    narrow = wide // n_samp
    mine = lax.dynamic_slice_in_dim(mine, samp * narrow, narrow, axis=1)
    cross_sum = mine[:rhs] + step_size[:, None] * mine[rhs : 2 * rhs]
    dosage_sum = mine[2 * rhs]
    sol_sum = sol_one + step_size * dir_one
    sol_square = sol_two + 2.0 * step_size * sol_dir + step_size * (step_size * dir_norm)
    dose_freq = (dosage_sum / 100.0 + 1.0) / (2.0 * samples + 2.0)
    dose_spread = jnp.sqrt(2.0 * dose_freq * (1.0 - dose_freq))
    scale_norm = math.sqrt(samples) * jnp.sqrt(sol_square / samples + 1e-06)
    scores = (cross_sum / 100.0 - 2.0 * dose_freq[None, :] * sol_sum[:, None]) / (
        dose_spread[None, :] * scale_norm[:, None]
    )
    return (solution_new.T, residual_new.T, direction_new.T, scores.T)


def solution(mesh):
    placed = (
        P("var", "samp"),
        P("var", "samp"),
        P(("samp", "var"), None),
        P(("samp", "var"), None),
        P(),
        P(("samp", "var"), None),
        P(("samp", "var"), None),
        P(("samp", "var"), None),
    )
    return jax.shard_map(
        body,
        mesh=mesh,
        in_specs=placed,
        out_specs=(
            P(("samp", "var"), None),
            P(("samp", "var"), None),
            P(("samp", "var"), None),
            P(("var", "samp"), None),
        ),
        check_vma=False,
    )
```

```python
import math

import jax
import jax.numpy as jnp
from jax import lax
from jax.sharding import PartitionSpec as P

BF16 = jnp.bfloat16
F32 = jnp.float32


def swap(values, axis, distance):
    size = lax.axis_size(axis)
    return lax.ppermute(values, axis, [(i, i ^ distance) for i in range(size)])


def sum_over(values, axis, stages):
    for distances in stages:
        total = values
        for arrived in [swap(values, axis, distance) for distance in distances]:
            total = total + arrived
        values = total
    return values


def stages_of(size, radices):
    stages = []
    step = 1
    while step < size:
        radix = min(radices[min(len(stages), len(radices) - 1)], size // step)
        stages.append([step * k for k in range(1, radix)])
        step *= radix
    return stages


def split2(values):
    high = lax.reduce_precision(values, 8, 7)
    return high.astype(BF16), (values - high).astype(BF16)


def split3(values):
    high = lax.reduce_precision(values, 8, 7)
    rest = values - high
    middle = lax.reduce_precision(rest, 8, 7)
    return high.astype(BF16), middle.astype(BF16), (rest - middle).astype(BF16)


def body(genotypes, called, dosage, sample_order, noise_ratio, solution, residual, direction):
    var = lax.axis_index("var")
    samp = lax.axis_index("samp")
    n_var = lax.axis_size("var")
    n_samp = lax.axis_size("samp")
    own, rhs = direction.shape
    variants = genotypes.shape[0] * n_var
    samples = own * n_samp * n_var
    imputed = dosage.shape[1]
    var_all = list(range(1, n_var))
    samp_stages = stages_of(n_samp, [2, 4])

    direction_t = direction.T
    residual_t = residual.T
    solution_t = solution.T

    direction_b = direction_t.astype(BF16)
    pieces = jnp.stack([direction_b] + [swap(direction_b, "var", k) for k in var_all])
    piece = jnp.concatenate(
        [lax.dynamic_index_in_dim(pieces, p ^ var, keepdims=False) for p in range(n_var)], axis=1
    )

    coded = genotypes * called
    coded_b = coded.astype(BF16)
    called_b = called.astype(BF16)
    allele_part = jnp.sum(coded, axis=1).astype(F32)
    called_part = jnp.sum(called, axis=1).astype(F32)

    order_row = sample_order[0]
    both = jnp.concatenate([solution_t, direction_t], axis=0)
    picked = jnp.take(both, order_row, axis=1)
    picked_high, picked_low = split2(picked)
    dosage_b = dosage.astype(BF16)
    stack = jnp.concatenate([picked_high, picked_low, jnp.ones((16, own), BF16)], axis=0)
    cross = jnp.dot(stack, dosage_b, preferred_element_type=F32)
    cross = jnp.concatenate([cross[: 2 * rhs] + cross[2 * rhs : 4 * rhs], cross[4 * rhs : 4 * rhs + 8]])

    sums = jnp.concatenate(
        [
            jnp.sum(residual_t * residual_t, axis=1),
            jnp.sum(direction_t * direction_t, axis=1),
            jnp.sum(solution_t, axis=1),
            jnp.sum(solution_t * solution_t, axis=1),
            jnp.sum(solution_t * direction_t, axis=1),
            jnp.sum(direction_t, axis=1),
        ]
    )
    rows = genotypes.shape[0]
    extra = jnp.zeros((6, rows), F32).at[0, : 6 * rhs].set(sums)

    nt = (((1,), (1,)), ((), ()))
    raw_part = lax.dot_general(piece, coded_b, nt, preferred_element_type=F32)
    called_proj_part = lax.dot_general(piece, called_b, nt, preferred_element_type=F32)
    message = jnp.concatenate([raw_part, called_proj_part, allele_part[None], called_part[None], extra])
    total = sum_over(message, "samp", samp_stages)
    raw_proj = total[:rhs]
    called_proj = total[rhs : 2 * rhs]
    allele_sum = total[2 * rhs]
    called_count = total[2 * rhs + 1]
    sums = total[2 * rhs + 2, : 6 * rhs]

    frequency = (allele_sum + 1.0) / (2.0 * called_count + 2.0)
    spread = jnp.sqrt(2.0 * frequency * (1.0 - frequency))
    loading = (raw_proj - 2.0 * frequency * called_proj) / spread
    scaled = loading / spread
    scaled_a = scaled.astype(BF16)
    scaled_b = (2.0 * frequency * scaled).astype(BF16)

    small = jnp.concatenate([sums, jnp.sum(loading * loading, axis=1)])
    parts = jnp.zeros((rhs, 128), BF16).at[:3, : small.shape[0]].set(jnp.stack(split3(small)))

    term = jnp.dot(scaled_a, coded_b, preferred_element_type=F32)
    term = term - jnp.dot(scaled_b, called_b, preferred_element_type=F32)
    term = (term / variants).astype(BF16)
    message = jnp.stack(
        [jnp.concatenate([term[:, p * own : (p + 1) * own], parts], axis=1) for p in range(n_var)]
    )
    message = lax.all_to_all(message, "var", split_axis=0, concat_axis=0)
    message = jnp.sum(message.astype(F32), axis=0)
    back = message[:, :own]
    small = message[0, own:] + message[1, own:] + message[2, own:]
    small = small[: 7 * rhs]

    res_norm, dir_norm, sol_one, sol_two, sol_dir, dir_one, load_square = small.reshape(7, rhs)
    applied = noise_ratio[:, None] * direction_t + back
    curvature = noise_ratio * dir_norm + load_square / variants
    step_size = res_norm / (curvature + 1e-06)
    solution_new = solution_t + step_size[:, None] * direction_t
    residual_new = residual_t - step_size[:, None] * applied
    res_new_norm = jnp.sum(residual_new * residual_new, axis=1)
    spread_out = jnp.broadcast_to(jnp.pad(res_new_norm, (0, 128 - rhs)), (n_var * n_samp, 1, 128))
    spread_out = lax.all_to_all(spread_out, ("var", "samp"), split_axis=0, concat_axis=0)
    res_new_norm = jnp.sum(spread_out, axis=(0, 1))[:rhs]
    direction_new = residual_new + (res_new_norm / (res_norm + 1e-06))[:, None] * direction_t

    wide = imputed // n_var
    cross = cross.reshape(cross.shape[0], n_var, wide)
    take_cross = lambda p: lax.dynamic_index_in_dim(cross, p, axis=1, keepdims=False)
    mine = take_cross(var)
    for arrived in [swap(take_cross(var ^ k), "var", k) for k in var_all]:
        mine = mine + arrived
    mine = sum_over(mine, "samp", samp_stages)
    narrow = wide // n_samp
    mine = lax.dynamic_slice_in_dim(mine, samp * narrow, narrow, axis=1)
    cross_sum = mine[:rhs] + step_size[:, None] * mine[rhs : 2 * rhs]
    dosage_sum = mine[2 * rhs]
    sol_sum = sol_one + step_size * dir_one
    sol_square = sol_two + 2.0 * step_size * sol_dir + step_size * (step_size * dir_norm)
    dose_freq = (dosage_sum / 100.0 + 1.0) / (2.0 * samples + 2.0)
    dose_spread = jnp.sqrt(2.0 * dose_freq * (1.0 - dose_freq))
    scale_norm = math.sqrt(samples) * jnp.sqrt(sol_square / samples + 1e-06)
    scores = (cross_sum / 100.0 - 2.0 * dose_freq[None, :] * sol_sum[:, None]) / (
        dose_spread[None, :] * scale_norm[:, None]
    )
    return (solution_new.T, residual_new.T, direction_new.T, scores.T)


def solution(mesh):
    placed = (
        P("var", "samp"),
        P("var", "samp"),
        P(("samp", "var"), None),
        P(("samp", "var"), None),
        P(),
        P(("samp", "var"), None),
        P(("samp", "var"), None),
        P(("samp", "var"), None),
    )
    return jax.shard_map(
        body,
        mesh=mesh,
        in_specs=placed,
        out_specs=(
            P(("samp", "var"), None),
            P(("samp", "var"), None),
            P(("samp", "var"), None),
            P(("var", "samp"), None),
        ),
        check_vma=False,
    )
```

```python
import functools
import math

import jax
import jax.numpy as jnp
from jax import lax
from jax.experimental import pallas as pl
from jax.experimental.pallas import tpu as pltpu
from jax.sharding import PartitionSpec as P

BF16 = jnp.bfloat16
F32 = jnp.float32
LANES = 128
NT = (((1,), (1,)), ((), ()))
VMEM = pl.BlockSpec(memory_space=pltpu.VMEM)
SMEM = pl.BlockSpec(memory_space=pltpu.SMEM)
ANY = pl.BlockSpec(memory_space=pl.ANY)
MIB = 1 << 20


def swap(values, axis, distance):
    size = lax.axis_size(axis)
    return lax.ppermute(values, axis, [(i, i ^ distance) for i in range(size)])


def halves(values):
    high = values.astype(BF16)
    return high, (values - high.astype(F32)).astype(BF16)


def thirds(values):
    high = values.astype(BF16)
    rest = values - high.astype(F32)
    middle = rest.astype(BF16)
    return high, middle, (rest - middle.astype(F32)).astype(BF16)


def lane_of(shape):
    return lax.broadcasted_iota(jnp.int32, shape, len(shape) - 1)


def columns(values, shape):
    lane = lane_of(shape)
    block = jnp.zeros(shape, F32)
    for q, column in enumerate(values):
        block = jnp.where(lane == q, column, block)
    return block


def to_column(row):
    shape = (16, LANES)
    same = lax.broadcasted_iota(jnp.int32, shape, 0) == lane_of(shape)
    return jnp.sum(jnp.where(same, row, 0.0), axis=1, keepdims=True)


def to_row(column):
    shape = (16, LANES)
    same = lax.broadcasted_iota(jnp.int32, shape, 0) == lane_of(shape)
    return jnp.sum(jnp.where(same, column, 0.0), axis=0, keepdims=True)


def pass_kernel(step_rows, order_ref, sol_ref, dir_ref, res_ref, gen_hbm, call_hbm, dose_hbm,
                coded_ref, called_ref, cross_ref, sums_ref, gbuf, cbuf, dbuf, sems, dsem):
    slots = gbuf.shape[0]
    rows = gen_hbm.shape[0]
    steps = rows // step_rows
    rhs = sol_ref.shape[0]

    def copies(step):
        slot = step % slots
        part = pl.ds(step * step_rows, step_rows)
        return (
            pltpu.make_async_copy(gen_hbm.at[part], gbuf.at[slot], sems.at[0, slot]),
            pltpu.make_async_copy(call_hbm.at[part], cbuf.at[slot], sems.at[1, slot]),
        )

    dose_copy = pltpu.make_async_copy(dose_hbm, dbuf, dsem)
    dose_copy.start()
    for step in range(slots):
        for copy in copies(step):
            copy.start()

    sol, dire, res = sol_ref[...], dir_ref[...], res_ref[...]
    total = lambda x: jnp.sum(x, axis=1, keepdims=True)
    sums_ref[...] = columns(
        [total(res * res), total(dire * dire), total(sol), total(sol * sol), total(sol * dire), total(dire)],
        sums_ref.shape,
    )
    sol_high, sol_low = halves(sol)
    dir_high, dir_low = halves(dire)
    stack = jnp.concatenate([sol_high, dir_high, sol_low, dir_low], axis=0)
    own = sol.shape[1]
    hot = lax.broadcasted_iota(jnp.int32, (own, own), 0) == order_ref[...]
    hot = jnp.where(hot, 1.0, 0.0).astype(BF16)
    picked = jnp.dot(stack, hot, preferred_element_type=F32).astype(BF16)
    picked = jnp.concatenate([picked, jnp.ones((16, own), BF16)], axis=0)
    dose_copy.wait()
    dose = dbuf[...].astype(F32).astype(BF16)
    cross = jnp.dot(picked, dose, preferred_element_type=F32)
    cross_ref[: 2 * rhs] = cross[: 2 * rhs] + cross[2 * rhs : 4 * rhs]
    cross_ref[2 * rhs :] = cross[4 * rhs : 4 * rhs + 8]

    for step in range(steps):
        slot = step % slots
        for copy in copies(step):
            copy.wait()

        def group(i, carry):
            part = pl.ds(pl.multiple_of(i * 16, 16), 16)
            out = pl.ds(pl.multiple_of(step * step_rows + i * 16, 16), 16)
            call = cbuf[slot, part, :]
            coded_ref[out, :] = (gbuf[slot, part, :] * call).astype(F32).astype(BF16)
            called_ref[out, :] = call.astype(F32).astype(BF16)
            return carry

        lax.fori_loop(0, step_rows // 16, group, 0)
        if step + slots < steps:
            for copy in copies(step + slots):
                copy.start()


def forward_kernel(block, place_ref, d0_ref, d1_ref, d2_ref, d3_ref, coded_ref, called_ref, sums_ref,
                   out_ref, w1, w2):
    var = place_ref[0]
    rhs, own = d0_ref.shape
    rows = coded_ref.shape[0]
    samples = coded_ref.shape[1]
    row = lax.broadcasted_iota(jnp.int32, (16, samples), 0)
    zero = jnp.zeros((16, samples), BF16)
    w1[16:32] = zero
    w1[32:48] = jnp.where(row == 0, 1.0, 0.0).astype(BF16)
    w2[0:16] = zero
    w2[32:48] = jnp.where(row == 1, 1.0, 0.0).astype(BF16)
    for k, ref in enumerate((d0_ref, d1_ref, d2_ref, d3_ref)):
        part = pl.ds(pl.multiple_of((var ^ k) * own, LANES), own)
        piece = ref[...].astype(BF16)
        w1[0:16, part] = piece
        w2[16:32, part] = piece
    for i in range(rows // block):
        part = pl.ds(i * block, block)
        got = lax.dot_general(coded_ref[part, :], w1[...], NT, preferred_element_type=F32)
        got = got + lax.dot_general(called_ref[part, :], w2[...], NT, preferred_element_type=F32)
        got = jnp.concatenate([got, jnp.zeros((block, LANES - got.shape[1]), F32)], axis=1)
        out_ref[:, i * block : (i + 1) * block] = got.T[: out_ref.shape[0]]
    out_ref[:, rows:] = jnp.zeros((out_ref.shape[0], LANES), F32)
    out_ref[0:16, rows:] = sums_ref[...]


def chunk_of(cross, start, n_var, width):
    wide = cross.shape[1] // n_var
    lane = lane_of((cross.shape[0], LANES))
    tile = (start // LANES) * LANES
    inside = start - tile
    block = jnp.zeros((cross.shape[0], LANES), F32)
    for v in range(n_var):
        piece = cross[:, pl.ds(pl.multiple_of(v * wide + tile, LANES), LANES)]
        turned = pltpu.roll(piece, (v * width - inside + LANES) % LANES, 1)
        block = jnp.where((lane >= v * width) & (lane < (v + 1) * width), turned, block)
    return block


def chips_kernel(n_var, width, place_ref, own_ref, other_ref, cross_ref, cross_other_ref,
                 total_ref, mine_ref, *rest):
    messages, (both,) = rest[:-1], rest[-1:]
    samp = place_ref[1]
    core = samp % 2
    chip = samp // 2
    rows = own_ref.shape[1] - LANES
    total = own_ref[...] + other_ref[...]
    total_ref[...] = total
    both[...] = cross_ref[...] + cross_other_ref[...]
    mine_ref[...] = chunk_of(both, samp * width, n_var, width)

    main = total[0:32, :rows].astype(BF16)
    counts = total[32:34, :rows]
    pieces = []
    for part in halves(counts):
        part = part.astype(F32)
        for which in range(2):
            for j in range(rows // LANES):
                pieces.append(part[which : which + 1, j * LANES : (j + 1) * LANES])
    while len(pieces) < 32:
        pieces.append(jnp.zeros((1, LANES), F32))
    counts = jnp.concatenate(pieces, axis=0).astype(BF16)
    sums = jnp.zeros((16, LANES), F32)
    for part, values in enumerate(thirds(total[0:16, rows:])):
        values = values.astype(F32)
        sums = sums + (pltpu.roll(values, 16 * part, 1) if part else values)
    for k, message in enumerate(messages):
        chunk = chunk_of(both, ((chip ^ (k + 1)) * 2 + core) * width, n_var, width)
        high, low = halves(chunk[0:32])
        dose = jnp.concatenate([p.astype(F32) for p in thirds(chunk[32:33])] + [jnp.zeros((13, LANES), F32)])
        message[:, :rows] = main
        message[:, rows : rows + LANES] = high
        message[:, rows + LANES : rows + 2 * LANES] = low
        message[:, rows + 2 * LANES : rows + 3 * LANES] = counts
        message[:, rows + 3 * LANES :] = jnp.concatenate([sums, dose], axis=0).astype(BF16)


def back_kernel(variants, width, n_arrived, place_ref, total_ref, mine_ref, coded_ref, called_ref, *rest):
    arrived, own_ref, messages = rest[:n_arrived], rest[n_arrived], rest[n_arrived + 1 :]
    var = place_ref[0]
    rows = total_ref.shape[1] - LANES
    lanes = lane_of((16, LANES))

    main = total_ref[0:32, :rows]
    allele, count = total_ref[32:33, :rows], total_ref[33:34, :rows]
    sums = total_ref[0:16, rows:]
    cross = mine_ref[0:32]
    dose = mine_ref[32:33]
    got_counts = jnp.zeros((32, LANES), F32)
    got_last = jnp.zeros((32, LANES), F32)
    for ref in arrived:
        main = main + ref[:, :rows].astype(F32)
        cross = cross + ref[:, rows : rows + LANES].astype(F32)
        cross = cross + ref[:, rows + LANES : rows + 2 * LANES].astype(F32)
        got_counts = got_counts + ref[:, rows + 2 * LANES : rows + 3 * LANES].astype(F32)
        got_last = got_last + ref[:, rows + 3 * LANES :].astype(F32)
    tiles = rows // LANES
    pick = lambda first: jnp.concatenate(
        [got_counts[first + j : first + j + 1] + got_counts[first + 2 * tiles + j : first + 2 * tiles + j + 1]
         for j in range(tiles)], axis=1
    )
    allele = allele + pick(0)
    count = count + pick(tiles)
    last = got_last[0:16]
    sums = sums + last + pltpu.roll(last, LANES - 16, 1) + pltpu.roll(last, LANES - 32, 1)
    dose = dose + got_last[16:17] + got_last[17:18] + got_last[18:19]

    frequency = (allele + 1.0) / (2.0 * count + 2.0)
    spread = jnp.sqrt(2.0 * frequency * (1.0 - frequency))
    loading = (main[0:16] - 2.0 * frequency * main[16:32]) / spread
    scaled = loading / spread
    scaled_a = scaled.astype(BF16)
    scaled_b = (-2.0 * frequency * scaled).astype(BF16)
    square = jnp.sum(loading * loading, axis=1, keepdims=True)
    sums = jnp.where(lanes < 6, sums, 0.0) + jnp.where(lanes == 6, square, 0.0)

    own = own_ref.shape[1] - 2 * LANES

    def term(p):
        part = pl.ds(pl.multiple_of(p * own, LANES), own)
        got = jnp.dot(scaled_a, coded_ref[:, part], preferred_element_type=F32)
        got = got + jnp.dot(scaled_b, called_ref[:, part], preferred_element_type=F32)
        return got / variants

    def segment(values, p):
        turned = pltpu.roll(values, (LANES - p * width) % LANES, 1)
        return jnp.where(lane_of(values.shape) < width, turned, 0.0)

    def cross_block(p, exact):
        chunk = segment(cross, p)
        sol, dire = chunk[0:16], chunk[16:32]
        if exact:
            return sol + pltpu.roll(dire, 32, 1)
        sol_high, sol_low = [x.astype(F32) for x in halves(sol)]
        dir_high, dir_low = [x.astype(F32) for x in halves(dire)]
        return (
            sol_high + pltpu.roll(dir_high, 32, 1) + pltpu.roll(sol_low, 64, 1) + pltpu.roll(dir_low, 96, 1)
        )

    row = lax.broadcasted_iota(jnp.int32, (16, LANES), 0)

    def sums_block(p, exact):
        own_dose = segment(jnp.broadcast_to(dose, (16, LANES)), p)
        own_dose = pltpu.roll(own_dose, 64, 1)
        if exact:
            return sums + jnp.where(row == 0, own_dose, 0.0)
        block = jnp.zeros((16, LANES), F32)
        for part, values in enumerate(thirds(sums)):
            values = values.astype(F32)
            block = block + (pltpu.roll(values, 16 * part, 1) if part else values)
        for part, values in enumerate(thirds(own_dose)):
            block = block + jnp.where(row == part, values.astype(F32), 0.0)
        return block

    for k, ref in enumerate(messages):
        p = var ^ (k + 1)
        ref[:, :own] = term(p).astype(BF16)
        ref[:, own : own + LANES] = cross_block(p, False).astype(BF16)
        ref[:, own + LANES :] = sums_block(p, False).astype(BF16)
    own_ref[:, :own] = term(var)
    own_ref[:, own : own + LANES] = cross_block(var, True)
    own_ref[:, own + LANES :] = sums_block(var, True)


def step_of(refs, noise_row, variants):
    got = refs[0][...]
    for ref in refs[1:]:
        got = got + ref[...].astype(F32)
    own = got.shape[1] - 2 * LANES
    back, cross, last = got[:, :own], got[:, own : own + LANES], got[:, own + LANES :]
    sums = last + pltpu.roll(last, LANES - 16, 1) + pltpu.roll(last, LANES - 32, 1)
    column = lambda q: sums[:, q : q + 1]
    noise = to_column(noise_row)
    curvature = noise * column(1) + column(6) / variants
    step = column(0) / (curvature + 1e-06)
    return back, cross, last, column, noise, step


def norm_kernel(variants, noise_ref, dir_ref, res_ref, *rest):
    out_ref = rest[-1]
    back, _, _, _, noise, step = step_of(rest[:-1], noise_ref[...], variants)
    new = res_ref[...] - step * (noise * dir_ref[...] + back)
    row = to_row(jnp.sum(new * new, axis=1, keepdims=True))
    out_ref[...] = jnp.broadcast_to(row[None], out_ref.shape)


def new_kernel(variants, samples, width, noise_ref, dir_ref, res_ref, sol_ref, *rest):
    refs, (sol_out, res_out, score_out, norm_out) = rest[:-4], rest[-4:]
    back, cross, last, column, noise, step = step_of(refs, noise_ref[...], variants)
    dire = dir_ref[...]
    sol_out[...] = sol_ref[...] + step * dire
    res_out[...] = res_ref[...] - step * (noise * dire + back)
    norm_out[...] = jnp.broadcast_to(column(0), norm_out.shape)
    cross = cross + pltpu.roll(cross, LANES - 64, 1)
    cross = cross + step * pltpu.roll(cross, LANES - 32, 1)
    dose = pltpu.roll(last, LANES - 64, 1)
    dose = dose[0:1] + dose[1:2] + dose[2:3]
    sol_sum = column(2) + step * column(5)
    sol_square = column(3) + 2.0 * step * column(4) + step * (step * column(1))
    dose_freq = (dose / 100.0 + 1.0) / (2.0 * samples + 2.0)
    dose_spread = jnp.sqrt(2.0 * dose_freq * (1.0 - dose_freq))
    scale = math.sqrt(samples) * jnp.sqrt(sol_square / samples + 1e-06)
    scores = (cross / 100.0 - 2.0 * dose_freq * sol_sum) / (dose_spread * scale)
    score_out[...] = scores[:, :width]


def direction_kernel(norms_ref, norm_ref, res_ref, dir_ref, out_ref):
    new_norm = to_column(jnp.sum(norms_ref[...], axis=0))
    out_ref[...] = res_ref[...] + (new_norm / (norm_ref[:, 0:1] + 1e-06)) * dir_ref[...]


def call(kernel, out, ins, args, scratch=(), limit=16, flops=0, moved=0):
    return pl.pallas_call(
        kernel,
        out_shape=[jax.ShapeDtypeStruct(*o) for o in out],
        in_specs=list(ins),
        out_specs=[VMEM] * len(out),
        scratch_shapes=list(scratch),
        compiler_params=pltpu.CompilerParams(vmem_limit_bytes=limit * MIB),
        cost_estimate=pl.CostEstimate(flops=flops, bytes_accessed=moved, transcendentals=0),
    )(*args)


def body(genotypes, called, dosage, sample_order, noise_ratio, solution, residual, direction):
    var = lax.axis_index("var").astype(jnp.int32)
    samp = lax.axis_index("samp").astype(jnp.int32)
    n_var = lax.axis_size("var")
    n_samp = lax.axis_size("samp")
    own, rhs = direction.shape
    rows, shard = genotypes.shape
    variants = rows * n_var
    samples = own * n_samp * n_var
    imputed = dosage.shape[1]
    width = imputed // (n_var * n_samp)
    place = jnp.stack([var, samp])
    noise = jnp.pad(noise_ratio, (0, LANES - rhs))[None]

    dire, res, sol = direction.T, residual.T, solution.T
    pieces = [dire] + [swap(dire, "var", k) for k in range(1, n_var)]

    step_rows = 128
    slots = 3
    coded, called_b, cross, sums = call(
        functools.partial(pass_kernel, step_rows),
        [((rows, shard), BF16), ((rows, shard), BF16), ((2 * rhs + 8, imputed), F32), ((rhs, LANES), F32)],
        [VMEM] * 4 + [ANY] * 3,
        (sample_order, sol, dire, res, genotypes, called, dosage),
        scratch=[
            pltpu.VMEM((slots, step_rows, shard), jnp.int32),
            pltpu.VMEM((slots, step_rows, shard), jnp.int32),
            pltpu.VMEM((own, imputed), jnp.int32),
            pltpu.SemaphoreType.DMA((2, slots)),
            pltpu.SemaphoreType.DMA,
        ],
        limit=32,
        flops=2 * 80 * own * (own + imputed),
        moved=4 * (2 * rows * shard + own * imputed),
    )
    cross_other = swap(cross, "samp", 1)

    (part,) = call(
        functools.partial(forward_kernel, 128),
        [((2 * rhs + 8, rows + LANES), F32)],
        [SMEM] + [VMEM] * (n_var + 3),
        (place, *pieces, coded, called_b, sums),
        scratch=[pltpu.VMEM((48, shard), BF16), pltpu.VMEM((48, shard), BF16)],
        flops=4 * rows * shard * 256,
        moved=4 * rows * shard,
    )
    part_other = swap(part, "samp", 1)

    n_chips = n_samp // 2
    message = ((2 * rhs, rows + 4 * LANES), BF16)
    total, mine, *messages = call(
        functools.partial(chips_kernel, n_var, width),
        [(part.shape, F32), ((2 * rhs + 8, LANES), F32)] + [message] * (n_chips - 1),
        [SMEM] + [VMEM] * 4,
        (place, part, part_other, cross, cross_other),
        scratch=[pltpu.VMEM(cross.shape, F32)],
        moved=1 * MIB,
    )
    arrived = [swap(m, "samp", 2 * (k + 1)) for k, m in enumerate(messages)]

    wide = own + 2 * LANES
    mine_back, *messages = call(
        functools.partial(back_kernel, variants, width, n_chips - 1),
        [((rhs, wide), F32)] + [((rhs, wide), BF16)] * (n_var - 1),
        [SMEM] + [VMEM] * (4 + n_chips - 1),
        (place, total, mine, coded, called_b, *arrived),
        flops=4 * rows * shard * 256,
        moved=4 * rows * shard,
    )
    backs = [mine_back] + [swap(m, "var", k + 1) for k, m in enumerate(messages)]

    n_all = n_var * n_samp
    (norms,) = call(
        functools.partial(norm_kernel, variants),
        [((n_all, 1, LANES), F32)],
        [VMEM] * (3 + n_var),
        (noise, dire, res, *backs),
        moved=4 * n_all * LANES,
    )
    norms = lax.all_to_all(norms, ("var", "samp"), split_axis=0, concat_axis=0)
    sol_new, res_new, scores, res_norm = call(
        functools.partial(new_kernel, variants, samples, width),
        [((rhs, own), F32), ((rhs, own), F32), ((rhs, width), F32), ((rhs, LANES), F32)],
        [VMEM] * (4 + n_var),
        (noise, dire, res, sol, *backs),
        moved=1 * MIB,
    )
    (dir_new,) = call(
        direction_kernel,
        [((rhs, own), F32)],
        [VMEM] * 4,
        (norms, res_norm, res_new, dire),
    )
    return (sol_new.T, res_new.T, dir_new.T, scores.T)


def solution(mesh):
    placed = (
        P("var", "samp"),
        P("var", "samp"),
        P(("samp", "var"), None),
        P(("samp", "var"), None),
        P(),
        P(("samp", "var"), None),
        P(("samp", "var"), None),
        P(("samp", "var"), None),
    )
    return jax.shard_map(
        body,
        mesh=mesh,
        in_specs=placed,
        out_specs=(
            P(("samp", "var"), None),
            P(("samp", "var"), None),
            P(("samp", "var"), None),
            P(("var", "samp"), None),
        ),
        check_vma=False,
    )
```

```python
import functools
import math

import jax
import jax.numpy as jnp
from jax import lax
from jax.experimental import pallas as pl
from jax.experimental.pallas import tpu as pltpu
from jax.sharding import PartitionSpec as P

BF16 = jnp.bfloat16
F32 = jnp.float32
LANES = 128
NT = (((1,), (1,)), ((), ()))
VMEM = pl.BlockSpec(memory_space=pltpu.VMEM)
HBM = pl.BlockSpec(memory_space=pltpu.HBM)
MIB = 1 << 20


def swap(values, axis, distance):
    size = lax.axis_size(axis)
    return lax.ppermute(values, axis, [(i, i ^ distance) for i in range(size)])


def halves(values):
    high = values.astype(BF16)
    return high, (values - high.astype(F32)).astype(BF16)


def thirds(values):
    high = values.astype(BF16)
    rest = values - high.astype(F32)
    middle = rest.astype(BF16)
    return high, middle, (rest - middle.astype(F32)).astype(BF16)


def lane_of(shape):
    return lax.broadcasted_iota(jnp.int32, shape, len(shape) - 1)


def columns(values, shape):
    lane = lane_of(shape)
    block = jnp.zeros(shape, F32)
    for q, column in enumerate(values):
        block = jnp.where(lane == q, column, block)
    return block


def to_column(row):
    shape = (16, row.shape[1])
    same = lax.broadcasted_iota(jnp.int32, shape, 0) == lane_of(shape)
    return jnp.sum(jnp.where(same, row, 0.0), axis=1, keepdims=True)


def to_row(column):
    shape = (16, LANES)
    same = lax.broadcasted_iota(jnp.int32, shape, 0) == lane_of(shape)
    return jnp.sum(jnp.where(same, column, 0.0), axis=0, keepdims=True)


def pass_kernel(step_rows, order_hbm, sol_hbm, dir_hbm, res_hbm, gen_hbm, call_hbm, dose_hbm,
                coded_ref, called_ref, cross_ref, sums_ref, gbuf, cbuf, dbuf, order_ref, sol_ref, dir_ref, res_ref,
                sems, small_sems):
    slots = gbuf.shape[0]
    rows = gen_hbm.shape[0]
    steps = rows // step_rows
    rhs = sol_hbm.shape[0]

    def copies(step):
        slot = step % slots
        part = pl.ds(step * step_rows, step_rows)
        return (
            pltpu.make_async_copy(gen_hbm.at[part], gbuf.at[slot], sems.at[0, slot]),
            pltpu.make_async_copy(call_hbm.at[part], cbuf.at[slot], sems.at[1, slot]),
        )

    small = [
        pltpu.make_async_copy(source, target, small_sems.at[i])
        for i, (source, target) in enumerate(
            ((order_hbm, order_ref), (sol_hbm, sol_ref), (dir_hbm, dir_ref), (res_hbm, res_ref), (dose_hbm, dbuf))
        )
    ]
    for copy in small:
        copy.start()
    for step in range(slots):
        for copy in copies(step):
            copy.start()

    for copy in small[:4]:
        copy.wait()
    sol, dire, res = sol_ref[...], dir_ref[...], res_ref[...]
    total = lambda x: jnp.sum(x, axis=1, keepdims=True)
    sums_ref[...] = columns(
        [total(res * res), total(dire * dire), total(sol), total(sol * sol), total(sol * dire), total(dire)],
        sums_ref.shape,
    )
    sol_high, sol_low = halves(sol)
    dir_high, dir_low = halves(dire)
    stack = jnp.concatenate([sol_high, dir_high, sol_low, dir_low], axis=0)
    own = sol.shape[1]
    hot = lax.broadcasted_iota(jnp.int32, (own, own), 0) == order_ref[...]
    hot = jnp.where(hot, 1.0, 0.0).astype(BF16)
    picked = jnp.dot(stack, hot, preferred_element_type=F32).astype(BF16)
    picked = jnp.concatenate([picked, jnp.ones((16, own), BF16)], axis=0)
    small[4].wait()
    dose = dbuf[...].astype(F32).astype(BF16)
    cross = jnp.dot(picked, dose, preferred_element_type=F32)
    cross_ref[: 2 * rhs] = cross[: 2 * rhs] + cross[2 * rhs : 4 * rhs]
    cross_ref[2 * rhs :] = cross[4 * rhs : 4 * rhs + 8]

    for step in range(steps):
        slot = step % slots
        for copy in copies(step):
            copy.wait()

        def group(i, carry):
            part = pl.ds(pl.multiple_of(i * 16, 16), 16)
            out = pl.ds(pl.multiple_of(step * step_rows + i * 16, 16), 16)
            call = cbuf[slot, part, :]
            coded_ref[out, :] = (gbuf[slot, part, :] * call).astype(F32).astype(BF16)
            called_ref[out, :] = call.astype(F32).astype(BF16)
            return carry

        lax.fori_loop(0, step_rows // 16, group, 0)
        if step + slots < steps:
            for copy in copies(step + slots):
                copy.start()


def forward_kernel(block, d0_ref, d1_ref, d2_ref, d3_ref, coded_ref, called_ref, sums_ref,
                   out_ref, w1, w2):
    var = lax.axis_index("var")
    own = d0_ref.shape[1]
    rows = coded_ref.shape[0]
    samples = coded_ref.shape[1]
    row = lax.broadcasted_iota(jnp.int32, (16, samples), 0)
    zero = jnp.zeros((16, samples), BF16)
    w1[16:32] = zero
    w1[32:48] = jnp.where(row == 0, 1.0, 0.0).astype(BF16)
    w2[0:16] = zero
    w2[32:48] = jnp.where(row == 1, 1.0, 0.0).astype(BF16)
    for k, ref in enumerate((d0_ref, d1_ref, d2_ref, d3_ref)):
        part = pl.ds(pl.multiple_of((var ^ k) * own, LANES), own)
        piece = ref[...].astype(BF16)
        w1[0:16, part] = piece
        w2[16:32, part] = piece
    for i in range(rows // block):
        part = pl.ds(i * block, block)
        got = lax.dot_general(coded_ref[part, :], w1[...], NT, preferred_element_type=F32)
        got = got + lax.dot_general(called_ref[part, :], w2[...], NT, preferred_element_type=F32)
        got = jnp.concatenate([got, jnp.zeros((block, LANES - got.shape[1]), F32)], axis=1)
        out_ref[:, i * block : (i + 1) * block] = got.T[: out_ref.shape[0]]
    out_ref[:, rows:] = jnp.zeros((out_ref.shape[0], LANES), F32)
    out_ref[0:16, rows:] = sums_ref[...]


def chunk_of(cross, start, n_var, width):
    wide = cross.shape[1] // n_var
    lane = lane_of((cross.shape[0], LANES))
    tile = (start // LANES) * LANES
    inside = start - tile
    block = jnp.zeros((cross.shape[0], LANES), F32)
    for v in range(n_var):
        piece = cross[:, pl.ds(pl.multiple_of(v * wide + tile, LANES), LANES)]
        turned = pltpu.roll(piece, (v * width - inside + LANES) % LANES, 1)
        block = jnp.where((lane >= v * width) & (lane < (v + 1) * width), turned, block)
    return block


def chips_kernel(n_var, width, own_ref, other_ref, cross_ref, cross_other_ref,
                 total_ref, mine_ref, *rest):
    messages, (both,) = rest[:-1], rest[-1:]
    samp = lax.axis_index("samp")
    core = samp % 2
    chip = samp // 2
    rows = own_ref.shape[1] - LANES
    total = own_ref[...] + other_ref[...]
    total_ref[...] = total
    both[...] = cross_ref[...] + cross_other_ref[...]
    mine_ref[...] = chunk_of(both, samp * width, n_var, width)

    main = total[0:32, :rows].astype(BF16)
    counts = total[32:34, :rows]
    pieces = []
    for part in halves(counts):
        part = part.astype(F32)
        for which in range(2):
            for j in range(rows // LANES):
                pieces.append(part[which : which + 1, j * LANES : (j + 1) * LANES])
    while len(pieces) < 32:
        pieces.append(jnp.zeros((1, LANES), F32))
    counts = jnp.concatenate(pieces, axis=0).astype(BF16)
    sums = jnp.zeros((16, LANES), F32)
    for part, values in enumerate(thirds(total[0:16, rows:])):
        values = values.astype(F32)
        sums = sums + (pltpu.roll(values, 16 * part, 1) if part else values)
    for k, message in enumerate(messages):
        chunk = chunk_of(both, ((chip ^ (k + 1)) * 2 + core) * width, n_var, width)
        high, low = halves(chunk[0:32])
        dose = jnp.concatenate([p.astype(F32) for p in thirds(chunk[32:33])] + [jnp.zeros((13, LANES), F32)])
        message[:, :rows] = main
        message[:, rows : rows + LANES] = high
        message[:, rows + LANES : rows + 2 * LANES] = low
        message[:, rows + 2 * LANES : rows + 3 * LANES] = counts
        message[:, rows + 3 * LANES :] = jnp.concatenate([sums, dose], axis=0).astype(BF16)


def back_kernel(variants, width, n_arrived, total_ref, mine_ref, coded_ref, called_ref, *rest):
    arrived, own_ref, messages = rest[:n_arrived], rest[n_arrived], rest[n_arrived + 1 :]
    var = lax.axis_index("var")
    rows = total_ref.shape[1] - LANES
    lanes = lane_of((16, LANES))

    main = total_ref[0:32, :rows]
    allele, count = total_ref[32:33, :rows], total_ref[33:34, :rows]
    sums = total_ref[0:16, rows:]
    cross = mine_ref[0:32]
    dose = mine_ref[32:33]
    got_counts = jnp.zeros((32, LANES), F32)
    got_last = jnp.zeros((32, LANES), F32)
    for ref in arrived:
        main = main + ref[:, :rows].astype(F32)
        cross = cross + ref[:, rows : rows + LANES].astype(F32)
        cross = cross + ref[:, rows + LANES : rows + 2 * LANES].astype(F32)
        got_counts = got_counts + ref[:, rows + 2 * LANES : rows + 3 * LANES].astype(F32)
        got_last = got_last + ref[:, rows + 3 * LANES :].astype(F32)
    tiles = rows // LANES
    pick = lambda first: jnp.concatenate(
        [got_counts[first + j : first + j + 1] + got_counts[first + 2 * tiles + j : first + 2 * tiles + j + 1]
         for j in range(tiles)], axis=1
    )
    allele = allele + pick(0)
    count = count + pick(tiles)
    last = got_last[0:16]
    sums = sums + last + pltpu.roll(last, LANES - 16, 1) + pltpu.roll(last, LANES - 32, 1)
    dose = dose + got_last[16:17] + got_last[17:18] + got_last[18:19]

    frequency = (allele + 1.0) / (2.0 * count + 2.0)
    spread = jnp.sqrt(2.0 * frequency * (1.0 - frequency))
    loading = (main[0:16] - 2.0 * frequency * main[16:32]) / spread
    scaled = loading / spread
    scaled_a = scaled.astype(BF16)
    scaled_b = (-2.0 * frequency * scaled).astype(BF16)
    square = jnp.sum(loading * loading, axis=1, keepdims=True)
    sums = jnp.where(lanes < 6, sums, 0.0) + jnp.where(lanes == 6, square, 0.0)

    own = own_ref.shape[1] - 2 * LANES

    def term(p):
        part = pl.ds(pl.multiple_of(p * own, LANES), own)
        got = jnp.dot(scaled_a, coded_ref[:, part], preferred_element_type=F32)
        got = got + jnp.dot(scaled_b, called_ref[:, part], preferred_element_type=F32)
        return got / variants

    def segment(values, p):
        turned = pltpu.roll(values, (LANES - p * width) % LANES, 1)
        return jnp.where(lane_of(values.shape) < width, turned, 0.0)

    def cross_block(p, exact):
        chunk = segment(cross, p)
        sol, dire = chunk[0:16], chunk[16:32]
        if exact:
            return sol + pltpu.roll(dire, 32, 1)
        sol_high, sol_low = [x.astype(F32) for x in halves(sol)]
        dir_high, dir_low = [x.astype(F32) for x in halves(dire)]
        return (
            sol_high + pltpu.roll(dir_high, 32, 1) + pltpu.roll(sol_low, 64, 1) + pltpu.roll(dir_low, 96, 1)
        )

    row = lax.broadcasted_iota(jnp.int32, (16, LANES), 0)

    def sums_block(p, exact):
        own_dose = segment(jnp.broadcast_to(dose, (16, LANES)), p)
        own_dose = pltpu.roll(own_dose, 64, 1)
        if exact:
            return sums + jnp.where(row == 0, own_dose, 0.0)
        block = jnp.zeros((16, LANES), F32)
        for part, values in enumerate(thirds(sums)):
            values = values.astype(F32)
            block = block + (pltpu.roll(values, 16 * part, 1) if part else values)
        for part, values in enumerate(thirds(own_dose)):
            block = block + jnp.where(row == part, values.astype(F32), 0.0)
        return block

    for k, ref in enumerate(messages):
        p = var ^ (k + 1)
        ref[:, :own] = term(p).astype(BF16)
        ref[:, own : own + LANES] = cross_block(p, False).astype(BF16)
        ref[:, own + LANES :] = sums_block(p, False).astype(BF16)
    own_ref[:, :own] = term(var)
    own_ref[:, own : own + LANES] = cross_block(var, True)
    own_ref[:, own + LANES :] = sums_block(var, True)


def step_of(refs, noise_row, variants):
    got = refs[0][...]
    for ref in refs[1:]:
        got = got + ref[...].astype(F32)
    own = got.shape[1] - 2 * LANES
    back, cross, last = got[:, :own], got[:, own : own + LANES], got[:, own + LANES :]
    sums = last + pltpu.roll(last, LANES - 16, 1) + pltpu.roll(last, LANES - 32, 1)
    column = lambda q: sums[:, q : q + 1]
    noise = to_column(noise_row)
    curvature = noise * column(1) + column(6) / variants
    step = column(0) / (curvature + 1e-06)
    return back, cross, last, column, noise, step


def norm_kernel(variants, noise_ref, dir_ref, res_ref, *rest):
    refs, (out_ref, new_ref) = rest[:-2], rest[-2:]
    back, _, _, _, noise, step = step_of(refs, noise_ref[...], variants)
    new = res_ref[...] - step * (noise * dir_ref[...] + back)
    new_ref[...] = new
    row = to_row(jnp.sum(new * new, axis=1, keepdims=True))
    out_ref[...] = jnp.broadcast_to(row[None], out_ref.shape)


def new_kernel(variants, samples, width, noise_ref, dir_ref, res_ref, sol_ref, *rest):
    refs, (sol_out, res_out, score_out, norm_out) = rest[:-4], rest[-4:]
    back, cross, last, column, noise, step = step_of(refs, noise_ref[...], variants)
    dire = dir_ref[...]
    sol_out[...] = sol_ref[...] + step * dire
    res_out[...] = res_ref[...] - step * (noise * dire + back)
    norm_out[...] = jnp.broadcast_to(column(0), norm_out.shape)
    cross = cross + pltpu.roll(cross, LANES - 64, 1)
    cross = cross + step * pltpu.roll(cross, LANES - 32, 1)
    dose = pltpu.roll(last, LANES - 64, 1)
    dose = dose[0:1] + dose[1:2] + dose[2:3]
    sol_sum = column(2) + step * column(5)
    sol_square = column(3) + 2.0 * step * column(4) + step * (step * column(1))
    dose_freq = (dose / 100.0 + 1.0) / (2.0 * samples + 2.0)
    dose_spread = jnp.sqrt(2.0 * dose_freq * (1.0 - dose_freq))
    scale = math.sqrt(samples) * jnp.sqrt(sol_square / samples + 1e-06)
    scores = (cross / 100.0 - 2.0 * dose_freq * sol_sum) / (dose_spread * scale)
    score_out[...] = scores[:, :width]


def direction_kernel(norms_ref, norm_ref, res_ref, dir_ref, out_ref):
    new_norm = to_column(jnp.sum(norms_ref[...], axis=0))
    out_ref[...] = res_ref[...] + (new_norm / (norm_ref[:, 0:1] + 1e-06)) * dir_ref[...]


def call(kernel, out, ins, args, scratch=(), limit=16, flops=0, moved=0):
    return pl.pallas_call(
        kernel,
        out_shape=[jax.ShapeDtypeStruct(*o) if len(o) == 2 else o[2](*o[:2]) for o in out],
        in_specs=list(ins),
        out_specs=[VMEM] * len(out),
        scratch_shapes=list(scratch),
        compiler_params=pltpu.CompilerParams(vmem_limit_bytes=limit * MIB),
        cost_estimate=pl.CostEstimate(flops=flops, bytes_accessed=moved, transcendentals=0),
    )(*[pltpu.with_memory_space_constraint(x, pltpu.HBM) if spec is HBM else x for spec, x in zip(ins, args)])


def body(genotypes, called, dosage, sample_order, noise_ratio, solution, residual, direction):
    n_var = lax.axis_size("var")
    n_samp = lax.axis_size("samp")
    own, rhs = direction.shape
    rows, shard = genotypes.shape
    variants = rows * n_var
    samples = own * n_samp * n_var
    imputed = dosage.shape[1]
    width = imputed // (n_var * n_samp)
    noise = noise_ratio[None]

    dire, res, sol = direction.T, residual.T, solution.T
    pieces = [dire] + [swap(dire, "var", k) for k in range(1, n_var)]

    step_rows = 128
    slots = 3
    coded, called_b, cross, sums = call(
        functools.partial(pass_kernel, step_rows),
        [((rows, shard), BF16, pltpu.VMEM), ((rows, shard), BF16, pltpu.VMEM), ((2 * rhs + 8, imputed), F32), ((rhs, LANES), F32)],
        [HBM] * 7,
        (sample_order, sol, dire, res, genotypes, called, dosage),
        scratch=[
            pltpu.VMEM((slots, step_rows, shard), jnp.int32),
            pltpu.VMEM((slots, step_rows, shard), jnp.int32),
            pltpu.VMEM((own, imputed), jnp.int32),
            pltpu.VMEM((1, own), jnp.int32),
            pltpu.VMEM((rhs, own), F32),
            pltpu.VMEM((rhs, own), F32),
            pltpu.VMEM((rhs, own), F32),
            pltpu.SemaphoreType.DMA((2, slots)),
            pltpu.SemaphoreType.DMA((5,)),
        ],
        limit=32,
        flops=2 * 80 * own * (own + imputed),
        moved=4 * (2 * rows * shard + own * imputed),
    )
    cross_other = swap(cross, "samp", 1)

    (part,) = call(
        functools.partial(forward_kernel, 128),
        [((2 * rhs + 8, rows + LANES), F32)],
        [VMEM] * (n_var + 3),
        (*pieces, coded, called_b, sums),
        scratch=[pltpu.VMEM((48, shard), BF16), pltpu.VMEM((48, shard), BF16)],
        flops=4 * rows * shard * 256,
        moved=4 * rows * shard,
    )
    part_other = swap(part, "samp", 1)

    n_chips = n_samp // 2
    message = ((2 * rhs, rows + 4 * LANES), BF16)
    total, mine, *messages = call(
        functools.partial(chips_kernel, n_var, width),
        [(part.shape, F32), ((2 * rhs + 8, LANES), F32)] + [message] * (n_chips - 1),
        [VMEM] * 4,
        (part, part_other, cross, cross_other),
        scratch=[pltpu.VMEM(cross.shape, F32)],
        moved=1 * MIB,
    )
    arrived = [swap(m, "samp", 2 * (k + 1)) for k, m in enumerate(messages)]

    wide = own + 2 * LANES
    mine_back, *messages = call(
        functools.partial(back_kernel, variants, width, n_chips - 1),
        [((rhs, wide), F32)] + [((rhs, wide), BF16)] * (n_var - 1),
        [VMEM] * (4 + n_chips - 1),
        (total, mine, coded, called_b, *arrived),
        flops=4 * rows * shard * 256,
        moved=4 * rows * shard,
    )
    backs = [mine_back] + [swap(m, "var", k + 1) for k, m in enumerate(messages)]

    n_all = n_var * n_samp
    norms, res_keep = call(
        functools.partial(norm_kernel, variants),
        [((n_all, 1, LANES), F32), ((rhs, own), F32)],
        [VMEM] * (3 + n_var),
        (noise, dire, res, *backs),
        moved=4 * n_all * LANES,
    )
    norms = lax.all_to_all(norms, ("var", "samp"), split_axis=0, concat_axis=0)
    sol_new, res_new, scores, res_norm = call(
        functools.partial(new_kernel, variants, samples, width),
        [((rhs, own), F32), ((rhs, own), F32), ((rhs, width), F32), ((rhs, LANES), F32)],
        [VMEM] * (4 + n_var),
        (noise, dire, res, sol, *backs),
        moved=1 * MIB,
    )
    (dir_new,) = call(
        direction_kernel,
        [((rhs, own), F32)],
        [VMEM] * 4,
        (norms, res_norm, res_keep, dire),
    )
    return (sol_new.T, res_new.T, dir_new.T, scores.T)


def solution(mesh):
    placed = (
        P("var", "samp"),
        P("var", "samp"),
        P(("samp", "var"), None),
        P(("samp", "var"), None),
        P(),
        P(("samp", "var"), None),
        P(("samp", "var"), None),
        P(("samp", "var"), None),
    )
    return jax.shard_map(
        body,
        mesh=mesh,
        in_specs=placed,
        out_specs=(
            P(("samp", "var"), None),
            P(("samp", "var"), None),
            P(("samp", "var"), None),
            P(("var", "samp"), None),
        ),
        check_vma=False,
    )
```

```python
import functools
import math

import jax
import jax.numpy as jnp
from jax import lax
from jax.experimental import pallas as pl
from jax.experimental.pallas import tpu as pltpu
from jax.sharding import PartitionSpec as P

BF16 = jnp.bfloat16
F32 = jnp.float32
LANES = 128
NT = (((1,), (1,)), ((), ()))
VMEM = pl.BlockSpec(memory_space=pltpu.VMEM)
HBM = pl.BlockSpec(memory_space=pltpu.HBM)
MIB = 1 << 20


def swap(values, axis, distance):
    size = lax.axis_size(axis)
    return lax.ppermute(values, axis, [(i, i ^ distance) for i in range(size)])


def halves(values):
    high = values.astype(BF16)
    return high, (values - high.astype(F32)).astype(BF16)


def thirds(values):
    high = values.astype(BF16)
    rest = values - high.astype(F32)
    middle = rest.astype(BF16)
    return high, middle, (rest - middle.astype(F32)).astype(BF16)


def lane_of(shape):
    return lax.broadcasted_iota(jnp.int32, shape, len(shape) - 1)


def columns(values, shape):
    lane = lane_of(shape)
    block = jnp.zeros(shape, F32)
    for q, column in enumerate(values):
        block = jnp.where(lane == q, column, block)
    return block


def to_column(row):
    shape = (16, row.shape[1])
    same = lax.broadcasted_iota(jnp.int32, shape, 0) == lane_of(shape)
    return jnp.sum(jnp.where(same, row, 0.0), axis=1, keepdims=True)


def to_row(column):
    shape = (16, LANES)
    same = lax.broadcasted_iota(jnp.int32, shape, 0) == lane_of(shape)
    return jnp.sum(jnp.where(same, column, 0.0), axis=0, keepdims=True)


def convert(gen_ref, call_ref, coded_ref, called_ref, first, rows):
    def group(i, carry):
        part = pl.ds(pl.multiple_of(first + i * 16, 16), 16)
        call = call_ref[part, :].astype(F32).astype(BF16)
        coded_ref[part, :] = gen_ref[part, :].astype(F32).astype(BF16) * call
        called_ref[part, :] = call
        return carry

    lax.fori_loop(0, rows // 16, group, 0)


def row_copies(first, chunk, rows, pairs, sems):
    return [
        [
            pltpu.make_async_copy(
                source.at[pl.ds(first + i * chunk, chunk)], target.at[pl.ds(i * chunk, chunk)], sems.at[j, i]
            )
            for j, (source, target) in enumerate(pairs)
        ]
        for i in range(rows // chunk)
    ]


def first_kernel(chunk, order_hbm, sol_hbm, dir_hbm, res_hbm, gen_hbm, call_hbm, dose_hbm,
                 coded_ref, called_ref, cross_ref, sums_ref,
                 order_ref, sol_ref, dir_ref, res_ref, gbuf, cbuf, dbuf, small_sems, sems):
    rhs = sol_hbm.shape[0]
    rows = gbuf.shape[0]
    small = [
        pltpu.make_async_copy(source, target, small_sems.at[i])
        for i, (source, target) in enumerate(
            ((order_hbm, order_ref), (sol_hbm, sol_ref), (dir_hbm, dir_ref), (res_hbm, res_ref), (dose_hbm, dbuf))
        )
    ]
    for copy in small:
        copy.start()
    parts = row_copies(0, chunk, rows, ((gen_hbm, gbuf), (call_hbm, cbuf)), sems)
    for part in parts:
        for copy in part:
            copy.start()
    for copy in small[:4]:
        copy.wait()
    sol, dire, res = sol_ref[...], dir_ref[...], res_ref[...]
    total = lambda x: jnp.sum(x, axis=1, keepdims=True)
    sums_ref[...] = columns(
        [total(res * res), total(dire * dire), total(sol), total(sol * sol), total(sol * dire), total(dire)],
        sums_ref.shape,
    )
    sol_high, sol_low = halves(sol)
    dir_high, dir_low = halves(dire)
    stack = jnp.concatenate([sol_high, dir_high, sol_low, dir_low], axis=0)
    own = sol.shape[1]
    hot = lax.broadcasted_iota(jnp.int32, (own, own), 0) == order_ref[...]
    hot = jnp.where(hot, 1.0, 0.0).astype(BF16)
    picked = jnp.dot(stack, hot, preferred_element_type=F32).astype(BF16)
    picked = jnp.concatenate([picked, jnp.ones((16, own), BF16)], axis=0)
    small[4].wait()
    dose = dbuf[...].astype(F32).astype(BF16)
    cross = jnp.dot(picked, dose, preferred_element_type=F32)
    cross_ref[: 2 * rhs] = cross[: 2 * rhs] + cross[2 * rhs : 4 * rhs]
    cross_ref[2 * rhs :] = cross[4 * rhs : 4 * rhs + 8]
    for i, part in enumerate(parts):
        for copy in part:
            copy.wait()
        convert(gbuf, cbuf, coded_ref, called_ref, i * chunk, chunk)


def pair_kernel(own_ref, other_ref, out_ref):
    upper = lax.axis_index("var") % 2
    rhs = own_ref.shape[0]
    own, other = own_ref[...], other_ref[...]
    out_ref[:rhs] = jnp.where(upper == 0, own, other).astype(BF16)
    out_ref[rhs:] = jnp.where(upper == 0, other, own).astype(BF16)


def weights(pair_ref, w1, w2):
    own = pair_ref.shape[1]
    zero = jnp.zeros((16, 2 * own), BF16)
    row = lax.broadcasted_iota(jnp.int32, (16, 2 * own), 0)
    w1[16:32] = zero
    w1[32:48] = jnp.where(row == 0, 1.0, 0.0).astype(BF16)
    w2[0:16] = zero
    w2[32:48] = jnp.where(row == 1, 1.0, 0.0).astype(BF16)
    for i in range(2):
        piece = pair_ref[16 * i : 16 * i + 16]
        w1[0:16, i * own : (i + 1) * own] = piece
        w2[16:32, i * own : (i + 1) * own] = piece


def product(coded_ref, called_ref, first, rows, samples, w1, w2):
    part = pl.ds(first, rows)
    got = lax.dot_general(coded_ref[part, samples], w1[...], NT, preferred_element_type=F32)
    got = got + lax.dot_general(called_ref[part, samples], w2[...], NT, preferred_element_type=F32)
    got = jnp.concatenate([got, jnp.zeros((rows, LANES - got.shape[1]), F32)], axis=1)
    return got.T[:40]


def pair_samples(pair, own):
    return pl.ds(pl.multiple_of(pair * 2 * own, LANES), 2 * own)


def second_kernel(chunk, pair_ref, coded_first, called_first, gen_hbm, call_hbm,
                  coded_ref, called_ref, out_ref, gbuf, cbuf, w1, w2, sems):
    first, rows = coded_first.shape[0], gbuf.shape[0]
    own = pair_ref.shape[1]
    parts = row_copies(first, chunk, rows, ((gen_hbm, gbuf), (call_hbm, cbuf)), sems)
    for part in parts:
        for copy in part:
            copy.start()
    samples = pair_samples(lax.axis_index("var") // 2, own)
    weights(pair_ref, w1, w2)
    for i in range(first // LANES):
        place = i * LANES
        out_ref[:, place : place + LANES] = product(coded_first, called_first, place, LANES, samples, w1, w2)
    for i, part in enumerate(parts):
        for copy in part:
            copy.wait()
        place = i * chunk
        convert(gbuf, cbuf, coded_ref, called_ref, place, chunk)
        out_ref[:, first + place : first + place + chunk] = product(
            coded_ref, called_ref, place, chunk, samples, w1, w2
        )


def third_kernel(pair_ref, coded_first, called_first, coded_ref, called_ref, half_ref, sums_ref, out_ref, w1, w2):
    own = pair_ref.shape[1]
    first, rest = coded_first.shape[0], coded_ref.shape[0]
    samples = pair_samples((lax.axis_index("var") // 2) ^ 1, own)
    weights(pair_ref, w1, w2)
    for i in range((first + rest) // LANES):
        place = i * LANES
        here = slice(place, place + LANES)
        if place < first:
            got = product(coded_first, called_first, place, LANES, samples, w1, w2)
        else:
            got = product(coded_ref, called_ref, place - first, LANES, samples, w1, w2)
        out_ref[:, here] = half_ref[:, here] + got
    out_ref[:, first + rest :] = jnp.zeros((out_ref.shape[0], LANES), F32)
    out_ref[0:16, first + rest :] = sums_ref[...]


def chunk_of(cross, start, n_var, width):
    wide = cross.shape[1] // n_var
    lane = lane_of((cross.shape[0], LANES))
    tile = (start // LANES) * LANES
    inside = start - tile
    block = jnp.zeros((cross.shape[0], LANES), F32)
    for v in range(n_var):
        piece = cross[:, pl.ds(pl.multiple_of(v * wide + tile, LANES), LANES)]
        turned = pltpu.roll(piece, (v * width - inside + LANES) % LANES, 1)
        block = jnp.where((lane >= v * width) & (lane < (v + 1) * width), turned, block)
    return block


def chips_kernel(n_var, width, own_ref, other_ref, cross_ref, cross_other_ref,
                 total_ref, mine_ref, *rest):
    messages, (both,) = rest[:-1], rest[-1:]
    samp = lax.axis_index("samp")
    core = samp % 2
    chip = samp // 2
    rows = own_ref.shape[1] - LANES
    total = own_ref[...] + other_ref[...]
    total_ref[...] = total
    both[...] = cross_ref[...] + cross_other_ref[...]
    mine_ref[...] = chunk_of(both, samp * width, n_var, width)

    main = total[0:32, :rows].astype(BF16)
    counts = total[32:34, :rows]
    pieces = []
    for part in halves(counts):
        part = part.astype(F32)
        for which in range(2):
            for j in range(rows // LANES):
                pieces.append(part[which : which + 1, j * LANES : (j + 1) * LANES])
    while len(pieces) < 32:
        pieces.append(jnp.zeros((1, LANES), F32))
    counts = jnp.concatenate(pieces, axis=0).astype(BF16)
    sums = jnp.zeros((16, LANES), F32)
    for part, values in enumerate(thirds(total[0:16, rows:])):
        values = values.astype(F32)
        sums = sums + (pltpu.roll(values, 16 * part, 1) if part else values)
    for k, message in enumerate(messages):
        chunk = chunk_of(both, ((chip ^ (k + 1)) * 2 + core) * width, n_var, width)
        high, low = halves(chunk[0:32])
        dose = jnp.concatenate([p.astype(F32) for p in thirds(chunk[32:33])] + [jnp.zeros((13, LANES), F32)])
        message[:, :rows] = main
        message[:, rows : rows + LANES] = high
        message[:, rows + LANES : rows + 2 * LANES] = low
        message[:, rows + 2 * LANES : rows + 3 * LANES] = counts
        message[:, rows + 3 * LANES :] = jnp.concatenate([sums, dose], axis=0).astype(BF16)


def back_kernel(variants, width, n_arrived, total_ref, mine_ref, coded_first, called_first,
                coded_ref, called_ref, *rest):
    arrived, own_ref, messages = rest[:n_arrived], rest[n_arrived], rest[n_arrived + 1 :]
    var = lax.axis_index("var")
    rows = total_ref.shape[1] - LANES
    lanes = lane_of((16, LANES))

    main = total_ref[0:32, :rows]
    allele, count = total_ref[32:33, :rows], total_ref[33:34, :rows]
    sums = total_ref[0:16, rows:]
    cross = mine_ref[0:32]
    dose = mine_ref[32:33]
    got_counts = jnp.zeros((32, LANES), F32)
    got_last = jnp.zeros((32, LANES), F32)
    for ref in arrived:
        main = main + ref[:, :rows].astype(F32)
        cross = cross + ref[:, rows : rows + LANES].astype(F32)
        cross = cross + ref[:, rows + LANES : rows + 2 * LANES].astype(F32)
        got_counts = got_counts + ref[:, rows + 2 * LANES : rows + 3 * LANES].astype(F32)
        got_last = got_last + ref[:, rows + 3 * LANES :].astype(F32)
    tiles = rows // LANES
    pick = lambda first: jnp.concatenate(
        [got_counts[first + j : first + j + 1] + got_counts[first + 2 * tiles + j : first + 2 * tiles + j + 1]
         for j in range(tiles)], axis=1
    )
    allele = allele + pick(0)
    count = count + pick(tiles)
    last = got_last[0:16]
    sums = sums + last + pltpu.roll(last, LANES - 16, 1) + pltpu.roll(last, LANES - 32, 1)
    dose = dose + got_last[16:17] + got_last[17:18] + got_last[18:19]

    frequency = (allele + 1.0) / (2.0 * count + 2.0)
    spread = jnp.sqrt(2.0 * frequency * (1.0 - frequency))
    loading = (main[0:16] - 2.0 * frequency * main[16:32]) / spread
    scaled = loading / spread
    scaled_a = scaled.astype(BF16)
    scaled_b = (-2.0 * frequency * scaled).astype(BF16)
    square = jnp.sum(loading * loading, axis=1, keepdims=True)
    sums = jnp.where(lanes < 6, sums, 0.0) + jnp.where(lanes == 6, square, 0.0)

    own = own_ref.shape[1] - 2 * LANES

    def term(p):
        part = pl.ds(pl.multiple_of(p * own, LANES), own)
        first = coded_first.shape[0]
        got = jnp.dot(scaled_a[:, :first], coded_first[:, part], preferred_element_type=F32)
        got = got + jnp.dot(scaled_a[:, first:], coded_ref[:, part], preferred_element_type=F32)
        got = got + jnp.dot(scaled_b[:, :first], called_first[:, part], preferred_element_type=F32)
        got = got + jnp.dot(scaled_b[:, first:], called_ref[:, part], preferred_element_type=F32)
        return got / variants

    def segment(values, p):
        turned = pltpu.roll(values, (LANES - p * width) % LANES, 1)
        return jnp.where(lane_of(values.shape) < width, turned, 0.0)

    def cross_block(p, exact):
        chunk = segment(cross, p)
        sol, dire = chunk[0:16], chunk[16:32]
        if exact:
            return sol + pltpu.roll(dire, 32, 1)
        sol_high, sol_low = [x.astype(F32) for x in halves(sol)]
        dir_high, dir_low = [x.astype(F32) for x in halves(dire)]
        return (
            sol_high + pltpu.roll(dir_high, 32, 1) + pltpu.roll(sol_low, 64, 1) + pltpu.roll(dir_low, 96, 1)
        )

    row = lax.broadcasted_iota(jnp.int32, (16, LANES), 0)

    def sums_block(p, exact):
        own_dose = segment(jnp.broadcast_to(dose, (16, LANES)), p)
        own_dose = pltpu.roll(own_dose, 64, 1)
        if exact:
            return sums + jnp.where(row == 0, own_dose, 0.0)
        block = jnp.zeros((16, LANES), F32)
        for part, values in enumerate(thirds(sums)):
            values = values.astype(F32)
            block = block + (pltpu.roll(values, 16 * part, 1) if part else values)
        for part, values in enumerate(thirds(own_dose)):
            block = block + jnp.where(row == part, values.astype(F32), 0.0)
        return block

    for k, ref in enumerate(messages):
        p = var ^ (k + 1)
        ref[:, :own] = term(p).astype(BF16)
        ref[:, own : own + LANES] = cross_block(p, False).astype(BF16)
        ref[:, own + LANES :] = sums_block(p, False).astype(BF16)
    own_ref[:, :own] = term(var)
    own_ref[:, own : own + LANES] = cross_block(var, True)
    own_ref[:, own + LANES :] = sums_block(var, True)


def step_of(refs, noise_row, variants):
    got = refs[0][...]
    for ref in refs[1:]:
        got = got + ref[...].astype(F32)
    own = got.shape[1] - 2 * LANES
    back, cross, last = got[:, :own], got[:, own : own + LANES], got[:, own + LANES :]
    sums = last + pltpu.roll(last, LANES - 16, 1) + pltpu.roll(last, LANES - 32, 1)
    column = lambda q: sums[:, q : q + 1]
    noise = to_column(noise_row)
    curvature = noise * column(1) + column(6) / variants
    step = column(0) / (curvature + 1e-06)
    return back, cross, last, column, noise, step


def norm_kernel(variants, noise_ref, dir_ref, res_ref, *rest):
    refs, (out_ref, new_ref) = rest[:-2], rest[-2:]
    back, _, _, _, noise, step = step_of(refs, noise_ref[...], variants)
    new = res_ref[...] - step * (noise * dir_ref[...] + back)
    new_ref[...] = new
    row = to_row(jnp.sum(new * new, axis=1, keepdims=True))
    out_ref[...] = jnp.broadcast_to(row[None], out_ref.shape)


def new_kernel(variants, samples, width, noise_ref, dir_ref, res_ref, sol_ref, *rest):
    refs, (sol_out, res_out, score_out, norm_out) = rest[:-4], rest[-4:]
    back, cross, last, column, noise, step = step_of(refs, noise_ref[...], variants)
    dire = dir_ref[...]
    sol_out[...] = sol_ref[...] + step * dire
    res_out[...] = res_ref[...] - step * (noise * dire + back)
    norm_out[...] = jnp.broadcast_to(column(0), norm_out.shape)
    cross = cross + pltpu.roll(cross, LANES - 64, 1)
    cross = cross + step * pltpu.roll(cross, LANES - 32, 1)
    dose = pltpu.roll(last, LANES - 64, 1)
    dose = dose[0:1] + dose[1:2] + dose[2:3]
    sol_sum = column(2) + step * column(5)
    sol_square = column(3) + 2.0 * step * column(4) + step * (step * column(1))
    dose_freq = (dose / 100.0 + 1.0) / (2.0 * samples + 2.0)
    dose_spread = jnp.sqrt(2.0 * dose_freq * (1.0 - dose_freq))
    scale = math.sqrt(samples) * jnp.sqrt(sol_square / samples + 1e-06)
    scores = (cross / 100.0 - 2.0 * dose_freq * sol_sum) / (dose_spread * scale)
    score_out[...] = scores[:, :width]


def direction_kernel(norms_ref, norm_ref, res_ref, dir_ref, out_ref):
    new_norm = to_column(jnp.sum(norms_ref[...], axis=0))
    out_ref[...] = res_ref[...] + (new_norm / (norm_ref[:, 0:1] + 1e-06)) * dir_ref[...]


def call(kernel, out, ins, args, scratch=(), limit=16, flops=0, moved=0):
    return pl.pallas_call(
        kernel,
        out_shape=[jax.ShapeDtypeStruct(*o) if len(o) == 2 else o[2](*o[:2]) for o in out],
        in_specs=list(ins),
        out_specs=[VMEM] * len(out),
        scratch_shapes=list(scratch),
        compiler_params=pltpu.CompilerParams(vmem_limit_bytes=limit * MIB),
        cost_estimate=pl.CostEstimate(flops=flops, bytes_accessed=moved, transcendentals=0),
    )(*[pltpu.with_memory_space_constraint(x, pltpu.HBM) if spec is HBM else x for spec, x in zip(ins, args)])


def body(genotypes, called, dosage, sample_order, noise_ratio, solution, residual, direction):
    n_var = lax.axis_size("var")
    n_samp = lax.axis_size("samp")
    own, rhs = direction.shape
    rows, shard = genotypes.shape
    variants = rows * n_var
    samples = own * n_samp * n_var
    imputed = dosage.shape[1]
    width = imputed // (n_var * n_samp)
    noise = noise_ratio[None]

    dire, res, sol = direction.T, residual.T, solution.T
    first, chunk = rows // 3, 128
    rest = rows - first
    matrix = lambda n: ((n, shard), BF16, pltpu.VMEM)

    neighbour = swap(dire, "var", 1)
    coded_a, called_a, cross, sums = call(
        functools.partial(first_kernel, chunk),
        [matrix(first), matrix(first), ((2 * rhs + 8, imputed), F32), ((rhs, LANES), F32)],
        [HBM] * 7,
        (sample_order, sol, dire, res, genotypes, called, dosage),
        scratch=[
            pltpu.VMEM((1, own), jnp.int32),
            pltpu.VMEM((rhs, own), F32),
            pltpu.VMEM((rhs, own), F32),
            pltpu.VMEM((rhs, own), F32),
            pltpu.VMEM((first, shard), jnp.int32),
            pltpu.VMEM((first, shard), jnp.int32),
            pltpu.VMEM((own, imputed), jnp.int32),
            pltpu.SemaphoreType.DMA((5,)),
            pltpu.SemaphoreType.DMA((2, first // chunk)),
        ],
        limit=24,
        flops=2 * 80 * own * (own + imputed),
        moved=4 * (2 * first * shard + own * imputed),
    )
    (pair,) = call(pair_kernel, [((2 * rhs, own), BF16)], [VMEM] * 2, (dire, neighbour))
    pair_other = swap(pair, "var", 2)
    cross_other = swap(cross, "samp", 1)
    both_weights = [pltpu.VMEM((48, 2 * own), BF16), pltpu.VMEM((48, 2 * own), BF16)]
    coded_b, called_b, half = call(
        functools.partial(second_kernel, chunk),
        [matrix(rest), matrix(rest), ((2 * rhs + 8, rows), F32)],
        [VMEM] * 3 + [HBM] * 2,
        (pair, coded_a, called_a, genotypes, called),
        scratch=[
            pltpu.VMEM((rest, shard), jnp.int32),
            pltpu.VMEM((rest, shard), jnp.int32),
            *both_weights,
            pltpu.SemaphoreType.DMA((2, rest // chunk)),
        ],
        limit=24,
        flops=2 * rows * shard * 256,
        moved=4 * 2 * rest * shard,
    )
    (part,) = call(
        third_kernel,
        [((2 * rhs + 8, rows + LANES), F32)],
        [VMEM] * 7,
        (pair_other, coded_a, called_a, coded_b, called_b, half, sums),
        scratch=both_weights,
        flops=2 * rows * shard * 256,
        moved=2 * rows * shard,
    )
    part_other = swap(part, "samp", 1)

    n_chips = n_samp // 2
    message = ((2 * rhs, rows + 4 * LANES), BF16)
    total, mine, *messages = call(
        functools.partial(chips_kernel, n_var, width),
        [(part.shape, F32), ((2 * rhs + 8, LANES), F32)] + [message] * (n_chips - 1),
        [VMEM] * 4,
        (part, part_other, cross, cross_other),
        scratch=[pltpu.VMEM(cross.shape, F32)],
        moved=1 * MIB,
    )
    arrived = [swap(messages[k], "samp", 2 * (k + 1)) for k in reversed(range(n_chips - 1))]

    wide = own + 2 * LANES
    mine_back, *messages = call(
        functools.partial(back_kernel, variants, width, n_chips - 1),
        [((rhs, wide), F32)] + [((rhs, wide), BF16)] * (n_var - 1),
        [VMEM] * (6 + n_chips - 1),
        (total, mine, coded_a, called_a, coded_b, called_b, *arrived),
        flops=4 * rows * shard * 256,
        moved=4 * rows * shard,
    )
    backs = [mine_back] + [swap(messages[k], "var", k + 1) for k in reversed(range(n_var - 1))]

    n_all = n_var * n_samp
    norms, res_keep = call(
        functools.partial(norm_kernel, variants),
        [((n_all, 1, LANES), F32), ((rhs, own), F32)],
        [VMEM] * (3 + n_var),
        (noise, dire, res, *backs),
        moved=4 * n_all * LANES,
    )
    norms = lax.all_to_all(norms, ("var", "samp"), split_axis=0, concat_axis=0)
    sol_new, res_new, scores, res_norm = call(
        functools.partial(new_kernel, variants, samples, width),
        [((rhs, own), F32), ((rhs, own), F32), ((rhs, width), F32), ((rhs, LANES), F32)],
        [VMEM] * (4 + n_var),
        (noise, dire, res, sol, *backs),
        moved=1 * MIB,
    )
    (dir_new,) = call(
        direction_kernel,
        [((rhs, own), F32)],
        [VMEM] * 4,
        (norms, res_norm, res_keep, dire),
    )
    return (sol_new.T, res_new.T, dir_new.T, scores.T)


def solution(mesh):
    placed = (
        P("var", "samp"),
        P("var", "samp"),
        P(("samp", "var"), None),
        P(("samp", "var"), None),
        P(),
        P(("samp", "var"), None),
        P(("samp", "var"), None),
        P(("samp", "var"), None),
    )
    return jax.shard_map(
        body,
        mesh=mesh,
        in_specs=placed,
        out_specs=(
            P(("samp", "var"), None),
            P(("samp", "var"), None),
            P(("samp", "var"), None),
            P(("var", "samp"), None),
        ),
        check_vma=False,
    )
```

```python
import functools
import math

import jax
import jax.numpy as jnp
from jax import lax
from jax.experimental import pallas as pl
from jax.experimental.pallas import tpu as pltpu
from jax.sharding import PartitionSpec as P

BF16 = jnp.bfloat16
F32 = jnp.float32
LANES = 128
NT = (((1,), (1,)), ((), ()))
VMEM = pl.BlockSpec(memory_space=pltpu.VMEM)
HBM = pl.BlockSpec(memory_space=pltpu.HBM)
MIB = 1 << 20


def swap(values, axis, distance):
    size = lax.axis_size(axis)
    return lax.ppermute(values, axis, [(i, i ^ distance) for i in range(size)])


def halves(values):
    high = values.astype(BF16)
    return high, (values - high.astype(F32)).astype(BF16)


def thirds(values):
    high = values.astype(BF16)
    rest = values - high.astype(F32)
    middle = rest.astype(BF16)
    return high, middle, (rest - middle.astype(F32)).astype(BF16)


def lane_of(shape):
    return lax.broadcasted_iota(jnp.int32, shape, len(shape) - 1)


def columns(values, shape):
    lane = lane_of(shape)
    block = jnp.zeros(shape, F32)
    for q, column in enumerate(values):
        block = jnp.where(lane == q, column, block)
    return block


def to_column(row):
    shape = (16, row.shape[1])
    same = lax.broadcasted_iota(jnp.int32, shape, 0) == lane_of(shape)
    return jnp.sum(jnp.where(same, row, 0.0), axis=1, keepdims=True)


def to_row(column):
    shape = (16, LANES)
    same = lax.broadcasted_iota(jnp.int32, shape, 0) == lane_of(shape)
    return jnp.sum(jnp.where(same, column, 0.0), axis=0, keepdims=True)


def convert(gen_ref, call_ref, coded_ref, called_ref, first, rows):
    def group(i, carry):
        part = pl.ds(pl.multiple_of(first + i * 16, 16), 16)
        call = call_ref[part, :].astype(F32).astype(BF16)
        coded_ref[part, :] = gen_ref[part, :].astype(F32).astype(BF16) * call
        called_ref[part, :] = call
        return carry

    lax.fori_loop(0, rows // 16, group, 0, unroll=2)


def row_copies(first, chunks, pairs, sems):
    starts = [sum(chunks[:i]) for i in range(len(chunks))]
    return [
        (
            start,
            rows,
            [
                pltpu.make_async_copy(
                    source.at[pl.ds(first + start, rows)], target.at[pl.ds(start, rows)], sems.at[j, i]
                )
                for j, (source, target) in enumerate(pairs)
            ],
        )
        for i, (start, rows) in enumerate(zip(starts, chunks))
    ]


def chunks_of(rows):
    return [LANES] * (rows // LANES - 1) + [LANES // 2] * 2


def first_kernel(chunks, order_hbm, sol_hbm, dir_hbm, res_hbm, gen_hbm, call_hbm, dose_hbm,
                 coded_ref, called_ref, cross_ref, sums_ref,
                 order_ref, sol_ref, dir_ref, res_ref, gbuf, cbuf, dbuf, small_sems, sems):
    rhs = sol_hbm.shape[0]
    small = [
        pltpu.make_async_copy(source, target, small_sems.at[i])
        for i, (source, target) in enumerate(
            ((order_hbm, order_ref), (sol_hbm, sol_ref), (dir_hbm, dir_ref), (res_hbm, res_ref), (dose_hbm, dbuf))
        )
    ]
    for copy in small:
        copy.start()
    parts = row_copies(0, chunks, ((gen_hbm, gbuf), (call_hbm, cbuf)), sems)
    for _, _, part in parts:
        for copy in part:
            copy.start()
    for copy in small[:4]:
        copy.wait()
    sol, dire, res = sol_ref[...], dir_ref[...], res_ref[...]
    total = lambda x: jnp.sum(x, axis=1, keepdims=True)
    sums_ref[...] = columns(
        [total(res * res), total(dire * dire), total(sol), total(sol * sol), total(sol * dire), total(dire)],
        sums_ref.shape,
    )
    sol_high, sol_low = halves(sol)
    dir_high, dir_low = halves(dire)
    stack = jnp.concatenate([sol_high, dir_high, sol_low, dir_low], axis=0)
    own = sol.shape[1]
    hot = lax.broadcasted_iota(jnp.int32, (own, own), 0) == order_ref[...]
    hot = jnp.where(hot, 1.0, 0.0).astype(BF16)
    picked = jnp.dot(stack, hot, preferred_element_type=F32).astype(BF16)
    picked = jnp.concatenate([picked, jnp.ones((16, own), BF16)], axis=0)
    small[4].wait()
    dose = dbuf[...].astype(F32).astype(BF16)
    cross = jnp.dot(picked, dose, preferred_element_type=F32)
    cross_ref[: 2 * rhs] = cross[: 2 * rhs] + cross[2 * rhs : 4 * rhs]
    cross_ref[2 * rhs :] = cross[4 * rhs : 4 * rhs + 8]
    for start, count, part in parts:
        for copy in part:
            copy.wait()
        convert(gbuf, cbuf, coded_ref, called_ref, start, count)


def pair_kernel(own_ref, other_ref, out_ref):
    upper = lax.axis_index("var") % 2
    rhs = own_ref.shape[0]
    own, other = own_ref[...], other_ref[...]
    out_ref[:rhs] = jnp.where(upper == 0, own, other).astype(BF16)
    out_ref[rhs:] = jnp.where(upper == 0, other, own).astype(BF16)


def weights(pair_ref, w1, w2):
    own = pair_ref.shape[1]
    zero = jnp.zeros((16, 2 * own), BF16)
    row = lax.broadcasted_iota(jnp.int32, (16, 2 * own), 0)
    w1[16:32] = zero
    w1[32:48] = jnp.where(row == 0, 1.0, 0.0).astype(BF16)
    w2[0:16] = zero
    w2[32:48] = jnp.where(row == 1, 1.0, 0.0).astype(BF16)
    for i in range(2):
        piece = pair_ref[16 * i : 16 * i + 16]
        w1[0:16, i * own : (i + 1) * own] = piece
        w2[16:32, i * own : (i + 1) * own] = piece


def product(coded_ref, called_ref, first, rows, samples, w1, w2):
    part = pl.ds(first, rows)
    got = lax.dot_general(coded_ref[part, samples], w1[...], NT, preferred_element_type=F32)
    got = got + lax.dot_general(called_ref[part, samples], w2[...], NT, preferred_element_type=F32)
    got = jnp.concatenate([got, jnp.zeros((rows, LANES - got.shape[1]), F32)], axis=1)
    return got.T[:40]


def pair_samples(pair, own):
    return pl.ds(pl.multiple_of(pair * 2 * own, LANES), 2 * own)


def second_kernel(chunks, pair_ref, coded_first, called_first, gen_hbm, call_hbm,
                  coded_ref, called_ref, out_ref, gbuf, cbuf, w1, w2, sems):
    first = coded_first.shape[0]
    own = pair_ref.shape[1]
    parts = row_copies(first, chunks, ((gen_hbm, gbuf), (call_hbm, cbuf)), sems)
    for _, _, part in parts:
        for copy in part:
            copy.start()
    samples = pair_samples(lax.axis_index("var") // 2, own)
    weights(pair_ref, w1, w2)
    for i in range(first // LANES):
        place = i * LANES
        out_ref[:, place : place + LANES] = product(coded_first, called_first, place, LANES, samples, w1, w2)
    for start, count, part in parts:
        for copy in part:
            copy.wait()
        convert(gbuf, cbuf, coded_ref, called_ref, start, count)
        if (start + count) % LANES == 0:
            place = start + count - LANES
            out_ref[:, first + place : first + place + LANES] = product(
                coded_ref, called_ref, place, LANES, samples, w1, w2
            )


def third_kernel(pair_ref, coded_first, called_first, coded_ref, called_ref, half_ref, sums_ref, out_ref, w1, w2):
    own = pair_ref.shape[1]
    first, rest = coded_first.shape[0], coded_ref.shape[0]
    samples = pair_samples((lax.axis_index("var") // 2) ^ 1, own)
    weights(pair_ref, w1, w2)
    for i in range((first + rest) // LANES):
        place = i * LANES
        here = slice(place, place + LANES)
        if place < first:
            got = product(coded_first, called_first, place, LANES, samples, w1, w2)
        else:
            got = product(coded_ref, called_ref, place - first, LANES, samples, w1, w2)
        out_ref[:, here] = half_ref[:, here] + got
    out_ref[:, first + rest :] = jnp.zeros((out_ref.shape[0], LANES), F32)
    out_ref[0:16, first + rest :] = sums_ref[...]


def chunk_of(cross, start, n_var, width):
    wide = cross.shape[1] // n_var
    lane = lane_of((cross.shape[0], LANES))
    tile = (start // LANES) * LANES
    inside = start - tile
    block = jnp.zeros((cross.shape[0], LANES), F32)
    for v in range(n_var):
        piece = cross[:, pl.ds(pl.multiple_of(v * wide + tile, LANES), LANES)]
        turned = pltpu.roll(piece, (v * width - inside + LANES) % LANES, 1)
        block = jnp.where((lane >= v * width) & (lane < (v + 1) * width), turned, block)
    return block


def partners(n_chips):
    far = list(reversed(range(n_chips // 2, n_chips)))
    near = list(reversed(range(1, n_chips // 2)))
    return list(zip(near + [0] * (len(far) - len(near)), far))


def chips_kernel(n_var, width, distances, own_ref, other_ref, cross_ref, cross_other_ref, total_ref, mine_ref, *rest):
    messages, both = rest[:-1], rest[-1]
    samp = lax.axis_index("samp")
    core = samp % 2
    chip = samp // 2
    rows = own_ref.shape[1] - LANES
    total = own_ref[...] + other_ref[...]
    total_ref[...] = total
    both[...] = cross_ref[...] + cross_other_ref[...]
    mine_ref[...] = chunk_of(both, samp * width, n_var, width)

    main = total[0:32, :rows].astype(BF16)
    counts = total[32:34, :rows]
    pieces = []
    for part in halves(counts):
        part = part.astype(F32)
        for which in range(2):
            for j in range(rows // LANES):
                pieces.append(part[which : which + 1, j * LANES : (j + 1) * LANES])
    while len(pieces) < 32:
        pieces.append(jnp.zeros((1, LANES), F32))
    counts = jnp.concatenate(pieces, axis=0).astype(BF16)
    sums = jnp.zeros((16, LANES), F32)
    for part, values in enumerate(thirds(total[0:16, rows:])):
        values = values.astype(F32)
        sums = sums + (pltpu.roll(values, 16 * part, 1) if part else values)
    for (zero, one), message in zip(distances, messages):
        target = chip ^ jnp.where(core == 0, zero, one)
        dose = []
        for c in range(2):
            chunk = chunk_of(both, (target * 2 + c) * width, n_var, width)
            for i, part in enumerate(halves(chunk[0:32])):
                at = rows + (2 * c + i) * LANES
                message[:, at : at + LANES] = part
            dose += [p.astype(F32) for p in thirds(chunk[32:33])]
        dose = jnp.concatenate(dose + [jnp.zeros((10, LANES), F32)])
        message[:, :rows] = main
        message[:, rows + 4 * LANES : rows + 5 * LANES] = counts
        message[:, rows + 5 * LANES :] = jnp.concatenate([sums, dose], axis=0).astype(BF16)


def back_kernel(variants, width, n_arrived, total_ref, mine_ref, coded_first, called_first,
                coded_ref, called_ref, *rest):
    arrived, own_ref, messages = rest[:n_arrived], rest[n_arrived], rest[n_arrived + 1 :]
    var = lax.axis_index("var")
    rows = total_ref.shape[1] - LANES
    lanes = lane_of((16, LANES))

    main = total_ref[0:32, :rows]
    allele, count = total_ref[32:33, :rows], total_ref[33:34, :rows]
    sums = total_ref[0:16, rows:]
    cross = mine_ref[0:32]
    dose = mine_ref[32:33]
    got_counts = jnp.zeros((32, LANES), F32)
    got_last = jnp.zeros((32, LANES), F32)
    core = lax.axis_index("samp") % 2
    for ref in arrived:
        main = main + ref[:, :rows].astype(F32)
        for i in range(2):
            at = pl.ds(pl.multiple_of(rows + (2 * core + i) * LANES, LANES), LANES)
            cross = cross + ref[:, at].astype(F32)
        got_counts = got_counts + ref[:, rows + 4 * LANES : rows + 5 * LANES].astype(F32)
        got_last = got_last + ref[:, rows + 5 * LANES :].astype(F32)
    tiles = rows // LANES
    pick = lambda first: jnp.concatenate(
        [got_counts[first + j : first + j + 1] + got_counts[first + 2 * tiles + j : first + 2 * tiles + j + 1]
         for j in range(tiles)], axis=1
    )
    allele = allele + pick(0)
    count = count + pick(tiles)
    last = got_last[0:16]
    sums = sums + last + pltpu.roll(last, LANES - 16, 1) + pltpu.roll(last, LANES - 32, 1)
    first_dose = got_last[16:17] + got_last[17:18] + got_last[18:19]
    second_dose = got_last[19:20] + got_last[20:21] + got_last[21:22]
    dose = dose + jnp.where(core == 0, first_dose, second_dose)

    frequency = (allele + 1.0) / (2.0 * count + 2.0)
    spread = jnp.sqrt(2.0 * frequency * (1.0 - frequency))
    loading = (main[0:16] - 2.0 * frequency * main[16:32]) / spread
    scaled = loading / spread
    scaled_a = scaled.astype(BF16)
    scaled_b = (-2.0 * frequency * scaled).astype(BF16)
    square = jnp.sum(loading * loading, axis=1, keepdims=True)
    sums = jnp.where(lanes < 6, sums, 0.0) + jnp.where(lanes == 6, square, 0.0)

    own = own_ref.shape[1] - 2 * LANES

    def term(p):
        part = pl.ds(pl.multiple_of(p * own, LANES), own)
        first = coded_first.shape[0]
        got = jnp.dot(scaled_a[:, :first], coded_first[:, part], preferred_element_type=F32)
        got = got + jnp.dot(scaled_a[:, first:], coded_ref[:, part], preferred_element_type=F32)
        got = got + jnp.dot(scaled_b[:, :first], called_first[:, part], preferred_element_type=F32)
        got = got + jnp.dot(scaled_b[:, first:], called_ref[:, part], preferred_element_type=F32)
        return got / variants

    def segment(values, p):
        turned = pltpu.roll(values, (LANES - p * width) % LANES, 1)
        return jnp.where(lane_of(values.shape) < width, turned, 0.0)

    def cross_block(p, exact):
        chunk = segment(cross, p)
        sol, dire = chunk[0:16], chunk[16:32]
        if exact:
            return sol + pltpu.roll(dire, 32, 1)
        sol_high, sol_low = [x.astype(F32) for x in halves(sol)]
        dir_high, dir_low = [x.astype(F32) for x in halves(dire)]
        return (
            sol_high + pltpu.roll(dir_high, 32, 1) + pltpu.roll(sol_low, 64, 1) + pltpu.roll(dir_low, 96, 1)
        )

    row = lax.broadcasted_iota(jnp.int32, (16, LANES), 0)

    def sums_block(p, exact):
        own_dose = segment(jnp.broadcast_to(dose, (16, LANES)), p)
        own_dose = pltpu.roll(own_dose, 64, 1)
        if exact:
            return sums + jnp.where(row == 0, own_dose, 0.0)
        block = jnp.zeros((16, LANES), F32)
        for part, values in enumerate(thirds(sums)):
            values = values.astype(F32)
            block = block + (pltpu.roll(values, 16 * part, 1) if part else values)
        for part, values in enumerate(thirds(own_dose)):
            block = block + jnp.where(row == part, values.astype(F32), 0.0)
        return block

    for k, ref in enumerate(messages):
        p = var ^ (k + 1)
        ref[:, :own] = term(p).astype(BF16)
        ref[:, own : own + LANES] = cross_block(p, False).astype(BF16)
        ref[:, own + LANES :] = sums_block(p, False).astype(BF16)
    own_ref[:, :own] = term(var)
    own_ref[:, own : own + LANES] = cross_block(var, True)
    own_ref[:, own + LANES :] = sums_block(var, True)


def step_of(refs, noise_row, variants):
    got = refs[0][...]
    for ref in refs[1:]:
        got = got + ref[...].astype(F32)
    own = got.shape[1] - 2 * LANES
    back, cross, last = got[:, :own], got[:, own : own + LANES], got[:, own + LANES :]
    sums = last + pltpu.roll(last, LANES - 16, 1) + pltpu.roll(last, LANES - 32, 1)
    column = lambda q: sums[:, q : q + 1]
    noise = to_column(noise_row)
    curvature = noise * column(1) + column(6) / variants
    step = column(0) / (curvature + 1e-06)
    return back, cross, last, column, noise, step


def norm_kernel(variants, noise_ref, dir_ref, res_ref, *rest):
    refs, (out_ref, new_ref) = rest[:-2], rest[-2:]
    back, _, _, _, noise, step = step_of(refs, noise_ref[...], variants)
    new = res_ref[...] - step * (noise * dir_ref[...] + back)
    new_ref[...] = new
    row = to_row(jnp.sum(new * new, axis=1, keepdims=True))
    out_ref[...] = jnp.broadcast_to(row[None], out_ref.shape)


def new_kernel(variants, samples, width, noise_ref, dir_ref, res_ref, sol_ref, *rest):
    refs, (sol_out, res_out, score_out, norm_out) = rest[:-4], rest[-4:]
    back, cross, last, column, noise, step = step_of(refs, noise_ref[...], variants)
    dire = dir_ref[...]
    sol_out[...] = sol_ref[...] + step * dire
    res_out[...] = res_ref[...] - step * (noise * dire + back)
    norm_out[...] = jnp.broadcast_to(column(0), norm_out.shape)
    cross = cross + pltpu.roll(cross, LANES - 64, 1)
    cross = cross + step * pltpu.roll(cross, LANES - 32, 1)
    dose = pltpu.roll(last, LANES - 64, 1)
    dose = dose[0:1] + dose[1:2] + dose[2:3]
    sol_sum = column(2) + step * column(5)
    sol_square = column(3) + 2.0 * step * column(4) + step * (step * column(1))
    dose_freq = (dose / 100.0 + 1.0) / (2.0 * samples + 2.0)
    dose_spread = jnp.sqrt(2.0 * dose_freq * (1.0 - dose_freq))
    scale = math.sqrt(samples) * jnp.sqrt(sol_square / samples + 1e-06)
    scores = (cross / 100.0 - 2.0 * dose_freq * sol_sum) / (dose_spread * scale)
    score_out[...] = scores[:, :width]


def direction_kernel(norms_ref, norm_ref, res_ref, dir_ref, out_ref):
    new_norm = to_column(jnp.sum(norms_ref[...], axis=0))
    out_ref[...] = res_ref[...] + (new_norm / (norm_ref[:, 0:1] + 1e-06)) * dir_ref[...]


def call(kernel, out, ins, args, scratch=(), limit=16, flops=0, moved=0):
    return pl.pallas_call(
        kernel,
        out_shape=[jax.ShapeDtypeStruct(*o) if len(o) == 2 else o[2](*o[:2]) for o in out],
        in_specs=list(ins),
        out_specs=[VMEM] * len(out),
        scratch_shapes=list(scratch),
        compiler_params=pltpu.CompilerParams(vmem_limit_bytes=limit * MIB),
        cost_estimate=pl.CostEstimate(flops=flops, bytes_accessed=moved, transcendentals=0),
    )(*[pltpu.with_memory_space_constraint(x, pltpu.HBM) if spec is HBM else x for spec, x in zip(ins, args)])


def body(genotypes, called, dosage, sample_order, noise_ratio, solution, residual, direction):
    n_var = lax.axis_size("var")
    n_samp = lax.axis_size("samp")
    own, rhs = direction.shape
    rows, shard = genotypes.shape
    variants = rows * n_var
    samples = own * n_samp * n_var
    imputed = dosage.shape[1]
    width = imputed // (n_var * n_samp)
    noise = noise_ratio[None]

    dire, res, sol = direction.T, residual.T, solution.T
    first = rows // 3
    rest = rows - first
    matrix = lambda n: ((n, shard), BF16, pltpu.VMEM)

    neighbour = swap(dire, "var", 1)
    coded_a, called_a, cross, sums = call(
        functools.partial(first_kernel, chunks_of(first)),
        [matrix(first), matrix(first), ((2 * rhs + 8, imputed), F32), ((rhs, LANES), F32)],
        [HBM] * 7,
        (sample_order, sol, dire, res, genotypes, called, dosage),
        scratch=[
            pltpu.VMEM((1, own), jnp.int32),
            pltpu.VMEM((rhs, own), F32),
            pltpu.VMEM((rhs, own), F32),
            pltpu.VMEM((rhs, own), F32),
            pltpu.VMEM((first, shard), jnp.int32),
            pltpu.VMEM((first, shard), jnp.int32),
            pltpu.VMEM((own, imputed), jnp.int32),
            pltpu.SemaphoreType.DMA((5,)),
            pltpu.SemaphoreType.DMA((2, len(chunks_of(first)))),
        ],
        limit=24,
        flops=2 * 80 * own * (own + imputed),
        moved=4 * (2 * first * shard + own * imputed),
    )
    (pair,) = call(pair_kernel, [((2 * rhs, own), BF16)], [VMEM] * 2, (dire, neighbour))
    pair_other = swap(pair, "var", 2)
    cross_other = swap(cross, "samp", 1)
    both_weights = [pltpu.VMEM((48, 2 * own), BF16), pltpu.VMEM((48, 2 * own), BF16)]
    coded_b, called_b, half = call(
        functools.partial(second_kernel, chunks_of(rest)),
        [matrix(rest), matrix(rest), ((2 * rhs + 8, rows), F32)],
        [VMEM] * 3 + [HBM] * 2,
        (pair, coded_a, called_a, genotypes, called),
        scratch=[
            pltpu.VMEM((rest, shard), jnp.int32),
            pltpu.VMEM((rest, shard), jnp.int32),
            *both_weights,
            pltpu.SemaphoreType.DMA((2, len(chunks_of(rest)))),
        ],
        limit=24,
        flops=2 * rows * shard * 256,
        moved=4 * 2 * rest * shard,
    )
    (part,) = call(
        third_kernel,
        [((2 * rhs + 8, rows + LANES), F32)],
        [VMEM] * 7,
        (pair_other, coded_a, called_a, coded_b, called_b, half, sums),
        scratch=both_weights,
        flops=2 * rows * shard * 256,
        moved=2 * rows * shard,
    )
    part_other = swap(part, "samp", 1)

    n_chips = n_samp // 2
    distances = partners(n_chips)
    message = ((2 * rhs, rows + 6 * LANES), BF16)
    total, mine, *messages = call(
        functools.partial(chips_kernel, n_var, width, distances),
        [(part.shape, F32), ((2 * rhs + 8, LANES), F32)] + [message] * len(distances),
        [VMEM] * 4,
        (part, part_other, cross, cross_other),
        scratch=[pltpu.VMEM(cross.shape, F32)],
        moved=1 * MIB,
    )
    came, handed = [], []
    for (zero, one), m in zip(distances, messages):
        pairs = [(i, i ^ (2 * (one if i % 2 else zero))) for i in range(n_samp) if i % 2 or zero]
        came.append(lax.ppermute(m, "samp", pairs))
    for (zero, one), m in zip(distances, came):
        handed.append(lax.ppermute(m, "samp", [(i, i ^ 1) for i in range(n_samp) if i % 2 or zero]))
    arrived = came + handed

    wide = own + 2 * LANES
    mine_back, *messages = call(
        functools.partial(back_kernel, variants, width, len(arrived)),
        [((rhs, wide), F32)] + [((rhs, wide), BF16)] * (n_var - 1),
        [VMEM] * (6 + len(arrived)),
        (total, mine, coded_a, called_a, coded_b, called_b, *arrived),
        flops=4 * rows * shard * 256,
        moved=4 * rows * shard,
    )
    backs = [mine_back] + [swap(messages[k], "var", k + 1) for k in reversed(range(n_var - 1))]

    n_all = n_var * n_samp
    norms, res_keep = call(
        functools.partial(norm_kernel, variants),
        [((n_all, 1, LANES), F32, pltpu.VMEM), ((rhs, own), F32)],
        [VMEM] * (3 + n_var),
        (noise, dire, res, *backs),
        moved=4 * n_all * LANES,
    )
    norms = lax.all_to_all(norms, ("var", "samp"), split_axis=0, concat_axis=0)
    sol_new, res_new, scores, res_norm = call(
        functools.partial(new_kernel, variants, samples, width),
        [((rhs, own), F32), ((rhs, own), F32), ((rhs, width), F32), ((rhs, LANES), F32)],
        [VMEM] * (4 + n_var),
        (noise, dire, res, sol, *backs),
        moved=1 * MIB,
    )
    (dir_new,) = call(
        direction_kernel,
        [((rhs, own), F32)],
        [VMEM] * 4,
        (norms, res_norm, res_keep, dire),
    )
    return (sol_new.T, res_new.T, dir_new.T, scores.T)


def solution(mesh):
    placed = (
        P("var", "samp"),
        P("var", "samp"),
        P(("samp", "var"), None),
        P(("samp", "var"), None),
        P(),
        P(("samp", "var"), None),
        P(("samp", "var"), None),
        P(("samp", "var"), None),
    )
    return jax.shard_map(
        body,
        mesh=mesh,
        in_specs=placed,
        out_specs=(
            P(("samp", "var"), None),
            P(("samp", "var"), None),
            P(("samp", "var"), None),
            P(("var", "samp"), None),
        ),
        check_vma=False,
    )
```

```python
import functools
import math

import jax
import jax.numpy as jnp
from jax import lax
from jax.experimental import pallas as pl
from jax.experimental.pallas import tpu as pltpu
from jax.sharding import PartitionSpec as P

BF16 = jnp.bfloat16
F32 = jnp.float32
LANES = 128
NT = (((1,), (1,)), ((), ()))
VMEM = pl.BlockSpec(memory_space=pltpu.VMEM)
HBM = pl.BlockSpec(memory_space=pltpu.HBM)
MIB = 1 << 20


def swap(values, axis, distance):
    size = lax.axis_size(axis)
    return lax.ppermute(values, axis, [(i, i ^ distance) for i in range(size)])


def halves(values):
    high = values.astype(BF16)
    return high, (values - high.astype(F32)).astype(BF16)


def thirds(values):
    high = values.astype(BF16)
    rest = values - high.astype(F32)
    middle = rest.astype(BF16)
    return high, middle, (rest - middle.astype(F32)).astype(BF16)


def lane_of(shape):
    return lax.broadcasted_iota(jnp.int32, shape, len(shape) - 1)


def columns(values, shape):
    lane = lane_of(shape)
    block = jnp.zeros(shape, F32)
    for q, column in enumerate(values):
        block = jnp.where(lane == q, column, block)
    return block


def to_column(row):
    shape = (16, row.shape[1])
    same = lax.broadcasted_iota(jnp.int32, shape, 0) == lane_of(shape)
    return jnp.sum(jnp.where(same, row, 0.0), axis=1, keepdims=True)


def to_row(column):
    shape = (16, LANES)
    same = lax.broadcasted_iota(jnp.int32, shape, 0) == lane_of(shape)
    return jnp.sum(jnp.where(same, column, 0.0), axis=0, keepdims=True)


def convert(gen_ref, call_ref, coded_ref, called_ref, first, rows):
    def group(i, carry):
        part = pl.ds(pl.multiple_of(first + i * 16, 16), 16)
        call = call_ref[part, :].astype(F32).astype(BF16)
        coded_ref[part, :] = gen_ref[part, :].astype(F32).astype(BF16) * call
        called_ref[part, :] = call
        return carry

    lax.fori_loop(0, rows // 16, group, 0)


def row_copies(first, chunks, pairs, sems):
    starts = [sum(chunks[:i]) for i in range(len(chunks))]
    return [
        (
            start,
            rows,
            [
                pltpu.make_async_copy(
                    source.at[pl.ds(first + start, rows)], target.at[pl.ds(start, rows)], sems.at[j, i]
                )
                for j, (source, target) in enumerate(pairs)
            ],
        )
        for i, (start, rows) in enumerate(zip(starts, chunks))
    ]


def chunks_of(rows):
    return [LANES] * (rows // LANES - 1) + [LANES // 2] * 2


def first_kernel(chunks, order_hbm, sol_hbm, dir_hbm, res_hbm, gen_hbm, call_hbm, dose_hbm,
                 coded_ref, called_ref, cross_ref, sums_ref,
                 order_ref, sol_ref, dir_ref, res_ref, gbuf, cbuf, dbuf, small_sems, sems):
    rhs = sol_hbm.shape[0]
    small = [
        pltpu.make_async_copy(source, target, small_sems.at[i])
        for i, (source, target) in enumerate(
            ((order_hbm, order_ref), (sol_hbm, sol_ref), (dir_hbm, dir_ref), (res_hbm, res_ref), (dose_hbm, dbuf))
        )
    ]
    for copy in small:
        copy.start()
    parts = row_copies(0, chunks, ((gen_hbm, gbuf), (call_hbm, cbuf)), sems)
    for _, _, part in parts:
        for copy in part:
            copy.start()
    for copy in small[:4]:
        copy.wait()
    sol, dire, res = sol_ref[...], dir_ref[...], res_ref[...]
    total = lambda x: jnp.sum(x, axis=1, keepdims=True)
    sums_ref[...] = columns(
        [total(res * res), total(dire * dire), total(sol), total(sol * sol), total(sol * dire), total(dire)],
        sums_ref.shape,
    )
    sol_high, sol_low = halves(sol)
    dir_high, dir_low = halves(dire)
    stack = jnp.concatenate([sol_high, dir_high, sol_low, dir_low], axis=0)
    own = sol.shape[1]
    hot = lax.broadcasted_iota(jnp.int32, (own, own), 0) == order_ref[...]
    hot = jnp.where(hot, 1.0, 0.0).astype(BF16)
    picked = jnp.dot(stack, hot, preferred_element_type=F32).astype(BF16)
    picked = jnp.concatenate([picked, jnp.ones((16, own), BF16)], axis=0)
    small[4].wait()
    dose = dbuf[...].astype(F32).astype(BF16)
    cross = jnp.dot(picked, dose, preferred_element_type=F32)
    cross_ref[: 2 * rhs] = cross[: 2 * rhs] + cross[2 * rhs : 4 * rhs]
    cross_ref[2 * rhs :] = cross[4 * rhs : 4 * rhs + 8]
    for start, count, part in parts:
        for copy in part:
            copy.wait()
        convert(gbuf, cbuf, coded_ref, called_ref, start, count)


def pair_kernel(own_ref, other_ref, out_ref):
    upper = lax.axis_index("var") % 2
    rhs = own_ref.shape[0]
    own, other = own_ref[...], other_ref[...]
    out_ref[:rhs] = jnp.where(upper == 0, own, other).astype(BF16)
    out_ref[rhs:] = jnp.where(upper == 0, other, own).astype(BF16)


def weights(pair_ref, w1, w2):
    own = pair_ref.shape[1]
    zero = jnp.zeros((16, 2 * own), BF16)
    row = lax.broadcasted_iota(jnp.int32, (16, 2 * own), 0)
    w1[16:32] = zero
    w1[32:48] = jnp.where(row == 0, 1.0, 0.0).astype(BF16)
    w2[0:16] = zero
    w2[32:48] = jnp.where(row == 1, 1.0, 0.0).astype(BF16)
    for i in range(2):
        piece = pair_ref[16 * i : 16 * i + 16]
        w1[0:16, i * own : (i + 1) * own] = piece
        w2[16:32, i * own : (i + 1) * own] = piece


def product(coded_ref, called_ref, first, rows, samples, w1, w2):
    part = pl.ds(first, rows)
    got = lax.dot_general(coded_ref[part, samples], w1[...], NT, preferred_element_type=F32)
    got = got + lax.dot_general(called_ref[part, samples], w2[...], NT, preferred_element_type=F32)
    got = jnp.concatenate([got, jnp.zeros((rows, LANES - got.shape[1]), F32)], axis=1)
    return got.T[:40]


def pair_samples(pair, own):
    return pl.ds(pl.multiple_of(pair * 2 * own, LANES), 2 * own)


def second_kernel(chunks, pair_ref, coded_first, called_first, gen_hbm, call_hbm,
                  coded_ref, called_ref, out_ref, gbuf, cbuf, w1, w2, sems):
    first = coded_first.shape[0]
    own = pair_ref.shape[1]
    parts = row_copies(first, chunks, ((gen_hbm, gbuf), (call_hbm, cbuf)), sems)
    for _, _, part in parts:
        for copy in part:
            copy.start()
    samples = pair_samples(lax.axis_index("var") // 2, own)
    weights(pair_ref, w1, w2)
    for i in range(first // LANES):
        place = i * LANES
        out_ref[:, place : place + LANES] = product(coded_first, called_first, place, LANES, samples, w1, w2)
    for start, count, part in parts:
        for copy in part:
            copy.wait()
        convert(gbuf, cbuf, coded_ref, called_ref, start, count)
        if (start + count) % LANES == 0:
            place = start + count - LANES
            out_ref[:, first + place : first + place + LANES] = product(
                coded_ref, called_ref, place, LANES, samples, w1, w2
            )


def third_kernel(pair_ref, coded_first, called_first, coded_ref, called_ref, half_ref, sums_ref, out_ref, w1, w2):
    own = pair_ref.shape[1]
    first, rest = coded_first.shape[0], coded_ref.shape[0]
    samples = pair_samples((lax.axis_index("var") // 2) ^ 1, own)
    weights(pair_ref, w1, w2)
    for i in range((first + rest) // LANES):
        place = i * LANES
        here = slice(place, place + LANES)
        if place < first:
            got = product(coded_first, called_first, place, LANES, samples, w1, w2)
        else:
            got = product(coded_ref, called_ref, place - first, LANES, samples, w1, w2)
        out_ref[:, here] = half_ref[:, here] + got
    out_ref[:, first + rest :] = jnp.zeros((out_ref.shape[0], LANES), F32)
    out_ref[0:16, first + rest :] = sums_ref[...]


def chunk_of(cross, start, n_var, width):
    wide = cross.shape[1] // n_var
    lane = lane_of((cross.shape[0], LANES))
    tile = (start // LANES) * LANES
    inside = start - tile
    block = jnp.zeros((cross.shape[0], LANES), F32)
    for v in range(n_var):
        piece = cross[:, pl.ds(pl.multiple_of(v * wide + tile, LANES), LANES)]
        turned = pltpu.roll(piece, (v * width - inside + LANES) % LANES, 1)
        block = jnp.where((lane >= v * width) & (lane < (v + 1) * width), turned, block)
    return block


def partners(n_chips):
    far = list(reversed(range(1, n_chips)))
    return list(zip(far, far[:-2] + far[-2:][::-1]))


def chips_kernel(n_var, width, distances, own_ref, other_ref, cross_ref, cross_other_ref,
                 total_ref, mine_ref, *rest):
    messages, (both,) = rest[:-1], rest[-1:]
    samp = lax.axis_index("samp")
    core = samp % 2
    chip = samp // 2
    rows = own_ref.shape[1] - LANES
    total = own_ref[...] + other_ref[...]
    total_ref[...] = total
    both[...] = cross_ref[...] + cross_other_ref[...]
    mine_ref[...] = chunk_of(both, samp * width, n_var, width)

    main = total[0:32, :rows].astype(BF16)
    counts = total[32:34, :rows]
    pieces = []
    for part in halves(counts):
        part = part.astype(F32)
        for which in range(2):
            for j in range(rows // LANES):
                pieces.append(part[which : which + 1, j * LANES : (j + 1) * LANES])
    while len(pieces) < 32:
        pieces.append(jnp.zeros((1, LANES), F32))
    counts = jnp.concatenate(pieces, axis=0).astype(BF16)
    sums = jnp.zeros((16, LANES), F32)
    for part, values in enumerate(thirds(total[0:16, rows:])):
        values = values.astype(F32)
        sums = sums + (pltpu.roll(values, 16 * part, 1) if part else values)
    for (zero, one), message in zip(distances, messages):
        target = chip ^ jnp.where(core == 0, zero, one)
        chunk = chunk_of(both, (target * 2 + core) * width, n_var, width)
        high, low = halves(chunk[0:32])
        dose = jnp.concatenate([p.astype(F32) for p in thirds(chunk[32:33])] + [jnp.zeros((13, LANES), F32)])
        message[:, :rows] = main
        message[:, rows : rows + LANES] = high
        message[:, rows + LANES : rows + 2 * LANES] = low
        message[:, rows + 2 * LANES : rows + 3 * LANES] = counts
        message[:, rows + 3 * LANES :] = jnp.concatenate([sums, dose], axis=0).astype(BF16)


def back_kernel(variants, width, n_arrived, total_ref, mine_ref, coded_first, called_first,
                coded_ref, called_ref, *rest):
    arrived, own_ref, messages = rest[:n_arrived], rest[n_arrived], rest[n_arrived + 1 :]
    var = lax.axis_index("var")
    rows = total_ref.shape[1] - LANES
    lanes = lane_of((16, LANES))

    main = total_ref[0:32, :rows]
    allele, count = total_ref[32:33, :rows], total_ref[33:34, :rows]
    sums = total_ref[0:16, rows:]
    cross = mine_ref[0:32]
    dose = mine_ref[32:33]
    got_counts = jnp.zeros((32, LANES), F32)
    got_last = jnp.zeros((32, LANES), F32)
    for ref in arrived:
        main = main + ref[:, :rows].astype(F32)
        cross = cross + ref[:, rows : rows + LANES].astype(F32)
        cross = cross + ref[:, rows + LANES : rows + 2 * LANES].astype(F32)
        got_counts = got_counts + ref[:, rows + 2 * LANES : rows + 3 * LANES].astype(F32)
        got_last = got_last + ref[:, rows + 3 * LANES :].astype(F32)
    tiles = rows // LANES
    pick = lambda first: jnp.concatenate(
        [got_counts[first + j : first + j + 1] + got_counts[first + 2 * tiles + j : first + 2 * tiles + j + 1]
         for j in range(tiles)], axis=1
    )
    allele = allele + pick(0)
    count = count + pick(tiles)
    last = got_last[0:16]
    sums = sums + last + pltpu.roll(last, LANES - 16, 1) + pltpu.roll(last, LANES - 32, 1)
    dose = dose + got_last[16:17] + got_last[17:18] + got_last[18:19]

    frequency = (allele + 1.0) / (2.0 * count + 2.0)
    spread = jnp.sqrt(2.0 * frequency * (1.0 - frequency))
    loading = (main[0:16] - 2.0 * frequency * main[16:32]) / spread
    scaled = loading / spread
    scaled_a = scaled.astype(BF16)
    scaled_b = (-2.0 * frequency * scaled).astype(BF16)
    square = jnp.sum(loading * loading, axis=1, keepdims=True)
    sums = jnp.where(lanes < 6, sums, 0.0) + jnp.where(lanes == 6, square, 0.0)

    own = own_ref.shape[1] - 2 * LANES

    def term(p):
        part = pl.ds(pl.multiple_of(p * own, LANES), own)
        first = coded_first.shape[0]
        got = jnp.dot(scaled_a[:, :first], coded_first[:, part], preferred_element_type=F32)
        got = got + jnp.dot(scaled_a[:, first:], coded_ref[:, part], preferred_element_type=F32)
        got = got + jnp.dot(scaled_b[:, :first], called_first[:, part], preferred_element_type=F32)
        got = got + jnp.dot(scaled_b[:, first:], called_ref[:, part], preferred_element_type=F32)
        return got / variants

    def segment(values, p):
        turned = pltpu.roll(values, (LANES - p * width) % LANES, 1)
        return jnp.where(lane_of(values.shape) < width, turned, 0.0)

    def cross_block(p, exact):
        chunk = segment(cross, p)
        sol, dire = chunk[0:16], chunk[16:32]
        if exact:
            return sol + pltpu.roll(dire, 32, 1)
        sol_high, sol_low = [x.astype(F32) for x in halves(sol)]
        dir_high, dir_low = [x.astype(F32) for x in halves(dire)]
        return (
            sol_high + pltpu.roll(dir_high, 32, 1) + pltpu.roll(sol_low, 64, 1) + pltpu.roll(dir_low, 96, 1)
        )

    row = lax.broadcasted_iota(jnp.int32, (16, LANES), 0)

    def sums_block(p, exact):
        own_dose = segment(jnp.broadcast_to(dose, (16, LANES)), p)
        own_dose = pltpu.roll(own_dose, 64, 1)
        if exact:
            return sums + jnp.where(row == 0, own_dose, 0.0)
        block = jnp.zeros((16, LANES), F32)
        for part, values in enumerate(thirds(sums)):
            values = values.astype(F32)
            block = block + (pltpu.roll(values, 16 * part, 1) if part else values)
        for part, values in enumerate(thirds(own_dose)):
            block = block + jnp.where(row == part, values.astype(F32), 0.0)
        return block

    for k, ref in enumerate(messages):
        p = var ^ (k + 1)
        ref[:, :own] = term(p).astype(BF16)
        ref[:, own : own + LANES] = cross_block(p, False).astype(BF16)
        ref[:, own + LANES :] = sums_block(p, False).astype(BF16)
    own_ref[:, :own] = term(var)
    own_ref[:, own : own + LANES] = cross_block(var, True)
    own_ref[:, own + LANES :] = sums_block(var, True)


def step_of(refs, noise_row, variants):
    got = refs[0][...]
    for ref in refs[1:]:
        got = got + ref[...].astype(F32)
    own = got.shape[1] - 2 * LANES
    back, cross, last = got[:, :own], got[:, own : own + LANES], got[:, own + LANES :]
    sums = last + pltpu.roll(last, LANES - 16, 1) + pltpu.roll(last, LANES - 32, 1)
    column = lambda q: sums[:, q : q + 1]
    noise = to_column(noise_row)
    curvature = noise * column(1) + column(6) / variants
    step = column(0) / (curvature + 1e-06)
    return back, cross, last, column, noise, step


def norm_kernel(variants, noise_ref, dir_ref, res_ref, *rest):
    refs, (out_ref, new_ref) = rest[:-2], rest[-2:]
    back, _, _, _, noise, step = step_of(refs, noise_ref[...], variants)
    new = res_ref[...] - step * (noise * dir_ref[...] + back)
    new_ref[...] = new
    row = to_row(jnp.sum(new * new, axis=1, keepdims=True))
    out_ref[...] = jnp.broadcast_to(row[None], out_ref.shape)


def new_kernel(variants, samples, width, noise_ref, dir_ref, res_ref, sol_ref, *rest):
    refs, (sol_out, res_out, score_out, norm_out) = rest[:-4], rest[-4:]
    back, cross, last, column, noise, step = step_of(refs, noise_ref[...], variants)
    dire = dir_ref[...]
    sol_out[...] = sol_ref[...] + step * dire
    res_out[...] = res_ref[...] - step * (noise * dire + back)
    norm_out[...] = jnp.broadcast_to(column(0), norm_out.shape)
    cross = cross + pltpu.roll(cross, LANES - 64, 1)
    cross = cross + step * pltpu.roll(cross, LANES - 32, 1)
    dose = pltpu.roll(last, LANES - 64, 1)
    dose = dose[0:1] + dose[1:2] + dose[2:3]
    sol_sum = column(2) + step * column(5)
    sol_square = column(3) + 2.0 * step * column(4) + step * (step * column(1))
    dose_freq = (dose / 100.0 + 1.0) / (2.0 * samples + 2.0)
    dose_spread = jnp.sqrt(2.0 * dose_freq * (1.0 - dose_freq))
    scale = math.sqrt(samples) * jnp.sqrt(sol_square / samples + 1e-06)
    scores = (cross / 100.0 - 2.0 * dose_freq * sol_sum) / (dose_spread * scale)
    score_out[...] = scores[:, :width]


def direction_kernel(norms_ref, norm_ref, res_ref, dir_ref, out_ref):
    new_norm = to_column(jnp.sum(norms_ref[...], axis=0))
    out_ref[...] = res_ref[...] + (new_norm / (norm_ref[:, 0:1] + 1e-06)) * dir_ref[...]


def call(kernel, out, ins, args, scratch=(), limit=16, flops=0, moved=0):
    return pl.pallas_call(
        kernel,
        out_shape=[jax.ShapeDtypeStruct(*o) if len(o) == 2 else o[2](*o[:2]) for o in out],
        in_specs=list(ins),
        out_specs=[VMEM] * len(out),
        scratch_shapes=list(scratch),
        compiler_params=pltpu.CompilerParams(vmem_limit_bytes=limit * MIB),
        cost_estimate=pl.CostEstimate(flops=flops, bytes_accessed=moved, transcendentals=0),
    )(*[pltpu.with_memory_space_constraint(x, pltpu.HBM) if spec is HBM else x for spec, x in zip(ins, args)])


def body(genotypes, called, dosage, sample_order, noise_ratio, solution, residual, direction):
    n_var = lax.axis_size("var")
    n_samp = lax.axis_size("samp")
    own, rhs = direction.shape
    rows, shard = genotypes.shape
    variants = rows * n_var
    samples = own * n_samp * n_var
    imputed = dosage.shape[1]
    width = imputed // (n_var * n_samp)
    noise = noise_ratio[None]

    dire, res, sol = direction.T, residual.T, solution.T
    first = rows // 3
    rest = rows - first
    matrix = lambda n: ((n, shard), BF16, pltpu.VMEM)

    neighbour = swap(dire, "var", 1)
    coded_a, called_a, cross, sums = call(
        functools.partial(first_kernel, [LANES] * (first // LANES)),
        [matrix(first), matrix(first), ((2 * rhs + 8, imputed), F32), ((rhs, LANES), F32)],
        [HBM] * 7,
        (sample_order, sol, dire, res, genotypes, called, dosage),
        scratch=[
            pltpu.VMEM((1, own), jnp.int32),
            pltpu.VMEM((rhs, own), F32),
            pltpu.VMEM((rhs, own), F32),
            pltpu.VMEM((rhs, own), F32),
            pltpu.VMEM((first, shard), jnp.int32),
            pltpu.VMEM((first, shard), jnp.int32),
            pltpu.VMEM((own, imputed), jnp.int32),
            pltpu.SemaphoreType.DMA((5,)),
            pltpu.SemaphoreType.DMA((2, first // LANES)),
        ],
        limit=24,
        flops=2 * 80 * own * (own + imputed),
        moved=4 * (2 * first * shard + own * imputed),
    )
    (pair,) = call(pair_kernel, [((2 * rhs, own), BF16)], [VMEM] * 2, (dire, neighbour))
    pair_other = swap(pair, "var", 2)
    cross_other = swap(cross, "samp", 1)
    both_weights = [pltpu.VMEM((48, 2 * own), BF16), pltpu.VMEM((48, 2 * own), BF16)]
    coded_b, called_b, half = call(
        functools.partial(second_kernel, chunks_of(rest)),
        [matrix(rest), matrix(rest), ((2 * rhs + 8, rows), F32)],
        [VMEM] * 3 + [HBM] * 2,
        (pair, coded_a, called_a, genotypes, called),
        scratch=[
            pltpu.VMEM((rest, shard), jnp.int32),
            pltpu.VMEM((rest, shard), jnp.int32),
            *both_weights,
            pltpu.SemaphoreType.DMA((2, len(chunks_of(rest)))),
        ],
        limit=24,
        flops=2 * rows * shard * 256,
        moved=4 * 2 * rest * shard,
    )
    (part,) = call(
        third_kernel,
        [((2 * rhs + 8, rows + LANES), F32)],
        [VMEM] * 7,
        (pair_other, coded_a, called_a, coded_b, called_b, half, sums),
        scratch=both_weights,
        flops=2 * rows * shard * 256,
        moved=2 * rows * shard,
    )
    part_other = swap(part, "samp", 1)

    n_chips = n_samp // 2
    distances = partners(n_chips)
    message = ((2 * rhs, rows + 4 * LANES), BF16)
    total, mine, *messages = call(
        functools.partial(chips_kernel, n_var, width, distances),
        [(part.shape, F32), ((2 * rhs + 8, LANES), F32)] + [message] * len(distances),
        [VMEM] * 4,
        (part, part_other, cross, cross_other),
        scratch=[pltpu.VMEM(cross.shape, F32)],
        moved=1 * MIB,
    )
    arrived = [
        lax.ppermute(m, "samp", [(i, i ^ (2 * (one if i % 2 else zero))) for i in range(n_samp)])
        for (zero, one), m in zip(distances, messages)
    ]

    wide = own + 2 * LANES
    mine_back, *messages = call(
        functools.partial(back_kernel, variants, width, len(arrived)),
        [((rhs, wide), F32)] + [((rhs, wide), BF16)] * (n_var - 1),
        [VMEM] * (6 + len(arrived)),
        (total, mine, coded_a, called_a, coded_b, called_b, *arrived),
        flops=4 * rows * shard * 256,
        moved=4 * rows * shard,
    )
    backs = [mine_back] + [swap(messages[k], "var", k + 1) for k in reversed(range(n_var - 1))]

    n_all = n_var * n_samp
    norms, res_keep = call(
        functools.partial(norm_kernel, variants),
        [((n_all, 1, LANES), F32), ((rhs, own), F32)],
        [VMEM] * (3 + n_var),
        (noise, dire, res, *backs),
        moved=4 * n_all * LANES,
    )
    middle = (n_var // 2 - 1) * n_samp + 1
    order = [middle] + [i for i in range(n_all) if i != middle]
    norms = lax.all_to_all(norms, ("var", "samp"), split_axis=0, concat_axis=0, axis_index_groups=[order])
    sol_new, res_new, scores, res_norm = call(
        functools.partial(new_kernel, variants, samples, width),
        [((rhs, own), F32), ((rhs, own), F32), ((rhs, width), F32), ((rhs, LANES), F32)],
        [VMEM] * (4 + n_var),
        (noise, dire, res, sol, *backs),
        moved=1 * MIB,
    )
    (dir_new,) = call(
        direction_kernel,
        [((rhs, own), F32)],
        [VMEM] * 4,
        (norms, res_norm, res_keep, dire),
    )
    return (sol_new.T, res_new.T, dir_new.T, scores.T)


def solution(mesh):
    placed = (
        P("var", "samp"),
        P("var", "samp"),
        P(("samp", "var"), None),
        P(("samp", "var"), None),
        P(),
        P(("samp", "var"), None),
        P(("samp", "var"), None),
        P(("samp", "var"), None),
    )
    return jax.shard_map(
        body,
        mesh=mesh,
        in_specs=placed,
        out_specs=(
            P(("samp", "var"), None),
            P(("samp", "var"), None),
            P(("samp", "var"), None),
            P(("var", "samp"), None),
        ),
        check_vma=False,
    )
```

```python
import functools
import math

import jax
import jax.numpy as jnp
from jax import lax
from jax.experimental import pallas as pl
from jax.experimental.pallas import tpu as pltpu
from jax.sharding import PartitionSpec as P

BF16 = jnp.bfloat16
F32 = jnp.float32
LANES = 128
NT = (((1,), (1,)), ((), ()))
VMEM = pl.BlockSpec(memory_space=pltpu.VMEM)
HBM = pl.BlockSpec(memory_space=pltpu.HBM)
MIB = 1 << 20


def swap(values, axis, distance):
    size = lax.axis_size(axis)
    return lax.ppermute(values, axis, [(i, i ^ distance) for i in range(size)])


def halves(values):
    high = values.astype(BF16)
    return high, (values - high.astype(F32)).astype(BF16)


def thirds(values):
    high = values.astype(BF16)
    rest = values - high.astype(F32)
    middle = rest.astype(BF16)
    return high, middle, (rest - middle.astype(F32)).astype(BF16)


def lane_of(shape):
    return lax.broadcasted_iota(jnp.int32, shape, len(shape) - 1)


def spot(q):
    shape = (16, LANES)
    return lane_of(shape) == 16 * q + lax.broadcasted_iota(jnp.int32, shape, 0)


def as_row(values):
    block = jnp.zeros((16, LANES), F32)
    for q, column in values.items():
        block = jnp.where(spot(q), column, block)
    return jnp.sum(block, axis=0, keepdims=True)


def as_column(row, q):
    return jnp.sum(jnp.where(spot(q), row, 0.0), axis=1, keepdims=True)


def to_column(row):
    shape = (16, row.shape[1])
    same = lax.broadcasted_iota(jnp.int32, shape, 0) == lane_of(shape)
    return jnp.sum(jnp.where(same, row, 0.0), axis=1, keepdims=True)


def convert(gen_ref, call_ref, coded_ref, called_ref, first, rows):
    def group(i, carry):
        part = pl.ds(pl.multiple_of(first + i * 16, 16), 16)
        call = call_ref[part, :].astype(F32).astype(BF16)
        coded_ref[part, :] = gen_ref[part, :].astype(F32).astype(BF16) * call
        called_ref[part, :] = call
        return carry

    lax.fori_loop(0, rows // 16, group, 0)


def row_copies(first, chunk, rows, pairs, sems):
    return [
        [
            pltpu.make_async_copy(
                source.at[pl.ds(first + i * chunk, chunk)], target.at[pl.ds(i * chunk, chunk)], sems.at[j, i]
            )
            for j, (source, target) in enumerate(pairs)
        ]
        for i in range(rows // chunk)
    ]


def first_kernel(chunk, sol_hbm, dir_hbm, res_hbm, gen_hbm, call_hbm, coded_ref, called_ref, sums_ref,
                 sol_ref, dir_ref, res_ref, gbuf, cbuf, small_sems, sems):
    rows = gbuf.shape[0]
    small = [
        pltpu.make_async_copy(source, target, small_sems.at[i])
        for i, (source, target) in enumerate(((sol_hbm, sol_ref), (dir_hbm, dir_ref), (res_hbm, res_ref)))
    ]
    for copy in small:
        copy.start()
    parts = row_copies(0, chunk, rows, ((gen_hbm, gbuf), (call_hbm, cbuf)), sems)
    for part in parts:
        for copy in part:
            copy.start()
    for copy in small:
        copy.wait()
    sol, dire, res = sol_ref[...], dir_ref[...], res_ref[...]
    products = (res * res, dire * dire, sol, sol * sol, sol * dire, dire)
    row = as_row({q: jnp.sum(x, axis=1, keepdims=True) for q, x in enumerate(products)})
    sums_ref[...] = jnp.broadcast_to(row, sums_ref.shape)
    for i, part in enumerate(parts):
        for copy in part:
            copy.wait()
        convert(gbuf, cbuf, coded_ref, called_ref, i * chunk, chunk)


def pair_kernel(own_ref, other_ref, out_ref):
    upper = lax.axis_index("var") % 2
    rhs = own_ref.shape[0]
    own, other = own_ref[...], other_ref[...]
    out_ref[:rhs] = jnp.where(upper == 0, own, other).astype(BF16)
    out_ref[rhs:] = jnp.where(upper == 0, other, own).astype(BF16)


def weights(pair_ref, w1, w2):
    own = pair_ref.shape[1]
    zero = jnp.zeros((16, 2 * own), BF16)
    row = lax.broadcasted_iota(jnp.int32, (16, 2 * own), 0)
    w1[16:32] = zero
    w1[32:48] = jnp.where(row == 0, 1.0, 0.0).astype(BF16)
    w2[0:16] = zero
    w2[32:48] = jnp.where(row == 1, 1.0, 0.0).astype(BF16)
    for i in range(2):
        piece = pair_ref[16 * i : 16 * i + 16]
        w1[0:16, i * own : (i + 1) * own] = piece
        w2[16:32, i * own : (i + 1) * own] = piece


def product(coded_ref, called_ref, first, rows, samples, w1, w2):
    part = pl.ds(first, rows)
    got = lax.dot_general(coded_ref[part, samples], w1[...], NT, preferred_element_type=F32)
    got = got + lax.dot_general(called_ref[part, samples], w2[...], NT, preferred_element_type=F32)
    got = jnp.concatenate([got, jnp.zeros((rows, LANES - got.shape[1]), F32)], axis=1)
    return got.T[:40]


def pair_samples(pair, own):
    return pl.ds(pl.multiple_of(pair * 2 * own, LANES), 2 * own)


def second_kernel(chunk, pair_ref, coded_first, called_first, gen_hbm, call_hbm,
                  coded_ref, called_ref, out_ref, gbuf, cbuf, w1, w2, sems):
    first, rows = coded_first.shape[0], gbuf.shape[0]
    own = pair_ref.shape[1]
    parts = row_copies(first, chunk, rows, ((gen_hbm, gbuf), (call_hbm, cbuf)), sems)
    for part in parts:
        for copy in part:
            copy.start()
    samples = pair_samples(lax.axis_index("var") // 2, own)
    weights(pair_ref, w1, w2)
    for i in range(first // LANES):
        place = i * LANES
        out_ref[:, place : place + LANES] = product(coded_first, called_first, place, LANES, samples, w1, w2)
    for i, part in enumerate(parts):
        for copy in part:
            copy.wait()
        place = i * chunk
        convert(gbuf, cbuf, coded_ref, called_ref, place, chunk)
        out_ref[:, first + place : first + place + chunk] = product(
            coded_ref, called_ref, place, chunk, samples, w1, w2
        )


def third_kernel(pair_ref, coded_first, called_first, coded_ref, called_ref, half_ref, sums_ref, out_ref, w1, w2):
    own = pair_ref.shape[1]
    first, rest = coded_first.shape[0], coded_ref.shape[0]
    samples = pair_samples((lax.axis_index("var") // 2) ^ 1, own)
    weights(pair_ref, w1, w2)
    for i in range((first + rest) // LANES):
        place = i * LANES
        here = slice(place, place + LANES)
        if place < first:
            got = product(coded_first, called_first, place, LANES, samples, w1, w2)
        else:
            got = product(coded_ref, called_ref, place - first, LANES, samples, w1, w2)
        out_ref[:, here] = half_ref[:, here] + got
    out_ref[:, first + rest :] = jnp.zeros((out_ref.shape[0], LANES), F32)
    out_ref[0:8, first + rest :] = sums_ref[...]


def chips_kernel(own_ref, other_ref, total_ref, message):
    rows = own_ref.shape[1] - LANES
    total = own_ref[...] + other_ref[...]
    total_ref[...] = total
    pieces = []
    for part in halves(total[32:34, :rows]):
        part = part.astype(F32)
        for which in range(2):
            for j in range(rows // LANES):
                pieces.append(part[which : which + 1, j * LANES : (j + 1) * LANES])
    pieces += [part.astype(F32) for part in thirds(total[0:1, rows:])]
    pieces.append(jnp.zeros((32 - len(pieces), LANES), F32))
    message[:, :rows] = total[0:32, :rows].astype(BF16)
    message[:, rows:] = jnp.concatenate(pieces, axis=0).astype(BF16)


def dosage_kernel(order_hbm, sol_hbm, dir_hbm, dose_hbm, after_ref, cross_ref,
                  order_ref, sol_ref, dir_ref, dbuf, sems):
    rhs = sol_hbm.shape[0]
    copies = [
        pltpu.make_async_copy(source, target, sems.at[i])
        for i, (source, target) in enumerate(
            ((order_hbm, order_ref), (sol_hbm, sol_ref), (dir_hbm, dir_ref), (dose_hbm, dbuf))
        )
    ]
    for copy in copies:
        copy.start()
    for copy in copies[:3]:
        copy.wait()
    sol_high, sol_low = halves(sol_ref[...])
    dir_high, dir_low = halves(dir_ref[...])
    stack = jnp.concatenate([sol_high, dir_high, sol_low, dir_low], axis=0)
    own = stack.shape[1]
    hot = lax.broadcasted_iota(jnp.int32, (own, own), 0) == order_ref[...]
    hot = jnp.where(hot, 1.0, 0.0).astype(BF16)
    picked = jnp.dot(stack, hot, preferred_element_type=F32).astype(BF16)
    picked = jnp.concatenate([picked, jnp.ones((16, own), BF16)], axis=0)
    copies[3].wait()
    dose = dbuf[...].astype(F32).astype(BF16)
    cross = jnp.dot(picked, dose, preferred_element_type=F32)
    cross_ref[: 2 * rhs] = cross[: 2 * rhs] + cross[2 * rhs : 4 * rhs]
    cross_ref[2 * rhs :] = cross[4 * rhs : 4 * rhs + 8]


def back_kernel(variants, n_arrived, total_ref, coded_first, called_first, coded_ref, called_ref, *rest):
    arrived, own_ref, messages = rest[:n_arrived], rest[n_arrived], rest[n_arrived + 1 :]
    var = lax.axis_index("var")
    rows = total_ref.shape[1] - LANES

    main = total_ref[0:32, :rows]
    allele, count = total_ref[32:33, :rows], total_ref[33:34, :rows]
    extra = jnp.zeros((32, LANES), F32)
    for ref in arrived:
        main = main + ref[:, :rows].astype(F32)
        extra = extra + ref[:, rows:].astype(F32)
    tiles = rows // LANES
    pick = lambda first: jnp.concatenate(
        [extra[first + j : first + j + 1] + extra[first + 2 * tiles + j : first + 2 * tiles + j + 1]
         for j in range(tiles)], axis=1
    )
    allele = allele + pick(0)
    count = count + pick(tiles)
    last = 4 * tiles
    sums = total_ref[0:1, rows:] + extra[last : last + 1] + extra[last + 1 : last + 2] + extra[last + 2 : last + 3]

    frequency = (allele + 1.0) / (2.0 * count + 2.0)
    spread = jnp.sqrt(2.0 * frequency * (1.0 - frequency))
    loading = (main[0:16] - 2.0 * frequency * main[16:32]) / spread
    scaled = loading / spread
    scaled_a = scaled.astype(BF16)
    scaled_b = (-2.0 * frequency * scaled).astype(BF16)
    square = as_row({6: jnp.sum(loading * loading, axis=1, keepdims=True)})
    sums = jnp.where(lane_of((1, LANES)) < 96, sums, square)

    own = own_ref.shape[1] - LANES
    first = coded_first.shape[0]

    def term(p):
        part = pl.ds(pl.multiple_of(p * own, LANES), own)
        got = jnp.dot(scaled_a[:, :first], coded_first[:, part], preferred_element_type=F32)
        got = got + jnp.dot(scaled_a[:, first:], coded_ref[:, part], preferred_element_type=F32)
        got = got + jnp.dot(scaled_b[:, :first], called_first[:, part], preferred_element_type=F32)
        got = got + jnp.dot(scaled_b[:, first:], called_ref[:, part], preferred_element_type=F32)
        return got / variants

    parts = [part.astype(F32) for part in thirds(sums)]
    block = jnp.concatenate(parts + [jnp.zeros((13, LANES), F32)], axis=0).astype(BF16)
    for k, ref in enumerate(messages):
        ref[:, :own] = term(var ^ (k + 1)).astype(BF16)
        ref[:, own:] = block
    own_ref[:, :own] = term(var)
    own_ref[:, own:] = jnp.concatenate([sums, jnp.zeros((15, LANES), F32)], axis=0)


def step_of(refs, noise_row, variants):
    got = refs[0][...]
    for ref in refs[1:]:
        got = got + ref[...].astype(F32)
    own = got.shape[1] - LANES
    back, last = got[:, :own], got[:, own:]
    sums = last[0:1] + last[1:2] + last[2:3]
    column = functools.partial(as_column, sums)
    noise = to_column(noise_row)
    curvature = noise * column(1) + column(6) / variants
    step = column(0) / (curvature + 1e-06)
    return back, column, noise, step


def norm_kernel(variants, width, noise_ref, dir_ref, res_ref, cross_ref, *rest):
    refs, (out_ref, new_ref) = rest[:-2], rest[-2:]
    back, _, noise, step = step_of(refs, noise_ref[...], variants)
    new = res_ref[...] - step * (noise * dir_ref[...] + back)
    new_ref[...] = new
    norm = as_row({6: jnp.sum(new * new, axis=1, keepdims=True)})
    cross = cross_ref[0:16] + step * cross_ref[16:32]
    lane = lane_of((8, LANES))
    top = lax.broadcasted_iota(jnp.int32, (8, LANES), 0) == 0
    norm = jnp.where(top, norm, 0.0)
    for j in range(out_ref.shape[0]):
        tile, inside = (j * width) // LANES * LANES, (j * width) % LANES
        turn = lambda x, to: pltpu.roll(x, (to - inside) % LANES, 1) if (to - inside) % LANES else x
        here = slice(tile, tile + LANES)
        block = jnp.where(lane < width, turn(cross[0:8, here], 0), norm)
        block = jnp.where((lane >= 32) & (lane < 32 + width), turn(cross[8:16, here], 32), block)
        dose = turn(cross_ref[32:40, here], 64)
        out_ref[j] = jnp.where((lane >= 64) & (lane < 64 + width) & top, dose, block)


def new_kernel(variants, noise_ref, dir_ref, res_ref, sol_ref, *rest):
    refs, (sol_out, res_out, stats_out) = rest[:-3], rest[-3:]
    back, column, noise, step = step_of(refs, noise_ref[...], variants)
    dire = dir_ref[...]
    sol_out[...] = sol_ref[...] + step * dire
    res_out[...] = res_ref[...] - step * (noise * dire + back)
    sol_sum = column(2) + step * column(5)
    sol_square = column(3) + 2.0 * step * column(4) + step * (step * column(1))
    lane = lane_of(stats_out.shape)
    stats_out[...] = jnp.where(lane == 0, column(0), jnp.where(lane == 1, sol_sum, sol_square))


def last_kernel(samples, width, came_ref, stats_ref, res_ref, dir_ref, out_ref, score_out):
    total = jnp.sum(came_ref[...], axis=0)
    new_norm = as_column(total[0:1], 6)
    out_ref[...] = res_ref[...] + (new_norm / (stats_ref[:, 0:1] + 1e-06)) * dir_ref[...]
    cross = jnp.concatenate([total, pltpu.roll(total, LANES - 32, 1)], axis=0)
    dose = pltpu.roll(total, LANES - 64, 1)[0:1]
    sol_sum, sol_square = stats_ref[:, 1:2], stats_ref[:, 2:3]
    dose_freq = (dose / 100.0 + 1.0) / (2.0 * samples + 2.0)
    dose_spread = jnp.sqrt(2.0 * dose_freq * (1.0 - dose_freq))
    scale = math.sqrt(samples) * jnp.sqrt(sol_square / samples + 1e-06)
    scores = (cross / 100.0 - 2.0 * dose_freq * sol_sum) / (dose_spread * scale)
    score_out[...] = scores[:, :width]


def call(kernel, out, ins, args, scratch=(), limit=16, flops=0, moved=0):
    return pl.pallas_call(
        kernel,
        out_shape=[jax.ShapeDtypeStruct(*o) if len(o) == 2 else o[2](*o[:2]) for o in out],
        in_specs=list(ins),
        out_specs=[VMEM] * len(out),
        scratch_shapes=list(scratch),
        compiler_params=pltpu.CompilerParams(vmem_limit_bytes=limit * MIB),
        cost_estimate=pl.CostEstimate(flops=flops, bytes_accessed=moved, transcendentals=0),
    )(*[pltpu.with_memory_space_constraint(x, pltpu.HBM) if spec is HBM else x for spec, x in zip(ins, args)])


def body(genotypes, called, dosage, sample_order, noise_ratio, solution, residual, direction):
    n_var = lax.axis_size("var")
    n_samp = lax.axis_size("samp")
    own, rhs = direction.shape
    rows, shard = genotypes.shape
    variants = rows * n_var
    samples = own * n_samp * n_var
    imputed = dosage.shape[1]
    width = imputed // (n_var * n_samp)
    noise = noise_ratio[None]

    dire, res, sol = direction.T, residual.T, solution.T
    first, chunk = rows // 3, 128
    rest = rows - first
    matrix = lambda n: ((n, shard), BF16, pltpu.VMEM)

    neighbour = swap(dire, "var", 1)
    coded_a, called_a, sums = call(
        functools.partial(first_kernel, chunk),
        [matrix(first), matrix(first), ((8, LANES), F32)],
        [HBM] * 5,
        (sol, dire, res, genotypes, called),
        scratch=[
            pltpu.VMEM((rhs, own), F32),
            pltpu.VMEM((rhs, own), F32),
            pltpu.VMEM((rhs, own), F32),
            pltpu.VMEM((first, shard), jnp.int32),
            pltpu.VMEM((first, shard), jnp.int32),
            pltpu.SemaphoreType.DMA((3,)),
            pltpu.SemaphoreType.DMA((2, first // chunk)),
        ],
        limit=24,
        moved=4 * 2 * first * shard,
    )
    (pair,) = call(pair_kernel, [((2 * rhs, own), BF16)], [VMEM] * 2, (dire, neighbour))
    pair_other = swap(pair, "var", 2)
    both_weights = [pltpu.VMEM((48, 2 * own), BF16), pltpu.VMEM((48, 2 * own), BF16)]
    coded_b, called_b, half = call(
        functools.partial(second_kernel, chunk),
        [matrix(rest), matrix(rest), ((2 * rhs + 8, rows), F32)],
        [VMEM] * 3 + [HBM] * 2,
        (pair, coded_a, called_a, genotypes, called),
        scratch=[
            pltpu.VMEM((rest, shard), jnp.int32),
            pltpu.VMEM((rest, shard), jnp.int32),
            *both_weights,
            pltpu.SemaphoreType.DMA((2, rest // chunk)),
        ],
        limit=24,
        flops=2 * rows * shard * 256,
        moved=4 * 2 * rest * shard,
    )
    (part,) = call(
        third_kernel,
        [((2 * rhs + 8, rows + LANES), F32)],
        [VMEM] * 7,
        (pair_other, coded_a, called_a, coded_b, called_b, half, sums),
        scratch=both_weights,
        flops=2 * rows * shard * 256,
        moved=2 * rows * shard,
    )
    part_other = swap(part, "samp", 1)

    n_chips = n_samp // 2
    total, message = call(
        chips_kernel,
        [(part.shape, F32), ((2 * rhs, rows + LANES), BF16)],
        [VMEM] * 2,
        (part, part_other),
        moved=1 * MIB,
    )
    arrived = [swap(message, "samp", 2 * k) for k in range(1, n_chips)]
    (cross,) = call(
        dosage_kernel,
        [((2 * rhs + 8, imputed), F32)],
        [HBM] * 4 + [VMEM],
        (sample_order, sol, dire, dosage, total),
        scratch=[
            pltpu.VMEM((1, own), jnp.int32),
            pltpu.VMEM((rhs, own), F32),
            pltpu.VMEM((rhs, own), F32),
            pltpu.VMEM((own, imputed), jnp.int32),
            pltpu.SemaphoreType.DMA((4,)),
        ],
        flops=2 * 80 * own * (own + imputed),
        moved=4 * own * imputed,
    )

    wide = own + LANES
    mine_back, *messages = call(
        functools.partial(back_kernel, variants, len(arrived)),
        [((rhs, wide), F32)] + [((rhs, wide), BF16)] * (n_var - 1),
        [VMEM] * (5 + len(arrived)),
        (total, coded_a, called_a, coded_b, called_b, *arrived),
        flops=4 * rows * shard * 256,
        moved=4 * rows * shard,
    )
    backs = [mine_back] + [swap(messages[k], "var", k + 1) for k in reversed(range(n_var - 1))]

    n_all = n_var * n_samp
    outgoing, res_keep = call(
        functools.partial(norm_kernel, variants, width),
        [((n_all, 8, LANES), F32), ((rhs, own), F32)],
        [VMEM] * (4 + n_var),
        (noise, dire, res, cross, *backs),
        moved=4 * 8 * n_all * LANES,
    )
    came = lax.all_to_all(outgoing, ("var", "samp"), split_axis=0, concat_axis=0)
    sol_new, res_new, stats = call(
        functools.partial(new_kernel, variants),
        [((rhs, own), F32), ((rhs, own), F32), ((rhs, LANES), F32)],
        [VMEM] * (4 + n_var),
        (noise, dire, res, sol, *backs),
        moved=1 * MIB,
    )
    dir_new, scores = call(
        functools.partial(last_kernel, samples, width),
        [((rhs, own), F32), ((rhs, width), F32)],
        [VMEM] * 4,
        (came, stats, res_keep, dire),
    )
    return (sol_new.T, res_new.T, dir_new.T, scores.T)


def solution(mesh):
    placed = (
        P("var", "samp"),
        P("var", "samp"),
        P(("samp", "var"), None),
        P(("samp", "var"), None),
        P(),
        P(("samp", "var"), None),
        P(("samp", "var"), None),
        P(("samp", "var"), None),
    )
    return jax.shard_map(
        body,
        mesh=mesh,
        in_specs=placed,
        out_specs=(
            P(("samp", "var"), None),
            P(("samp", "var"), None),
            P(("samp", "var"), None),
            P(("var", "samp"), None),
        ),
        check_vma=False,
    )
```

```python
import functools
import math

import jax
import jax.numpy as jnp
from jax import lax
from jax.experimental import pallas as pl
from jax.experimental.pallas import tpu as pltpu
from jax.sharding import PartitionSpec as P

BF16 = jnp.bfloat16
F32 = jnp.float32
LANES = 128
NT = (((1,), (1,)), ((), ()))
VMEM = pl.BlockSpec(memory_space=pltpu.VMEM)
HBM = pl.BlockSpec(memory_space=pltpu.HBM)
MIB = 1 << 20


def swap(values, axis, distance):
    size = lax.axis_size(axis)
    return lax.ppermute(values, axis, [(i, i ^ distance) for i in range(size)])


def halves(values):
    high = values.astype(BF16)
    return high, (values - high.astype(F32)).astype(BF16)


def thirds(values):
    high = values.astype(BF16)
    rest = values - high.astype(F32)
    middle = rest.astype(BF16)
    return high, middle, (rest - middle.astype(F32)).astype(BF16)


def lane_of(shape):
    return lax.broadcasted_iota(jnp.int32, shape, len(shape) - 1)


def spot(q):
    shape = (16, LANES)
    return lane_of(shape) == 16 * q + lax.broadcasted_iota(jnp.int32, shape, 0)


def as_row(values):
    block = jnp.zeros((16, LANES), F32)
    for q, column in values.items():
        block = jnp.where(spot(q), column, block)
    return jnp.sum(block, axis=0, keepdims=True)


def as_column(row, q):
    return jnp.sum(jnp.where(spot(q), row, 0.0), axis=1, keepdims=True)


def to_column(row):
    shape = (16, row.shape[1])
    same = lax.broadcasted_iota(jnp.int32, shape, 0) == lane_of(shape)
    return jnp.sum(jnp.where(same, row, 0.0), axis=1, keepdims=True)


def rows_of_16(count, step):
    def group(i, carry):
        step(pl.ds(pl.multiple_of(i * 16, 16), 16))
        return carry

    lax.fori_loop(0, count // 16, group, 0)


def row_copies(source, target, first, chunk, sems):
    return [
        pltpu.make_async_copy(source.at[pl.ds(first + i, chunk)], target.at[pl.ds(i, chunk)], sems.at[i // chunk])
        for i in range(0, target.shape[0], chunk)
    ]


def genotype_kernel(chunk, sol_hbm, dir_hbm, res_hbm, gen_hbm, out_ref, sums_ref,
                    sol_ref, dir_ref, res_ref, gbuf, small_sems, sems):
    small = [
        pltpu.make_async_copy(source, target, small_sems.at[i])
        for i, (source, target) in enumerate(((sol_hbm, sol_ref), (dir_hbm, dir_ref), (res_hbm, res_ref)))
    ]
    for copy in small:
        copy.start()
    parts = row_copies(gen_hbm, gbuf, 0, chunk, sems)
    for copy in parts:
        copy.start()
    for copy in small:
        copy.wait()
    sol, dire, res = sol_ref[...], dir_ref[...], res_ref[...]
    products = (res * res, dire * dire, sol, sol * sol, sol * dire, dire)
    row = as_row({q: jnp.sum(x, axis=1, keepdims=True) for q, x in enumerate(products)})
    sums_ref[...] = jnp.broadcast_to(row, sums_ref.shape)
    for i, copy in enumerate(parts):
        copy.wait()
        source, target = gbuf.at[pl.ds(i * chunk, chunk)], out_ref.at[pl.ds(i * chunk, chunk)]

        def step(part):
            target[part, :] = source[part, :].astype(F32).astype(BF16)

        rows_of_16(chunk, step)


def pair_kernel(own_ref, other_ref, out_ref):
    upper = lax.axis_index("var") % 2
    rhs = own_ref.shape[0]
    own, other = own_ref[...], other_ref[...]
    out_ref[:rhs] = jnp.where(upper == 0, own, other).astype(BF16)
    out_ref[rhs:] = jnp.where(upper == 0, other, own).astype(BF16)


def weights(pair_ref, w1, w2):
    own = pair_ref.shape[1]
    zero = jnp.zeros((16, 2 * own), BF16)
    row = lax.broadcasted_iota(jnp.int32, (16, 2 * own), 0)
    w1[16:32] = zero
    w1[32:48] = jnp.where(row == 0, 1.0, 0.0).astype(BF16)
    w2[0:16] = zero
    w2[32:48] = jnp.where(row == 1, 1.0, 0.0).astype(BF16)
    for i in range(2):
        piece = pair_ref[16 * i : 16 * i + 16]
        w1[0:16, i * own : (i + 1) * own] = piece
        w2[16:32, i * own : (i + 1) * own] = piece


def product(coded_ref, called_ref, first, rows, samples, w1, w2):
    part = pl.ds(first, rows)
    got = lax.dot_general(coded_ref[part, samples], w1[...], NT, preferred_element_type=F32)
    got = got + lax.dot_general(called_ref[part, samples], w2[...], NT, preferred_element_type=F32)
    got = jnp.concatenate([got, jnp.zeros((rows, LANES - got.shape[1]), F32)], axis=1)
    return got.T[:40]


def pair_samples(pair, own):
    return pl.ds(pl.multiple_of(pair * 2 * own, LANES), 2 * own)


def mask_kernel(pair_ref, first_ref, call_ref, gen_hbm, coded_ref, called_ref, out_ref, gbuf, w1, w2, sems):
    own = pair_ref.shape[1]
    first = first_ref.shape[0]
    copies = row_copies(gen_hbm, gbuf, first, LANES, sems)
    for copy in copies:
        copy.start()
    samples = pair_samples(lax.axis_index("var") // 2, own)
    weights(pair_ref, w1, w2)
    for place in range(0, call_ref.shape[0], LANES):
        here = pl.ds(place, LANES)
        if place < first:
            gen = first_ref.at[here]
        else:
            gen = gbuf.at[pl.ds(place - first, LANES)]
            copies[(place - first) // LANES].wait()
        call, coded, called = call_ref.at[here], coded_ref.at[here], called_ref.at[here]

        def step(part):
            mask = call[part, :].astype(F32).astype(BF16)
            coded[part, :] = gen[part, :].astype(F32).astype(BF16) * mask
            called[part, :] = mask

        rows_of_16(LANES, step)
        out_ref[:, place : place + LANES] = product(coded_ref, called_ref, place, LANES, samples, w1, w2)


def forward_kernel(pair_ref, coded_ref, called_ref, half_ref, sums_ref, out_ref, w1, w2):
    own = pair_ref.shape[1]
    rows = coded_ref.shape[0]
    samples = pair_samples((lax.axis_index("var") // 2) ^ 1, own)
    weights(pair_ref, w1, w2)
    for place in range(0, rows, LANES):
        here = slice(place, place + LANES)
        out_ref[:, here] = half_ref[:, here] + product(coded_ref, called_ref, place, LANES, samples, w1, w2)
    out_ref[:, rows:] = jnp.zeros((out_ref.shape[0], LANES), F32)
    out_ref[0:8, rows:] = sums_ref[...]


def chips_kernel(own_ref, other_ref, total_ref, *messages):
    rows = own_ref.shape[1] - LANES
    total = own_ref[...] + other_ref[...]
    total_ref[...] = total
    pieces = []
    for part in halves(total[32:34, :rows]):
        part = part.astype(F32)
        for which in range(2):
            for j in range(rows // LANES):
                pieces.append(part[which : which + 1, j * LANES : (j + 1) * LANES])
    pieces += [part.astype(F32) for part in thirds(total[0:1, rows:])]
    pieces.append(jnp.zeros((32 - len(pieces), LANES), F32))
    extra = jnp.concatenate(pieces, axis=0).astype(BF16)
    for message in messages:
        message[:, :rows] = total[0:32, :rows].astype(BF16)
        message[:, rows:] = extra


def dosage_kernel(order_ref, sol_ref, dir_ref, dose_ref, after_ref, cross_ref):
    rhs = sol_ref.shape[0]
    sol_high, sol_low = halves(sol_ref[...])
    dir_high, dir_low = halves(dir_ref[...])
    stack = jnp.concatenate([sol_high, dir_high, sol_low, dir_low], axis=0)
    own = stack.shape[1]
    hot = lax.broadcasted_iota(jnp.int32, (own, own), 0) == order_ref[...]
    hot = jnp.where(hot, 1.0, 0.0).astype(BF16)
    picked = jnp.dot(stack, hot, preferred_element_type=F32).astype(BF16)
    picked = jnp.concatenate([picked, jnp.ones((16, own), BF16)], axis=0)
    dose = dose_ref[...].astype(F32).astype(BF16)
    cross = jnp.dot(picked, dose, preferred_element_type=F32)
    cross_ref[: 2 * rhs] = cross[: 2 * rhs] + cross[2 * rhs : 4 * rhs]
    cross_ref[2 * rhs :] = cross[4 * rhs : 4 * rhs + 8]


def back_kernel(variants, n_arrived, total_ref, coded_ref, called_ref, *rest):
    arrived, own_ref, messages = rest[:n_arrived], rest[n_arrived], rest[n_arrived + 1 :]
    var = lax.axis_index("var")
    rows = total_ref.shape[1] - LANES

    main = total_ref[0:32, :rows]
    allele, count = total_ref[32:33, :rows], total_ref[33:34, :rows]
    extra = jnp.zeros((32, LANES), F32)
    for ref in arrived:
        main = main + ref[:, :rows].astype(F32)
        extra = extra + ref[:, rows:].astype(F32)
    tiles = rows // LANES
    pick = lambda first: jnp.concatenate(
        [extra[first + j : first + j + 1] + extra[first + 2 * tiles + j : first + 2 * tiles + j + 1]
         for j in range(tiles)], axis=1
    )
    allele = allele + pick(0)
    count = count + pick(tiles)
    last = 4 * tiles
    sums = total_ref[0:1, rows:] + extra[last : last + 1] + extra[last + 1 : last + 2] + extra[last + 2 : last + 3]

    frequency = (allele + 1.0) / (2.0 * count + 2.0)
    spread = jnp.sqrt(2.0 * frequency * (1.0 - frequency))
    loading = (main[0:16] - 2.0 * frequency * main[16:32]) / spread
    scaled = loading / spread
    scaled_a = scaled.astype(BF16)
    scaled_b = (-2.0 * frequency * scaled).astype(BF16)
    square = as_row({6: jnp.sum(loading * loading, axis=1, keepdims=True)})
    sums = jnp.where(lane_of((1, LANES)) < 96, sums, square)

    own = own_ref.shape[1] - LANES

    def term(p):
        part = pl.ds(pl.multiple_of(p * own, LANES), own)
        got = jnp.dot(scaled_a, coded_ref[:, part], preferred_element_type=F32)
        got = got + jnp.dot(scaled_b, called_ref[:, part], preferred_element_type=F32)
        return got / variants

    parts = [part.astype(F32) for part in thirds(sums)]
    block = jnp.concatenate(parts + [jnp.zeros((13, LANES), F32)], axis=0).astype(BF16)
    for k, ref in enumerate(messages):
        ref[:, :own] = term(var ^ (k + 1)).astype(BF16)
        ref[:, own:] = block
    own_ref[:, :own] = term(var)
    own_ref[:, own:] = jnp.concatenate([sums, jnp.zeros((15, LANES), F32)], axis=0)


def step_of(refs, noise_row, variants):
    got = refs[0][...]
    for ref in refs[1:]:
        got = got + ref[...].astype(F32)
    own = got.shape[1] - LANES
    back, last = got[:, :own], got[:, own:]
    sums = last[0:1] + last[1:2] + last[2:3]
    column = functools.partial(as_column, sums)
    noise = to_column(noise_row)
    curvature = noise * column(1) + column(6) / variants
    step = column(0) / (curvature + 1e-06)
    return back, column, noise, step


def norm_kernel(variants, width, noise_ref, dir_ref, res_ref, cross_ref, *rest):
    refs, (out_ref, new_ref) = rest[:-2], rest[-2:]
    back, _, noise, step = step_of(refs, noise_ref[...], variants)
    new = res_ref[...] - step * (noise * dir_ref[...] + back)
    new_ref[...] = new
    norm = as_row({6: jnp.sum(new * new, axis=1, keepdims=True)})
    cross = cross_ref[0:16] + step * cross_ref[16:32]
    dose = cross_ref[32:40]
    lane = lane_of((16, LANES))
    row = lax.broadcasted_iota(jnp.int32, (16, LANES), 0)
    turned = {}

    def turn(values, name, tile, by):
        if (name, tile, by) not in turned:
            piece = values[:, tile : tile + LANES]
            turned[name, tile, by] = pltpu.roll(piece, by, 1) if by else piece
        return turned[name, tile, by]

    for j in range(out_ref.shape[0]):
        tile, inside = (j * width) // LANES * LANES, (j * width) % LANES
        block = jnp.zeros((16, LANES), F32)
        for m in range(4):
            here = (row // 4 == m) & (lane >= 32 * m) & (lane < 32 * m + width)
            block = jnp.where(here, turn(cross, "cross", tile, (32 * m - inside) % LANES), block)
        block = block[0:8] + block[8:16]
        block = block[0:4] + block[4:8]
        last = jnp.where(lane[0:1] < width, turn(dose, "dose", tile, -inside % LANES)[0:1], norm)
        for k in range(4):
            out_ref[j, :, k * LANES : (k + 1) * LANES] = block[k : k + 1]
        out_ref[j, :, 4 * LANES :] = last


def new_kernel(variants, noise_ref, dir_ref, res_ref, sol_ref, *rest):
    refs, (sol_out, res_out, stats_out) = rest[:-3], rest[-3:]
    back, column, noise, step = step_of(refs, noise_ref[...], variants)
    dire = dir_ref[...]
    sol_out[...] = sol_ref[...] + step * dire
    res_out[...] = res_ref[...] - step * (noise * dire + back)
    sol_sum = column(2) + step * column(5)
    sol_square = column(3) + 2.0 * step * column(4) + step * (step * column(1))
    lane = lane_of(stats_out.shape)
    stats_out[...] = jnp.where(lane == 0, column(0), jnp.where(lane == 1, sol_sum, sol_square))


def last_kernel(samples, width, came_ref, stats_ref, res_ref, dir_ref, out_ref, score_out):
    total = jnp.sum(came_ref[...], axis=0)
    last = total[:, 4 * LANES :]
    out_ref[...] = res_ref[...] + (as_column(last, 6) / (stats_ref[:, 0:1] + 1e-06)) * dir_ref[...]
    row = lax.broadcasted_iota(jnp.int32, (16, LANES), 0)
    spread = jnp.zeros((16, LANES), F32)
    for k in range(4):
        spread = jnp.where(row % 4 == k, total[:, k * LANES : (k + 1) * LANES], spread)
    cross = spread
    for m in range(1, 4):
        cross = jnp.where(row // 4 == m, pltpu.roll(spread, LANES - 32 * m, 1), cross)
    dose = last
    sol_sum, sol_square = stats_ref[:, 1:2], stats_ref[:, 2:3]
    dose_freq = (dose / 100.0 + 1.0) / (2.0 * samples + 2.0)
    dose_spread = jnp.sqrt(2.0 * dose_freq * (1.0 - dose_freq))
    scale = math.sqrt(samples) * jnp.sqrt(sol_square / samples + 1e-06)
    scores = (cross / 100.0 - 2.0 * dose_freq * sol_sum) / (dose_spread * scale)
    score_out[...] = scores[:, :width]


def call(kernel, out, ins, args, scratch=(), limit=16, flops=0, moved=0):
    return pl.pallas_call(
        kernel,
        out_shape=[jax.ShapeDtypeStruct(*o) if len(o) == 2 else o[2](*o[:2]) for o in out],
        in_specs=list(ins),
        out_specs=[VMEM] * len(out),
        scratch_shapes=list(scratch),
        compiler_params=pltpu.CompilerParams(vmem_limit_bytes=limit * MIB),
        cost_estimate=pl.CostEstimate(flops=flops, bytes_accessed=moved, transcendentals=0),
    )(*[pltpu.with_memory_space_constraint(x, pltpu.HBM) if spec is HBM else x for spec, x in zip(ins, args)])


def body(genotypes, called, dosage, sample_order, noise_ratio, solution, residual, direction):
    n_var = lax.axis_size("var")
    n_samp = lax.axis_size("samp")
    own, rhs = direction.shape
    rows, shard = genotypes.shape
    variants = rows * n_var
    samples = own * n_samp * n_var
    imputed = dosage.shape[1]
    width = imputed // (n_var * n_samp)
    noise = noise_ratio[None]

    dire, res, sol = direction.T, residual.T, solution.T
    first, chunk = rows // 3, 128
    matrix = lambda n: ((n, shard), BF16, pltpu.VMEM)

    neighbour = swap(dire, "var", 1)
    coarse, sums = call(
        functools.partial(genotype_kernel, chunk),
        [matrix(first), ((8, LANES), F32)],
        [HBM] * 4,
        (sol, dire, res, genotypes),
        scratch=[
            pltpu.VMEM((rhs, own), F32),
            pltpu.VMEM((rhs, own), F32),
            pltpu.VMEM((rhs, own), F32),
            pltpu.VMEM((first, shard), jnp.int32),
            pltpu.SemaphoreType.DMA((3,)),
            pltpu.SemaphoreType.DMA((first // chunk,)),
        ],
        limit=6,
        moved=4 * first * shard,
    )
    (pair,) = call(pair_kernel, [((2 * rhs, own), BF16)], [VMEM] * 2, (dire, neighbour), limit=4)
    pair_other = swap(pair, "var", 2)
    both_weights = [pltpu.VMEM((48, 2 * own), BF16), pltpu.VMEM((48, 2 * own), BF16)]
    coded, called_b, half = call(
        mask_kernel,
        [matrix(rows), matrix(rows), ((2 * rhs + 8, rows), F32)],
        [VMEM] * 3 + [HBM],
        (pair, coarse, called, genotypes),
        scratch=[
            pltpu.VMEM((rows - first, shard), jnp.int32),
            *both_weights,
            pltpu.SemaphoreType.DMA(((rows - first) // LANES,)),
        ],
        limit=12,
        flops=2 * rows * shard * 256,
        moved=4 * rows * shard,
    )
    (part,) = call(
        forward_kernel,
        [((2 * rhs + 8, rows + LANES), F32)],
        [VMEM] * 5,
        (pair_other, coded, called_b, half, sums),
        scratch=both_weights,
        flops=2 * rows * shard * 256,
        moved=2 * rows * shard,
    )
    part_other = swap(part, "samp", 1)

    n_chips = n_samp // 2
    total, *messages = call(
        chips_kernel,
        [(part.shape, F32)] + [((2 * rhs, rows + LANES), BF16)] * (n_chips - 1),
        [VMEM] * 2,
        (part, part_other),
        moved=1 * MIB,
    )
    arrived = [swap(messages[k], "samp", 2 * (k + 1)) for k in reversed(range(n_chips - 1))]
    (cross,) = call(
        dosage_kernel,
        [((2 * rhs + 8, imputed), F32)],
        [VMEM] * 5,
        (sample_order, sol, dire, dosage, total),
        flops=2 * 80 * own * (own + imputed),
        moved=4 * own * imputed,
    )

    wide = own + LANES
    mine_back, *messages = call(
        functools.partial(back_kernel, variants, len(arrived)),
        [((rhs, wide), F32)] + [((rhs, wide), BF16)] * (n_var - 1),
        [VMEM] * (3 + len(arrived)),
        (total, coded, called_b, *arrived),
        flops=4 * rows * shard * 256,
        moved=4 * rows * shard,
    )
    backs = [mine_back] + [swap(messages[k], "var", k + 1) for k in reversed(range(n_var - 1))]

    n_all = n_var * n_samp
    outgoing, res_keep = call(
        functools.partial(norm_kernel, variants, width),
        [((n_all, 1, 5 * LANES), F32), ((rhs, own), F32)],
        [VMEM] * (4 + n_var),
        (noise, dire, res, cross, *backs),
        moved=4 * 5 * n_all * LANES,
    )
    came = lax.all_to_all(outgoing, ("var", "samp"), split_axis=0, concat_axis=0)
    sol_new, res_new, stats = call(
        functools.partial(new_kernel, variants),
        [((rhs, own), F32), ((rhs, own), F32), ((rhs, LANES), F32)],
        [VMEM] * (4 + n_var),
        (noise, dire, res, sol, *backs),
        moved=1 * MIB,
    )
    dir_new, scores = call(
        functools.partial(last_kernel, samples, width),
        [((rhs, own), F32), ((rhs, width), F32)],
        [VMEM] * 4,
        (came, stats, res_keep, dire),
    )
    return (sol_new.T, res_new.T, dir_new.T, scores.T)


def solution(mesh):
    placed = (
        P("var", "samp"),
        P("var", "samp"),
        P(("samp", "var"), None),
        P(("samp", "var"), None),
        P(),
        P(("samp", "var"), None),
        P(("samp", "var"), None),
        P(("samp", "var"), None),
    )
    return jax.shard_map(
        body,
        mesh=mesh,
        in_specs=placed,
        out_specs=(
            P(("samp", "var"), None),
            P(("samp", "var"), None),
            P(("samp", "var"), None),
            P(("var", "samp"), None),
        ),
        check_vma=False,
    )
```

```python
import functools
import math

import jax
import jax.numpy as jnp
from jax import lax
from jax.experimental import pallas as pl
from jax.experimental.pallas import tpu as pltpu
from jax.sharding import PartitionSpec as P

BF16 = jnp.bfloat16
F32 = jnp.float32
LANES = 128
NT = (((1,), (1,)), ((), ()))
VMEM = pl.BlockSpec(memory_space=pltpu.VMEM)
HBM = pl.BlockSpec(memory_space=pltpu.HBM)
MIB = 1 << 20


def swap(values, axis, distance):
    size = lax.axis_size(axis)
    return lax.ppermute(values, axis, [(i, i ^ distance) for i in range(size)])


def halves(values):
    high = values.astype(BF16)
    return high, (values - high.astype(F32)).astype(BF16)


def thirds(values):
    high = values.astype(BF16)
    rest = values - high.astype(F32)
    middle = rest.astype(BF16)
    return high, middle, (rest - middle.astype(F32)).astype(BF16)


def lane_of(shape):
    return lax.broadcasted_iota(jnp.int32, shape, len(shape) - 1)


def spot(q):
    shape = (16, LANES)
    return lane_of(shape) == 16 * q + lax.broadcasted_iota(jnp.int32, shape, 0)


def as_row(values):
    block = jnp.zeros((16, LANES), F32)
    for q, column in values.items():
        block = jnp.where(spot(q), column, block)
    return jnp.sum(block, axis=0, keepdims=True)


def as_column(row, q):
    return jnp.sum(jnp.where(spot(q), row, 0.0), axis=1, keepdims=True)


def to_column(row):
    shape = (16, row.shape[1])
    same = lax.broadcasted_iota(jnp.int32, shape, 0) == lane_of(shape)
    return jnp.sum(jnp.where(same, row, 0.0), axis=1, keepdims=True)


BLOCK = 512


def blocks(rows, samples):
    return [
        (pl.ds(row, 16), pl.ds(sample, BLOCK)) for row in range(0, rows, 16) for sample in range(0, samples, BLOCK)
    ]


def row_copies(source, target, first, chunk, sems):
    return [
        pltpu.make_async_copy(source.at[pl.ds(first + i, chunk)], target.at[pl.ds(i, chunk)], sems.at[i // chunk])
        for i in range(0, target.shape[0], chunk)
    ]


def genotype_kernel(chunk, sol_hbm, dir_hbm, res_hbm, gen_hbm, out_ref, sums_ref,
                    sol_ref, dir_ref, res_ref, gbuf, small_sems, sems):
    small = [
        pltpu.make_async_copy(source, target, small_sems.at[i])
        for i, (source, target) in enumerate(((sol_hbm, sol_ref), (dir_hbm, dir_ref), (res_hbm, res_ref)))
    ]
    for copy in small:
        copy.start()
    parts = row_copies(gen_hbm, gbuf, 0, chunk, sems)
    for copy in parts:
        copy.start()
    for copy in small:
        copy.wait()
    sol, dire, res = sol_ref[...], dir_ref[...], res_ref[...]
    products = (res * res, dire * dire, sol, sol * sol, sol * dire, dire)
    row = as_row({q: jnp.sum(x, axis=1, keepdims=True) for q, x in enumerate(products)})
    sums_ref[...] = jnp.broadcast_to(row, sums_ref.shape)
    for i, copy in enumerate(parts):
        copy.wait()
        source, target = gbuf.at[pl.ds(i * chunk, chunk)], out_ref.at[pl.ds(i * chunk, chunk)]
        for here in blocks(chunk, source.shape[1]):
            target[here] = source[here].astype(F32).astype(BF16)


def pair_kernel(own_ref, other_ref, out_ref):
    upper = lax.axis_index("var") % 2
    rhs = own_ref.shape[0]
    own, other = own_ref[...], other_ref[...]
    out_ref[:rhs] = jnp.where(upper == 0, own, other).astype(BF16)
    out_ref[rhs:] = jnp.where(upper == 0, other, own).astype(BF16)


def weights(pair_ref, w1, w2):
    own = pair_ref.shape[1]
    zero = jnp.zeros((16, 2 * own), BF16)
    row = lax.broadcasted_iota(jnp.int32, (16, 2 * own), 0)
    w1[16:32] = zero
    w1[32:48] = jnp.where(row == 0, 1.0, 0.0).astype(BF16)
    w2[0:16] = zero
    w2[32:48] = jnp.where(row == 1, 1.0, 0.0).astype(BF16)
    for i in range(2):
        piece = pair_ref[16 * i : 16 * i + 16]
        w1[0:16, i * own : (i + 1) * own] = piece
        w2[16:32, i * own : (i + 1) * own] = piece


def product(coded_ref, called_ref, first, rows, samples, w1, w2):
    part = pl.ds(first, rows)
    got = lax.dot_general(coded_ref[part, samples], w1[...], NT, preferred_element_type=F32)
    got = got + lax.dot_general(called_ref[part, samples], w2[...], NT, preferred_element_type=F32)
    got = jnp.concatenate([got, jnp.zeros((rows, LANES - got.shape[1]), F32)], axis=1)
    return got.T[:40]


def pair_samples(pair, own):
    return pl.ds(pl.multiple_of(pair * 2 * own, LANES), 2 * own)


def mask_kernel(pair_ref, first_ref, call_ref, gen_hbm, coded_ref, called_ref, out_ref, gbuf, w1, w2, sems):
    own = pair_ref.shape[1]
    first = first_ref.shape[0]
    copies = row_copies(gen_hbm, gbuf, first, LANES, sems)
    for copy in copies:
        copy.start()
    samples = pair_samples(lax.axis_index("var") // 2, own)
    weights(pair_ref, w1, w2)
    rows, shard = call_ref.shape

    def convert(place):
        here = pl.ds(place, LANES)
        gen = first_ref.at[here] if place < first else gbuf.at[pl.ds(place - first, LANES)]
        call, coded, called = call_ref.at[here], coded_ref.at[here], called_ref.at[here]
        for block in blocks(LANES, shard):
            mask = call[block].astype(F32).astype(BF16)
            value = gen[block] if place < first else gen[block].astype(F32).astype(BF16)
            coded[block] = value * mask
            called[block] = mask

    for place in range(0, rows + LANES, LANES):
        if first <= place < rows:
            copies[(place - first) // LANES].wait()
        if place < rows:
            convert(place)
        if place:
            before = place - LANES
            out_ref[:, before:place] = product(coded_ref, called_ref, before, LANES, samples, w1, w2)


def forward_kernel(pair_ref, coded_ref, called_ref, half_ref, sums_ref, out_ref, w1, w2):
    own = pair_ref.shape[1]
    rows = coded_ref.shape[0]
    samples = pair_samples((lax.axis_index("var") // 2) ^ 1, own)
    weights(pair_ref, w1, w2)
    for place in range(0, rows, LANES):
        here = slice(place, place + LANES)
        out_ref[:, here] = half_ref[:, here] + product(coded_ref, called_ref, place, LANES, samples, w1, w2)
    out_ref[:, rows:] = jnp.zeros((out_ref.shape[0], LANES), F32)
    out_ref[0:8, rows:] = sums_ref[...]


def chips_kernel(own_ref, other_ref, total_ref, *messages):
    rows = own_ref.shape[1] - LANES
    total = own_ref[...] + other_ref[...]
    total_ref[...] = total
    pieces = []
    for part in halves(total[32:34, :rows]):
        part = part.astype(F32)
        for which in range(2):
            for j in range(rows // LANES):
                pieces.append(part[which : which + 1, j * LANES : (j + 1) * LANES])
    pieces += [part.astype(F32) for part in thirds(total[0:1, rows:])]
    pieces.append(jnp.zeros((32 - len(pieces), LANES), F32))
    extra = jnp.concatenate(pieces, axis=0).astype(BF16)
    for message in messages:
        message[:, :rows] = total[0:32, :rows].astype(BF16)
        message[:, rows:] = extra


def dosage_kernel(order_ref, sol_ref, dir_ref, dose_ref, after_ref, cross_ref):
    rhs = sol_ref.shape[0]
    sol_high, sol_low = halves(sol_ref[...])
    dir_high, dir_low = halves(dir_ref[...])
    stack = jnp.concatenate([sol_high, dir_high, sol_low, dir_low], axis=0)
    own = stack.shape[1]
    hot = lax.broadcasted_iota(jnp.int32, (own, own), 0) == order_ref[...]
    hot = jnp.where(hot, 1.0, 0.0).astype(BF16)
    picked = jnp.dot(stack, hot, preferred_element_type=F32).astype(BF16)
    picked = jnp.concatenate([picked, jnp.ones((16, own), BF16)], axis=0)
    dose = dose_ref[...].astype(F32).astype(BF16)
    cross = jnp.dot(picked, dose, preferred_element_type=F32)
    cross_ref[: 2 * rhs] = cross[: 2 * rhs] + cross[2 * rhs : 4 * rhs]
    cross_ref[2 * rhs :] = cross[4 * rhs : 4 * rhs + 8]


def back_kernel(variants, n_arrived, total_ref, coded_ref, called_ref, *rest):
    arrived, own_ref, messages = rest[:n_arrived], rest[n_arrived], rest[n_arrived + 1 :]
    var = lax.axis_index("var")
    rows = total_ref.shape[1] - LANES

    main = total_ref[0:32, :rows]
    allele, count = total_ref[32:33, :rows], total_ref[33:34, :rows]
    extra = jnp.zeros((32, LANES), F32)
    for ref in arrived:
        main = main + ref[:, :rows].astype(F32)
        extra = extra + ref[:, rows:].astype(F32)
    tiles = rows // LANES
    pick = lambda first: jnp.concatenate(
        [extra[first + j : first + j + 1] + extra[first + 2 * tiles + j : first + 2 * tiles + j + 1]
         for j in range(tiles)], axis=1
    )
    allele = allele + pick(0)
    count = count + pick(tiles)
    last = 4 * tiles
    sums = total_ref[0:1, rows:] + extra[last : last + 1] + extra[last + 1 : last + 2] + extra[last + 2 : last + 3]

    frequency = (allele + 1.0) / (2.0 * count + 2.0)
    spread = jnp.sqrt(2.0 * frequency * (1.0 - frequency))
    loading = (main[0:16] - 2.0 * frequency * main[16:32]) / spread
    scaled = loading / spread
    scaled_a = scaled.astype(BF16)
    scaled_b = (-2.0 * frequency * scaled).astype(BF16)
    square = as_row({6: jnp.sum(loading * loading, axis=1, keepdims=True)})
    sums = jnp.where(lane_of((1, LANES)) < 96, sums, square)

    own = own_ref.shape[1] - LANES

    def term(p):
        part = pl.ds(pl.multiple_of(p * own, LANES), own)
        got = jnp.dot(scaled_a, coded_ref[:, part], preferred_element_type=F32)
        got = got + jnp.dot(scaled_b, called_ref[:, part], preferred_element_type=F32)
        return got / variants

    parts = [part.astype(F32) for part in thirds(sums)]
    block = jnp.concatenate(parts + [jnp.zeros((13, LANES), F32)], axis=0).astype(BF16)
    for k, ref in enumerate(messages):
        ref[:, :own] = term(var ^ (k + 1)).astype(BF16)
        ref[:, own:] = block
    own_ref[:, :own] = term(var)
    own_ref[:, own:] = jnp.concatenate([sums, jnp.zeros((15, LANES), F32)], axis=0)


def step_of(refs, noise_row, variants):
    got = refs[0][...]
    for ref in refs[1:]:
        got = got + ref[...].astype(F32)
    own = got.shape[1] - LANES
    back, last = got[:, :own], got[:, own:]
    sums = last[0:1] + last[1:2] + last[2:3]
    column = functools.partial(as_column, sums)
    noise = to_column(noise_row)
    curvature = noise * column(1) + column(6) / variants
    step = column(0) / (curvature + 1e-06)
    return back, column, noise, step


def norm_kernel(variants, width, noise_ref, dir_ref, res_ref, cross_ref, *rest):
    refs, (out_ref, new_ref) = rest[:-2], rest[-2:]
    back, _, noise, step = step_of(refs, noise_ref[...], variants)
    new = res_ref[...] - step * (noise * dir_ref[...] + back)
    new_ref[...] = new
    norm = as_row({6: jnp.sum(new * new, axis=1, keepdims=True)})
    cross = cross_ref[0:16] + step * cross_ref[16:32]
    dose = cross_ref[32:40]
    lane = lane_of((16, LANES))
    row = lax.broadcasted_iota(jnp.int32, (16, LANES), 0)
    turned = {}

    def turn(values, name, tile, by):
        if (name, tile, by) not in turned:
            piece = values[:, tile : tile + LANES]
            turned[name, tile, by] = pltpu.roll(piece, by, 1) if by else piece
        return turned[name, tile, by]

    for j in range(out_ref.shape[0]):
        tile, inside = (j * width) // LANES * LANES, (j * width) % LANES
        block = jnp.zeros((16, LANES), F32)
        for m in range(4):
            here = (row // 4 == m) & (lane >= 32 * m) & (lane < 32 * m + width)
            block = jnp.where(here, turn(cross, "cross", tile, (32 * m - inside) % LANES), block)
        block = block[0:8] + block[8:16]
        block = block[0:4] + block[4:8]
        last = jnp.where(lane[0:1] < width, turn(dose, "dose", tile, -inside % LANES)[0:1], norm)
        for k in range(4):
            out_ref[j, :, k * LANES : (k + 1) * LANES] = block[k : k + 1]
        out_ref[j, :, 4 * LANES :] = last


def new_kernel(variants, noise_ref, dir_ref, res_ref, sol_ref, *rest):
    refs, (sol_out, res_out, stats_out) = rest[:-3], rest[-3:]
    back, column, noise, step = step_of(refs, noise_ref[...], variants)
    dire = dir_ref[...]
    sol_out[...] = sol_ref[...] + step * dire
    res_out[...] = res_ref[...] - step * (noise * dire + back)
    sol_sum = column(2) + step * column(5)
    sol_square = column(3) + 2.0 * step * column(4) + step * (step * column(1))
    lane = lane_of(stats_out.shape)
    stats_out[...] = jnp.where(lane == 0, column(0), jnp.where(lane == 1, sol_sum, sol_square))


def last_kernel(samples, width, came_ref, stats_ref, res_ref, dir_ref, out_ref, score_out):
    total = jnp.sum(came_ref[...], axis=0)
    last = total[:, 4 * LANES :]
    out_ref[...] = res_ref[...] + (as_column(last, 6) / (stats_ref[:, 0:1] + 1e-06)) * dir_ref[...]
    row = lax.broadcasted_iota(jnp.int32, (16, LANES), 0)
    spread = jnp.zeros((16, LANES), F32)
    for k in range(4):
        spread = jnp.where(row % 4 == k, total[:, k * LANES : (k + 1) * LANES], spread)
    cross = spread
    for m in range(1, 4):
        cross = jnp.where(row // 4 == m, pltpu.roll(spread, LANES - 32 * m, 1), cross)
    dose = last
    sol_sum, sol_square = stats_ref[:, 1:2], stats_ref[:, 2:3]
    dose_freq = (dose / 100.0 + 1.0) / (2.0 * samples + 2.0)
    dose_spread = jnp.sqrt(2.0 * dose_freq * (1.0 - dose_freq))
    scale = math.sqrt(samples) * jnp.sqrt(sol_square / samples + 1e-06)
    scores = (cross / 100.0 - 2.0 * dose_freq * sol_sum) / (dose_spread * scale)
    score_out[...] = scores[:, :width]


def call(kernel, out, ins, args, scratch=(), limit=16, flops=0, moved=0):
    return pl.pallas_call(
        kernel,
        out_shape=[jax.ShapeDtypeStruct(*o) if len(o) == 2 else o[2](*o[:2]) for o in out],
        in_specs=list(ins),
        out_specs=[VMEM] * len(out),
        scratch_shapes=list(scratch),
        compiler_params=pltpu.CompilerParams(vmem_limit_bytes=limit * MIB),
        cost_estimate=pl.CostEstimate(flops=flops, bytes_accessed=moved, transcendentals=0),
    )(*[pltpu.with_memory_space_constraint(x, pltpu.HBM) if spec is HBM else x for spec, x in zip(ins, args)])


def body(genotypes, called, dosage, sample_order, noise_ratio, solution, residual, direction):
    n_var = lax.axis_size("var")
    n_samp = lax.axis_size("samp")
    own, rhs = direction.shape
    rows, shard = genotypes.shape
    variants = rows * n_var
    samples = own * n_samp * n_var
    imputed = dosage.shape[1]
    width = imputed // (n_var * n_samp)
    noise = noise_ratio[None]

    dire, res, sol = direction.T, residual.T, solution.T
    first, chunk = rows // 2, 128
    matrix = lambda n: ((n, shard), BF16, pltpu.VMEM)

    neighbour = swap(dire, "var", 1)
    coarse, sums = call(
        functools.partial(genotype_kernel, chunk),
        [matrix(first), ((8, LANES), F32)],
        [HBM] * 4,
        (sol, dire, res, genotypes),
        scratch=[
            pltpu.VMEM((rhs, own), F32),
            pltpu.VMEM((rhs, own), F32),
            pltpu.VMEM((rhs, own), F32),
            pltpu.VMEM((first, shard), jnp.int32),
            pltpu.SemaphoreType.DMA((3,)),
            pltpu.SemaphoreType.DMA((first // chunk,)),
        ],
        limit=6,
        moved=4 * first * shard,
    )
    (pair,) = call(pair_kernel, [((2 * rhs, own), BF16)], [VMEM] * 2, (dire, neighbour), limit=4)
    pair_other = swap(pair, "var", 2)
    both_weights = [pltpu.VMEM((48, 2 * own), BF16), pltpu.VMEM((48, 2 * own), BF16)]
    coded, called_b, half = call(
        mask_kernel,
        [matrix(rows), matrix(rows), ((2 * rhs + 8, rows), F32)],
        [VMEM] * 3 + [HBM],
        (pair, coarse, called, genotypes),
        scratch=[
            pltpu.VMEM((rows - first, shard), jnp.int32),
            *both_weights,
            pltpu.SemaphoreType.DMA(((rows - first) // LANES,)),
        ],
        limit=12,
        flops=2 * rows * shard * 256,
        moved=4 * rows * shard,
    )
    (part,) = call(
        forward_kernel,
        [((2 * rhs + 8, rows + LANES), F32)],
        [VMEM] * 5,
        (pair_other, coded, called_b, half, sums),
        scratch=both_weights,
        flops=2 * rows * shard * 256,
        moved=2 * rows * shard,
    )
    part_other = swap(part, "samp", 1)

    n_chips = n_samp // 2
    total, *messages = call(
        chips_kernel,
        [(part.shape, F32)] + [((2 * rhs, rows + LANES), BF16)] * (n_chips - 1),
        [VMEM] * 2,
        (part, part_other),
        moved=1 * MIB,
    )
    arrived = [swap(messages[k], "samp", 2 * (k + 1)) for k in reversed(range(n_chips - 1))]
    (cross,) = call(
        dosage_kernel,
        [((2 * rhs + 8, imputed), F32)],
        [VMEM] * 5,
        (sample_order, sol, dire, dosage, total),
        flops=2 * 80 * own * (own + imputed),
        moved=4 * own * imputed,
    )

    wide = own + LANES
    mine_back, *messages = call(
        functools.partial(back_kernel, variants, len(arrived)),
        [((rhs, wide), F32)] + [((rhs, wide), BF16)] * (n_var - 1),
        [VMEM] * (3 + len(arrived)),
        (total, coded, called_b, *arrived),
        flops=4 * rows * shard * 256,
        moved=4 * rows * shard,
    )
    backs = [mine_back] + [swap(messages[k], "var", k + 1) for k in reversed(range(n_var - 1))]

    n_all = n_var * n_samp
    outgoing, res_keep = call(
        functools.partial(norm_kernel, variants, width),
        [((n_all, 1, 5 * LANES), F32), ((rhs, own), F32)],
        [VMEM] * (4 + n_var),
        (noise, dire, res, cross, *backs),
        moved=4 * 5 * n_all * LANES,
    )
    came = lax.all_to_all(outgoing, ("var", "samp"), split_axis=0, concat_axis=0)
    sol_new, res_new, stats = call(
        functools.partial(new_kernel, variants),
        [((rhs, own), F32), ((rhs, own), F32), ((rhs, LANES), F32)],
        [VMEM] * (4 + n_var),
        (noise, dire, res, sol, *backs),
        moved=1 * MIB,
    )
    dir_new, scores = call(
        functools.partial(last_kernel, samples, width),
        [((rhs, own), F32), ((rhs, width), F32)],
        [VMEM] * 4,
        (came, stats, res_keep, dire),
    )
    return (sol_new.T, res_new.T, dir_new.T, scores.T)


def solution(mesh):
    placed = (
        P("var", "samp"),
        P("var", "samp"),
        P(("samp", "var"), None),
        P(("samp", "var"), None),
        P(),
        P(("samp", "var"), None),
        P(("samp", "var"), None),
        P(("samp", "var"), None),
    )
    return jax.shard_map(
        body,
        mesh=mesh,
        in_specs=placed,
        out_specs=(
            P(("samp", "var"), None),
            P(("samp", "var"), None),
            P(("samp", "var"), None),
            P(("var", "samp"), None),
        ),
        check_vma=False,
    )
```

```python
import functools
import math

import jax
import jax.numpy as jnp
from jax import lax
from jax.experimental import pallas as pl
from jax.experimental.pallas import tpu as pltpu
from jax.sharding import PartitionSpec as P

BF16 = jnp.bfloat16
F32 = jnp.float32
LANES = 128
NT = (((1,), (1,)), ((), ()))
VMEM = pl.BlockSpec(memory_space=pltpu.VMEM)
HBM = pl.BlockSpec(memory_space=pltpu.HBM)
MIB = 1 << 20


def swap(values, axis, distance):
    size = lax.axis_size(axis)
    return lax.ppermute(values, axis, [(i, i ^ distance) for i in range(size)])


def halves(values):
    high = values.astype(BF16)
    return high, (values - high.astype(F32)).astype(BF16)


def thirds(values):
    high = values.astype(BF16)
    rest = values - high.astype(F32)
    middle = rest.astype(BF16)
    return high, middle, (rest - middle.astype(F32)).astype(BF16)


def lane_of(shape):
    return lax.broadcasted_iota(jnp.int32, shape, len(shape) - 1)


def spot(q):
    shape = (16, LANES)
    return lane_of(shape) == 16 * q + lax.broadcasted_iota(jnp.int32, shape, 0)


def as_row(values):
    block = jnp.zeros((16, LANES), F32)
    for q, column in values.items():
        block = jnp.where(spot(q), column, block)
    return jnp.sum(block, axis=0, keepdims=True)


def as_column(row, q):
    return jnp.sum(jnp.where(spot(q), row, 0.0), axis=1, keepdims=True)


def to_column(row):
    shape = (16, row.shape[1])
    same = lax.broadcasted_iota(jnp.int32, shape, 0) == lane_of(shape)
    return jnp.sum(jnp.where(same, row, 0.0), axis=1, keepdims=True)


BLOCK = 1024


def blocks(rows, samples):
    return [
        (pl.ds(row, 16), pl.ds(sample, BLOCK)) for row in range(0, rows, 16) for sample in range(0, samples, BLOCK)
    ]


def row_copies(source, target, first, chunk, sems):
    return [
        pltpu.make_async_copy(source.at[pl.ds(first + i, chunk)], target.at[pl.ds(i, chunk)], sems.at[i // chunk])
        for i in range(0, target.shape[0], chunk)
    ]


def genotype_kernel(chunk, sol_hbm, dir_hbm, res_hbm, gen_hbm, out_ref, sums_ref,
                    sol_ref, dir_ref, res_ref, gbuf, small_sems, sems):
    small = [
        pltpu.make_async_copy(source, target, small_sems.at[i])
        for i, (source, target) in enumerate(((sol_hbm, sol_ref), (dir_hbm, dir_ref), (res_hbm, res_ref)))
    ]
    for copy in small:
        copy.start()
    parts = row_copies(gen_hbm, gbuf, 0, chunk, sems)
    for copy in parts:
        copy.start()
    for copy in small:
        copy.wait()
    sol, dire, res = sol_ref[...], dir_ref[...], res_ref[...]
    products = (res * res, dire * dire, sol, sol * sol, sol * dire, dire)
    row = as_row({q: jnp.sum(x, axis=1, keepdims=True) for q, x in enumerate(products)})
    sums_ref[...] = jnp.broadcast_to(row, sums_ref.shape)
    for i, copy in enumerate(parts):
        copy.wait()
        source, target = gbuf.at[pl.ds(i * chunk, chunk)], out_ref.at[pl.ds(i * chunk, chunk)]
        for here in blocks(chunk, source.shape[1]):
            target[here] = source[here].astype(F32).astype(BF16)


def pair_kernel(own_ref, other_ref, out_ref):
    upper = lax.axis_index("var") % 2
    rhs = own_ref.shape[0]
    own, other = own_ref[...], other_ref[...]
    out_ref[:rhs] = jnp.where(upper == 0, own, other).astype(BF16)
    out_ref[rhs:] = jnp.where(upper == 0, other, own).astype(BF16)


def weights(pair_ref, w):
    own = pair_ref.shape[1]
    row = lax.broadcasted_iota(jnp.int32, (16, 2 * own), 0)
    w[16:32] = jnp.where(row == 0, 1.0, 0.0).astype(BF16)
    for i in range(2):
        w[0:16, i * own : (i + 1) * own] = pair_ref[16 * i : 16 * i + 16]


def product(coded_ref, called_ref, first, rows, samples, w):
    part = pl.ds(first, rows)
    coded = lax.dot_general(w[...], coded_ref[part, samples], NT, preferred_element_type=F32)
    called = lax.dot_general(w[...], called_ref[part, samples], NT, preferred_element_type=F32)
    counts = jnp.concatenate([coded[16:17], called[16:17], jnp.zeros((6, rows), F32)], axis=0)
    return jnp.concatenate([coded[0:16], called[0:16], counts], axis=0)


def pair_samples(pair, own):
    return pl.ds(pl.multiple_of(pair * 2 * own, LANES), 2 * own)


def mask_kernel(pair_ref, first_ref, call_ref, gen_hbm, coded_ref, called_ref, out_ref, gbuf, w, sems):
    own = pair_ref.shape[1]
    first = first_ref.shape[0]
    copies = row_copies(gen_hbm, gbuf, first, LANES, sems)
    for copy in copies:
        copy.start()
    samples = pair_samples(lax.axis_index("var") // 2, own)
    weights(pair_ref, w)
    rows, shard = call_ref.shape

    def convert(place):
        here = pl.ds(place, LANES)
        gen = first_ref.at[here] if place < first else gbuf.at[pl.ds(place - first, LANES)]
        call, coded, called = call_ref.at[here], coded_ref.at[here], called_ref.at[here]
        for block in blocks(LANES, shard):
            mask = call[block].astype(F32).astype(BF16)
            value = gen[block] if place < first else gen[block].astype(F32).astype(BF16)
            coded[block] = value * mask
            called[block] = mask

    chunk = 2 * LANES
    for place in range(0, rows + chunk, chunk):
        for part in range(place, min(place + chunk, rows), LANES):
            if part >= first:
                copies[(part - first) // LANES].wait()
            convert(part)
        if place:
            before = place - chunk
            out_ref[:, before:place] = product(coded_ref, called_ref, before, chunk, samples, w)


def forward_kernel(pair_ref, coded_ref, called_ref, half_ref, sums_ref, out_ref, w):
    own = pair_ref.shape[1]
    rows = coded_ref.shape[0]
    samples = pair_samples((lax.axis_index("var") // 2) ^ 1, own)
    weights(pair_ref, w)
    for place in range(0, rows, 2 * LANES):
        here = slice(place, place + 2 * LANES)
        out_ref[:, here] = half_ref[:, here] + product(coded_ref, called_ref, place, 2 * LANES, samples, w)
    out_ref[:, rows:] = jnp.zeros((out_ref.shape[0], LANES), F32)
    out_ref[0:8, rows:] = sums_ref[...]


def chips_kernel(own_ref, other_ref, total_ref, *messages):
    rows = own_ref.shape[1] - LANES
    total = own_ref[...] + other_ref[...]
    total_ref[...] = total
    pieces = []
    for part in halves(total[32:34, :rows]):
        part = part.astype(F32)
        for which in range(2):
            for j in range(rows // LANES):
                pieces.append(part[which : which + 1, j * LANES : (j + 1) * LANES])
    pieces += [part.astype(F32) for part in thirds(total[0:1, rows:])]
    pieces.append(jnp.zeros((32 - len(pieces), LANES), F32))
    extra = jnp.concatenate(pieces, axis=0).astype(BF16)
    for message in messages:
        message[:, :rows] = total[0:32, :rows].astype(BF16)
        message[:, rows:] = extra


def dosage_kernel(order_ref, sol_ref, dir_ref, dose_ref, after_ref, cross_ref):
    rhs = sol_ref.shape[0]
    sol_high, sol_low = halves(sol_ref[...])
    dir_high, dir_low = halves(dir_ref[...])
    stack = jnp.concatenate([sol_high, dir_high, sol_low, dir_low], axis=0)
    own = stack.shape[1]
    hot = lax.broadcasted_iota(jnp.int32, (own, own), 0) == order_ref[...]
    hot = jnp.where(hot, 1.0, 0.0).astype(BF16)
    picked = jnp.dot(stack, hot, preferred_element_type=F32).astype(BF16)
    picked = jnp.concatenate([picked, jnp.ones((16, own), BF16)], axis=0)
    dose = dose_ref[...].astype(F32).astype(BF16)
    cross = jnp.dot(picked, dose, preferred_element_type=F32)
    cross_ref[: 2 * rhs] = cross[: 2 * rhs] + cross[2 * rhs : 4 * rhs]
    cross_ref[2 * rhs :] = cross[4 * rhs : 4 * rhs + 8]


def back_kernel(variants, n_arrived, total_ref, coded_ref, called_ref, *rest):
    arrived, own_ref, messages = rest[:n_arrived], rest[n_arrived], rest[n_arrived + 1 :]
    var = lax.axis_index("var")
    rows = total_ref.shape[1] - LANES

    main = total_ref[0:32, :rows]
    allele, count = total_ref[32:33, :rows], total_ref[33:34, :rows]
    extra = jnp.zeros((32, LANES), F32)
    for ref in arrived:
        main = main + ref[:, :rows].astype(F32)
        extra = extra + ref[:, rows:].astype(F32)
    tiles = rows // LANES
    pick = lambda first: jnp.concatenate(
        [extra[first + j : first + j + 1] + extra[first + 2 * tiles + j : first + 2 * tiles + j + 1]
         for j in range(tiles)], axis=1
    )
    allele = allele + pick(0)
    count = count + pick(tiles)
    last = 4 * tiles
    sums = total_ref[0:1, rows:] + extra[last : last + 1] + extra[last + 1 : last + 2] + extra[last + 2 : last + 3]

    frequency = (allele + 1.0) / (2.0 * count + 2.0)
    spread = jnp.sqrt(2.0 * frequency * (1.0 - frequency))
    loading = (main[0:16] - 2.0 * frequency * main[16:32]) / spread
    scaled = loading / spread
    scaled_a = scaled.astype(BF16)
    scaled_b = (-2.0 * frequency * scaled).astype(BF16)
    square = as_row({6: jnp.sum(loading * loading, axis=1, keepdims=True)})
    sums = jnp.where(lane_of((1, LANES)) < 96, sums, square)

    own = own_ref.shape[1] - LANES

    def term(p):
        part = pl.ds(pl.multiple_of(p * own, LANES), own)
        got = jnp.dot(scaled_a, coded_ref[:, part], preferred_element_type=F32)
        got = got + jnp.dot(scaled_b, called_ref[:, part], preferred_element_type=F32)
        return got / variants

    parts = [part.astype(F32) for part in thirds(sums)]
    block = jnp.concatenate(parts + [jnp.zeros((13, LANES), F32)], axis=0).astype(BF16)
    for k, ref in enumerate(messages):
        ref[:, :own] = term(var ^ (k + 1)).astype(BF16)
        ref[:, own:] = block
    own_ref[:, :own] = term(var)
    own_ref[:, own:] = jnp.concatenate([sums, jnp.zeros((15, LANES), F32)], axis=0)


def step_of(refs, noise_row, variants):
    got = refs[0][...]
    for ref in refs[1:]:
        got = got + ref[...].astype(F32)
    own = got.shape[1] - LANES
    back, last = got[:, :own], got[:, own:]
    sums = last[0:1] + last[1:2] + last[2:3]
    column = functools.partial(as_column, sums)
    noise = to_column(noise_row)
    curvature = noise * column(1) + column(6) / variants
    step = column(0) / (curvature + 1e-06)
    return back, column, noise, step


def norm_kernel(variants, width, noise_ref, dir_ref, res_ref, cross_ref, *rest):
    refs, (out_ref, new_ref) = rest[:-2], rest[-2:]
    back, _, noise, step = step_of(refs, noise_ref[...], variants)
    new = res_ref[...] - step * (noise * dir_ref[...] + back)
    new_ref[...] = new
    norm = as_row({6: jnp.sum(new * new, axis=1, keepdims=True)})
    cross = cross_ref[0:16] + step * cross_ref[16:32]
    dose = cross_ref[32:40]
    lane = lane_of((16, LANES))
    row = lax.broadcasted_iota(jnp.int32, (16, LANES), 0)
    turned = {}

    def turn(values, name, tile, by):
        if (name, tile, by) not in turned:
            piece = values[:, tile : tile + LANES]
            turned[name, tile, by] = pltpu.roll(piece, by, 1) if by else piece
        return turned[name, tile, by]

    for j in range(out_ref.shape[0]):
        tile, inside = (j * width) // LANES * LANES, (j * width) % LANES
        block = jnp.zeros((16, LANES), F32)
        for m in range(4):
            here = (row // 4 == m) & (lane >= 32 * m) & (lane < 32 * m + width)
            block = jnp.where(here, turn(cross, "cross", tile, (32 * m - inside) % LANES), block)
        block = block[0:8] + block[8:16]
        block = block[0:4] + block[4:8]
        last = jnp.where(lane[0:1] < width, turn(dose, "dose", tile, -inside % LANES)[0:1], norm)
        for k in range(4):
            out_ref[j, :, k * LANES : (k + 1) * LANES] = block[k : k + 1]
        out_ref[j, :, 4 * LANES :] = last


def new_kernel(variants, noise_ref, dir_ref, res_ref, sol_ref, *rest):
    refs, (sol_out, res_out, stats_out) = rest[:-3], rest[-3:]
    back, column, noise, step = step_of(refs, noise_ref[...], variants)
    dire = dir_ref[...]
    sol_out[...] = sol_ref[...] + step * dire
    res_out[...] = res_ref[...] - step * (noise * dire + back)
    sol_sum = column(2) + step * column(5)
    sol_square = column(3) + 2.0 * step * column(4) + step * (step * column(1))
    lane = lane_of(stats_out.shape)
    stats_out[...] = jnp.where(lane == 0, column(0), jnp.where(lane == 1, sol_sum, sol_square))


def last_kernel(samples, width, came_ref, stats_ref, res_ref, dir_ref, out_ref, score_out):
    total = jnp.sum(came_ref[...], axis=0)
    last = total[:, 4 * LANES :]
    out_ref[...] = res_ref[...] + (as_column(last, 6) / (stats_ref[:, 0:1] + 1e-06)) * dir_ref[...]
    row = lax.broadcasted_iota(jnp.int32, (16, LANES), 0)
    spread = jnp.zeros((16, LANES), F32)
    for k in range(4):
        spread = jnp.where(row % 4 == k, total[:, k * LANES : (k + 1) * LANES], spread)
    cross = spread
    for m in range(1, 4):
        cross = jnp.where(row // 4 == m, pltpu.roll(spread, LANES - 32 * m, 1), cross)
    dose = last
    sol_sum, sol_square = stats_ref[:, 1:2], stats_ref[:, 2:3]
    dose_freq = (dose / 100.0 + 1.0) / (2.0 * samples + 2.0)
    dose_spread = jnp.sqrt(2.0 * dose_freq * (1.0 - dose_freq))
    scale = math.sqrt(samples) * jnp.sqrt(sol_square / samples + 1e-06)
    scores = (cross / 100.0 - 2.0 * dose_freq * sol_sum) / (dose_spread * scale)
    score_out[...] = scores[:, :width]


def call(kernel, out, ins, args, scratch=(), limit=16, flops=0, moved=0):
    return pl.pallas_call(
        kernel,
        out_shape=[jax.ShapeDtypeStruct(*o) if len(o) == 2 else o[2](*o[:2]) for o in out],
        in_specs=list(ins),
        out_specs=[VMEM] * len(out),
        scratch_shapes=list(scratch),
        compiler_params=pltpu.CompilerParams(vmem_limit_bytes=limit * MIB),
        cost_estimate=pl.CostEstimate(flops=flops, bytes_accessed=moved, transcendentals=0),
    )(*[pltpu.with_memory_space_constraint(x, pltpu.HBM) if spec is HBM else x for spec, x in zip(ins, args)])


def body(genotypes, called, dosage, sample_order, noise_ratio, solution, residual, direction):
    n_var = lax.axis_size("var")
    n_samp = lax.axis_size("samp")
    own, rhs = direction.shape
    rows, shard = genotypes.shape
    variants = rows * n_var
    samples = own * n_samp * n_var
    imputed = dosage.shape[1]
    width = imputed // (n_var * n_samp)
    noise = noise_ratio[None]

    dire, res, sol = direction.T, residual.T, solution.T
    first, chunk = rows // 2, 128
    matrix = lambda n: ((n, shard), BF16, pltpu.VMEM)

    neighbour = swap(dire, "var", 1)
    coarse, sums = call(
        functools.partial(genotype_kernel, chunk),
        [matrix(first), ((8, LANES), F32)],
        [HBM] * 4,
        (sol, dire, res, genotypes),
        scratch=[
            pltpu.VMEM((rhs, own), F32),
            pltpu.VMEM((rhs, own), F32),
            pltpu.VMEM((rhs, own), F32),
            pltpu.VMEM((first, shard), jnp.int32),
            pltpu.SemaphoreType.DMA((3,)),
            pltpu.SemaphoreType.DMA((first // chunk,)),
        ],
        limit=6,
        moved=4 * first * shard,
    )
    (pair,) = call(pair_kernel, [((2 * rhs, own), BF16)], [VMEM] * 2, (dire, neighbour), limit=4)
    pair_other = swap(pair, "var", 2)
    row_weights = pltpu.VMEM((2 * rhs, 2 * own), BF16)
    coded, called_b, half = call(
        mask_kernel,
        [matrix(rows), matrix(rows), ((2 * rhs + 8, rows), F32)],
        [VMEM] * 3 + [HBM],
        (pair, coarse, called, genotypes),
        scratch=[
            pltpu.VMEM((rows - first, shard), jnp.int32),
            row_weights,
            pltpu.SemaphoreType.DMA(((rows - first) // LANES,)),
        ],
        limit=12,
        flops=2 * rows * shard * 256,
        moved=4 * rows * shard,
    )
    (part,) = call(
        forward_kernel,
        [((2 * rhs + 8, rows + LANES), F32)],
        [VMEM] * 5,
        (pair_other, coded, called_b, half, sums),
        scratch=[row_weights],
        flops=2 * rows * shard * 256,
        moved=2 * rows * shard,
    )
    part_other = swap(part, "samp", 1)

    n_chips = n_samp // 2
    total, *messages = call(
        chips_kernel,
        [(part.shape, F32)] + [((2 * rhs, rows + LANES), BF16)] * (n_chips - 1),
        [VMEM] * 2,
        (part, part_other),
        moved=1 * MIB,
    )
    arrived = [swap(messages[k], "samp", 2 * (k + 1)) for k in reversed(range(n_chips - 1))]
    (cross,) = call(
        dosage_kernel,
        [((2 * rhs + 8, imputed), F32)],
        [VMEM] * 5,
        (sample_order, sol, dire, dosage, total),
        flops=2 * 80 * own * (own + imputed),
        moved=4 * own * imputed,
    )

    wide = own + LANES
    mine_back, *messages = call(
        functools.partial(back_kernel, variants, len(arrived)),
        [((rhs, wide), F32)] + [((rhs, wide), BF16)] * (n_var - 1),
        [VMEM] * (3 + len(arrived)),
        (total, coded, called_b, *arrived),
        flops=4 * rows * shard * 256,
        moved=4 * rows * shard,
    )
    backs = [mine_back] + [swap(messages[k], "var", k + 1) for k in reversed(range(n_var - 1))]

    n_all = n_var * n_samp
    outgoing, res_keep = call(
        functools.partial(norm_kernel, variants, width),
        [((n_all, 1, 5 * LANES), F32), ((rhs, own), F32)],
        [VMEM] * (4 + n_var),
        (noise, dire, res, cross, *backs),
        moved=4 * 5 * n_all * LANES,
    )
    came = lax.all_to_all(outgoing, ("var", "samp"), split_axis=0, concat_axis=0)
    sol_new, res_new, stats = call(
        functools.partial(new_kernel, variants),
        [((rhs, own), F32), ((rhs, own), F32), ((rhs, LANES), F32)],
        [VMEM] * (4 + n_var),
        (noise, dire, res, sol, *backs),
        moved=1 * MIB,
    )
    dir_new, scores = call(
        functools.partial(last_kernel, samples, width),
        [((rhs, own), F32), ((rhs, width), F32)],
        [VMEM] * 4,
        (came, stats, res_keep, dire),
    )
    return (sol_new.T, res_new.T, dir_new.T, scores.T)


def solution(mesh):
    placed = (
        P("var", "samp"),
        P("var", "samp"),
        P(("samp", "var"), None),
        P(("samp", "var"), None),
        P(),
        P(("samp", "var"), None),
        P(("samp", "var"), None),
        P(("samp", "var"), None),
    )
    return jax.shard_map(
        body,
        mesh=mesh,
        in_specs=placed,
        out_specs=(
            P(("samp", "var"), None),
            P(("samp", "var"), None),
            P(("samp", "var"), None),
            P(("var", "samp"), None),
        ),
        check_vma=False,
    )
```

```python
import functools
import math

import jax
import jax.numpy as jnp
from jax import lax
from jax.experimental import pallas as pl
from jax.experimental.pallas import tpu as pltpu
from jax.sharding import PartitionSpec as P

BF16 = jnp.bfloat16
F32 = jnp.float32
LANES = 128
NT = (((1,), (1,)), ((), ()))
VMEM = pl.BlockSpec(memory_space=pltpu.VMEM)
HBM = pl.BlockSpec(memory_space=pltpu.HBM)
MIB = 1 << 20


def swap(values, axis, distance):
    size = lax.axis_size(axis)
    return lax.ppermute(values, axis, [(i, i ^ distance) for i in range(size)])


def halves(values):
    high = values.astype(BF16)
    return high, (values - high.astype(F32)).astype(BF16)


def thirds(values):
    high = values.astype(BF16)
    rest = values - high.astype(F32)
    middle = rest.astype(BF16)
    return high, middle, (rest - middle.astype(F32)).astype(BF16)


def lane_of(shape):
    return lax.broadcasted_iota(jnp.int32, shape, len(shape) - 1)


def spot(q):
    shape = (16, LANES)
    return lane_of(shape) == 16 * q + lax.broadcasted_iota(jnp.int32, shape, 0)


def as_row(values):
    block = jnp.zeros((16, LANES), F32)
    for q, column in values.items():
        block = jnp.where(spot(q), column, block)
    return jnp.sum(block, axis=0, keepdims=True)


def as_column(row, q):
    return jnp.sum(jnp.where(spot(q), row, 0.0), axis=1, keepdims=True)


def to_column(row):
    shape = (16, row.shape[1])
    same = lax.broadcasted_iota(jnp.int32, shape, 0) == lane_of(shape)
    return jnp.sum(jnp.where(same, row, 0.0), axis=1, keepdims=True)


BLOCK = 1024


def blocks(rows, samples):
    return [
        (pl.ds(row, 16), pl.ds(sample, BLOCK)) for row in range(0, rows, 16) for sample in range(0, samples, BLOCK)
    ]


def row_copies(source, target, first, chunk, sems):
    return [
        pltpu.make_async_copy(source.at[pl.ds(first + i, chunk)], target.at[pl.ds(i, chunk)], sems.at[i // chunk])
        for i in range(0, target.shape[0], chunk)
    ]


def genotype_kernel(chunk, sol_hbm, dir_hbm, res_hbm, gen_hbm, out_ref, sums_ref,
                    sol_ref, dir_ref, res_ref, gbuf, small_sems, sems):
    small = [
        pltpu.make_async_copy(source, target, small_sems.at[i])
        for i, (source, target) in enumerate(((sol_hbm, sol_ref), (dir_hbm, dir_ref), (res_hbm, res_ref)))
    ]
    for copy in small:
        copy.start()
    parts = row_copies(gen_hbm, gbuf, 0, chunk, sems)
    for copy in parts:
        copy.start()
    for copy in small:
        copy.wait()
    sol, dire, res = sol_ref[...], dir_ref[...], res_ref[...]
    products = (res * res, dire * dire, sol, sol * sol, sol * dire, dire)
    row = as_row({q: jnp.sum(x, axis=1, keepdims=True) for q, x in enumerate(products)})
    sums_ref[...] = jnp.broadcast_to(row, sums_ref.shape)
    for i, copy in enumerate(parts):
        copy.wait()
        source, target = gbuf.at[pl.ds(i * chunk, chunk)], out_ref.at[pl.ds(i * chunk, chunk)]
        for here in blocks(chunk, source.shape[1]):
            target[here] = source[here].astype(F32).astype(BF16)


def pair_kernel(own_ref, other_ref, out_ref):
    upper = lax.axis_index("var") % 2
    rhs = own_ref.shape[0]
    own, other = own_ref[...], other_ref[...]
    out_ref[:rhs] = jnp.where(upper == 0, own, other).astype(BF16)
    out_ref[rhs:] = jnp.where(upper == 0, other, own).astype(BF16)


def weights(pair_ref, w):
    own = pair_ref.shape[1]
    row = lax.broadcasted_iota(jnp.int32, (16, 2 * own), 0)
    w[16:32] = jnp.where(row == 0, 1.0, 0.0).astype(BF16)
    for i in range(2):
        w[0:16, i * own : (i + 1) * own] = pair_ref[16 * i : 16 * i + 16]


def product(coded_ref, called_ref, first, rows, samples, w):
    part = pl.ds(first, rows)
    coded = lax.dot_general(w[...], coded_ref[part, samples], NT, preferred_element_type=F32)
    called = lax.dot_general(w[...], called_ref[part, samples], NT, preferred_element_type=F32)
    counts = jnp.concatenate([coded[16:17], called[16:17], jnp.zeros((6, rows), F32)], axis=0)
    return jnp.concatenate([coded[0:16], called[0:16], counts], axis=0)


def pair_samples(pair, own):
    return pl.ds(pl.multiple_of(pair * 2 * own, LANES), 2 * own)


def mask_kernel(pair_ref, first_ref, call_ref, gen_hbm, coded_ref, called_ref, out_ref, gbuf, w, sems):
    own = pair_ref.shape[1]
    first = first_ref.shape[0]
    copies = row_copies(gen_hbm, gbuf, first, LANES, sems)
    for copy in copies:
        copy.start()
    samples = pair_samples(lax.axis_index("var") // 2, own)
    weights(pair_ref, w)
    rows, shard = call_ref.shape

    def convert(place):
        here = pl.ds(place, LANES)
        gen = first_ref.at[here] if place < first else gbuf.at[pl.ds(place - first, LANES)]
        call, coded, called = call_ref.at[here], coded_ref.at[here], called_ref.at[here]

        def store(block, value, mask):
            coded[block] = value
            called[block] = mask

        held = None
        for block in blocks(LANES, shard):
            mask = call[block].astype(F32).astype(BF16)
            value = gen[block] if place < first else gen[block].astype(F32).astype(BF16)
            if held:
                store(*held)
            held = (block, value * mask, mask)
        store(*held)

    chunk = 2 * LANES
    for place in range(0, rows + chunk, chunk):
        for part in range(place, min(place + chunk, rows), LANES):
            if part >= first:
                copies[(part - first) // LANES].wait()
            convert(part)
        if place:
            before = place - chunk
            out_ref[:, before:place] = product(coded_ref, called_ref, before, chunk, samples, w)


def forward_kernel(pair_ref, coded_ref, called_ref, half_ref, sums_ref, out_ref, w):
    own = pair_ref.shape[1]
    rows = coded_ref.shape[0]
    samples = pair_samples((lax.axis_index("var") // 2) ^ 1, own)
    weights(pair_ref, w)
    for place in range(0, rows, 2 * LANES):
        here = slice(place, place + 2 * LANES)
        out_ref[:, here] = half_ref[:, here] + product(coded_ref, called_ref, place, 2 * LANES, samples, w)
    out_ref[:, rows:] = jnp.zeros((out_ref.shape[0], LANES), F32)
    out_ref[0:8, rows:] = sums_ref[...]


def chips_kernel(own_ref, other_ref, total_ref, *messages):
    rows = own_ref.shape[1] - LANES
    total = own_ref[...] + other_ref[...]
    total_ref[...] = total
    pieces = []
    for part in halves(total[32:34, :rows]):
        part = part.astype(F32)
        for which in range(2):
            for j in range(rows // LANES):
                pieces.append(part[which : which + 1, j * LANES : (j + 1) * LANES])
    pieces += [part.astype(F32) for part in thirds(total[0:1, rows:])]
    pieces.append(jnp.zeros((32 - len(pieces), LANES), F32))
    extra = jnp.concatenate(pieces, axis=0).astype(BF16)
    for message in messages:
        message[:, :rows] = total[0:32, :rows].astype(BF16)
        message[:, rows:] = extra


def dosage_kernel(order_ref, sol_ref, dir_ref, dose_ref, after_ref, cross_ref):
    rhs = sol_ref.shape[0]
    sol_high, sol_low = halves(sol_ref[...])
    dir_high, dir_low = halves(dir_ref[...])
    stack = jnp.concatenate([sol_high, dir_high, sol_low, dir_low], axis=0)
    own = stack.shape[1]
    hot = lax.broadcasted_iota(jnp.int32, (own, own), 0) == order_ref[...]
    hot = jnp.where(hot, 1.0, 0.0).astype(BF16)
    picked = jnp.dot(stack, hot, preferred_element_type=F32).astype(BF16)
    picked = jnp.concatenate([picked, jnp.ones((16, own), BF16)], axis=0)
    dose = dose_ref[...].astype(F32).astype(BF16)
    cross = jnp.dot(picked, dose, preferred_element_type=F32)
    cross_ref[: 2 * rhs] = cross[: 2 * rhs] + cross[2 * rhs : 4 * rhs]
    cross_ref[2 * rhs :] = cross[4 * rhs : 4 * rhs + 8]


def back_kernel(variants, n_arrived, total_ref, coded_ref, called_ref, *rest):
    arrived, own_ref, messages = rest[:n_arrived], rest[n_arrived], rest[n_arrived + 1 :]
    var = lax.axis_index("var")
    rows = total_ref.shape[1] - LANES

    main = total_ref[0:32, :rows]
    allele, count = total_ref[32:33, :rows], total_ref[33:34, :rows]
    extra = jnp.zeros((32, LANES), F32)
    for ref in arrived:
        main = main + ref[:, :rows].astype(F32)
        extra = extra + ref[:, rows:].astype(F32)
    tiles = rows // LANES
    pick = lambda first: jnp.concatenate(
        [extra[first + j : first + j + 1] + extra[first + 2 * tiles + j : first + 2 * tiles + j + 1]
         for j in range(tiles)], axis=1
    )
    allele = allele + pick(0)
    count = count + pick(tiles)
    last = 4 * tiles
    sums = total_ref[0:1, rows:] + extra[last : last + 1] + extra[last + 1 : last + 2] + extra[last + 2 : last + 3]

    frequency = (allele + 1.0) / (2.0 * count + 2.0)
    spread = jnp.sqrt(2.0 * frequency * (1.0 - frequency))
    loading = (main[0:16] - 2.0 * frequency * main[16:32]) / spread
    scaled = loading / spread
    scaled_a = scaled.astype(BF16)
    scaled_b = (-2.0 * frequency * scaled).astype(BF16)
    square = as_row({6: jnp.sum(loading * loading, axis=1, keepdims=True)})
    sums = jnp.where(lane_of((1, LANES)) < 96, sums, square)

    own = own_ref.shape[1] - LANES

    def term(p):
        part = pl.ds(pl.multiple_of(p * own, LANES), own)
        got = jnp.dot(scaled_a, coded_ref[:, part], preferred_element_type=F32)
        got = got + jnp.dot(scaled_b, called_ref[:, part], preferred_element_type=F32)
        return got / variants

    parts = [part.astype(F32) for part in thirds(sums)]
    block = jnp.concatenate(parts + [jnp.zeros((13, LANES), F32)], axis=0).astype(BF16)
    for k, ref in enumerate(messages):
        ref[:, :own] = term(var ^ (k + 1)).astype(BF16)
        ref[:, own:] = block
    own_ref[:, :own] = term(var)
    own_ref[:, own:] = jnp.concatenate([sums, jnp.zeros((15, LANES), F32)], axis=0)


def step_of(refs, noise_row, variants):
    got = refs[0][...]
    for ref in refs[1:]:
        got = got + ref[...].astype(F32)
    own = got.shape[1] - LANES
    back, last = got[:, :own], got[:, own:]
    sums = last[0:1] + last[1:2] + last[2:3]
    column = functools.partial(as_column, sums)
    noise = to_column(noise_row)
    curvature = noise * column(1) + column(6) / variants
    step = column(0) / (curvature + 1e-06)
    return back, column, noise, step


def norm_kernel(variants, width, noise_ref, dir_ref, res_ref, cross_ref, *rest):
    refs, (out_ref, new_ref) = rest[:-2], rest[-2:]
    back, _, noise, step = step_of(refs, noise_ref[...], variants)
    new = res_ref[...] - step * (noise * dir_ref[...] + back)
    new_ref[...] = new
    norm = as_row({6: jnp.sum(new * new, axis=1, keepdims=True)})
    cross = cross_ref[0:16] + step * cross_ref[16:32]
    dose = cross_ref[32:40]
    lane = lane_of((16, LANES))
    row = lax.broadcasted_iota(jnp.int32, (16, LANES), 0)
    turned = {}

    def turn(values, name, tile, by):
        if (name, tile, by) not in turned:
            piece = values[:, tile : tile + LANES]
            turned[name, tile, by] = pltpu.roll(piece, by, 1) if by else piece
        return turned[name, tile, by]

    for j in range(out_ref.shape[0]):
        tile, inside = (j * width) // LANES * LANES, (j * width) % LANES
        block = jnp.zeros((16, LANES), F32)
        for m in range(4):
            here = (row // 4 == m) & (lane >= 32 * m) & (lane < 32 * m + width)
            block = jnp.where(here, turn(cross, "cross", tile, (32 * m - inside) % LANES), block)
        block = block[0:8] + block[8:16]
        block = block[0:4] + block[4:8]
        last = jnp.where(lane[0:1] < width, turn(dose, "dose", tile, -inside % LANES)[0:1], norm)
        for k in range(4):
            out_ref[j, :, k * LANES : (k + 1) * LANES] = block[k : k + 1]
        out_ref[j, :, 4 * LANES :] = last


def new_kernel(variants, noise_ref, dir_ref, res_ref, sol_ref, *rest):
    refs, (sol_out, res_out, stats_out) = rest[:-3], rest[-3:]
    back, column, noise, step = step_of(refs, noise_ref[...], variants)
    dire = dir_ref[...]
    sol_out[...] = sol_ref[...] + step * dire
    res_out[...] = res_ref[...] - step * (noise * dire + back)
    sol_sum = column(2) + step * column(5)
    sol_square = column(3) + 2.0 * step * column(4) + step * (step * column(1))
    lane = lane_of(stats_out.shape)
    stats_out[...] = jnp.where(lane == 0, column(0), jnp.where(lane == 1, sol_sum, sol_square))


def last_kernel(samples, width, came_ref, stats_ref, res_ref, dir_ref, out_ref, score_out):
    total = jnp.sum(came_ref[...], axis=0)
    last = total[:, 4 * LANES :]
    out_ref[...] = res_ref[...] + (as_column(last, 6) / (stats_ref[:, 0:1] + 1e-06)) * dir_ref[...]
    row = lax.broadcasted_iota(jnp.int32, (16, LANES), 0)
    spread = jnp.zeros((16, LANES), F32)
    for k in range(4):
        spread = jnp.where(row % 4 == k, total[:, k * LANES : (k + 1) * LANES], spread)
    cross = spread
    for m in range(1, 4):
        cross = jnp.where(row // 4 == m, pltpu.roll(spread, LANES - 32 * m, 1), cross)
    dose = last
    sol_sum, sol_square = stats_ref[:, 1:2], stats_ref[:, 2:3]
    dose_freq = (dose / 100.0 + 1.0) / (2.0 * samples + 2.0)
    dose_spread = jnp.sqrt(2.0 * dose_freq * (1.0 - dose_freq))
    scale = math.sqrt(samples) * jnp.sqrt(sol_square / samples + 1e-06)
    scores = (cross / 100.0 - 2.0 * dose_freq * sol_sum) / (dose_spread * scale)
    score_out[...] = scores[:, :width]


def call(kernel, out, ins, args, scratch=(), limit=16, flops=0, moved=0):
    return pl.pallas_call(
        kernel,
        out_shape=[jax.ShapeDtypeStruct(*o) if len(o) == 2 else o[2](*o[:2]) for o in out],
        in_specs=list(ins),
        out_specs=[VMEM] * len(out),
        scratch_shapes=list(scratch),
        compiler_params=pltpu.CompilerParams(vmem_limit_bytes=limit * MIB),
        cost_estimate=pl.CostEstimate(flops=flops, bytes_accessed=moved, transcendentals=0),
    )(*[pltpu.with_memory_space_constraint(x, pltpu.HBM) if spec is HBM else x for spec, x in zip(ins, args)])


def body(genotypes, called, dosage, sample_order, noise_ratio, solution, residual, direction):
    n_var = lax.axis_size("var")
    n_samp = lax.axis_size("samp")
    own, rhs = direction.shape
    rows, shard = genotypes.shape
    variants = rows * n_var
    samples = own * n_samp * n_var
    imputed = dosage.shape[1]
    width = imputed // (n_var * n_samp)
    noise = noise_ratio[None]

    dire, res, sol = direction.T, residual.T, solution.T
    first, chunk = rows // 3 * 2, 128
    matrix = lambda n: ((n, shard), BF16, pltpu.VMEM)

    neighbour = swap(dire, "var", 1)
    coarse, sums = call(
        functools.partial(genotype_kernel, chunk),
        [matrix(first), ((8, LANES), F32)],
        [HBM] * 4,
        (sol, dire, res, genotypes),
        scratch=[
            pltpu.VMEM((rhs, own), F32),
            pltpu.VMEM((rhs, own), F32),
            pltpu.VMEM((rhs, own), F32),
            pltpu.VMEM((first, shard), jnp.int32),
            pltpu.SemaphoreType.DMA((3,)),
            pltpu.SemaphoreType.DMA((first // chunk,)),
        ],
        limit=10,
        moved=4 * first * shard,
    )
    (pair,) = call(pair_kernel, [((2 * rhs, own), BF16)], [VMEM] * 2, (dire, neighbour), limit=4)
    pair_other = swap(pair, "var", 2)
    row_weights = pltpu.VMEM((2 * rhs, 2 * own), BF16)
    coded, called_b, half = call(
        mask_kernel,
        [matrix(rows), matrix(rows), ((2 * rhs + 8, rows), F32)],
        [VMEM] * 3 + [HBM],
        (pair, coarse, called, genotypes),
        scratch=[
            pltpu.VMEM((rows - first, shard), jnp.int32),
            row_weights,
            pltpu.SemaphoreType.DMA(((rows - first) // LANES,)),
        ],
        limit=12,
        flops=2 * rows * shard * 256,
        moved=4 * rows * shard,
    )
    (part,) = call(
        forward_kernel,
        [((2 * rhs + 8, rows + LANES), F32)],
        [VMEM] * 5,
        (pair_other, coded, called_b, half, sums),
        scratch=[row_weights],
        flops=2 * rows * shard * 256,
        moved=2 * rows * shard,
    )
    part_other = swap(part, "samp", 1)

    n_chips = n_samp // 2
    total, *messages = call(
        chips_kernel,
        [(part.shape, F32)] + [((2 * rhs, rows + LANES), BF16)] * (n_chips - 1),
        [VMEM] * 2,
        (part, part_other),
        moved=1 * MIB,
    )
    arrived = [swap(messages[k], "samp", 2 * (k + 1) + 1) for k in reversed(range(n_chips - 1))]
    (cross,) = call(
        dosage_kernel,
        [((2 * rhs + 8, imputed), F32)],
        [VMEM] * 5,
        (sample_order, sol, dire, dosage, total),
        flops=2 * 80 * own * (own + imputed),
        moved=4 * own * imputed,
    )

    wide = own + LANES
    mine_back, *messages = call(
        functools.partial(back_kernel, variants, len(arrived)),
        [((rhs, wide), F32)] + [((rhs, wide), BF16)] * (n_var - 1),
        [VMEM] * (3 + len(arrived)),
        (total, coded, called_b, *arrived),
        flops=4 * rows * shard * 256,
        moved=4 * rows * shard,
    )
    backs = [mine_back] + [swap(messages[k], "var", k + 1) for k in reversed(range(n_var - 1))]

    n_all = n_var * n_samp
    outgoing, res_keep = call(
        functools.partial(norm_kernel, variants, width),
        [((n_all, 1, 5 * LANES), F32), ((rhs, own), F32)],
        [VMEM] * (4 + n_var),
        (noise, dire, res, cross, *backs),
        moved=4 * 5 * n_all * LANES,
    )
    came = lax.all_to_all(outgoing, ("var", "samp"), split_axis=0, concat_axis=0)
    sol_new, res_new, stats = call(
        functools.partial(new_kernel, variants),
        [((rhs, own), F32), ((rhs, own), F32), ((rhs, LANES), F32)],
        [VMEM] * (4 + n_var),
        (noise, dire, res, sol, *backs),
        moved=1 * MIB,
    )
    dir_new, scores = call(
        functools.partial(last_kernel, samples, width),
        [((rhs, own), F32), ((rhs, width), F32)],
        [VMEM] * 4,
        (came, stats, res_keep, dire),
    )
    return (sol_new.T, res_new.T, dir_new.T, scores.T)


def solution(mesh):
    placed = (
        P("var", "samp"),
        P("var", "samp"),
        P(("samp", "var"), None),
        P(("samp", "var"), None),
        P(),
        P(("samp", "var"), None),
        P(("samp", "var"), None),
        P(("samp", "var"), None),
    )
    return jax.shard_map(
        body,
        mesh=mesh,
        in_specs=placed,
        out_specs=(
            P(("samp", "var"), None),
            P(("samp", "var"), None),
            P(("samp", "var"), None),
            P(("var", "samp"), None),
        ),
        check_vma=False,
    )
```

```python
import functools
import math

import jax
import jax.numpy as jnp
from jax import lax
from jax.experimental import pallas as pl
from jax.experimental.pallas import tpu as pltpu
from jax.sharding import PartitionSpec as P

BF16 = jnp.bfloat16
F32 = jnp.float32
LANES = 128
NT = (((1,), (1,)), ((), ()))
VMEM = pl.BlockSpec(memory_space=pltpu.VMEM)
HBM = pl.BlockSpec(memory_space=pltpu.HBM)
MIB = 1 << 20


def swap(values, axis, distance):
    size = lax.axis_size(axis)
    return lax.ppermute(values, axis, [(i, i ^ distance) for i in range(size)])


def halves(values):
    high = values.astype(BF16)
    return high, (values - high.astype(F32)).astype(BF16)


def thirds(values):
    high = values.astype(BF16)
    rest = values - high.astype(F32)
    middle = rest.astype(BF16)
    return high, middle, (rest - middle.astype(F32)).astype(BF16)


def lane_of(shape):
    return lax.broadcasted_iota(jnp.int32, shape, len(shape) - 1)


def spot(q):
    shape = (16, LANES)
    return lane_of(shape) == 16 * q + lax.broadcasted_iota(jnp.int32, shape, 0)


def as_row(values):
    block = jnp.zeros((16, LANES), F32)
    for q, column in values.items():
        block = jnp.where(spot(q), column, block)
    return jnp.sum(block, axis=0, keepdims=True)


def as_column(row, q):
    return jnp.sum(jnp.where(spot(q), row, 0.0), axis=1, keepdims=True)


def to_column(row):
    shape = (16, row.shape[1])
    same = lax.broadcasted_iota(jnp.int32, shape, 0) == lane_of(shape)
    return jnp.sum(jnp.where(same, row, 0.0), axis=1, keepdims=True)


BLOCK = 1024


def blocks(rows, samples):
    return [
        (pl.ds(row, 16), pl.ds(sample, BLOCK)) for row in range(0, rows, 16) for sample in range(0, samples, BLOCK)
    ]


def row_copies(source, target, first, chunk, sems):
    return [
        pltpu.make_async_copy(source.at[pl.ds(first + i, chunk)], target.at[pl.ds(i, chunk)], sems.at[i // chunk])
        for i in range(0, target.shape[0], chunk)
    ]


def genotype_kernel(chunk, sol_hbm, dir_hbm, res_hbm, gen_hbm, out_ref, sums_ref,
                    sol_ref, dir_ref, res_ref, gbuf, small_sems, sems):
    small = [
        pltpu.make_async_copy(source, target, small_sems.at[i])
        for i, (source, target) in enumerate(((sol_hbm, sol_ref), (dir_hbm, dir_ref), (res_hbm, res_ref)))
    ]
    for copy in small:
        copy.start()
    parts = row_copies(gen_hbm, gbuf, 0, chunk, sems)
    for copy in parts:
        copy.start()
    for copy in small:
        copy.wait()
    sol, dire, res = sol_ref[...], dir_ref[...], res_ref[...]
    products = (res * res, dire * dire, sol, sol * sol, sol * dire, dire)
    row = as_row({q: jnp.sum(x, axis=1, keepdims=True) for q, x in enumerate(products)})
    sums_ref[...] = jnp.broadcast_to(row, sums_ref.shape)
    for i, copy in enumerate(parts):
        copy.wait()
        source, target = gbuf.at[pl.ds(i * chunk, chunk)], out_ref.at[pl.ds(i * chunk, chunk)]
        for here in blocks(chunk, source.shape[1]):
            target[here] = source[here].astype(F32).astype(BF16)


def pair_kernel(own_ref, other_ref, out_ref):
    upper = lax.axis_index("var") % 2
    rhs = own_ref.shape[0]
    own, other = own_ref[...], other_ref[...]
    out_ref[:rhs] = jnp.where(upper == 0, own, other).astype(BF16)
    out_ref[rhs:] = jnp.where(upper == 0, other, own).astype(BF16)


def weights(pair_ref, w):
    own = pair_ref.shape[1]
    row = lax.broadcasted_iota(jnp.int32, (16, 2 * own), 0)
    w[16:32] = jnp.where(row == 0, 1.0, 0.0).astype(BF16)
    for i in range(2):
        w[0:16, i * own : (i + 1) * own] = pair_ref[16 * i : 16 * i + 16]


def rows_of(coded, called):
    counts = jnp.concatenate([coded[16:17], called[16:17], jnp.zeros((6, coded.shape[1]), F32)], axis=0)
    return jnp.concatenate([coded[0:16], called[0:16], counts], axis=0)


def product(coded_ref, called_ref, first, rows, samples, w):
    part = pl.ds(first, rows)
    coded = lax.dot_general(w[...], coded_ref[part, samples], NT, preferred_element_type=F32)
    called = lax.dot_general(w[...], called_ref[part, samples], NT, preferred_element_type=F32)
    return rows_of(coded, called)


def pair_samples(pair, own):
    return pl.ds(pl.multiple_of(pair * 2 * own, LANES), 2 * own)


def mask_kernel(pair_ref, first_ref, call_ref, gen_hbm, coded_ref, called_ref, out_ref, gbuf, w, sems):
    own = pair_ref.shape[1]
    first = first_ref.shape[0]
    copies = row_copies(gen_hbm, gbuf, first, LANES, sems)
    for copy in copies:
        copy.start()
    weights(pair_ref, w)
    rows, shard = call_ref.shape
    chunk = 2 * LANES
    depth = 2 * LANES
    start = pl.multiple_of((lax.axis_index("var") // 2) * 2 * own, LANES)

    def convert(place):
        held = None
        for part in range(place, place + chunk, LANES):
            here = pl.ds(part, LANES)
            if part >= first:
                copies[(part - first) // LANES].wait()
            gen = first_ref.at[here] if part < first else gbuf.at[pl.ds(part - first, LANES)]
            call, coded, called = call_ref.at[here], coded_ref.at[here], called_ref.at[here]
            for block in blocks(LANES, shard):
                mask = call[block].astype(F32).astype(BF16)
                value = gen[block] if part < first else gen[block].astype(F32).astype(BF16)
                if held:
                    held[0][held[2]], held[1][held[2]] = held[3], held[4]
                held = (coded, called, block, value * mask, mask)
                yield
        held[0][held[2]], held[1][held[2]] = held[3], held[4]

    def multiply(place):
        part = pl.ds(place, chunk)
        coded = called = jnp.zeros((w.shape[0], chunk), F32)
        for at in range(0, 2 * own, depth):
            here = pl.ds(pl.multiple_of(start + at, LANES), depth)
            piece = w[:, at : at + depth]
            coded = coded + lax.dot_general(piece, coded_ref[part, here], NT, preferred_element_type=F32)
            yield
            called = called + lax.dot_general(piece, called_ref[part, here], NT, preferred_element_type=F32)
            yield
        out_ref[:, place : place + chunk] = rows_of(coded, called)

    for place in range(0, rows + chunk, chunk):
        steps = convert(place) if place < rows else iter(())
        n_steps = chunk // 16 * (shard // BLOCK)
        if place:
            products = multiply(place - chunk)
            n_products = 2 * (2 * own // depth)
            for _ in products:
                for _ in range(-(-n_steps // n_products)):
                    next(steps, None)
        for _ in steps:
            pass


def forward_kernel(pair_ref, coded_ref, called_ref, half_ref, sums_ref, out_ref, w):
    own = pair_ref.shape[1]
    rows = coded_ref.shape[0]
    samples = pair_samples((lax.axis_index("var") // 2) ^ 1, own)
    weights(pair_ref, w)
    for place in range(0, rows, 2 * LANES):
        here = slice(place, place + 2 * LANES)
        out_ref[:, here] = half_ref[:, here] + product(coded_ref, called_ref, place, 2 * LANES, samples, w)
    out_ref[:, rows:] = jnp.zeros((out_ref.shape[0], LANES), F32)
    out_ref[0:8, rows:] = sums_ref[...]


def chips_kernel(own_ref, other_ref, total_ref, *messages):
    rows = own_ref.shape[1] - LANES
    total = own_ref[...] + other_ref[...]
    total_ref[...] = total
    pieces = []
    for part in halves(total[32:34, :rows]):
        part = part.astype(F32)
        for which in range(2):
            for j in range(rows // LANES):
                pieces.append(part[which : which + 1, j * LANES : (j + 1) * LANES])
    pieces += [part.astype(F32) for part in thirds(total[0:1, rows:])]
    pieces.append(jnp.zeros((32 - len(pieces), LANES), F32))
    extra = jnp.concatenate(pieces, axis=0).astype(BF16)
    for message in messages:
        message[:, :rows] = total[0:32, :rows].astype(BF16)
        message[:, rows:] = extra


def dosage_kernel(order_ref, sol_ref, dir_ref, dose_ref, after_ref, cross_ref):
    rhs = sol_ref.shape[0]
    sol_high, sol_low = halves(sol_ref[...])
    dir_high, dir_low = halves(dir_ref[...])
    stack = jnp.concatenate([sol_high, dir_high, sol_low, dir_low], axis=0)
    own = stack.shape[1]
    hot = lax.broadcasted_iota(jnp.int32, (own, own), 0) == order_ref[...]
    hot = jnp.where(hot, 1.0, 0.0).astype(BF16)
    picked = jnp.dot(stack, hot, preferred_element_type=F32).astype(BF16)
    picked = jnp.concatenate([picked, jnp.ones((16, own), BF16)], axis=0)
    dose = dose_ref[...].astype(F32).astype(BF16)
    cross = jnp.dot(picked, dose, preferred_element_type=F32)
    cross_ref[: 2 * rhs] = cross[: 2 * rhs] + cross[2 * rhs : 4 * rhs]
    cross_ref[2 * rhs :] = cross[4 * rhs : 4 * rhs + 8]


def back_kernel(variants, n_arrived, total_ref, coded_ref, called_ref, *rest):
    arrived, own_ref, messages = rest[:n_arrived], rest[n_arrived], rest[n_arrived + 1 :]
    var = lax.axis_index("var")
    rows = total_ref.shape[1] - LANES

    main = total_ref[0:32, :rows]
    allele, count = total_ref[32:33, :rows], total_ref[33:34, :rows]
    extra = jnp.zeros((32, LANES), F32)
    for ref in arrived:
        main = main + ref[:, :rows].astype(F32)
        extra = extra + ref[:, rows:].astype(F32)
    tiles = rows // LANES
    pick = lambda first: jnp.concatenate(
        [extra[first + j : first + j + 1] + extra[first + 2 * tiles + j : first + 2 * tiles + j + 1]
         for j in range(tiles)], axis=1
    )
    allele = allele + pick(0)
    count = count + pick(tiles)
    last = 4 * tiles
    sums = total_ref[0:1, rows:] + extra[last : last + 1] + extra[last + 1 : last + 2] + extra[last + 2 : last + 3]

    frequency = (allele + 1.0) / (2.0 * count + 2.0)
    spread = jnp.sqrt(2.0 * frequency * (1.0 - frequency))
    loading = (main[0:16] - 2.0 * frequency * main[16:32]) / spread
    scaled = loading / spread
    scaled_a = scaled.astype(BF16)
    scaled_b = (-2.0 * frequency * scaled).astype(BF16)
    square = as_row({6: jnp.sum(loading * loading, axis=1, keepdims=True)})
    sums = jnp.where(lane_of((1, LANES)) < 96, sums, square)

    own = own_ref.shape[1] - LANES

    def term(p):
        part = pl.ds(pl.multiple_of(p * own, LANES), own)
        got = jnp.dot(scaled_a, coded_ref[:, part], preferred_element_type=F32)
        got = got + jnp.dot(scaled_b, called_ref[:, part], preferred_element_type=F32)
        return got / variants

    parts = [part.astype(F32) for part in thirds(sums)]
    block = jnp.concatenate(parts + [jnp.zeros((13, LANES), F32)], axis=0).astype(BF16)
    for k, ref in enumerate(messages):
        ref[:, :own] = term(var ^ (k + 1)).astype(BF16)
        ref[:, own:] = block
    own_ref[:, :own] = term(var)
    own_ref[:, own:] = jnp.concatenate([sums, jnp.zeros((15, LANES), F32)], axis=0)


def step_of(refs, noise_row, variants):
    got = refs[0][...]
    for ref in refs[1:]:
        got = got + ref[...].astype(F32)
    own = got.shape[1] - LANES
    back, last = got[:, :own], got[:, own:]
    sums = last[0:1] + last[1:2] + last[2:3]
    column = functools.partial(as_column, sums)
    noise = to_column(noise_row)
    curvature = noise * column(1) + column(6) / variants
    step = column(0) / (curvature + 1e-06)
    return back, column, noise, step


def norm_kernel(variants, width, noise_ref, dir_ref, res_ref, cross_ref, *rest):
    refs, (out_ref, new_ref) = rest[:-2], rest[-2:]
    back, _, noise, step = step_of(refs, noise_ref[...], variants)
    new = res_ref[...] - step * (noise * dir_ref[...] + back)
    new_ref[...] = new
    norm = as_row({6: jnp.sum(new * new, axis=1, keepdims=True)})
    cross = cross_ref[0:16] + step * cross_ref[16:32]
    dose = cross_ref[32:40]
    lane = lane_of((16, LANES))
    row = lax.broadcasted_iota(jnp.int32, (16, LANES), 0)
    turned = {}

    def turn(values, name, tile, by):
        if (name, tile, by) not in turned:
            piece = values[:, tile : tile + LANES]
            turned[name, tile, by] = pltpu.roll(piece, by, 1) if by else piece
        return turned[name, tile, by]

    for j in range(out_ref.shape[0]):
        tile, inside = (j * width) // LANES * LANES, (j * width) % LANES
        block = jnp.zeros((16, LANES), F32)
        for m in range(4):
            here = (row // 4 == m) & (lane >= 32 * m) & (lane < 32 * m + width)
            block = jnp.where(here, turn(cross, "cross", tile, (32 * m - inside) % LANES), block)
        block = block[0:8] + block[8:16]
        block = block[0:4] + block[4:8]
        last = jnp.where(lane[0:1] < width, turn(dose, "dose", tile, -inside % LANES)[0:1], norm)
        for k in range(4):
            out_ref[j, :, k * LANES : (k + 1) * LANES] = block[k : k + 1]
        out_ref[j, :, 4 * LANES :] = last


def new_kernel(variants, noise_ref, dir_ref, res_ref, sol_ref, *rest):
    refs, (sol_out, res_out, stats_out) = rest[:-3], rest[-3:]
    back, column, noise, step = step_of(refs, noise_ref[...], variants)
    dire = dir_ref[...]
    sol_out[...] = sol_ref[...] + step * dire
    res_out[...] = res_ref[...] - step * (noise * dire + back)
    sol_sum = column(2) + step * column(5)
    sol_square = column(3) + 2.0 * step * column(4) + step * (step * column(1))
    lane = lane_of(stats_out.shape)
    stats_out[...] = jnp.where(lane == 0, column(0), jnp.where(lane == 1, sol_sum, sol_square))


def last_kernel(samples, width, came_ref, stats_ref, res_ref, dir_ref, out_ref, score_out):
    total = jnp.sum(came_ref[...], axis=0)
    last = total[:, 4 * LANES :]
    out_ref[...] = res_ref[...] + (as_column(last, 6) / (stats_ref[:, 0:1] + 1e-06)) * dir_ref[...]
    row = lax.broadcasted_iota(jnp.int32, (16, LANES), 0)
    spread = jnp.zeros((16, LANES), F32)
    for k in range(4):
        spread = jnp.where(row % 4 == k, total[:, k * LANES : (k + 1) * LANES], spread)
    cross = spread
    for m in range(1, 4):
        cross = jnp.where(row // 4 == m, pltpu.roll(spread, LANES - 32 * m, 1), cross)
    dose = last
    sol_sum, sol_square = stats_ref[:, 1:2], stats_ref[:, 2:3]
    dose_freq = (dose / 100.0 + 1.0) / (2.0 * samples + 2.0)
    dose_spread = jnp.sqrt(2.0 * dose_freq * (1.0 - dose_freq))
    scale = math.sqrt(samples) * jnp.sqrt(sol_square / samples + 1e-06)
    scores = (cross / 100.0 - 2.0 * dose_freq * sol_sum) / (dose_spread * scale)
    score_out[...] = scores[:, :width]


def call(kernel, out, ins, args, scratch=(), limit=16, flops=0, moved=0):
    return pl.pallas_call(
        kernel,
        out_shape=[jax.ShapeDtypeStruct(*o) if len(o) == 2 else o[2](*o[:2]) for o in out],
        in_specs=list(ins),
        out_specs=[VMEM] * len(out),
        scratch_shapes=list(scratch),
        compiler_params=pltpu.CompilerParams(vmem_limit_bytes=limit * MIB),
        cost_estimate=pl.CostEstimate(flops=flops, bytes_accessed=moved, transcendentals=0),
    )(*[pltpu.with_memory_space_constraint(x, pltpu.HBM) if spec is HBM else x for spec, x in zip(ins, args)])


def body(genotypes, called, dosage, sample_order, noise_ratio, solution, residual, direction):
    n_var = lax.axis_size("var")
    n_samp = lax.axis_size("samp")
    own, rhs = direction.shape
    rows, shard = genotypes.shape
    variants = rows * n_var
    samples = own * n_samp * n_var
    imputed = dosage.shape[1]
    width = imputed // (n_var * n_samp)
    noise = noise_ratio[None]

    dire, res, sol = direction.T, residual.T, solution.T
    first, chunk = rows // 3 * 2, 128
    matrix = lambda n: ((n, shard), BF16, pltpu.VMEM)

    neighbour = swap(dire, "var", 1)
    coarse, sums = call(
        functools.partial(genotype_kernel, chunk),
        [matrix(first), ((8, LANES), F32)],
        [HBM] * 4,
        (sol, dire, res, genotypes),
        scratch=[
            pltpu.VMEM((rhs, own), F32),
            pltpu.VMEM((rhs, own), F32),
            pltpu.VMEM((rhs, own), F32),
            pltpu.VMEM((first, shard), jnp.int32),
            pltpu.SemaphoreType.DMA((3,)),
            pltpu.SemaphoreType.DMA((first // chunk,)),
        ],
        limit=10,
        moved=4 * first * shard,
    )
    (pair,) = call(pair_kernel, [((2 * rhs, own), BF16)], [VMEM] * 2, (dire, neighbour), limit=4)
    pair_other = swap(pair, "var", 2)
    row_weights = pltpu.VMEM((2 * rhs, 2 * own), BF16)
    coded, called_b, half = call(
        mask_kernel,
        [matrix(rows), matrix(rows), ((2 * rhs + 8, rows), F32)],
        [VMEM] * 3 + [HBM],
        (pair, coarse, called, genotypes),
        scratch=[
            pltpu.VMEM((rows - first, shard), jnp.int32),
            row_weights,
            pltpu.SemaphoreType.DMA(((rows - first) // LANES,)),
        ],
        limit=12,
        flops=2 * rows * shard * 256,
        moved=4 * rows * shard,
    )
    (part,) = call(
        forward_kernel,
        [((2 * rhs + 8, rows + LANES), F32)],
        [VMEM] * 5,
        (pair_other, coded, called_b, half, sums),
        scratch=[row_weights],
        flops=2 * rows * shard * 256,
        moved=2 * rows * shard,
    )
    part_other = swap(part, "samp", 1)

    n_chips = n_samp // 2
    total, *messages = call(
        chips_kernel,
        [(part.shape, F32)] + [((2 * rhs, rows + LANES), BF16)] * (n_chips - 1),
        [VMEM] * 2,
        (part, part_other),
        moved=1 * MIB,
    )
    arrived = [swap(messages[k], "samp", 2 * (k + 1) + 1) for k in reversed(range(n_chips - 1))]
    (cross,) = call(
        dosage_kernel,
        [((2 * rhs + 8, imputed), F32)],
        [VMEM] * 5,
        (sample_order, sol, dire, dosage, total),
        flops=2 * 80 * own * (own + imputed),
        moved=4 * own * imputed,
    )

    wide = own + LANES
    mine_back, *messages = call(
        functools.partial(back_kernel, variants, len(arrived)),
        [((rhs, wide), F32)] + [((rhs, wide), BF16)] * (n_var - 1),
        [VMEM] * (3 + len(arrived)),
        (total, coded, called_b, *arrived),
        flops=4 * rows * shard * 256,
        moved=4 * rows * shard,
    )
    backs = [mine_back] + [swap(messages[k], "var", k + 1) for k in reversed(range(n_var - 1))]

    n_all = n_var * n_samp
    outgoing, res_keep = call(
        functools.partial(norm_kernel, variants, width),
        [((n_all, 1, 5 * LANES), F32), ((rhs, own), F32)],
        [VMEM] * (4 + n_var),
        (noise, dire, res, cross, *backs),
        moved=4 * 5 * n_all * LANES,
    )
    came = lax.all_to_all(outgoing, ("var", "samp"), split_axis=0, concat_axis=0)
    sol_new, res_new, stats = call(
        functools.partial(new_kernel, variants),
        [((rhs, own), F32), ((rhs, own), F32), ((rhs, LANES), F32)],
        [VMEM] * (4 + n_var),
        (noise, dire, res, sol, *backs),
        moved=1 * MIB,
    )
    dir_new, scores = call(
        functools.partial(last_kernel, samples, width),
        [((rhs, own), F32), ((rhs, width), F32)],
        [VMEM] * 4,
        (came, stats, res_keep, dire),
    )
    return (sol_new.T, res_new.T, dir_new.T, scores.T)


def solution(mesh):
    placed = (
        P("var", "samp"),
        P("var", "samp"),
        P(("samp", "var"), None),
        P(("samp", "var"), None),
        P(),
        P(("samp", "var"), None),
        P(("samp", "var"), None),
        P(("samp", "var"), None),
    )
    return jax.shard_map(
        body,
        mesh=mesh,
        in_specs=placed,
        out_specs=(
            P(("samp", "var"), None),
            P(("samp", "var"), None),
            P(("samp", "var"), None),
            P(("var", "samp"), None),
        ),
        check_vma=False,
    )
```

```python
import functools
import math

import jax
import jax.numpy as jnp
from jax import lax
from jax.experimental import pallas as pl
from jax.experimental.pallas import tpu as pltpu
from jax.sharding import PartitionSpec as P

BF16 = jnp.bfloat16
F32 = jnp.float32
LANES = 128
NT = (((1,), (1,)), ((), ()))
VMEM = pl.BlockSpec(memory_space=pltpu.VMEM)
HBM = pl.BlockSpec(memory_space=pltpu.HBM)
MIB = 1 << 20


def swap(values, axis, distance):
    size = lax.axis_size(axis)
    return lax.ppermute(values, axis, [(i, i ^ distance) for i in range(size)])


def halves(values):
    high = values.astype(BF16)
    return high, (values - high.astype(F32)).astype(BF16)


def thirds(values):
    high = values.astype(BF16)
    rest = values - high.astype(F32)
    middle = rest.astype(BF16)
    return high, middle, (rest - middle.astype(F32)).astype(BF16)


def lane_of(shape):
    return lax.broadcasted_iota(jnp.int32, shape, len(shape) - 1)


def spot(q):
    shape = (16, LANES)
    return lane_of(shape) == 16 * q + lax.broadcasted_iota(jnp.int32, shape, 0)


def as_row(values):
    block = jnp.zeros((16, LANES), F32)
    for q, column in values.items():
        block = jnp.where(spot(q), column, block)
    return jnp.sum(block, axis=0, keepdims=True)


def as_column(row, q):
    return jnp.sum(jnp.where(spot(q), row, 0.0), axis=1, keepdims=True)


def to_column(row):
    shape = (16, row.shape[1])
    same = lax.broadcasted_iota(jnp.int32, shape, 0) == lane_of(shape)
    return jnp.sum(jnp.where(same, row, 0.0), axis=1, keepdims=True)


BLOCK = 1024
CHUNK = 256


def blocks(rows, samples):
    return [
        (pl.ds(row, 16), pl.ds(sample, BLOCK)) for row in range(0, rows, 16) for sample in range(0, samples, BLOCK)
    ]


def row_copies(source, target, first, chunk, sems):
    return [
        pltpu.make_async_copy(source.at[pl.ds(first + i, chunk)], target.at[pl.ds(i, chunk)], sems.at[i // chunk])
        for i in range(0, target.shape[0], chunk)
    ]


def called_kernel(chunk, sol_hbm, dir_hbm, res_hbm, call_hbm, out_ref, sums_ref,
                  sol_ref, dir_ref, res_ref, cbuf, small_sems, sems):
    small = [
        pltpu.make_async_copy(source, target, small_sems.at[i])
        for i, (source, target) in enumerate(((sol_hbm, sol_ref), (dir_hbm, dir_ref), (res_hbm, res_ref)))
    ]
    for copy in small:
        copy.start()
    parts = row_copies(call_hbm, cbuf, 0, chunk, sems)
    for copy in parts:
        copy.start()
    for copy in small:
        copy.wait()
    sol, dire, res = sol_ref[...], dir_ref[...], res_ref[...]
    products = (res * res, dire * dire, sol, sol * sol, sol * dire, dire)
    row = as_row({q: jnp.sum(x, axis=1, keepdims=True) for q, x in enumerate(products)})
    sums_ref[...] = jnp.broadcast_to(row, sums_ref.shape)
    for i, copy in enumerate(parts):
        copy.wait()
        source, target = cbuf.at[pl.ds(i * chunk, chunk)], out_ref.at[pl.ds(i * chunk, chunk)]
        for here in blocks(chunk, source.shape[1]):
            target[here] = source[here].astype(F32).astype(BF16)


def pair_kernel(own_ref, other_ref, out_ref):
    upper = lax.axis_index("var") % 2
    rhs = own_ref.shape[0]
    own, other = own_ref[...], other_ref[...]
    out_ref[:rhs] = jnp.where(upper == 0, own, other).astype(BF16)
    out_ref[rhs:] = jnp.where(upper == 0, other, own).astype(BF16)


def weights(pair_ref, w):
    own = pair_ref.shape[1]
    row = lax.broadcasted_iota(jnp.int32, (16, 2 * own), 0)
    w[16:32] = jnp.where(row == 0, 1.0, 0.0).astype(BF16)
    for i in range(2):
        w[0:16, i * own : (i + 1) * own] = pair_ref[16 * i : 16 * i + 16]


def product(w, matrix, first, rows, samples):
    return lax.dot_general(w[...], matrix[pl.ds(first, rows), samples], NT, preferred_element_type=F32)


def split_product(w, head, tail, first, rows, samples):
    if first < head.shape[0]:
        return product(w, head, first, rows, samples)
    return product(w, tail, first - head.shape[0], rows, samples)


def rows_of(coded, called):
    counts = jnp.concatenate([coded[16:17], called[16:17], jnp.zeros((6, coded.shape[1]), F32)], axis=0)
    return jnp.concatenate([coded[0:16], called[0:16], counts], axis=0)


def pair_samples(pair, own):
    return pl.ds(pl.multiple_of(pair * 2 * own, LANES), 2 * own)


def called_product_kernel(pair_ref, called_first, out_ref, w):
    own = pair_ref.shape[1]
    samples = pair_samples(lax.axis_index("var") // 2, own)
    weights(pair_ref, w)
    for place in range(0, called_first.shape[0], CHUNK):
        out_ref[:, place : place + CHUNK] = product(w, called_first, place, CHUNK, samples)


def mask_kernel(pair_ref, called_first, done_ref, gen_ref, call_hbm, coded_ref, called_ref, out_ref, cbuf, w, sems):
    own = pair_ref.shape[1]
    rows, shard = gen_ref.shape
    first = called_first.shape[0]
    copies = row_copies(call_hbm, cbuf, first, LANES, sems)
    for copy in copies:
        copy.start()
    samples = pair_samples(lax.axis_index("var") // 2, own)
    weights(pair_ref, w)

    def convert(place):
        here, after = pl.ds(place, LANES), place - first
        gen, coded = gen_ref.at[here], coded_ref.at[here]
        if after >= 0:
            copies[after // LANES].wait()
            call, called = cbuf.at[pl.ds(after, LANES)], called_ref.at[pl.ds(after, LANES)]
        else:
            mask_ref = called_first.at[here]

        def store(block, value, mask):
            coded[block] = value
            if after >= 0:
                called[block] = mask

        held = None
        for block in blocks(LANES, shard):
            mask = call[block].astype(F32).astype(BF16) if after >= 0 else mask_ref[block]
            value = gen[block].astype(F32).astype(BF16) * mask
            if held:
                store(*held)
            held = (block, value, mask)
        store(*held)

    for place in range(0, rows + CHUNK, CHUNK):
        for part in range(place, min(place + CHUNK, rows), LANES):
            convert(part)
        if place:
            before = place - CHUNK
            coded = product(w, coded_ref, before, CHUNK, samples)
            if before < first:
                called = done_ref[:, before:place]
            else:
                called = product(w, called_ref, before - first, CHUNK, samples)
            out_ref[:, before:place] = rows_of(coded, called)


def forward_kernel(pair_ref, coded_ref, called_first, called_ref, half_ref, sums_ref, out_ref, w):
    own = pair_ref.shape[1]
    rows = coded_ref.shape[0]
    samples = pair_samples((lax.axis_index("var") // 2) ^ 1, own)
    weights(pair_ref, w)
    for place in range(0, rows, CHUNK):
        here = slice(place, place + CHUNK)
        coded = product(w, coded_ref, place, CHUNK, samples)
        called = split_product(w, called_first, called_ref, place, CHUNK, samples)
        out_ref[:, here] = half_ref[:, here] + rows_of(coded, called)
    out_ref[:, rows:] = jnp.zeros((out_ref.shape[0], LANES), F32)
    out_ref[0:8, rows:] = sums_ref[...]


def chips_kernel(own_ref, other_ref, total_ref, *messages):
    rows = own_ref.shape[1] - LANES
    total = own_ref[...] + other_ref[...]
    total_ref[...] = total
    pieces = []
    for part in halves(total[32:34, :rows]):
        part = part.astype(F32)
        for which in range(2):
            for j in range(rows // LANES):
                pieces.append(part[which : which + 1, j * LANES : (j + 1) * LANES])
    pieces += [part.astype(F32) for part in thirds(total[0:1, rows:])]
    pieces.append(jnp.zeros((32 - len(pieces), LANES), F32))
    extra = jnp.concatenate(pieces, axis=0).astype(BF16)
    for message in messages:
        message[:, :rows] = total[0:32, :rows].astype(BF16)
        message[:, rows:] = extra


def dosage_kernel(order_ref, sol_ref, dir_ref, dose_ref, after_ref, cross_ref):
    rhs = sol_ref.shape[0]
    sol_high, sol_low = halves(sol_ref[...])
    dir_high, dir_low = halves(dir_ref[...])
    stack = jnp.concatenate([sol_high, dir_high, sol_low, dir_low], axis=0)
    own = stack.shape[1]
    hot = lax.broadcasted_iota(jnp.int32, (own, own), 0) == order_ref[...]
    hot = jnp.where(hot, 1.0, 0.0).astype(BF16)
    picked = jnp.dot(stack, hot, preferred_element_type=F32).astype(BF16)
    picked = jnp.concatenate([picked, jnp.ones((16, own), BF16)], axis=0)
    dose = dose_ref[...].astype(F32).astype(BF16)
    cross = jnp.dot(picked, dose, preferred_element_type=F32)
    cross_ref[: 2 * rhs] = cross[: 2 * rhs] + cross[2 * rhs : 4 * rhs]
    cross_ref[2 * rhs :] = cross[4 * rhs : 4 * rhs + 8]


def back_kernel(variants, n_arrived, total_ref, coded_ref, called_first, called_ref, *rest):
    arrived, own_ref, messages = rest[:n_arrived], rest[n_arrived], rest[n_arrived + 1 :]
    var = lax.axis_index("var")
    rows = total_ref.shape[1] - LANES

    main = total_ref[0:32, :rows]
    allele, count = total_ref[32:33, :rows], total_ref[33:34, :rows]
    extra = jnp.zeros((32, LANES), F32)
    for ref in arrived:
        main = main + ref[:, :rows].astype(F32)
        extra = extra + ref[:, rows:].astype(F32)
    tiles = rows // LANES
    pick = lambda first: jnp.concatenate(
        [extra[first + j : first + j + 1] + extra[first + 2 * tiles + j : first + 2 * tiles + j + 1]
         for j in range(tiles)], axis=1
    )
    allele = allele + pick(0)
    count = count + pick(tiles)
    last = 4 * tiles
    sums = total_ref[0:1, rows:] + extra[last : last + 1] + extra[last + 1 : last + 2] + extra[last + 2 : last + 3]

    frequency = (allele + 1.0) / (2.0 * count + 2.0)
    spread = jnp.sqrt(2.0 * frequency * (1.0 - frequency))
    loading = (main[0:16] - 2.0 * frequency * main[16:32]) / spread
    scaled = loading / spread
    scaled_a = scaled.astype(BF16)
    scaled_b = (-2.0 * frequency * scaled).astype(BF16)
    square = as_row({6: jnp.sum(loading * loading, axis=1, keepdims=True)})
    sums = jnp.where(lane_of((1, LANES)) < 96, sums, square)

    own = own_ref.shape[1] - LANES

    def term(p):
        part = pl.ds(pl.multiple_of(p * own, LANES), own)
        got = jnp.dot(scaled_a, coded_ref[:, part], preferred_element_type=F32)
        first = called_first.shape[0]
        got = got + jnp.dot(scaled_b[:, :first], called_first[:, part], preferred_element_type=F32)
        got = got + jnp.dot(scaled_b[:, first:], called_ref[:, part], preferred_element_type=F32)
        return got / variants

    parts = [part.astype(F32) for part in thirds(sums)]
    block = jnp.concatenate(parts + [jnp.zeros((13, LANES), F32)], axis=0).astype(BF16)
    for k, ref in enumerate(messages):
        ref[:, :own] = term(var ^ (k + 1)).astype(BF16)
        ref[:, own:] = block
    own_ref[:, :own] = term(var)
    own_ref[:, own:] = jnp.concatenate([sums, jnp.zeros((15, LANES), F32)], axis=0)


def step_of(refs, noise_row, variants):
    got = refs[0][...]
    for ref in refs[1:]:
        got = got + ref[...].astype(F32)
    own = got.shape[1] - LANES
    back, last = got[:, :own], got[:, own:]
    sums = last[0:1] + last[1:2] + last[2:3]
    column = functools.partial(as_column, sums)
    noise = to_column(noise_row)
    curvature = noise * column(1) + column(6) / variants
    step = column(0) / (curvature + 1e-06)
    return back, column, noise, step


def norm_kernel(variants, width, noise_ref, dir_ref, res_ref, cross_ref, *rest):
    refs, (out_ref, new_ref) = rest[:-2], rest[-2:]
    back, _, noise, step = step_of(refs, noise_ref[...], variants)
    new = res_ref[...] - step * (noise * dir_ref[...] + back)
    new_ref[...] = new
    norm = as_row({6: jnp.sum(new * new, axis=1, keepdims=True)})
    cross = cross_ref[0:16] + step * cross_ref[16:32]
    dose = cross_ref[32:40]
    lane = lane_of((16, LANES))
    row = lax.broadcasted_iota(jnp.int32, (16, LANES), 0)
    turned = {}

    def turn(values, name, tile, by):
        if (name, tile, by) not in turned:
            piece = values[:, tile : tile + LANES]
            turned[name, tile, by] = pltpu.roll(piece, by, 1) if by else piece
        return turned[name, tile, by]

    for j in range(out_ref.shape[0]):
        tile, inside = (j * width) // LANES * LANES, (j * width) % LANES
        block = jnp.zeros((16, LANES), F32)
        for m in range(4):
            here = (row // 4 == m) & (lane >= 32 * m) & (lane < 32 * m + width)
            block = jnp.where(here, turn(cross, "cross", tile, (32 * m - inside) % LANES), block)
        block = block[0:8] + block[8:16]
        block = block[0:4] + block[4:8]
        last = jnp.where(lane[0:1] < width, turn(dose, "dose", tile, -inside % LANES)[0:1], norm)
        for k in range(4):
            out_ref[j, :, k * LANES : (k + 1) * LANES] = block[k : k + 1]
        out_ref[j, :, 4 * LANES :] = last


def new_kernel(variants, noise_ref, dir_ref, res_ref, sol_ref, *rest):
    refs, (sol_out, res_out, stats_out) = rest[:-3], rest[-3:]
    back, column, noise, step = step_of(refs, noise_ref[...], variants)
    dire = dir_ref[...]
    sol_out[...] = sol_ref[...] + step * dire
    res_out[...] = res_ref[...] - step * (noise * dire + back)
    sol_sum = column(2) + step * column(5)
    sol_square = column(3) + 2.0 * step * column(4) + step * (step * column(1))
    lane = lane_of(stats_out.shape)
    stats_out[...] = jnp.where(lane == 0, column(0), jnp.where(lane == 1, sol_sum, sol_square))


def last_kernel(samples, width, came_ref, stats_ref, res_ref, dir_ref, out_ref, score_out):
    total = jnp.sum(came_ref[...], axis=0)
    last = total[:, 4 * LANES :]
    out_ref[...] = res_ref[...] + (as_column(last, 6) / (stats_ref[:, 0:1] + 1e-06)) * dir_ref[...]
    row = lax.broadcasted_iota(jnp.int32, (16, LANES), 0)
    spread = jnp.zeros((16, LANES), F32)
    for k in range(4):
        spread = jnp.where(row % 4 == k, total[:, k * LANES : (k + 1) * LANES], spread)
    cross = spread
    for m in range(1, 4):
        cross = jnp.where(row // 4 == m, pltpu.roll(spread, LANES - 32 * m, 1), cross)
    dose = last
    sol_sum, sol_square = stats_ref[:, 1:2], stats_ref[:, 2:3]
    dose_freq = (dose / 100.0 + 1.0) / (2.0 * samples + 2.0)
    dose_spread = jnp.sqrt(2.0 * dose_freq * (1.0 - dose_freq))
    scale = math.sqrt(samples) * jnp.sqrt(sol_square / samples + 1e-06)
    scores = (cross / 100.0 - 2.0 * dose_freq * sol_sum) / (dose_spread * scale)
    score_out[...] = scores[:, :width]


def call(kernel, out, ins, args, scratch=(), limit=16, flops=0, moved=0):
    return pl.pallas_call(
        kernel,
        out_shape=[jax.ShapeDtypeStruct(*o) if len(o) == 2 else o[2](*o[:2]) for o in out],
        in_specs=list(ins),
        out_specs=[VMEM] * len(out),
        scratch_shapes=list(scratch),
        compiler_params=pltpu.CompilerParams(vmem_limit_bytes=limit * MIB),
        cost_estimate=pl.CostEstimate(flops=flops, bytes_accessed=moved, transcendentals=0),
    )(*[pltpu.with_memory_space_constraint(x, pltpu.HBM) if spec is HBM else x for spec, x in zip(ins, args)])


def body(genotypes, called, dosage, sample_order, noise_ratio, solution, residual, direction):
    n_var = lax.axis_size("var")
    n_samp = lax.axis_size("samp")
    own, rhs = direction.shape
    rows, shard = genotypes.shape
    variants = rows * n_var
    samples = own * n_samp * n_var
    imputed = dosage.shape[1]
    width = imputed // (n_var * n_samp)
    noise = noise_ratio[None]

    dire, res, sol = direction.T, residual.T, solution.T
    first, chunk = rows // 3 * 2, 128
    matrix = lambda n: ((n, shard), BF16, pltpu.VMEM)

    neighbour = swap(dire, "var", 1)
    called_a, sums = call(
        functools.partial(called_kernel, chunk),
        [matrix(first), ((8, LANES), F32)],
        [HBM] * 4,
        (sol, dire, res, called),
        scratch=[
            pltpu.VMEM((rhs, own), F32),
            pltpu.VMEM((rhs, own), F32),
            pltpu.VMEM((rhs, own), F32),
            pltpu.VMEM((first, shard), jnp.int32),
            pltpu.SemaphoreType.DMA((3,)),
            pltpu.SemaphoreType.DMA((first // chunk,)),
        ],
        limit=10,
        moved=4 * first * shard,
    )
    (pair,) = call(pair_kernel, [((2 * rhs, own), BF16)], [VMEM] * 2, (dire, neighbour), limit=4)
    pair_other = swap(pair, "var", 2)
    row_weights = pltpu.VMEM((2 * rhs, 2 * own), BF16)
    (done,) = call(
        called_product_kernel,
        [((2 * rhs, first), F32)],
        [VMEM] * 2,
        (pair, called_a),
        scratch=[row_weights],
        limit=4,
        flops=first * shard * 256,
        moved=first * shard,
    )
    coded, called_b, half = call(
        mask_kernel,
        [matrix(rows), matrix(rows - first), ((2 * rhs + 8, rows), F32)],
        [VMEM] * 4 + [HBM],
        (pair, called_a, done, genotypes, called),
        scratch=[
            pltpu.VMEM((rows - first, shard), jnp.int32),
            row_weights,
            pltpu.SemaphoreType.DMA(((rows - first) // LANES,)),
        ],
        limit=12,
        flops=2 * rows * shard * 256,
        moved=4 * rows * shard,
    )
    (part,) = call(
        forward_kernel,
        [((2 * rhs + 8, rows + LANES), F32)],
        [VMEM] * 6,
        (pair_other, coded, called_a, called_b, half, sums),
        scratch=[row_weights],
        flops=2 * rows * shard * 256,
        moved=2 * rows * shard,
    )
    part_other = swap(part, "samp", 1)

    n_chips = n_samp // 2
    total, *messages = call(
        chips_kernel,
        [(part.shape, F32)] + [((2 * rhs, rows + LANES), BF16)] * (n_chips - 1),
        [VMEM] * 2,
        (part, part_other),
        moved=1 * MIB,
    )
    arrived = [swap(messages[k], "samp", 2 * (k + 1) + 1) for k in reversed(range(n_chips - 1))]
    (cross,) = call(
        dosage_kernel,
        [((2 * rhs + 8, imputed), F32)],
        [VMEM] * 5,
        (sample_order, sol, dire, dosage, total),
        flops=2 * 80 * own * (own + imputed),
        moved=4 * own * imputed,
    )

    wide = own + LANES
    mine_back, *messages = call(
        functools.partial(back_kernel, variants, len(arrived)),
        [((rhs, wide), F32)] + [((rhs, wide), BF16)] * (n_var - 1),
        [VMEM] * (4 + len(arrived)),
        (total, coded, called_a, called_b, *arrived),
        flops=4 * rows * shard * 256,
        moved=4 * rows * shard,
    )
    backs = [mine_back] + [swap(messages[k], "var", k + 1) for k in reversed(range(n_var - 1))]

    n_all = n_var * n_samp
    outgoing, res_keep = call(
        functools.partial(norm_kernel, variants, width),
        [((n_all, 1, 5 * LANES), F32), ((rhs, own), F32)],
        [VMEM] * (4 + n_var),
        (noise, dire, res, cross, *backs),
        moved=4 * 5 * n_all * LANES,
    )
    came = lax.all_to_all(outgoing, ("var", "samp"), split_axis=0, concat_axis=0)
    sol_new, res_new, stats = call(
        functools.partial(new_kernel, variants),
        [((rhs, own), F32), ((rhs, own), F32), ((rhs, LANES), F32)],
        [VMEM] * (4 + n_var),
        (noise, dire, res, sol, *backs),
        moved=1 * MIB,
    )
    dir_new, scores = call(
        functools.partial(last_kernel, samples, width),
        [((rhs, own), F32), ((rhs, width), F32)],
        [VMEM] * 4,
        (came, stats, res_keep, dire),
    )
    return (sol_new.T, res_new.T, dir_new.T, scores.T)


def solution(mesh):
    placed = (
        P("var", "samp"),
        P("var", "samp"),
        P(("samp", "var"), None),
        P(("samp", "var"), None),
        P(),
        P(("samp", "var"), None),
        P(("samp", "var"), None),
        P(("samp", "var"), None),
    )
    return jax.shard_map(
        body,
        mesh=mesh,
        in_specs=placed,
        out_specs=(
            P(("samp", "var"), None),
            P(("samp", "var"), None),
            P(("samp", "var"), None),
            P(("var", "samp"), None),
        ),
        check_vma=False,
    )
```

```python
import functools
import math

import jax
import jax.numpy as jnp
from jax import lax
from jax.experimental import pallas as pl
from jax.experimental.pallas import tpu as pltpu
from jax.sharding import PartitionSpec as P

BF16 = jnp.bfloat16
F32 = jnp.float32
LANES = 128
NT = (((1,), (1,)), ((), ()))
VMEM = pl.BlockSpec(memory_space=pltpu.VMEM)
HBM = pl.BlockSpec(memory_space=pltpu.HBM)
MIB = 1 << 20


def swap(values, axis, distance):
    size = lax.axis_size(axis)
    return lax.ppermute(values, axis, [(i, i ^ distance) for i in range(size)])


def halves(values):
    high = values.astype(BF16)
    return high, (values - high.astype(F32)).astype(BF16)


def thirds(values):
    high = values.astype(BF16)
    rest = values - high.astype(F32)
    middle = rest.astype(BF16)
    return high, middle, (rest - middle.astype(F32)).astype(BF16)


def lane_of(shape):
    return lax.broadcasted_iota(jnp.int32, shape, len(shape) - 1)


def spot(q):
    shape = (16, LANES)
    return lane_of(shape) == 16 * q + lax.broadcasted_iota(jnp.int32, shape, 0)


def as_row(values):
    block = jnp.zeros((16, LANES), F32)
    for q, column in values.items():
        block = jnp.where(spot(q), column, block)
    return jnp.sum(block, axis=0, keepdims=True)


def as_column(row, q):
    return jnp.sum(jnp.where(spot(q), row, 0.0), axis=1, keepdims=True)


def to_column(row):
    shape = (16, row.shape[1])
    same = lax.broadcasted_iota(jnp.int32, shape, 0) == lane_of(shape)
    return jnp.sum(jnp.where(same, row, 0.0), axis=1, keepdims=True)


BLOCK = 512
CHUNK = 256


def blocks(rows, samples):
    return [
        (pl.ds(row, 16), pl.ds(sample, BLOCK)) for row in range(0, rows, 16) for sample in range(0, samples, BLOCK)
    ]


def row_copies(source, target, first, chunk, sems):
    return [
        pltpu.make_async_copy(source.at[pl.ds(first + i, chunk)], target.at[pl.ds(i, chunk)], sems.at[i // chunk])
        for i in range(0, target.shape[0], chunk)
    ]


def called_kernel(chunk, sol_hbm, dir_hbm, res_hbm, call_hbm, out_ref, sums_ref,
                  sol_ref, dir_ref, res_ref, cbuf, small_sems, sems):
    small = [
        pltpu.make_async_copy(source, target, small_sems.at[i])
        for i, (source, target) in enumerate(((sol_hbm, sol_ref), (dir_hbm, dir_ref), (res_hbm, res_ref)))
    ]
    for copy in small:
        copy.start()
    parts = row_copies(call_hbm, cbuf, 0, chunk, sems)
    for copy in parts:
        copy.start()
    for copy in small:
        copy.wait()
    sol, dire, res = sol_ref[...], dir_ref[...], res_ref[...]
    products = (res * res, dire * dire, sol, sol * sol, sol * dire, dire)
    row = as_row({q: jnp.sum(x, axis=1, keepdims=True) for q, x in enumerate(products)})
    sums_ref[...] = jnp.broadcast_to(row, sums_ref.shape)
    for i, copy in enumerate(parts):
        copy.wait()
        source, target = cbuf.at[pl.ds(i * chunk, chunk)], out_ref.at[pl.ds(i * chunk, chunk)]
        for here in blocks(chunk, source.shape[1]):
            target[here] = source[here].astype(F32).astype(BF16)


def pair_kernel(own_ref, other_ref, out_ref):
    upper = lax.axis_index("var") % 2
    rhs = own_ref.shape[0]
    own, other = own_ref[...], other_ref[...]
    out_ref[:rhs] = jnp.where(upper == 0, own, other).astype(BF16)
    out_ref[rhs:] = jnp.where(upper == 0, other, own).astype(BF16)


def weights(pair_ref, w):
    own = pair_ref.shape[1]
    row = lax.broadcasted_iota(jnp.int32, (16, 2 * own), 0)
    w[16:32] = jnp.where(row == 0, 1.0, 0.0).astype(BF16)
    for i in range(2):
        w[0:16, i * own : (i + 1) * own] = pair_ref[16 * i : 16 * i + 16]


def product(w, matrix, first, rows, samples):
    return lax.dot_general(w[...], matrix[pl.ds(first, rows), samples], NT, preferred_element_type=F32)


def split_product(w, head, tail, first, rows, samples):
    if first < head.shape[0]:
        return product(w, head, first, rows, samples)
    return product(w, tail, first - head.shape[0], rows, samples)


def rows_of(coded, called):
    counts = jnp.concatenate([coded[16:17], called[16:17], jnp.zeros((6, coded.shape[1]), F32)], axis=0)
    return jnp.concatenate([coded[0:16], called[0:16], counts], axis=0)


def pair_samples(pair, own):
    return pl.ds(pl.multiple_of(pair * 2 * own, LANES), 2 * own)


def called_product_kernel(pair_ref, called_first, out_ref, w):
    own = pair_ref.shape[1]
    samples = pair_samples(lax.axis_index("var") // 2, own)
    weights(pair_ref, w)
    for place in range(0, called_first.shape[0], CHUNK):
        out_ref[:, place : place + CHUNK] = product(w, called_first, place, CHUNK, samples)


def mask_kernel(pair_ref, called_first, done_ref, gen_ref, call_hbm, coded_ref, called_ref, out_ref, cbuf, w, sems):
    own = pair_ref.shape[1]
    rows, shard = gen_ref.shape
    first = called_first.shape[0]
    copies = row_copies(call_hbm, cbuf, first, LANES, sems)
    for copy in copies:
        copy.start()
    samples = pair_samples(lax.axis_index("var") // 2, own)
    weights(pair_ref, w)

    def convert(place):
        here, after = pl.ds(place, LANES), place - first
        gen, coded = gen_ref.at[here], coded_ref.at[here]
        if after >= 0:
            copies[after // LANES].wait()
            call, called = cbuf.at[pl.ds(after, LANES)], called_ref.at[pl.ds(after, LANES)]
        else:
            mask_ref = called_first.at[here]

        def store(block, value, mask):
            coded[block] = value
            if after >= 0:
                called[block] = mask

        held = []
        for block in blocks(LANES, shard):
            mask = call[block].astype(F32).astype(BF16) if after >= 0 else mask_ref[block]
            held.append((block, gen[block].astype(F32).astype(BF16) * mask, mask))
            if len(held) > 4:
                store(*held.pop(0))
        for item in held:
            store(*item)

    for place in range(0, rows + CHUNK, CHUNK):
        if place:
            before = place - CHUNK
            coded = product(w, coded_ref, before, CHUNK, samples)
            if before < first:
                called = done_ref[:, before:place]
            else:
                called = product(w, called_ref, before - first, CHUNK, samples)
            out_ref[:, before:place] = rows_of(coded, called)
        for part in range(place, min(place + CHUNK, rows), LANES):
            convert(part)


def forward_kernel(pair_ref, coded_ref, called_first, called_ref, half_ref, sums_ref, out_ref, w):
    own = pair_ref.shape[1]
    rows = coded_ref.shape[0]
    samples = pair_samples((lax.axis_index("var") // 2) ^ 1, own)
    weights(pair_ref, w)
    for place in range(0, rows, CHUNK):
        here = slice(place, place + CHUNK)
        coded = product(w, coded_ref, place, CHUNK, samples)
        called = split_product(w, called_first, called_ref, place, CHUNK, samples)
        out_ref[:, here] = half_ref[:, here] + rows_of(coded, called)
    out_ref[:, rows:] = jnp.zeros((out_ref.shape[0], LANES), F32)
    out_ref[0:8, rows:] = sums_ref[...]


def chips_kernel(own_ref, other_ref, total_ref, *messages):
    rows = own_ref.shape[1] - LANES
    total = own_ref[...] + other_ref[...]
    total_ref[...] = total
    pieces = []
    for part in halves(total[32:34, :rows]):
        part = part.astype(F32)
        for which in range(2):
            for j in range(rows // LANES):
                pieces.append(part[which : which + 1, j * LANES : (j + 1) * LANES])
    pieces += [part.astype(F32) for part in thirds(total[0:1, rows:])]
    pieces.append(jnp.zeros((32 - len(pieces), LANES), F32))
    extra = jnp.concatenate(pieces, axis=0).astype(BF16)
    for message in messages:
        message[:, :rows] = total[0:32, :rows].astype(BF16)
        message[:, rows:] = extra


def dosage_kernel(order_ref, sol_ref, dir_ref, dose_ref, after_ref, cross_ref):
    rhs = sol_ref.shape[0]
    sol_high, sol_low = halves(sol_ref[...])
    dir_high, dir_low = halves(dir_ref[...])
    stack = jnp.concatenate([sol_high, dir_high, sol_low, dir_low], axis=0)
    own = stack.shape[1]
    hot = lax.broadcasted_iota(jnp.int32, (own, own), 0) == order_ref[...]
    hot = jnp.where(hot, 1.0, 0.0).astype(BF16)
    picked = jnp.dot(stack, hot, preferred_element_type=F32).astype(BF16)
    picked = jnp.concatenate([picked, jnp.ones((16, own), BF16)], axis=0)
    dose = dose_ref[...].astype(F32).astype(BF16)
    cross = jnp.dot(picked, dose, preferred_element_type=F32)
    cross_ref[: 2 * rhs] = cross[: 2 * rhs] + cross[2 * rhs : 4 * rhs]
    cross_ref[2 * rhs :] = cross[4 * rhs : 4 * rhs + 8]


def back_kernel(variants, n_arrived, total_ref, coded_ref, called_first, called_ref, *rest):
    arrived, own_ref, messages = rest[:n_arrived], rest[n_arrived], rest[n_arrived + 1 :]
    var = lax.axis_index("var")
    rows = total_ref.shape[1] - LANES

    main = total_ref[0:32, :rows]
    allele, count = total_ref[32:33, :rows], total_ref[33:34, :rows]
    extra = jnp.zeros((32, LANES), F32)
    for ref in arrived:
        main = main + ref[:, :rows].astype(F32)
        extra = extra + ref[:, rows:].astype(F32)
    tiles = rows // LANES
    pick = lambda first: jnp.concatenate(
        [extra[first + j : first + j + 1] + extra[first + 2 * tiles + j : first + 2 * tiles + j + 1]
         for j in range(tiles)], axis=1
    )
    allele = allele + pick(0)
    count = count + pick(tiles)
    last = 4 * tiles
    sums = total_ref[0:1, rows:] + extra[last : last + 1] + extra[last + 1 : last + 2] + extra[last + 2 : last + 3]

    frequency = (allele + 1.0) / (2.0 * count + 2.0)
    spread = jnp.sqrt(2.0 * frequency * (1.0 - frequency))
    loading = (main[0:16] - 2.0 * frequency * main[16:32]) / spread
    scaled = loading / spread
    scaled_a = scaled.astype(BF16)
    scaled_b = (-2.0 * frequency * scaled).astype(BF16)
    square = as_row({6: jnp.sum(loading * loading, axis=1, keepdims=True)})
    sums = jnp.where(lane_of((1, LANES)) < 96, sums, square)

    own = own_ref.shape[1] - LANES

    def term(p):
        part = pl.ds(pl.multiple_of(p * own, LANES), own)
        got = jnp.dot(scaled_a, coded_ref[:, part], preferred_element_type=F32)
        first = called_first.shape[0]
        got = got + jnp.dot(scaled_b[:, :first], called_first[:, part], preferred_element_type=F32)
        got = got + jnp.dot(scaled_b[:, first:], called_ref[:, part], preferred_element_type=F32)
        return got / variants

    parts = [part.astype(F32) for part in thirds(sums)]
    block = jnp.concatenate(parts + [jnp.zeros((13, LANES), F32)], axis=0).astype(BF16)
    for k, ref in enumerate(messages):
        ref[:, :own] = term(var ^ (k + 1)).astype(BF16)
        ref[:, own:] = block
    own_ref[:, :own] = term(var)
    own_ref[:, own:] = jnp.concatenate([sums, jnp.zeros((15, LANES), F32)], axis=0)


def step_of(refs, noise_row, variants):
    got = refs[0][...]
    for ref in refs[1:]:
        got = got + ref[...].astype(F32)
    own = got.shape[1] - LANES
    back, last = got[:, :own], got[:, own:]
    sums = last[0:1] + last[1:2] + last[2:3]
    column = functools.partial(as_column, sums)
    noise = to_column(noise_row)
    curvature = noise * column(1) + column(6) / variants
    step = column(0) / (curvature + 1e-06)
    return back, column, noise, step


def norm_kernel(variants, width, noise_ref, dir_ref, res_ref, cross_ref, *rest):
    refs, (out_ref, new_ref) = rest[:-2], rest[-2:]
    back, _, noise, step = step_of(refs, noise_ref[...], variants)
    new = res_ref[...] - step * (noise * dir_ref[...] + back)
    new_ref[...] = new
    norm = as_row({6: jnp.sum(new * new, axis=1, keepdims=True)})
    cross = cross_ref[0:16] + step * cross_ref[16:32]
    dose = cross_ref[32:40]
    lane = lane_of((16, LANES))
    row = lax.broadcasted_iota(jnp.int32, (16, LANES), 0)
    turned = {}

    def turn(values, name, tile, by):
        if (name, tile, by) not in turned:
            piece = values[:, tile : tile + LANES]
            turned[name, tile, by] = pltpu.roll(piece, by, 1) if by else piece
        return turned[name, tile, by]

    for j in range(out_ref.shape[0]):
        tile, inside = (j * width) // LANES * LANES, (j * width) % LANES
        block = jnp.zeros((16, LANES), F32)
        for m in range(4):
            here = (row // 4 == m) & (lane >= 32 * m) & (lane < 32 * m + width)
            block = jnp.where(here, turn(cross, "cross", tile, (32 * m - inside) % LANES), block)
        block = block[0:8] + block[8:16]
        block = block[0:4] + block[4:8]
        last = jnp.where(lane[0:1] < width, turn(dose, "dose", tile, -inside % LANES)[0:1], norm)
        for k in range(4):
            out_ref[j, :, k * LANES : (k + 1) * LANES] = block[k : k + 1]
        out_ref[j, :, 4 * LANES :] = last


def new_kernel(variants, noise_ref, dir_ref, res_ref, sol_ref, *rest):
    refs, (sol_out, res_out, stats_out) = rest[:-3], rest[-3:]
    back, column, noise, step = step_of(refs, noise_ref[...], variants)
    dire = dir_ref[...]
    sol_out[...] = sol_ref[...] + step * dire
    res_out[...] = res_ref[...] - step * (noise * dire + back)
    sol_sum = column(2) + step * column(5)
    sol_square = column(3) + 2.0 * step * column(4) + step * (step * column(1))
    lane = lane_of(stats_out.shape)
    stats_out[...] = jnp.where(lane == 0, column(0), jnp.where(lane == 1, sol_sum, sol_square))


def last_kernel(samples, width, came_ref, stats_ref, res_ref, dir_ref, out_ref, score_out):
    total = jnp.sum(came_ref[...], axis=0)
    last = total[:, 4 * LANES :]
    out_ref[...] = res_ref[...] + (as_column(last, 6) / (stats_ref[:, 0:1] + 1e-06)) * dir_ref[...]
    row = lax.broadcasted_iota(jnp.int32, (16, LANES), 0)
    spread = jnp.zeros((16, LANES), F32)
    for k in range(4):
        spread = jnp.where(row % 4 == k, total[:, k * LANES : (k + 1) * LANES], spread)
    cross = spread
    for m in range(1, 4):
        cross = jnp.where(row // 4 == m, pltpu.roll(spread, LANES - 32 * m, 1), cross)
    dose = last
    sol_sum, sol_square = stats_ref[:, 1:2], stats_ref[:, 2:3]
    dose_freq = (dose / 100.0 + 1.0) / (2.0 * samples + 2.0)
    dose_spread = jnp.sqrt(2.0 * dose_freq * (1.0 - dose_freq))
    scale = math.sqrt(samples) * jnp.sqrt(sol_square / samples + 1e-06)
    scores = (cross / 100.0 - 2.0 * dose_freq * sol_sum) / (dose_spread * scale)
    score_out[...] = scores[:, :width]


def call(kernel, out, ins, args, scratch=(), limit=16, flops=0, moved=0):
    return pl.pallas_call(
        kernel,
        out_shape=[jax.ShapeDtypeStruct(*o) if len(o) == 2 else o[2](*o[:2]) for o in out],
        in_specs=list(ins),
        out_specs=[VMEM] * len(out),
        scratch_shapes=list(scratch),
        compiler_params=pltpu.CompilerParams(vmem_limit_bytes=limit * MIB),
        cost_estimate=pl.CostEstimate(flops=flops, bytes_accessed=moved, transcendentals=0),
    )(*[pltpu.with_memory_space_constraint(x, pltpu.HBM) if spec is HBM else x for spec, x in zip(ins, args)])


def body(genotypes, called, dosage, sample_order, noise_ratio, solution, residual, direction):
    n_var = lax.axis_size("var")
    n_samp = lax.axis_size("samp")
    own, rhs = direction.shape
    rows, shard = genotypes.shape
    variants = rows * n_var
    samples = own * n_samp * n_var
    imputed = dosage.shape[1]
    width = imputed // (n_var * n_samp)
    noise = noise_ratio[None]

    dire, res, sol = direction.T, residual.T, solution.T
    first, chunk = rows // 3 * 2, 128
    matrix = lambda n: ((n, shard), BF16, pltpu.VMEM)

    neighbour = swap(dire, "var", 1)
    called_a, sums = call(
        functools.partial(called_kernel, chunk),
        [matrix(first), ((8, LANES), F32)],
        [HBM] * 4,
        (sol, dire, res, called),
        scratch=[
            pltpu.VMEM((rhs, own), F32),
            pltpu.VMEM((rhs, own), F32),
            pltpu.VMEM((rhs, own), F32),
            pltpu.VMEM((first, shard), jnp.int32),
            pltpu.SemaphoreType.DMA((3,)),
            pltpu.SemaphoreType.DMA((first // chunk,)),
        ],
        limit=10,
        moved=4 * first * shard,
    )
    (pair,) = call(pair_kernel, [((2 * rhs, own), BF16)], [VMEM] * 2, (dire, neighbour), limit=4)
    pair_other = swap(pair, "var", 2)
    row_weights = pltpu.VMEM((2 * rhs, 2 * own), BF16)
    (done,) = call(
        called_product_kernel,
        [((2 * rhs, first), F32)],
        [VMEM] * 2,
        (pair, called_a),
        scratch=[row_weights],
        limit=4,
        flops=first * shard * 256,
        moved=first * shard,
    )
    coded, called_b, half = call(
        mask_kernel,
        [matrix(rows), matrix(rows - first), ((2 * rhs + 8, rows), F32)],
        [VMEM] * 4 + [HBM],
        (pair, called_a, done, genotypes, called),
        scratch=[
            pltpu.VMEM((rows - first, shard), jnp.int32),
            row_weights,
            pltpu.SemaphoreType.DMA(((rows - first) // LANES,)),
        ],
        limit=12,
        flops=2 * rows * shard * 256,
        moved=4 * rows * shard,
    )
    (part,) = call(
        forward_kernel,
        [((2 * rhs + 8, rows + LANES), F32)],
        [VMEM] * 6,
        (pair_other, coded, called_a, called_b, half, sums),
        scratch=[row_weights],
        flops=2 * rows * shard * 256,
        moved=2 * rows * shard,
    )
    part_other = swap(part, "samp", 1)

    n_chips = n_samp // 2
    total, *messages = call(
        chips_kernel,
        [(part.shape, F32)] + [((2 * rhs, rows + LANES), BF16)] * (n_chips - 1),
        [VMEM] * 2,
        (part, part_other),
        moved=1 * MIB,
    )
    arrived = [swap(messages[k], "samp", 2 * (k + 1) + 1) for k in reversed(range(n_chips - 1))]
    (cross,) = call(
        dosage_kernel,
        [((2 * rhs + 8, imputed), F32)],
        [VMEM] * 5,
        (sample_order, sol, dire, dosage, total),
        flops=2 * 80 * own * (own + imputed),
        moved=4 * own * imputed,
    )

    wide = own + LANES
    mine_back, *messages = call(
        functools.partial(back_kernel, variants, len(arrived)),
        [((rhs, wide), F32)] + [((rhs, wide), BF16)] * (n_var - 1),
        [VMEM] * (4 + len(arrived)),
        (total, coded, called_a, called_b, *arrived),
        flops=4 * rows * shard * 256,
        moved=4 * rows * shard,
    )
    backs = [mine_back] + [swap(messages[k], "var", k + 1) for k in reversed(range(n_var - 1))]

    n_all = n_var * n_samp
    outgoing, res_keep = call(
        functools.partial(norm_kernel, variants, width),
        [((n_all, 1, 5 * LANES), F32), ((rhs, own), F32)],
        [VMEM] * (4 + n_var),
        (noise, dire, res, cross, *backs),
        moved=4 * 5 * n_all * LANES,
    )
    came = lax.all_to_all(outgoing, ("var", "samp"), split_axis=0, concat_axis=0)
    sol_new, res_new, stats = call(
        functools.partial(new_kernel, variants),
        [((rhs, own), F32), ((rhs, own), F32), ((rhs, LANES), F32)],
        [VMEM] * (4 + n_var),
        (noise, dire, res, sol, *backs),
        moved=1 * MIB,
    )
    dir_new, scores = call(
        functools.partial(last_kernel, samples, width),
        [((rhs, own), F32), ((rhs, width), F32)],
        [VMEM] * 4,
        (came, stats, res_keep, dire),
    )
    return (sol_new.T, res_new.T, dir_new.T, scores.T)


def solution(mesh):
    placed = (
        P("var", "samp"),
        P("var", "samp"),
        P(("samp", "var"), None),
        P(("samp", "var"), None),
        P(),
        P(("samp", "var"), None),
        P(("samp", "var"), None),
        P(("samp", "var"), None),
    )
    return jax.shard_map(
        body,
        mesh=mesh,
        in_specs=placed,
        out_specs=(
            P(("samp", "var"), None),
            P(("samp", "var"), None),
            P(("samp", "var"), None),
            P(("var", "samp"), None),
        ),
        check_vma=False,
    )
```

```python
import functools
import math

import jax
import jax.numpy as jnp
from jax import lax
from jax.experimental import pallas as pl
from jax.experimental.pallas import tpu as pltpu
from jax.sharding import PartitionSpec as P

BF16 = jnp.bfloat16
F32 = jnp.float32
LANES = 128
NT = (((1,), (1,)), ((), ()))
VMEM = pl.BlockSpec(memory_space=pltpu.VMEM)
HBM = pl.BlockSpec(memory_space=pltpu.HBM)
MIB = 1 << 20


def swap(values, axis, distance):
    size = lax.axis_size(axis)
    return lax.ppermute(values, axis, [(i, i ^ distance) for i in range(size)])


def halves(values):
    high = values.astype(BF16)
    return high, (values - high.astype(F32)).astype(BF16)


def thirds(values):
    high = values.astype(BF16)
    rest = values - high.astype(F32)
    middle = rest.astype(BF16)
    return high, middle, (rest - middle.astype(F32)).astype(BF16)


def lane_of(shape):
    return lax.broadcasted_iota(jnp.int32, shape, len(shape) - 1)


def spot(q):
    shape = (16, LANES)
    return lane_of(shape) == 16 * q + lax.broadcasted_iota(jnp.int32, shape, 0)


def as_row(values):
    block = jnp.zeros((16, LANES), F32)
    for q, column in values.items():
        block = jnp.where(spot(q), column, block)
    return jnp.sum(block, axis=0, keepdims=True)


def as_column(row, q):
    return jnp.sum(jnp.where(spot(q), row, 0.0), axis=1, keepdims=True)


def to_column(row):
    shape = (16, row.shape[1])
    same = lax.broadcasted_iota(jnp.int32, shape, 0) == lane_of(shape)
    return jnp.sum(jnp.where(same, row, 0.0), axis=1, keepdims=True)


BLOCK = 512
CHUNK = 256


def blocks(rows, samples):
    return [
        (pl.ds(row, 16), pl.ds(sample, BLOCK)) for row in range(0, rows, 16) for sample in range(0, samples, BLOCK)
    ]


def row_copies(source, target, first, chunk, sems):
    return [
        pltpu.make_async_copy(source.at[pl.ds(first + i, chunk)], target.at[pl.ds(i, chunk)], sems.at[i // chunk])
        for i in range(0, target.shape[0], chunk)
    ]


def called_kernel(chunk, sol_hbm, dir_hbm, res_hbm, call_hbm, out_ref, sums_ref,
                  sol_ref, dir_ref, res_ref, cbuf, small_sems, sems):
    small = [
        pltpu.make_async_copy(source, target, small_sems.at[i])
        for i, (source, target) in enumerate(((sol_hbm, sol_ref), (dir_hbm, dir_ref), (res_hbm, res_ref)))
    ]
    for copy in small:
        copy.start()
    parts = row_copies(call_hbm, cbuf, 0, chunk, sems)
    for copy in parts:
        copy.start()
    for copy in small:
        copy.wait()
    sol, dire, res = sol_ref[...], dir_ref[...], res_ref[...]
    products = (res * res, dire * dire, sol, sol * sol, sol * dire, dire)
    row = as_row({q: jnp.sum(x, axis=1, keepdims=True) for q, x in enumerate(products)})
    sums_ref[...] = jnp.broadcast_to(row, sums_ref.shape)
    for i, copy in enumerate(parts):
        copy.wait()
        source, target = cbuf.at[pl.ds(i * chunk, chunk)], out_ref.at[pl.ds(i * chunk, chunk)]
        for here in blocks(chunk, source.shape[1]):
            target[here] = source[here].astype(F32).astype(BF16)


def pair_kernel(own_ref, other_ref, out_ref):
    upper = lax.axis_index("var") % 2
    rhs = own_ref.shape[0]
    own, other = own_ref[...], other_ref[...]
    out_ref[:rhs] = jnp.where(upper == 0, own, other).astype(BF16)
    out_ref[rhs:] = jnp.where(upper == 0, other, own).astype(BF16)


def weights(pair_ref, w):
    own = pair_ref.shape[1]
    row = lax.broadcasted_iota(jnp.int32, (16, 2 * own), 0)
    w[16:32] = jnp.where(row == 0, 1.0, 0.0).astype(BF16)
    for i in range(2):
        w[0:16, i * own : (i + 1) * own] = pair_ref[16 * i : 16 * i + 16]


def product(w, matrix, first, rows, samples):
    return lax.dot_general(w[...], matrix[pl.ds(first, rows), samples], NT, preferred_element_type=F32)


def split_product(w, head, tail, first, rows, samples):
    if first < head.shape[0]:
        return product(w, head, first, rows, samples)
    return product(w, tail, first - head.shape[0], rows, samples)


def rows_of(coded, called):
    counts = jnp.concatenate([coded[16:17], called[16:17], jnp.zeros((6, coded.shape[1]), F32)], axis=0)
    return jnp.concatenate([coded[0:16], called[0:16], counts], axis=0)


def pair_samples(pair, own):
    return pl.ds(pl.multiple_of(pair * 2 * own, LANES), 2 * own)


def called_product_kernel(pair_ref, called_first, out_ref, w):
    own = pair_ref.shape[1]
    samples = pair_samples(lax.axis_index("var") // 2, own)
    weights(pair_ref, w)
    for place in range(0, called_first.shape[0], CHUNK):
        out_ref[:, place : place + CHUNK] = product(w, called_first, place, CHUNK, samples)


def mask_kernel(pair_ref, called_first, done_ref, gen_ref, call_hbm, coded_ref, called_ref, out_ref, cbuf, w, sems):
    own = pair_ref.shape[1]
    rows, shard = gen_ref.shape
    first = called_first.shape[0]
    copies = row_copies(call_hbm, cbuf, first, LANES, sems)
    for copy in copies:
        copy.start()
    samples = pair_samples(lax.axis_index("var") // 2, own)
    weights(pair_ref, w)

    def convert(place):
        here, after = pl.ds(place, LANES), place - first
        gen, coded = gen_ref.at[here], coded_ref.at[here]
        if after >= 0:
            copies[after // LANES].wait()
            call, called = cbuf.at[pl.ds(after, LANES)], called_ref.at[pl.ds(after, LANES)]
        else:
            mask_ref = called_first.at[here]

        def store(block, value, mask):
            coded[block] = value
            if after >= 0:
                called[block] = mask

        held = []
        for block in blocks(LANES, shard):
            mask = call[block].astype(F32).astype(BF16) if after >= 0 else mask_ref[block]
            held.append((block, gen[block].astype(F32).astype(BF16) * mask, mask))
            if len(held) > 4:
                store(*held.pop(0))
        for item in held:
            store(*item)

    for place in range(0, rows + CHUNK, CHUNK):
        if place:
            before = place - CHUNK
            coded = product(w, coded_ref, before, CHUNK, samples)
            if before < first:
                called = done_ref[:, before:place]
            else:
                called = product(w, called_ref, before - first, CHUNK, samples)
            out_ref[:, before:place] = rows_of(coded, called)
        for part in range(place, min(place + CHUNK, rows), LANES):
            convert(part)


def forward_kernel(pair_ref, coded_ref, called_first, called_ref, half_ref, sums_ref, out_ref, w):
    own = pair_ref.shape[1]
    rows = coded_ref.shape[0]
    samples = pair_samples((lax.axis_index("var") // 2) ^ 1, own)
    weights(pair_ref, w)
    for place in range(0, rows, CHUNK):
        here = slice(place, place + CHUNK)
        coded = product(w, coded_ref, place, CHUNK, samples)
        called = split_product(w, called_first, called_ref, place, CHUNK, samples)
        out_ref[:, here] = half_ref[:, here] + rows_of(coded, called)
    out_ref[:, rows:] = jnp.zeros((out_ref.shape[0], LANES), F32)
    out_ref[0:8, rows:] = sums_ref[...]


def chips_kernel(own_ref, other_ref, total_ref, *messages):
    rows = own_ref.shape[1] - LANES
    total = own_ref[...] + other_ref[...]
    total_ref[...] = total
    pieces = []
    for part in halves(total[32:34, :rows]):
        part = part.astype(F32)
        for which in range(2):
            for j in range(rows // LANES):
                pieces.append(part[which : which + 1, j * LANES : (j + 1) * LANES])
    pieces += [part.astype(F32) for part in thirds(total[0:1, rows:])]
    pieces.append(jnp.zeros((32 - len(pieces), LANES), F32))
    extra = jnp.concatenate(pieces, axis=0).astype(BF16)
    for message in messages:
        message[:, :rows] = total[0:32, :rows].astype(BF16)
        message[:, rows:] = extra


def dosage_kernel(order_ref, sol_ref, dir_ref, dose_ref, after_ref, cross_ref):
    rhs = sol_ref.shape[0]
    sol_high, sol_low = halves(sol_ref[...])
    dir_high, dir_low = halves(dir_ref[...])
    stack = jnp.concatenate([sol_high, dir_high, sol_low, dir_low], axis=0)
    own = stack.shape[1]
    hot = lax.broadcasted_iota(jnp.int32, (own, own), 0) == order_ref[...]
    hot = jnp.where(hot, 1.0, 0.0).astype(BF16)
    picked = jnp.dot(stack, hot, preferred_element_type=F32).astype(BF16)
    picked = jnp.concatenate([picked, jnp.ones((16, own), BF16)], axis=0)
    dose = dose_ref[...].astype(F32).astype(BF16)
    cross = jnp.dot(picked, dose, preferred_element_type=F32)
    cross_ref[: 2 * rhs] = cross[: 2 * rhs] + cross[2 * rhs : 4 * rhs]
    cross_ref[2 * rhs :] = cross[4 * rhs : 4 * rhs + 8]


def term(scaled_ref, coded_ref, called_first, called_ref, p, own, variants):
    part = pl.ds(pl.multiple_of(p * own, LANES), own)
    first = called_first.shape[0]
    got = jnp.dot(scaled_ref[0:16], coded_ref[:, part], preferred_element_type=F32)
    got = got + jnp.dot(scaled_ref[16:32, :first], called_first[:, part], preferred_element_type=F32)
    got = got + jnp.dot(scaled_ref[16:32, first:], called_ref[:, part], preferred_element_type=F32)
    return got / variants


def sums_block(sums):
    parts = [part.astype(F32) for part in thirds(sums)]
    return jnp.concatenate(parts + [jnp.zeros((13, LANES), F32)], axis=0).astype(BF16)


def back_kernel(variants, n_arrived, total_ref, coded_ref, called_first, called_ref, *rest):
    arrived = rest[:n_arrived]
    scaled_ref, sums_ref, *messages = rest[n_arrived:]
    var = lax.axis_index("var")
    rows = total_ref.shape[1] - LANES

    main = total_ref[0:32, :rows]
    allele, count = total_ref[32:33, :rows], total_ref[33:34, :rows]
    extra = jnp.zeros((32, LANES), F32)
    for ref in arrived:
        main = main + ref[:, :rows].astype(F32)
        extra = extra + ref[:, rows:].astype(F32)
    tiles = rows // LANES
    pick = lambda first: jnp.concatenate(
        [extra[first + j : first + j + 1] + extra[first + 2 * tiles + j : first + 2 * tiles + j + 1]
         for j in range(tiles)], axis=1
    )
    allele = allele + pick(0)
    count = count + pick(tiles)
    last = 4 * tiles
    sums = total_ref[0:1, rows:] + extra[last : last + 1] + extra[last + 1 : last + 2] + extra[last + 2 : last + 3]

    frequency = (allele + 1.0) / (2.0 * count + 2.0)
    spread = jnp.sqrt(2.0 * frequency * (1.0 - frequency))
    loading = (main[0:16] - 2.0 * frequency * main[16:32]) / spread
    scaled = loading / spread
    scaled_ref[0:16] = scaled.astype(BF16)
    scaled_ref[16:32] = (-2.0 * frequency * scaled).astype(BF16)
    square = as_row({6: jnp.sum(loading * loading, axis=1, keepdims=True)})
    sums = jnp.where(lane_of((1, LANES)) < 96, sums, square)

    sums_ref[...] = jnp.broadcast_to(sums, sums_ref.shape)

    for k, ref in enumerate(messages):
        own = ref.shape[1] - LANES
        ref[:, :own] = term(scaled_ref, coded_ref, called_first, called_ref, var ^ (k + 1), own, variants).astype(BF16)
        ref[:, own:] = sums_block(sums)


def own_kernel(variants, scaled_ref, sums_ref, coded_ref, called_first, called_ref, own_ref):
    own = own_ref.shape[1] - LANES
    p = lax.axis_index("var")
    own_ref[:, :own] = term(scaled_ref, coded_ref, called_first, called_ref, p, own, variants)
    own_ref[:, own:] = jnp.concatenate([sums_ref[0:1], jnp.zeros((15, LANES), F32)], axis=0)


def step_of(refs, noise_row, variants):
    got = refs[0][...]
    for ref in refs[1:]:
        got = got + ref[...].astype(F32)
    own = got.shape[1] - LANES
    back, last = got[:, :own], got[:, own:]
    sums = last[0:1] + last[1:2] + last[2:3]
    column = functools.partial(as_column, sums)
    noise = to_column(noise_row)
    curvature = noise * column(1) + column(6) / variants
    step = column(0) / (curvature + 1e-06)
    return back, column, noise, step


def norm_kernel(variants, width, noise_ref, dir_ref, res_ref, cross_ref, *rest):
    refs, (out_ref, new_ref) = rest[:-2], rest[-2:]
    back, _, noise, step = step_of(refs, noise_ref[...], variants)
    new = res_ref[...] - step * (noise * dir_ref[...] + back)
    new_ref[...] = new
    norm = as_row({6: jnp.sum(new * new, axis=1, keepdims=True)})
    cross = cross_ref[0:16] + step * cross_ref[16:32]
    dose = cross_ref[32:40]
    lane = lane_of((16, LANES))
    row = lax.broadcasted_iota(jnp.int32, (16, LANES), 0)
    turned = {}

    def turn(values, name, tile, by):
        if (name, tile, by) not in turned:
            piece = values[:, tile : tile + LANES]
            turned[name, tile, by] = pltpu.roll(piece, by, 1) if by else piece
        return turned[name, tile, by]

    for j in range(out_ref.shape[0]):
        tile, inside = (j * width) // LANES * LANES, (j * width) % LANES
        block = jnp.zeros((16, LANES), F32)
        for m in range(4):
            here = (row // 4 == m) & (lane >= 32 * m) & (lane < 32 * m + width)
            block = jnp.where(here, turn(cross, "cross", tile, (32 * m - inside) % LANES), block)
        block = block[0:8] + block[8:16]
        block = block[0:4] + block[4:8]
        last = jnp.where(lane[0:1] < width, turn(dose, "dose", tile, -inside % LANES)[0:1], norm)
        for k in range(4):
            out_ref[j, :, k * LANES : (k + 1) * LANES] = block[k : k + 1]
        out_ref[j, :, 4 * LANES :] = last


def new_kernel(variants, noise_ref, dir_ref, res_ref, sol_ref, *rest):
    refs, (sol_out, res_out, stats_out) = rest[:-3], rest[-3:]
    back, column, noise, step = step_of(refs, noise_ref[...], variants)
    dire = dir_ref[...]
    sol_out[...] = sol_ref[...] + step * dire
    res_out[...] = res_ref[...] - step * (noise * dire + back)
    sol_sum = column(2) + step * column(5)
    sol_square = column(3) + 2.0 * step * column(4) + step * (step * column(1))
    lane = lane_of(stats_out.shape)
    stats_out[...] = jnp.where(lane == 0, column(0), jnp.where(lane == 1, sol_sum, sol_square))


def last_kernel(samples, width, came_ref, stats_ref, res_ref, dir_ref, out_ref, score_out):
    total = jnp.sum(came_ref[...], axis=0)
    last = total[:, 4 * LANES :]
    out_ref[...] = res_ref[...] + (as_column(last, 6) / (stats_ref[:, 0:1] + 1e-06)) * dir_ref[...]
    row = lax.broadcasted_iota(jnp.int32, (16, LANES), 0)
    spread = jnp.zeros((16, LANES), F32)
    for k in range(4):
        spread = jnp.where(row % 4 == k, total[:, k * LANES : (k + 1) * LANES], spread)
    cross = spread
    for m in range(1, 4):
        cross = jnp.where(row // 4 == m, pltpu.roll(spread, LANES - 32 * m, 1), cross)
    dose = last
    sol_sum, sol_square = stats_ref[:, 1:2], stats_ref[:, 2:3]
    dose_freq = (dose / 100.0 + 1.0) / (2.0 * samples + 2.0)
    dose_spread = jnp.sqrt(2.0 * dose_freq * (1.0 - dose_freq))
    scale = math.sqrt(samples) * jnp.sqrt(sol_square / samples + 1e-06)
    scores = (cross / 100.0 - 2.0 * dose_freq * sol_sum) / (dose_spread * scale)
    score_out[...] = scores[:, :width]


def call(kernel, out, ins, args, scratch=(), limit=16, flops=0, moved=0):
    return pl.pallas_call(
        kernel,
        out_shape=[jax.ShapeDtypeStruct(*o) if len(o) == 2 else o[2](*o[:2]) for o in out],
        in_specs=list(ins),
        out_specs=[VMEM] * len(out),
        scratch_shapes=list(scratch),
        compiler_params=pltpu.CompilerParams(vmem_limit_bytes=limit * MIB),
        cost_estimate=pl.CostEstimate(flops=flops, bytes_accessed=moved, transcendentals=0),
    )(*[pltpu.with_memory_space_constraint(x, pltpu.HBM) if spec is HBM else x for spec, x in zip(ins, args)])


def body(genotypes, called, dosage, sample_order, noise_ratio, solution, residual, direction):
    n_var = lax.axis_size("var")
    n_samp = lax.axis_size("samp")
    own, rhs = direction.shape
    rows, shard = genotypes.shape
    variants = rows * n_var
    samples = own * n_samp * n_var
    imputed = dosage.shape[1]
    width = imputed // (n_var * n_samp)
    noise = noise_ratio[None]

    dire, res, sol = direction.T, residual.T, solution.T
    first, chunk = rows // 3 * 2, 128
    matrix = lambda n: ((n, shard), BF16, pltpu.VMEM)

    neighbour = swap(dire, "var", 1)
    called_a, sums = call(
        functools.partial(called_kernel, chunk),
        [matrix(first), ((8, LANES), F32)],
        [HBM] * 4,
        (sol, dire, res, called),
        scratch=[
            pltpu.VMEM((rhs, own), F32),
            pltpu.VMEM((rhs, own), F32),
            pltpu.VMEM((rhs, own), F32),
            pltpu.VMEM((first, shard), jnp.int32),
            pltpu.SemaphoreType.DMA((3,)),
            pltpu.SemaphoreType.DMA((first // chunk,)),
        ],
        limit=10,
        moved=4 * first * shard,
    )
    (pair,) = call(pair_kernel, [((2 * rhs, own), BF16)], [VMEM] * 2, (dire, neighbour), limit=4)
    pair_other = swap(pair, "var", 2)
    row_weights = pltpu.VMEM((2 * rhs, 2 * own), BF16)
    (done,) = call(
        called_product_kernel,
        [((2 * rhs, first), F32)],
        [VMEM] * 2,
        (pair, called_a),
        scratch=[row_weights],
        limit=4,
        flops=first * shard * 256,
        moved=first * shard,
    )
    coded, called_b, half = call(
        mask_kernel,
        [matrix(rows), matrix(rows - first), ((2 * rhs + 8, rows), F32)],
        [VMEM] * 4 + [HBM],
        (pair, called_a, done, genotypes, called),
        scratch=[
            pltpu.VMEM((rows - first, shard), jnp.int32),
            row_weights,
            pltpu.SemaphoreType.DMA(((rows - first) // LANES,)),
        ],
        limit=12,
        flops=2 * rows * shard * 256,
        moved=4 * rows * shard,
    )
    (part,) = call(
        forward_kernel,
        [((2 * rhs + 8, rows + LANES), F32)],
        [VMEM] * 6,
        (pair_other, coded, called_a, called_b, half, sums),
        scratch=[row_weights],
        flops=2 * rows * shard * 256,
        moved=2 * rows * shard,
    )
    part_other = swap(part, "samp", 1)

    n_chips = n_samp // 2
    total, *messages = call(
        chips_kernel,
        [(part.shape, F32)] + [((2 * rhs, rows + LANES), BF16)] * (n_chips - 1),
        [VMEM] * 2,
        (part, part_other),
        moved=1 * MIB,
    )
    arrived = [swap(messages[k], "samp", 2 * (k + 1) + 1) for k in reversed(range(n_chips - 1))]
    wide = own + LANES
    scaled, sums, *messages = call(
        functools.partial(back_kernel, variants, len(arrived)),
        [((2 * rhs, rows), BF16), ((8, LANES), F32)] + [((rhs, wide), BF16)] * (n_var - 1),
        [VMEM] * (4 + len(arrived)),
        (total, coded, called_a, called_b, *arrived),
        flops=2 * rows * shard * 256,
        moved=2 * rows * shard,
    )
    backs = [swap(messages[k], "var", k + 1) for k in reversed(range(n_var - 1))]
    (mine_back,) = call(
        functools.partial(own_kernel, variants),
        [((rhs, wide), F32)],
        [VMEM] * 5,
        (scaled, sums, coded, called_a, called_b),
        flops=rows * shard * 256,
        moved=rows * shard,
    )
    backs = [mine_back] + backs
    (cross,) = call(
        dosage_kernel,
        [((2 * rhs + 8, imputed), F32)],
        [VMEM] * 5,
        (sample_order, sol, dire, dosage, total),
        flops=2 * 80 * own * (own + imputed),
        moved=4 * own * imputed,
    )


    n_all = n_var * n_samp
    outgoing, res_keep = call(
        functools.partial(norm_kernel, variants, width),
        [((n_all, 1, 5 * LANES), F32), ((rhs, own), F32)],
        [VMEM] * (4 + n_var),
        (noise, dire, res, cross, *backs),
        moved=4 * 5 * n_all * LANES,
    )
    came = lax.all_to_all(outgoing, ("var", "samp"), split_axis=0, concat_axis=0)
    sol_new, res_new, stats = call(
        functools.partial(new_kernel, variants),
        [((rhs, own), F32), ((rhs, own), F32), ((rhs, LANES), F32)],
        [VMEM] * (4 + n_var),
        (noise, dire, res, sol, *backs),
        moved=1 * MIB,
    )
    dir_new, scores = call(
        functools.partial(last_kernel, samples, width),
        [((rhs, own), F32), ((rhs, width), F32)],
        [VMEM] * 4,
        (came, stats, res_keep, dire),
    )
    return (sol_new.T, res_new.T, dir_new.T, scores.T)


def solution(mesh):
    placed = (
        P("var", "samp"),
        P("var", "samp"),
        P(("samp", "var"), None),
        P(("samp", "var"), None),
        P(),
        P(("samp", "var"), None),
        P(("samp", "var"), None),
        P(("samp", "var"), None),
    )
    return jax.shard_map(
        body,
        mesh=mesh,
        in_specs=placed,
        out_specs=(
            P(("samp", "var"), None),
            P(("samp", "var"), None),
            P(("samp", "var"), None),
            P(("var", "samp"), None),
        ),
        check_vma=False,
    )
```

```python
import functools
import math

import jax
import jax.numpy as jnp
from jax import lax
from jax.experimental import pallas as pl
from jax.experimental.pallas import tpu as pltpu
from jax.sharding import PartitionSpec as P

BF16 = jnp.bfloat16
F32 = jnp.float32
LANES = 128
NT = (((1,), (1,)), ((), ()))
VMEM = pl.BlockSpec(memory_space=pltpu.VMEM)
HBM = pl.BlockSpec(memory_space=pltpu.HBM)
MIB = 1 << 20


def swap(values, axis, distance):
    size = lax.axis_size(axis)
    return lax.ppermute(values, axis, [(i, i ^ distance) for i in range(size)])


def halves(values):
    high = values.astype(BF16)
    return high, (values - high.astype(F32)).astype(BF16)


def thirds(values):
    high = values.astype(BF16)
    rest = values - high.astype(F32)
    middle = rest.astype(BF16)
    return high, middle, (rest - middle.astype(F32)).astype(BF16)


def lane_of(shape):
    return lax.broadcasted_iota(jnp.int32, shape, len(shape) - 1)


def spot(q):
    shape = (16, LANES)
    return lane_of(shape) == 16 * q + lax.broadcasted_iota(jnp.int32, shape, 0)


def as_row(values):
    block = jnp.zeros((16, LANES), F32)
    for q, column in values.items():
        block = jnp.where(spot(q), column, block)
    return jnp.sum(block, axis=0, keepdims=True)


def as_column(row, q):
    return jnp.sum(jnp.where(spot(q), row, 0.0), axis=1, keepdims=True)


def to_column(row):
    shape = (16, row.shape[1])
    same = lax.broadcasted_iota(jnp.int32, shape, 0) == lane_of(shape)
    return jnp.sum(jnp.where(same, row, 0.0), axis=1, keepdims=True)


BLOCK = 512
CHUNK = 256


def pieces(*ends):
    found = []
    at = 0
    for end in ends:
        while at < end:
            size = min(CHUNK, end - at)
            found.append((at, size))
            at += size
    return found


def blocks(rows, samples):
    return [
        (pl.ds(row, 16), pl.ds(sample, BLOCK)) for row in range(0, rows, 16) for sample in range(0, samples, BLOCK)
    ]


def row_copies(source, target, first, chunk, sems):
    return [
        pltpu.make_async_copy(source.at[pl.ds(first + i, chunk)], target.at[pl.ds(i, chunk)], sems.at[i // chunk])
        for i in range(0, target.shape[0], chunk)
    ]


def called_kernel(chunk, sol_hbm, dir_hbm, res_hbm, call_hbm, out_ref, sums_ref,
                  sol_ref, dir_ref, res_ref, cbuf, small_sems, sems):
    small = [
        pltpu.make_async_copy(source, target, small_sems.at[i])
        for i, (source, target) in enumerate(((sol_hbm, sol_ref), (dir_hbm, dir_ref), (res_hbm, res_ref)))
    ]
    for copy in small:
        copy.start()
    parts = row_copies(call_hbm, cbuf, 0, chunk, sems)
    for copy in parts:
        copy.start()
    for copy in small:
        copy.wait()
    sol, dire, res = sol_ref[...], dir_ref[...], res_ref[...]
    products = (res * res, dire * dire, sol, sol * sol, sol * dire, dire)
    row = as_row({q: jnp.sum(x, axis=1, keepdims=True) for q, x in enumerate(products)})
    sums_ref[...] = jnp.broadcast_to(row, sums_ref.shape)
    for i, copy in enumerate(parts):
        copy.wait()
        source, target = cbuf.at[pl.ds(i * chunk, chunk)], out_ref.at[pl.ds(i * chunk, chunk)]
        for here in blocks(chunk, source.shape[1]):
            target[here] = source[here].astype(F32).astype(BF16)


def pair_kernel(own_ref, other_ref, out_ref):
    upper = lax.axis_index("var") % 2
    rhs = own_ref.shape[0]
    own, other = own_ref[...], other_ref[...]
    out_ref[:rhs] = jnp.where(upper == 0, own, other).astype(BF16)
    out_ref[rhs:] = jnp.where(upper == 0, other, own).astype(BF16)


def weights(pair_ref, w):
    own = pair_ref.shape[1]
    row = lax.broadcasted_iota(jnp.int32, (16, 2 * own), 0)
    w[16:32] = jnp.where(row == 0, 1.0, 0.0).astype(BF16)
    for i in range(2):
        w[0:16, i * own : (i + 1) * own] = pair_ref[16 * i : 16 * i + 16]


def product(w, matrix, first, rows, samples):
    return lax.dot_general(w[...], matrix[pl.ds(first, rows), samples], NT, preferred_element_type=F32)


def split_product(w, head, tail, first, rows, samples):
    if first < head.shape[0]:
        return product(w, head, first, rows, samples)
    return product(w, tail, first - head.shape[0], rows, samples)


def rows_of(coded, called):
    counts = jnp.concatenate([coded[16:17], called[16:17], jnp.zeros((6, coded.shape[1]), F32)], axis=0)
    return jnp.concatenate([coded[0:16], called[0:16], counts], axis=0)


def pair_samples(pair, own):
    return pl.ds(pl.multiple_of(pair * 2 * own, LANES), 2 * own)


def called_product_kernel(pair_ref, called_first, out_ref, w):
    own = pair_ref.shape[1]
    samples = pair_samples(lax.axis_index("var") // 2, own)
    weights(pair_ref, w)
    for place, size in pieces(called_first.shape[0]):
        out_ref[:, place : place + size] = product(w, called_first, place, size, samples)


def mask_kernel(pair_ref, called_first, done_ref, gen_ref, call_hbm, coded_ref, called_ref, out_ref, cbuf, w, sems):
    own = pair_ref.shape[1]
    rows, shard = gen_ref.shape
    first = called_first.shape[0]
    copies = row_copies(call_hbm, cbuf, first, LANES, sems)
    for copy in copies:
        copy.start()
    samples = pair_samples(lax.axis_index("var") // 2, own)
    weights(pair_ref, w)

    def convert(place):
        here, after = pl.ds(place, LANES), place - first
        gen, coded = gen_ref.at[here], coded_ref.at[here]
        if after >= 0:
            copies[after // LANES].wait()
            call, called = cbuf.at[pl.ds(after, LANES)], called_ref.at[pl.ds(after, LANES)]
        else:
            mask_ref = called_first.at[here]

        def store(block, value, mask):
            coded[block] = value
            if after >= 0:
                called[block] = mask

        held = []
        for block in blocks(LANES, shard):
            mask = call[block].astype(F32).astype(BF16) if after >= 0 else mask_ref[block]
            held.append((block, gen[block].astype(F32).astype(BF16) * mask, mask))
            if len(held) > 4:
                store(*held.pop(0))
        for item in held:
            store(*item)

    before = None
    for place, size in pieces(first, rows) + [(rows, 0)]:
        if before:
            at, count = before
            coded = product(w, coded_ref, at, count, samples)
            if at < first:
                called = done_ref[:, at : at + count]
            else:
                called = product(w, called_ref, at - first, count, samples)
            out_ref[:, at : at + count] = rows_of(coded, called)
        for part in range(place, place + size, LANES):
            convert(part)
        before = (place, size)


def forward_kernel(pair_ref, coded_ref, called_first, called_ref, half_ref, sums_ref, out_ref, w):
    own = pair_ref.shape[1]
    rows = coded_ref.shape[0]
    samples = pair_samples((lax.axis_index("var") // 2) ^ 1, own)
    weights(pair_ref, w)
    for place, size in pieces(called_first.shape[0], rows):
        here = slice(place, place + size)
        coded = product(w, coded_ref, place, size, samples)
        called = split_product(w, called_first, called_ref, place, size, samples)
        out_ref[:, here] = half_ref[:, here] + rows_of(coded, called)
    out_ref[:, rows:] = jnp.zeros((out_ref.shape[0], LANES), F32)
    out_ref[0:8, rows:] = sums_ref[...]


def chips_kernel(own_ref, other_ref, total_ref, *messages):
    rows = own_ref.shape[1] - LANES
    total = own_ref[...] + other_ref[...]
    total_ref[...] = total
    pieces = []
    for part in halves(total[32:34, :rows]):
        part = part.astype(F32)
        for which in range(2):
            for j in range(rows // LANES):
                pieces.append(part[which : which + 1, j * LANES : (j + 1) * LANES])
    pieces += [part.astype(F32) for part in thirds(total[0:1, rows:])]
    pieces.append(jnp.zeros((32 - len(pieces), LANES), F32))
    extra = jnp.concatenate(pieces, axis=0).astype(BF16)
    for message in messages:
        message[:, :rows] = total[0:32, :rows].astype(BF16)
        message[:, rows:] = extra


def dosage_kernel(order_ref, sol_ref, dir_ref, dose_ref, after_ref, cross_ref):
    rhs = sol_ref.shape[0]
    sol_high, sol_low = halves(sol_ref[...])
    dir_high, dir_low = halves(dir_ref[...])
    stack = jnp.concatenate([sol_high, dir_high, sol_low, dir_low], axis=0)
    own = stack.shape[1]
    hot = lax.broadcasted_iota(jnp.int32, (own, own), 0) == order_ref[...]
    hot = jnp.where(hot, 1.0, 0.0).astype(BF16)
    picked = jnp.dot(stack, hot, preferred_element_type=F32).astype(BF16)
    picked = jnp.concatenate([picked, jnp.ones((16, own), BF16)], axis=0)
    dose = dose_ref[...].astype(F32).astype(BF16)
    cross = jnp.dot(picked, dose, preferred_element_type=F32)
    cross_ref[: 2 * rhs] = cross[: 2 * rhs] + cross[2 * rhs : 4 * rhs]
    cross_ref[2 * rhs :] = cross[4 * rhs : 4 * rhs + 8]


def term(scaled_ref, coded_ref, called_first, called_ref, p, own, variants):
    part = pl.ds(pl.multiple_of(p * own, LANES), own)
    first = called_first.shape[0]
    got = jnp.dot(scaled_ref[0:16], coded_ref[:, part], preferred_element_type=F32)
    got = got + jnp.dot(scaled_ref[16:32, :first], called_first[:, part], preferred_element_type=F32)
    got = got + jnp.dot(scaled_ref[16:32, first:], called_ref[:, part], preferred_element_type=F32)
    return got / variants


def sums_block(sums):
    parts = [part.astype(F32) for part in thirds(sums)]
    return jnp.concatenate(parts + [jnp.zeros((13, LANES), F32)], axis=0).astype(BF16)


def var_distances(n_var):
    far = list(reversed(range(1, n_var)))
    return list(zip(far, far[-1:] + far[:-1]))


def back_kernel(variants, n_arrived, total_ref, coded_ref, called_first, called_ref, *rest):
    arrived = rest[:n_arrived]
    scaled_ref, sums_ref, *messages = rest[n_arrived:]
    var = lax.axis_index("var")
    rows = total_ref.shape[1] - LANES

    main = total_ref[0:32, :rows]
    allele, count = total_ref[32:33, :rows], total_ref[33:34, :rows]
    extra = jnp.zeros((32, LANES), F32)
    for ref in arrived:
        main = main + ref[:, :rows].astype(F32)
        extra = extra + ref[:, rows:].astype(F32)
    tiles = rows // LANES
    pick = lambda first: jnp.concatenate(
        [extra[first + j : first + j + 1] + extra[first + 2 * tiles + j : first + 2 * tiles + j + 1]
         for j in range(tiles)], axis=1
    )
    allele = allele + pick(0)
    count = count + pick(tiles)
    last = 4 * tiles
    sums = total_ref[0:1, rows:] + extra[last : last + 1] + extra[last + 1 : last + 2] + extra[last + 2 : last + 3]

    frequency = (allele + 1.0) / (2.0 * count + 2.0)
    spread = jnp.sqrt(2.0 * frequency * (1.0 - frequency))
    loading = (main[0:16] - 2.0 * frequency * main[16:32]) / spread
    scaled = loading / spread
    scaled_ref[0:16] = scaled.astype(BF16)
    scaled_ref[16:32] = (-2.0 * frequency * scaled).astype(BF16)
    square = as_row({6: jnp.sum(loading * loading, axis=1, keepdims=True)})
    sums = jnp.where(lane_of((1, LANES)) < 96, sums, square)

    sums_ref[...] = jnp.broadcast_to(sums, sums_ref.shape)

    core = lax.axis_index("samp") % 2
    for (zero, one), ref in zip(var_distances(len(messages) + 1), messages):
        own = ref.shape[1] - LANES
        p = var ^ jnp.where(core == 0, zero, one)
        ref[:, :own] = term(scaled_ref, coded_ref, called_first, called_ref, p, own, variants).astype(BF16)
        ref[:, own:] = sums_block(sums)


def own_kernel(variants, scaled_ref, sums_ref, coded_ref, called_first, called_ref, own_ref):
    own = own_ref.shape[1] - LANES
    p = lax.axis_index("var")
    own_ref[:, :own] = term(scaled_ref, coded_ref, called_first, called_ref, p, own, variants)
    own_ref[:, own:] = jnp.concatenate([sums_ref[0:1], jnp.zeros((15, LANES), F32)], axis=0)


def step_of(refs, noise_row, variants):
    got = refs[0][...]
    for ref in refs[1:]:
        got = got + ref[...].astype(F32)
    own = got.shape[1] - LANES
    back, last = got[:, :own], got[:, own:]
    sums = last[0:1] + last[1:2] + last[2:3]
    column = functools.partial(as_column, sums)
    noise = to_column(noise_row)
    curvature = noise * column(1) + column(6) / variants
    step = column(0) / (curvature + 1e-06)
    return back, column, noise, step


def norm_kernel(variants, width, noise_ref, dir_ref, res_ref, cross_ref, *rest):
    refs, (out_ref, new_ref) = rest[:-2], rest[-2:]
    back, _, noise, step = step_of(refs, noise_ref[...], variants)
    new = res_ref[...] - step * (noise * dir_ref[...] + back)
    new_ref[...] = new
    norm = as_row({6: jnp.sum(new * new, axis=1, keepdims=True)})
    cross = cross_ref[0:16] + step * cross_ref[16:32]
    dose = cross_ref[32:40]
    lane = lane_of((16, LANES))
    row = lax.broadcasted_iota(jnp.int32, (16, LANES), 0)
    turned = {}

    def turn(values, name, tile, by):
        if (name, tile, by) not in turned:
            piece = values[:, tile : tile + LANES]
            turned[name, tile, by] = pltpu.roll(piece, by, 1) if by else piece
        return turned[name, tile, by]

    for j in range(out_ref.shape[0]):
        tile, inside = (j * width) // LANES * LANES, (j * width) % LANES
        block = jnp.zeros((16, LANES), F32)
        for m in range(4):
            here = (row // 4 == m) & (lane >= 32 * m) & (lane < 32 * m + width)
            block = jnp.where(here, turn(cross, "cross", tile, (32 * m - inside) % LANES), block)
        block = block[0:8] + block[8:16]
        block = block[0:4] + block[4:8]
        last = jnp.where(lane[0:1] < width, turn(dose, "dose", tile, -inside % LANES)[0:1], norm)
        for k in range(4):
            out_ref[j, :, k * LANES : (k + 1) * LANES] = block[k : k + 1]
        out_ref[j, :, 4 * LANES :] = last


def new_kernel(variants, noise_ref, dir_ref, res_ref, sol_ref, *rest):
    refs, (sol_out, res_out, stats_out) = rest[:-3], rest[-3:]
    back, column, noise, step = step_of(refs, noise_ref[...], variants)
    dire = dir_ref[...]
    sol_out[...] = sol_ref[...] + step * dire
    res_out[...] = res_ref[...] - step * (noise * dire + back)
    sol_sum = column(2) + step * column(5)
    sol_square = column(3) + 2.0 * step * column(4) + step * (step * column(1))
    lane = lane_of(stats_out.shape)
    stats_out[...] = jnp.where(lane == 0, column(0), jnp.where(lane == 1, sol_sum, sol_square))


def last_kernel(samples, width, came_ref, stats_ref, res_ref, dir_ref, out_ref, score_out):
    total = jnp.sum(came_ref[...], axis=0)
    last = total[:, 4 * LANES :]
    out_ref[...] = res_ref[...] + (as_column(last, 6) / (stats_ref[:, 0:1] + 1e-06)) * dir_ref[...]
    row = lax.broadcasted_iota(jnp.int32, (16, LANES), 0)
    spread = jnp.zeros((16, LANES), F32)
    for k in range(4):
        spread = jnp.where(row % 4 == k, total[:, k * LANES : (k + 1) * LANES], spread)
    cross = spread
    for m in range(1, 4):
        cross = jnp.where(row // 4 == m, pltpu.roll(spread, LANES - 32 * m, 1), cross)
    dose = last
    sol_sum, sol_square = stats_ref[:, 1:2], stats_ref[:, 2:3]
    dose_freq = (dose / 100.0 + 1.0) / (2.0 * samples + 2.0)
    dose_spread = jnp.sqrt(2.0 * dose_freq * (1.0 - dose_freq))
    scale = math.sqrt(samples) * jnp.sqrt(sol_square / samples + 1e-06)
    scores = (cross / 100.0 - 2.0 * dose_freq * sol_sum) / (dose_spread * scale)
    score_out[...] = scores[:, :width]


def call(kernel, out, ins, args, scratch=(), limit=16, flops=0, moved=0):
    return pl.pallas_call(
        kernel,
        out_shape=[jax.ShapeDtypeStruct(*o) if len(o) == 2 else o[2](*o[:2]) for o in out],
        in_specs=list(ins),
        out_specs=[VMEM] * len(out),
        scratch_shapes=list(scratch),
        compiler_params=pltpu.CompilerParams(vmem_limit_bytes=limit * MIB),
        cost_estimate=pl.CostEstimate(flops=flops, bytes_accessed=moved, transcendentals=0),
    )(*[pltpu.with_memory_space_constraint(x, pltpu.HBM) if spec is HBM else x for spec, x in zip(ins, args)])


def body(genotypes, called, dosage, sample_order, noise_ratio, solution, residual, direction):
    n_var = lax.axis_size("var")
    n_samp = lax.axis_size("samp")
    own, rhs = direction.shape
    rows, shard = genotypes.shape
    variants = rows * n_var
    samples = own * n_samp * n_var
    imputed = dosage.shape[1]
    width = imputed // (n_var * n_samp)
    noise = noise_ratio[None]

    dire, res, sol = direction.T, residual.T, solution.T
    first, chunk = rows // 2, 128
    matrix = lambda n: ((n, shard), BF16, pltpu.VMEM)

    neighbour = swap(dire, "var", 1)
    called_a, sums = call(
        functools.partial(called_kernel, chunk),
        [matrix(first), ((8, LANES), F32)],
        [HBM] * 4,
        (sol, dire, res, called),
        scratch=[
            pltpu.VMEM((rhs, own), F32),
            pltpu.VMEM((rhs, own), F32),
            pltpu.VMEM((rhs, own), F32),
            pltpu.VMEM((first, shard), jnp.int32),
            pltpu.SemaphoreType.DMA((3,)),
            pltpu.SemaphoreType.DMA((first // chunk,)),
        ],
        limit=10,
        moved=4 * first * shard,
    )
    (pair,) = call(pair_kernel, [((2 * rhs, own), BF16)], [VMEM] * 2, (dire, neighbour), limit=4)
    pair_other = swap(pair, "var", 2)
    row_weights = pltpu.VMEM((2 * rhs, 2 * own), BF16)
    (done,) = call(
        called_product_kernel,
        [((2 * rhs, first), F32)],
        [VMEM] * 2,
        (pair, called_a),
        scratch=[row_weights],
        limit=4,
        flops=first * shard * 256,
        moved=first * shard,
    )
    coded, called_b, half = call(
        mask_kernel,
        [matrix(rows), matrix(rows - first), ((2 * rhs + 8, rows), F32)],
        [VMEM] * 4 + [HBM],
        (pair, called_a, done, genotypes, called),
        scratch=[
            pltpu.VMEM((rows - first, shard), jnp.int32),
            row_weights,
            pltpu.SemaphoreType.DMA(((rows - first) // LANES,)),
        ],
        limit=12,
        flops=2 * rows * shard * 256,
        moved=4 * rows * shard,
    )
    (part,) = call(
        forward_kernel,
        [((2 * rhs + 8, rows + LANES), F32)],
        [VMEM] * 6,
        (pair_other, coded, called_a, called_b, half, sums),
        scratch=[row_weights],
        flops=2 * rows * shard * 256,
        moved=2 * rows * shard,
    )
    part_other = swap(part, "samp", 1)

    n_chips = n_samp // 2
    total, *messages = call(
        chips_kernel,
        [(part.shape, F32)] + [((2 * rhs, rows + LANES), BF16)] * (n_chips - 1),
        [VMEM] * 2,
        (part, part_other),
        moved=1 * MIB,
    )
    arrived = [swap(messages[k], "samp", 2 * (k + 1) + 1) for k in reversed(range(n_chips - 1))]
    wide = own + LANES
    scaled, sums, *messages = call(
        functools.partial(back_kernel, variants, len(arrived)),
        [((2 * rhs, rows), BF16), ((8, LANES), F32)] + [((rhs, wide), BF16)] * (n_var - 1),
        [VMEM] * (4 + len(arrived)),
        (total, coded, called_a, called_b, *arrived),
        flops=2 * rows * shard * 256,
        moved=2 * rows * shard,
    )
    backs = []
    for distances, m in zip(var_distances(n_var), messages):
        pairs = [(i, i ^ (distances[i % 2] * n_samp)) for i in range(n_var * n_samp)]
        backs.append(lax.ppermute(m, ("var", "samp"), pairs))
    (mine_back,) = call(
        functools.partial(own_kernel, variants),
        [((rhs, wide), F32)],
        [VMEM] * 5,
        (scaled, sums, coded, called_a, called_b),
        flops=rows * shard * 256,
        moved=rows * shard,
    )
    backs = [mine_back] + backs
    (cross,) = call(
        dosage_kernel,
        [((2 * rhs + 8, imputed), F32)],
        [VMEM] * 5,
        (sample_order, sol, dire, dosage, total),
        flops=2 * 80 * own * (own + imputed),
        moved=4 * own * imputed,
    )


    n_all = n_var * n_samp
    outgoing, res_keep = call(
        functools.partial(norm_kernel, variants, width),
        [((n_all, 1, 5 * LANES), F32), ((rhs, own), F32)],
        [VMEM] * (4 + n_var),
        (noise, dire, res, cross, *backs),
        moved=4 * 5 * n_all * LANES,
    )
    came = lax.all_to_all(outgoing, ("var", "samp"), split_axis=0, concat_axis=0)
    sol_new, res_new, stats = call(
        functools.partial(new_kernel, variants),
        [((rhs, own), F32), ((rhs, own), F32), ((rhs, LANES), F32)],
        [VMEM] * (4 + n_var),
        (noise, dire, res, sol, *backs),
        moved=1 * MIB,
    )
    dir_new, scores = call(
        functools.partial(last_kernel, samples, width),
        [((rhs, own), F32), ((rhs, width), F32)],
        [VMEM] * 4,
        (came, stats, res_keep, dire),
    )
    return (sol_new.T, res_new.T, dir_new.T, scores.T)


def solution(mesh):
    placed = (
        P("var", "samp"),
        P("var", "samp"),
        P(("samp", "var"), None),
        P(("samp", "var"), None),
        P(),
        P(("samp", "var"), None),
        P(("samp", "var"), None),
        P(("samp", "var"), None),
    )
    return jax.shard_map(
        body,
        mesh=mesh,
        in_specs=placed,
        out_specs=(
            P(("samp", "var"), None),
            P(("samp", "var"), None),
            P(("samp", "var"), None),
            P(("var", "samp"), None),
        ),
        check_vma=False,
    )
```

```python
import functools
import math

import jax
import jax.numpy as jnp
from jax import lax
from jax.experimental import pallas as pl
from jax.experimental.pallas import tpu as pltpu
from jax.sharding import PartitionSpec as P

BF16 = jnp.bfloat16
F32 = jnp.float32
LANES = 128
NT = (((1,), (1,)), ((), ()))
VMEM = pl.BlockSpec(memory_space=pltpu.VMEM)
HBM = pl.BlockSpec(memory_space=pltpu.HBM)
MIB = 1 << 20


def swap(values, axis, distance):
    size = lax.axis_size(axis)
    return lax.ppermute(values, axis, [(i, i ^ distance) for i in range(size)])


def halves(values):
    high = values.astype(BF16)
    return high, (values - high.astype(F32)).astype(BF16)


def thirds(values):
    high = values.astype(BF16)
    rest = values - high.astype(F32)
    middle = rest.astype(BF16)
    return high, middle, (rest - middle.astype(F32)).astype(BF16)


def lane_of(shape):
    return lax.broadcasted_iota(jnp.int32, shape, len(shape) - 1)


def spot(q):
    shape = (16, LANES)
    return lane_of(shape) == 16 * q + lax.broadcasted_iota(jnp.int32, shape, 0)


def as_row(values):
    block = jnp.zeros((16, LANES), F32)
    for q, column in values.items():
        block = jnp.where(spot(q), column, block)
    return jnp.sum(block, axis=0, keepdims=True)


def as_column(row, q):
    return jnp.sum(jnp.where(spot(q), row, 0.0), axis=1, keepdims=True)


def to_column(row):
    shape = (16, row.shape[1])
    same = lax.broadcasted_iota(jnp.int32, shape, 0) == lane_of(shape)
    return jnp.sum(jnp.where(same, row, 0.0), axis=1, keepdims=True)


BLOCK = 512
CHUNK = 256


def blocks(rows, samples):
    return [
        (pl.ds(row, 16), pl.ds(sample, BLOCK)) for row in range(0, rows, 16) for sample in range(0, samples, BLOCK)
    ]


def row_copies(source, target, first, chunk, sems):
    return [
        pltpu.make_async_copy(source.at[pl.ds(first + i, chunk)], target.at[pl.ds(i, chunk)], sems.at[i // chunk])
        for i in range(0, target.shape[0], chunk)
    ]


def called_kernel(chunk, sol_hbm, dir_hbm, res_hbm, call_hbm, out_ref, sums_ref,
                  sol_ref, dir_ref, res_ref, cbuf, small_sems, sems):
    small = [
        pltpu.make_async_copy(source, target, small_sems.at[i])
        for i, (source, target) in enumerate(((sol_hbm, sol_ref), (dir_hbm, dir_ref), (res_hbm, res_ref)))
    ]
    for copy in small:
        copy.start()
    parts = row_copies(call_hbm, cbuf, 0, chunk, sems)
    for copy in parts:
        copy.start()
    for copy in small:
        copy.wait()
    sol, dire, res = sol_ref[...], dir_ref[...], res_ref[...]
    products = (res * res, dire * dire, sol, sol * sol, sol * dire, dire)
    row = as_row({q: jnp.sum(x, axis=1, keepdims=True) for q, x in enumerate(products)})
    sums_ref[...] = jnp.broadcast_to(row, sums_ref.shape)
    for i, copy in enumerate(parts):
        copy.wait()
        source, target = cbuf.at[pl.ds(i * chunk, chunk)], out_ref.at[pl.ds(i * chunk, chunk)]
        for here in blocks(chunk, source.shape[1]):
            target[here] = source[here].astype(F32).astype(BF16)


def pair_kernel(own_ref, other_ref, out_ref):
    upper = lax.axis_index("var") % 2
    rhs = own_ref.shape[0]
    own, other = own_ref[...], other_ref[...]
    out_ref[:rhs] = jnp.where(upper == 0, own, other).astype(BF16)
    out_ref[rhs:] = jnp.where(upper == 0, other, own).astype(BF16)


def weights(pair_ref, w):
    own = pair_ref.shape[1]
    row = lax.broadcasted_iota(jnp.int32, (16, 2 * own), 0)
    w[16:32] = jnp.where(row == 0, 1.0, 0.0).astype(BF16)
    for i in range(2):
        w[0:16, i * own : (i + 1) * own] = pair_ref[16 * i : 16 * i + 16]


def product(w, matrix, first, rows, samples):
    return lax.dot_general(w[...], matrix[pl.ds(first, rows), samples], NT, preferred_element_type=F32)


def split_product(w, head, tail, first, rows, samples):
    if first < head.shape[0]:
        return product(w, head, first, rows, samples)
    return product(w, tail, first - head.shape[0], rows, samples)


def rows_of(coded, called):
    counts = jnp.concatenate([coded[16:17], called[16:17], jnp.zeros((6, coded.shape[1]), F32)], axis=0)
    return jnp.concatenate([coded[0:16], called[0:16], counts], axis=0)


def pair_samples(pair, own):
    return pl.ds(pl.multiple_of(pair * 2 * own, LANES), 2 * own)


def called_product_kernel(pair_ref, called_first, out_ref, w):
    own = pair_ref.shape[1]
    samples = pair_samples(lax.axis_index("var") // 2, own)
    weights(pair_ref, w)
    for place in range(0, called_first.shape[0], CHUNK):
        out_ref[:, place : place + CHUNK] = product(w, called_first, place, CHUNK, samples)


def mask_kernel(pair_ref, called_first, done_ref, gen_ref, call_hbm, coded_ref, called_ref, out_ref, cbuf, w, sems):
    own = pair_ref.shape[1]
    rows, shard = gen_ref.shape
    first = called_first.shape[0]
    copies = row_copies(call_hbm, cbuf, first, LANES, sems)
    for copy in copies:
        copy.start()
    samples = pair_samples(lax.axis_index("var") // 2, own)
    weights(pair_ref, w)

    def convert(place):
        here, after = pl.ds(place, LANES), place - first
        gen, coded = gen_ref.at[here], coded_ref.at[here]
        if after >= 0:
            copies[after // LANES].wait()
            call, called = cbuf.at[pl.ds(after, LANES)], called_ref.at[pl.ds(after, LANES)]
        else:
            mask_ref = called_first.at[here]

        def store(block, value, mask):
            coded[block] = value
            if after >= 0:
                called[block] = mask

        held = []
        for block in blocks(LANES, shard):
            mask = call[block].astype(F32).astype(BF16) if after >= 0 else mask_ref[block]
            held.append((block, gen[block].astype(F32).astype(BF16) * mask, mask))
            if len(held) > 4:
                store(*held.pop(0))
        for item in held:
            store(*item)

    for place in range(0, rows + CHUNK, CHUNK):
        if place:
            before = place - CHUNK
            coded = product(w, coded_ref, before, CHUNK, samples)
            if before < first:
                called = done_ref[:, before:place]
            else:
                called = product(w, called_ref, before - first, CHUNK, samples)
            out_ref[:, before:place] = rows_of(coded, called)
        for part in range(place, min(place + CHUNK, rows), LANES):
            convert(part)


def forward_kernel(pair_ref, coded_ref, called_first, called_ref, half_ref, sums_ref, out_ref, w):
    own = pair_ref.shape[1]
    rows = coded_ref.shape[0]
    samples = pair_samples((lax.axis_index("var") // 2) ^ 1, own)
    weights(pair_ref, w)
    for place in range(0, rows, CHUNK):
        here = slice(place, place + CHUNK)
        coded = product(w, coded_ref, place, CHUNK, samples)
        called = split_product(w, called_first, called_ref, place, CHUNK, samples)
        out_ref[:, here] = half_ref[:, here] + rows_of(coded, called)
    out_ref[:, rows:] = jnp.zeros((out_ref.shape[0], LANES), F32)
    out_ref[0:8, rows:] = sums_ref[...]


def chips_kernel(own_ref, other_ref, total_ref, *messages):
    rows = own_ref.shape[1] - LANES
    total = own_ref[...] + other_ref[...]
    total_ref[...] = total
    pieces = []
    for part in halves(total[32:34, :rows]):
        part = part.astype(F32)
        for which in range(2):
            for j in range(rows // LANES):
                pieces.append(part[which : which + 1, j * LANES : (j + 1) * LANES])
    pieces += [part.astype(F32) for part in thirds(total[0:1, rows:])]
    pieces.append(jnp.zeros((32 - len(pieces), LANES), F32))
    extra = jnp.concatenate(pieces, axis=0).astype(BF16)
    for message in messages:
        message[:, :rows] = total[0:32, :rows].astype(BF16)
        message[:, rows:] = extra


def dosage_kernel(order_ref, sol_ref, dir_ref, dose_ref, after_ref, cross_ref):
    rhs = sol_ref.shape[0]
    sol_high, sol_low = halves(sol_ref[...])
    dir_high, dir_low = halves(dir_ref[...])
    stack = jnp.concatenate([sol_high, dir_high, sol_low, dir_low], axis=0)
    own = stack.shape[1]
    hot = lax.broadcasted_iota(jnp.int32, (own, own), 0) == order_ref[...]
    hot = jnp.where(hot, 1.0, 0.0).astype(BF16)
    picked = jnp.dot(stack, hot, preferred_element_type=F32).astype(BF16)
    picked = jnp.concatenate([picked, jnp.ones((16, own), BF16)], axis=0)
    dose = dose_ref[...].astype(F32).astype(BF16)
    cross = jnp.dot(picked, dose, preferred_element_type=F32)
    cross_ref[: 2 * rhs] = cross[: 2 * rhs] + cross[2 * rhs : 4 * rhs]
    cross_ref[2 * rhs :] = cross[4 * rhs : 4 * rhs + 8]


def term(scaled_ref, coded_ref, called_first, called_ref, p, own, variants):
    part = pl.ds(pl.multiple_of(p * own, LANES), own)
    first = called_first.shape[0]
    got = jnp.dot(scaled_ref[0:16], coded_ref[:, part], preferred_element_type=F32)
    got = got + jnp.dot(scaled_ref[16:32, :first], called_first[:, part], preferred_element_type=F32)
    got = got + jnp.dot(scaled_ref[16:32, first:], called_ref[:, part], preferred_element_type=F32)
    return got / variants


def sums_block(sums):
    parts = [part.astype(F32) for part in thirds(sums)]
    return jnp.concatenate(parts + [jnp.zeros((13, LANES), F32)], axis=0).astype(BF16)


def back_kernel(variants, n_arrived, total_ref, coded_ref, called_first, called_ref, *rest):
    arrived = rest[:n_arrived]
    scaled_ref, sums_ref, *messages = rest[n_arrived:]
    var = lax.axis_index("var")
    rows = total_ref.shape[1] - LANES

    main = total_ref[0:32, :rows]
    allele, count = total_ref[32:33, :rows], total_ref[33:34, :rows]
    extra = jnp.zeros((32, LANES), F32)
    for ref in arrived:
        main = main + ref[:, :rows].astype(F32)
        extra = extra + ref[:, rows:].astype(F32)
    tiles = rows // LANES
    pick = lambda first: jnp.concatenate(
        [extra[first + j : first + j + 1] + extra[first + 2 * tiles + j : first + 2 * tiles + j + 1]
         for j in range(tiles)], axis=1
    )
    allele = allele + pick(0)
    count = count + pick(tiles)
    last = 4 * tiles
    sums = total_ref[0:1, rows:] + extra[last : last + 1] + extra[last + 1 : last + 2] + extra[last + 2 : last + 3]

    frequency = (allele + 1.0) / (2.0 * count + 2.0)
    spread = jnp.sqrt(2.0 * frequency * (1.0 - frequency))
    loading = (main[0:16] - 2.0 * frequency * main[16:32]) / spread
    scaled = loading / spread
    scaled_ref[0:16] = scaled.astype(BF16)
    scaled_ref[16:32] = (-2.0 * frequency * scaled).astype(BF16)
    square = as_row({6: jnp.sum(loading * loading, axis=1, keepdims=True)})
    sums = jnp.where(lane_of((1, LANES)) < 96, sums, square)

    sums_ref[...] = jnp.broadcast_to(sums, sums_ref.shape)

    for k, ref in enumerate(messages):
        own = ref.shape[1] - LANES
        ref[:, :own] = term(scaled_ref, coded_ref, called_first, called_ref, var ^ (k + 1), own, variants).astype(BF16)
        ref[:, own:] = sums_block(sums)


def own_kernel(variants, scaled_ref, sums_ref, coded_ref, called_first, called_ref,
               cross_ref, other_ref, own_ref, both_ref):
    both_ref[...] = cross_ref[...] + other_ref[...]
    own = own_ref.shape[1] - LANES
    p = lax.axis_index("var")
    own_ref[:, :own] = term(scaled_ref, coded_ref, called_first, called_ref, p, own, variants)
    own_ref[:, own:] = jnp.concatenate([sums_ref[0:1], jnp.zeros((15, LANES), F32)], axis=0)


def step_of(refs, noise_row, variants):
    got = refs[0][...]
    for ref in refs[1:]:
        got = got + ref[...].astype(F32)
    own = got.shape[1] - LANES
    back, last = got[:, :own], got[:, own:]
    sums = last[0:1] + last[1:2] + last[2:3]
    column = functools.partial(as_column, sums)
    noise = to_column(noise_row)
    curvature = noise * column(1) + column(6) / variants
    step = column(0) / (curvature + 1e-06)
    return back, column, noise, step


def norm_kernel(variants, width, noise_ref, dir_ref, res_ref, both_ref, *rest):
    refs, (out_ref, new_ref) = rest[:-2], rest[-2:]
    back, _, noise, step = step_of(refs, noise_ref[...], variants)
    new = res_ref[...] - step * (noise * dir_ref[...] + back)
    new_ref[...] = new
    norm = as_row({6: jnp.sum(new * new, axis=1, keepdims=True)})
    both = both_ref[...]
    core = lax.axis_index("samp") % 2
    half = lambda x: jnp.where(core == 0, x[0:8], x[8:16])
    cross = half(both[0:16]) + half(step) * half(both[16:32])
    dose = both[32:40]
    lane = lane_of((8, LANES))
    row = lax.broadcasted_iota(jnp.int32, (8, LANES), 0)
    turned = {}

    def turn(values, name, tile, by):
        if (name, tile, by) not in turned:
            piece = values[:, tile : tile + LANES]
            turned[name, tile, by] = pltpu.roll(piece, by, 1) if by else piece
        return turned[name, tile, by]

    for j in range(out_ref.shape[0]):
        tile, inside = (j * width) // LANES * LANES, (j * width) % LANES
        block = jnp.zeros((8, LANES), F32)
        for m in range(4):
            here = (row // 2 == m) & (lane >= 32 * m) & (lane < 32 * m + width)
            block = jnp.where(here, turn(cross, "cross", tile, (32 * m - inside) % LANES), block)
        block = block[0:4] + block[4:8]
        block = block[0:2] + block[2:4]
        last = jnp.where(lane[0:1] < width, turn(dose, "dose", tile, -inside % LANES)[0:1], norm)
        for k in range(2):
            out_ref[j, :, k * LANES : (k + 1) * LANES] = block[k : k + 1]
        out_ref[j, :, 2 * LANES :] = last


def new_kernel(variants, noise_ref, dir_ref, res_ref, sol_ref, *rest):
    refs, (sol_out, res_out, stats_out) = rest[:-3], rest[-3:]
    back, column, noise, step = step_of(refs, noise_ref[...], variants)
    dire = dir_ref[...]
    sol_out[...] = sol_ref[...] + step * dire
    res_out[...] = res_ref[...] - step * (noise * dire + back)
    sol_sum = column(2) + step * column(5)
    sol_square = column(3) + 2.0 * step * column(4) + step * (step * column(1))
    lane = lane_of(stats_out.shape)
    stats_out[...] = jnp.where(lane == 0, column(0), jnp.where(lane == 1, sol_sum, sol_square))


def last_kernel(samples, width, came_ref, stats_ref, res_ref, dir_ref, out_ref, score_out):
    row = lax.broadcasted_iota(jnp.int32, (8, LANES), 0)
    halves_of, lasts = [], []
    for core in range(2):
        total = came_ref[core]
        for i in range(core + 2, came_ref.shape[0], 2):
            total = total + came_ref[i]
        spread = jnp.where(row % 2 == 0, total[:, :LANES], total[:, LANES : 2 * LANES])
        part = spread
        for m in range(1, 4):
            part = jnp.where(row // 2 == m, pltpu.roll(spread, LANES - 32 * m, 1), part)
        halves_of.append(part)
        lasts.append(total[:, 2 * LANES :])
    new_norm = as_column(lasts[0] + lasts[1], 6)
    out_ref[...] = res_ref[...] + (new_norm / (stats_ref[:, 0:1] + 1e-06)) * dir_ref[...]
    cross = jnp.concatenate(halves_of, axis=0)
    dose = lasts[0]
    sol_sum, sol_square = stats_ref[:, 1:2], stats_ref[:, 2:3]
    dose_freq = (dose / 100.0 + 1.0) / (2.0 * samples + 2.0)
    dose_spread = jnp.sqrt(2.0 * dose_freq * (1.0 - dose_freq))
    scale = math.sqrt(samples) * jnp.sqrt(sol_square / samples + 1e-06)
    scores = (cross / 100.0 - 2.0 * dose_freq * sol_sum) / (dose_spread * scale)
    score_out[...] = scores[:, :width]


def call(kernel, out, ins, args, scratch=(), limit=16, flops=0, moved=0):
    return pl.pallas_call(
        kernel,
        out_shape=[jax.ShapeDtypeStruct(*o) if len(o) == 2 else o[2](*o[:2]) for o in out],
        in_specs=list(ins),
        out_specs=[VMEM] * len(out),
        scratch_shapes=list(scratch),
        compiler_params=pltpu.CompilerParams(vmem_limit_bytes=limit * MIB),
        cost_estimate=pl.CostEstimate(flops=flops, bytes_accessed=moved, transcendentals=0),
    )(*[pltpu.with_memory_space_constraint(x, pltpu.HBM) if spec is HBM else x for spec, x in zip(ins, args)])


def body(genotypes, called, dosage, sample_order, noise_ratio, solution, residual, direction):
    n_var = lax.axis_size("var")
    n_samp = lax.axis_size("samp")
    own, rhs = direction.shape
    rows, shard = genotypes.shape
    variants = rows * n_var
    samples = own * n_samp * n_var
    imputed = dosage.shape[1]
    width = imputed // (n_var * n_samp)
    noise = noise_ratio[None]

    dire, res, sol = direction.T, residual.T, solution.T
    first, chunk = rows // 3 * 2, 128
    matrix = lambda n: ((n, shard), BF16, pltpu.VMEM)

    neighbour = swap(dire, "var", 1)
    called_a, sums = call(
        functools.partial(called_kernel, chunk),
        [matrix(first), ((8, LANES), F32)],
        [HBM] * 4,
        (sol, dire, res, called),
        scratch=[
            pltpu.VMEM((rhs, own), F32),
            pltpu.VMEM((rhs, own), F32),
            pltpu.VMEM((rhs, own), F32),
            pltpu.VMEM((first, shard), jnp.int32),
            pltpu.SemaphoreType.DMA((3,)),
            pltpu.SemaphoreType.DMA((first // chunk,)),
        ],
        limit=10,
        moved=4 * first * shard,
    )
    (pair,) = call(pair_kernel, [((2 * rhs, own), BF16)], [VMEM] * 2, (dire, neighbour), limit=4)
    pair_other = swap(pair, "var", 2)
    row_weights = pltpu.VMEM((2 * rhs, 2 * own), BF16)
    (done,) = call(
        called_product_kernel,
        [((2 * rhs, first), F32)],
        [VMEM] * 2,
        (pair, called_a),
        scratch=[row_weights],
        limit=4,
        flops=first * shard * 256,
        moved=first * shard,
    )
    coded, called_b, half = call(
        mask_kernel,
        [matrix(rows), matrix(rows - first), ((2 * rhs + 8, rows), F32)],
        [VMEM] * 4 + [HBM],
        (pair, called_a, done, genotypes, called),
        scratch=[
            pltpu.VMEM((rows - first, shard), jnp.int32),
            row_weights,
            pltpu.SemaphoreType.DMA(((rows - first) // LANES,)),
        ],
        limit=12,
        flops=2 * rows * shard * 256,
        moved=4 * rows * shard,
    )
    (part,) = call(
        forward_kernel,
        [((2 * rhs + 8, rows + LANES), F32)],
        [VMEM] * 6,
        (pair_other, coded, called_a, called_b, half, sums),
        scratch=[row_weights],
        flops=2 * rows * shard * 256,
        moved=2 * rows * shard,
    )
    part_other = swap(part, "samp", 1)

    n_chips = n_samp // 2
    total, *messages = call(
        chips_kernel,
        [(part.shape, F32)] + [((2 * rhs, rows + LANES), BF16)] * (n_chips - 1),
        [VMEM] * 2,
        (part, part_other),
        moved=1 * MIB,
    )
    arrived = [swap(messages[k], "samp", 2 * (k + 1) + 1) for k in reversed(range(n_chips - 1))]
    (cross,) = call(
        dosage_kernel,
        [((2 * rhs + 8, imputed), F32)],
        [VMEM] * 5,
        (sample_order, sol, dire, dosage, total),
        flops=2 * 80 * own * (own + imputed),
        moved=4 * own * imputed,
    )
    cross_other = swap(cross, "samp", 1)

    wide = own + LANES
    scaled, sums, *messages = call(
        functools.partial(back_kernel, variants, len(arrived)),
        [((2 * rhs, rows), BF16), ((8, LANES), F32)] + [((rhs, wide), BF16)] * (n_var - 1),
        [VMEM] * (4 + len(arrived)),
        (total, coded, called_a, called_b, *arrived),
        flops=2 * rows * shard * 256,
        moved=2 * rows * shard,
    )
    backs = [swap(messages[k], "var", k + 1) for k in reversed(range(n_var - 1))]
    mine_back, both = call(
        functools.partial(own_kernel, variants),
        [((rhs, wide), F32), (cross.shape, F32)],
        [VMEM] * 7,
        (scaled, sums, coded, called_a, called_b, cross, cross_other),
        flops=rows * shard * 256,
        moved=rows * shard,
    )
    backs = [mine_back] + backs


    n_all = n_var * n_samp
    outgoing, res_keep = call(
        functools.partial(norm_kernel, variants, width),
        [((n_all, 1, 3 * LANES), F32), ((rhs, own), F32)],
        [VMEM] * (4 + n_var),
        (noise, dire, res, both, *backs),
        moved=4 * 3 * n_all * LANES,
    )
    came = lax.all_to_all(outgoing, ("var", "samp"), split_axis=0, concat_axis=0)
    sol_new, res_new, stats = call(
        functools.partial(new_kernel, variants),
        [((rhs, own), F32), ((rhs, own), F32), ((rhs, LANES), F32)],
        [VMEM] * (4 + n_var),
        (noise, dire, res, sol, *backs),
        moved=1 * MIB,
    )
    dir_new, scores = call(
        functools.partial(last_kernel, samples, width),
        [((rhs, own), F32), ((rhs, width), F32)],
        [VMEM] * 4,
        (came, stats, res_keep, dire),
    )
    return (sol_new.T, res_new.T, dir_new.T, scores.T)


def solution(mesh):
    placed = (
        P("var", "samp"),
        P("var", "samp"),
        P(("samp", "var"), None),
        P(("samp", "var"), None),
        P(),
        P(("samp", "var"), None),
        P(("samp", "var"), None),
        P(("samp", "var"), None),
    )
    return jax.shard_map(
        body,
        mesh=mesh,
        in_specs=placed,
        out_specs=(
            P(("samp", "var"), None),
            P(("samp", "var"), None),
            P(("samp", "var"), None),
            P(("var", "samp"), None),
        ),
        check_vma=False,
    )
```

```python
import functools
import math

import jax
import jax.numpy as jnp
from jax import lax
from jax.experimental import pallas as pl
from jax.experimental.pallas import tpu as pltpu
from jax.sharding import PartitionSpec as P

BF16 = jnp.bfloat16
F32 = jnp.float32
LANES = 128
NT = (((1,), (1,)), ((), ()))
VMEM = pl.BlockSpec(memory_space=pltpu.VMEM)
HBM = pl.BlockSpec(memory_space=pltpu.HBM)
MIB = 1 << 20


def swap(values, axis, distance):
    size = lax.axis_size(axis)
    return lax.ppermute(values, axis, [(i, i ^ distance) for i in range(size)])


def halves(values):
    high = values.astype(BF16)
    return high, (values - high.astype(F32)).astype(BF16)


def thirds(values):
    high = values.astype(BF16)
    rest = values - high.astype(F32)
    middle = rest.astype(BF16)
    return high, middle, (rest - middle.astype(F32)).astype(BF16)


def lane_of(shape):
    return lax.broadcasted_iota(jnp.int32, shape, len(shape) - 1)


def spot(q):
    shape = (16, LANES)
    return lane_of(shape) == 16 * q + lax.broadcasted_iota(jnp.int32, shape, 0)


def as_row(values):
    block = jnp.zeros((16, LANES), F32)
    for q, column in values.items():
        block = jnp.where(spot(q), column, block)
    return jnp.sum(block, axis=0, keepdims=True)


def as_column(row, q):
    return jnp.sum(jnp.where(spot(q), row, 0.0), axis=1, keepdims=True)


def to_column(row):
    shape = (16, row.shape[1])
    same = lax.broadcasted_iota(jnp.int32, shape, 0) == lane_of(shape)
    return jnp.sum(jnp.where(same, row, 0.0), axis=1, keepdims=True)


BLOCK = 512
CHUNK = 256


def blocks(rows, samples):
    return [
        (pl.ds(row, 16), pl.ds(sample, BLOCK)) for row in range(0, rows, 16) for sample in range(0, samples, BLOCK)
    ]


def row_copies(source, target, first, chunk, sems):
    return [
        pltpu.make_async_copy(source.at[pl.ds(first + i, chunk)], target.at[pl.ds(i, chunk)], sems.at[i // chunk])
        for i in range(0, target.shape[0], chunk)
    ]


def called_kernel(chunk, sol_hbm, dir_hbm, res_hbm, call_hbm, out_ref, sums_ref,
                  sol_ref, dir_ref, res_ref, cbuf, small_sems, sems):
    small = [
        pltpu.make_async_copy(source, target, small_sems.at[i])
        for i, (source, target) in enumerate(((sol_hbm, sol_ref), (dir_hbm, dir_ref), (res_hbm, res_ref)))
    ]
    for copy in small:
        copy.start()
    parts = row_copies(call_hbm, cbuf, 0, chunk, sems)
    for copy in parts:
        copy.start()
    for copy in small:
        copy.wait()
    sol, dire, res = sol_ref[...], dir_ref[...], res_ref[...]
    products = (res * res, dire * dire, sol, sol * sol, sol * dire, dire)
    row = as_row({q: jnp.sum(x, axis=1, keepdims=True) for q, x in enumerate(products)})
    sums_ref[...] = jnp.broadcast_to(row, sums_ref.shape)
    for i, copy in enumerate(parts):
        copy.wait()
        source, target = cbuf.at[pl.ds(i * chunk, chunk)], out_ref.at[pl.ds(i * chunk, chunk)]
        for here in blocks(chunk, source.shape[1]):
            target[here] = source[here].astype(F32).astype(BF16)


def pair_kernel(own_ref, other_ref, out_ref):
    upper = lax.axis_index("var") % 2
    rhs = own_ref.shape[0]
    own, other = own_ref[...], other_ref[...]
    out_ref[:rhs] = jnp.where(upper == 0, own, other).astype(BF16)
    out_ref[rhs:] = jnp.where(upper == 0, other, own).astype(BF16)


def weights(pair_ref, w):
    own = pair_ref.shape[1]
    row = lax.broadcasted_iota(jnp.int32, (16, 2 * own), 0)
    w[16:32] = jnp.where(row == 0, 1.0, 0.0).astype(BF16)
    for i in range(2):
        w[0:16, i * own : (i + 1) * own] = pair_ref[16 * i : 16 * i + 16]


def product(w, matrix, first, rows, samples):
    return lax.dot_general(w[...], matrix[pl.ds(first, rows), samples], NT, preferred_element_type=F32)


def split_product(w, head, tail, first, rows, samples):
    if first < head.shape[0]:
        return product(w, head, first, rows, samples)
    return product(w, tail, first - head.shape[0], rows, samples)


def rows_of(coded, called):
    counts = jnp.concatenate([coded[16:17], called[16:17], jnp.zeros((6, coded.shape[1]), F32)], axis=0)
    return jnp.concatenate([coded[0:16], called[0:16], counts], axis=0)


def pair_samples(pair, own):
    return pl.ds(pl.multiple_of(pair * 2 * own, LANES), 2 * own)


def called_product_kernel(pair_ref, called_first, out_ref, w):
    own = pair_ref.shape[1]
    samples = pair_samples(lax.axis_index("var") // 2, own)
    weights(pair_ref, w)
    for place in range(0, called_first.shape[0], CHUNK):
        out_ref[:, place : place + CHUNK] = product(w, called_first, place, CHUNK, samples)


def mask_kernel(pair_ref, called_first, done_ref, gen_ref, call_hbm, coded_ref, called_ref, out_ref, cbuf, w, sems):
    own = pair_ref.shape[1]
    rows, shard = gen_ref.shape
    first = called_first.shape[0]
    copies = row_copies(call_hbm, cbuf, first, LANES, sems)
    for copy in copies:
        copy.start()
    samples = pair_samples(lax.axis_index("var") // 2, own)
    weights(pair_ref, w)

    def convert(place):
        here, after = pl.ds(place, LANES), place - first
        gen, coded = gen_ref.at[here], coded_ref.at[here]
        if after >= 0:
            copies[after // LANES].wait()
            call, called = cbuf.at[pl.ds(after, LANES)], called_ref.at[pl.ds(after, LANES)]
        else:
            mask_ref = called_first.at[here]

        def store(block, value, mask):
            coded[block] = value
            if after >= 0:
                called[block] = mask

        held = []
        for block in blocks(LANES, shard):
            mask = call[block].astype(F32).astype(BF16) if after >= 0 else mask_ref[block]
            held.append((block, gen[block].astype(F32).astype(BF16) * mask, mask))
            if len(held) > 4:
                store(*held.pop(0))
        for item in held:
            store(*item)

    for place in range(0, rows + CHUNK, CHUNK):
        if place:
            before = place - CHUNK
            coded = product(w, coded_ref, before, CHUNK, samples)
            if before < first:
                called = done_ref[:, before:place]
            else:
                called = product(w, called_ref, before - first, CHUNK, samples)
            out_ref[:, before:place] = rows_of(coded, called)
        for part in range(place, min(place + CHUNK, rows), LANES):
            convert(part)


def forward_kernel(pair_ref, coded_ref, called_first, called_ref, half_ref, sums_ref, out_ref, w):
    own = pair_ref.shape[1]
    rows = coded_ref.shape[0]
    samples = pair_samples((lax.axis_index("var") // 2) ^ 1, own)
    weights(pair_ref, w)
    for place in range(0, rows, CHUNK):
        here = slice(place, place + CHUNK)
        coded = product(w, coded_ref, place, CHUNK, samples)
        called = split_product(w, called_first, called_ref, place, CHUNK, samples)
        out_ref[:, here] = half_ref[:, here] + rows_of(coded, called)
    out_ref[:, rows:] = jnp.zeros((out_ref.shape[0], LANES), F32)
    out_ref[0:8, rows:] = sums_ref[...]


def chips_kernel(own_ref, other_ref, total_ref, *messages):
    rows = own_ref.shape[1] - LANES
    total = own_ref[...] + other_ref[...]
    total_ref[...] = total
    pieces = []
    for part in halves(total[32:34, :rows]):
        part = part.astype(F32)
        for which in range(2):
            for j in range(rows // LANES):
                pieces.append(part[which : which + 1, j * LANES : (j + 1) * LANES])
    pieces += [part.astype(F32) for part in thirds(total[0:1, rows:])]
    pieces.append(jnp.zeros((32 - len(pieces), LANES), F32))
    extra = jnp.concatenate(pieces, axis=0).astype(BF16)
    for message in messages:
        message[:, :rows] = total[0:32, :rows].astype(BF16)
        message[:, rows:] = extra


def dosage_kernel(order_ref, sol_ref, dir_ref, dose_ref, after_ref, cross_ref):
    rhs = sol_ref.shape[0]
    sol_high, sol_low = halves(sol_ref[...])
    dir_high, dir_low = halves(dir_ref[...])
    stack = jnp.concatenate([sol_high, dir_high, sol_low, dir_low], axis=0)
    own = stack.shape[1]
    hot = lax.broadcasted_iota(jnp.int32, (own, own), 0) == order_ref[...]
    hot = jnp.where(hot, 1.0, 0.0).astype(BF16)
    picked = jnp.dot(stack, hot, preferred_element_type=F32).astype(BF16)
    picked = jnp.concatenate([picked, jnp.ones((16, own), BF16)], axis=0)
    dose = dose_ref[...].astype(F32).astype(BF16)
    cross = jnp.dot(picked, dose, preferred_element_type=F32)
    cross_ref[: 2 * rhs] = cross[: 2 * rhs] + cross[2 * rhs : 4 * rhs]
    cross_ref[2 * rhs :] = cross[4 * rhs : 4 * rhs + 8]


def term(scaled_ref, coded_ref, called_first, called_ref, p, own, variants):
    part = pl.ds(pl.multiple_of(p * own, LANES), own)
    first = called_first.shape[0]
    got = jnp.dot(scaled_ref[0:16], coded_ref[:, part], preferred_element_type=F32)
    got = got + jnp.dot(scaled_ref[16:32, :first], called_first[:, part], preferred_element_type=F32)
    got = got + jnp.dot(scaled_ref[16:32, first:], called_ref[:, part], preferred_element_type=F32)
    return got / variants


def sums_block(sums):
    parts = [part.astype(F32) for part in thirds(sums)]
    return jnp.concatenate(parts + [jnp.zeros((13, LANES), F32)], axis=0).astype(BF16)


def back_kernel(variants, n_arrived, total_ref, coded_ref, called_first, called_ref, *rest):
    arrived = rest[:n_arrived]
    scaled_ref, sums_ref, *messages = rest[n_arrived:]
    var = lax.axis_index("var")
    rows = total_ref.shape[1] - LANES

    main = total_ref[0:32, :rows]
    allele, count = total_ref[32:33, :rows], total_ref[33:34, :rows]
    extra = jnp.zeros((32, LANES), F32)
    for ref in arrived:
        main = main + ref[:, :rows].astype(F32)
        extra = extra + ref[:, rows:].astype(F32)
    tiles = rows // LANES
    pick = lambda first: jnp.concatenate(
        [extra[first + j : first + j + 1] + extra[first + 2 * tiles + j : first + 2 * tiles + j + 1]
         for j in range(tiles)], axis=1
    )
    allele = allele + pick(0)
    count = count + pick(tiles)
    last = 4 * tiles
    sums = total_ref[0:1, rows:] + extra[last : last + 1] + extra[last + 1 : last + 2] + extra[last + 2 : last + 3]

    frequency = (allele + 1.0) / (2.0 * count + 2.0)
    spread = jnp.sqrt(2.0 * frequency * (1.0 - frequency))
    loading = (main[0:16] - 2.0 * frequency * main[16:32]) / spread
    scaled = loading / spread
    scaled_ref[0:16] = scaled.astype(BF16)
    scaled_ref[16:32] = (-2.0 * frequency * scaled).astype(BF16)
    square = as_row({6: jnp.sum(loading * loading, axis=1, keepdims=True)})
    sums = jnp.where(lane_of((1, LANES)) < 96, sums, square)

    sums_ref[...] = jnp.broadcast_to(sums, sums_ref.shape)

    for k, ref in enumerate(messages):
        own = ref.shape[1] - LANES
        ref[:, :own] = term(scaled_ref, coded_ref, called_first, called_ref, var ^ (k + 1), own, variants).astype(BF16)
        ref[:, own:] = sums_block(sums)


def own_kernel(variants, scaled_ref, sums_ref, coded_ref, called_first, called_ref,
               cross_ref, other_ref, own_ref, both_ref):
    both_ref[...] = cross_ref[...] + other_ref[...]
    own = own_ref.shape[1] - LANES
    p = lax.axis_index("var")
    own_ref[:, :own] = term(scaled_ref, coded_ref, called_first, called_ref, p, own, variants)
    own_ref[:, own:] = jnp.concatenate([sums_ref[0:1], jnp.zeros((15, LANES), F32)], axis=0)


def step_of(refs, noise_row, variants):
    got = refs[0][...]
    for ref in refs[1:]:
        got = got + ref[...].astype(F32)
    own = got.shape[1] - LANES
    back, last = got[:, :own], got[:, own:]
    sums = last[0:1] + last[1:2] + last[2:3]
    column = functools.partial(as_column, sums)
    noise = to_column(noise_row)
    curvature = noise * column(1) + column(6) / variants
    step = column(0) / (curvature + 1e-06)
    return back, column, noise, step


def norm_kernel(variants, width, noise_ref, dir_ref, res_ref, both_ref, *rest):
    refs, (out_ref, new_ref) = rest[:-2], rest[-2:]
    back, _, noise, step = step_of(refs, noise_ref[...], variants)
    new = res_ref[...] - step * (noise * dir_ref[...] + back)
    new_ref[...] = new
    norm = as_row({6: jnp.sum(new * new, axis=1, keepdims=True)})
    both = both_ref[...]
    core = lax.axis_index("samp") % 2
    half = lambda x: jnp.where(core == 0, x[0:8], x[8:16])
    cross = half(both[0:16]) + half(step) * half(both[16:32])
    dose = both[32:40]
    lane = lane_of((8, LANES))
    row = lax.broadcasted_iota(jnp.int32, (8, LANES), 0)
    turned = {}

    def turn(values, name, tile, by):
        if (name, tile, by) not in turned:
            piece = values[:, tile : tile + LANES]
            turned[name, tile, by] = pltpu.roll(piece, by, 1) if by else piece
        return turned[name, tile, by]

    for j in range(out_ref.shape[0]):
        tile, inside = (j * width) // LANES * LANES, (j * width) % LANES
        block = jnp.zeros((8, LANES), F32)
        for m in range(4):
            here = (row // 2 == m) & (lane >= 32 * m) & (lane < 32 * m + width)
            block = jnp.where(here, turn(cross, "cross", tile, (32 * m - inside) % LANES), block)
        block = block[0:4] + block[4:8]
        block = block[0:2] + block[2:4]
        last = jnp.where(lane[0:1] < width, turn(dose, "dose", tile, -inside % LANES)[0:1], norm)
        for k in range(2):
            out_ref[j, :, k * LANES : (k + 1) * LANES] = block[k : k + 1]
        out_ref[j, :, 2 * LANES :] = last


def new_kernel(variants, noise_ref, dir_ref, res_ref, sol_ref, *rest):
    refs, (sol_out, res_out, stats_out) = rest[:-3], rest[-3:]
    back, column, noise, step = step_of(refs, noise_ref[...], variants)
    dire = dir_ref[...]
    sol_out[...] = sol_ref[...] + step * dire
    res_out[...] = res_ref[...] - step * (noise * dire + back)
    sol_sum = column(2) + step * column(5)
    sol_square = column(3) + 2.0 * step * column(4) + step * (step * column(1))
    lane = lane_of(stats_out.shape)
    stats_out[...] = jnp.where(lane == 0, column(0), jnp.where(lane == 1, sol_sum, sol_square))


def last_kernel(samples, width, came_ref, stats_ref, res_ref, dir_ref, out_ref, score_out):
    row = lax.broadcasted_iota(jnp.int32, (8, LANES), 0)
    halves_of, lasts = [], []
    for core in range(2):
        total = came_ref[core]
        for i in range(core + 2, came_ref.shape[0], 2):
            total = total + came_ref[i]
        spread = jnp.where(row % 2 == 0, total[:, :LANES], total[:, LANES : 2 * LANES])
        part = spread
        for m in range(1, 4):
            part = jnp.where(row // 2 == m, pltpu.roll(spread, LANES - 32 * m, 1), part)
        halves_of.append(part)
        lasts.append(total[:, 2 * LANES :])
    new_norm = as_column(lasts[0] + lasts[1], 6)
    out_ref[...] = res_ref[...] + (new_norm / (stats_ref[:, 0:1] + 1e-06)) * dir_ref[...]
    cross = jnp.concatenate(halves_of, axis=0)
    dose = lasts[0]
    sol_sum, sol_square = stats_ref[:, 1:2], stats_ref[:, 2:3]
    dose_freq = (dose / 100.0 + 1.0) / (2.0 * samples + 2.0)
    dose_spread = jnp.sqrt(2.0 * dose_freq * (1.0 - dose_freq))
    scale = math.sqrt(samples) * jnp.sqrt(sol_square / samples + 1e-06)
    scores = (cross / 100.0 - 2.0 * dose_freq * sol_sum) / (dose_spread * scale)
    score_out[...] = scores[:, :width]


def call(kernel, out, ins, args, scratch=(), limit=16, flops=0, moved=0):
    return pl.pallas_call(
        kernel,
        out_shape=[jax.ShapeDtypeStruct(*o) if len(o) == 2 else o[2](*o[:2]) for o in out],
        in_specs=list(ins),
        out_specs=[VMEM] * len(out),
        scratch_shapes=list(scratch),
        compiler_params=pltpu.CompilerParams(vmem_limit_bytes=limit * MIB),
        cost_estimate=pl.CostEstimate(flops=flops, bytes_accessed=moved, transcendentals=0),
    )(*[pltpu.with_memory_space_constraint(x, pltpu.HBM) if spec is HBM else x for spec, x in zip(ins, args)])


def body(genotypes, called, dosage, sample_order, noise_ratio, solution, residual, direction):
    n_var = lax.axis_size("var")
    n_samp = lax.axis_size("samp")
    own, rhs = direction.shape
    rows, shard = genotypes.shape
    variants = rows * n_var
    samples = own * n_samp * n_var
    imputed = dosage.shape[1]
    width = imputed // (n_var * n_samp)
    noise = noise_ratio[None]

    dire, res, sol = direction.T, residual.T, solution.T
    first, chunk = rows // 3 * 2, 64
    matrix = lambda n: ((n, shard), BF16, pltpu.VMEM)

    neighbour = swap(dire, "var", 1)
    called_a, sums = call(
        functools.partial(called_kernel, chunk),
        [matrix(first), ((8, LANES), F32)],
        [HBM] * 4,
        (sol, dire, res, called),
        scratch=[
            pltpu.VMEM((rhs, own), F32),
            pltpu.VMEM((rhs, own), F32),
            pltpu.VMEM((rhs, own), F32),
            pltpu.VMEM((first, shard), jnp.int32),
            pltpu.SemaphoreType.DMA((3,)),
            pltpu.SemaphoreType.DMA((first // chunk,)),
        ],
        limit=10,
        moved=4 * first * shard,
    )
    (pair,) = call(pair_kernel, [((2 * rhs, own), BF16)], [VMEM] * 2, (dire, neighbour), limit=4)
    pair_other = swap(pair, "var", 2)
    row_weights = pltpu.VMEM((2 * rhs, 2 * own), BF16)
    (done,) = call(
        called_product_kernel,
        [((2 * rhs, first), F32)],
        [VMEM] * 2,
        (pair, called_a),
        scratch=[row_weights],
        limit=4,
        flops=first * shard * 256,
        moved=first * shard,
    )
    coded, called_b, half = call(
        mask_kernel,
        [matrix(rows), matrix(rows - first), ((2 * rhs + 8, rows), F32)],
        [VMEM] * 4 + [HBM],
        (pair, called_a, done, genotypes, called),
        scratch=[
            pltpu.VMEM((rows - first, shard), jnp.int32),
            row_weights,
            pltpu.SemaphoreType.DMA(((rows - first) // LANES,)),
        ],
        limit=12,
        flops=2 * rows * shard * 256,
        moved=4 * rows * shard,
    )
    (part,) = call(
        forward_kernel,
        [((2 * rhs + 8, rows + LANES), F32)],
        [VMEM] * 6,
        (pair_other, coded, called_a, called_b, half, sums),
        scratch=[row_weights],
        flops=2 * rows * shard * 256,
        moved=2 * rows * shard,
    )
    part_other = swap(part, "samp", 1)

    n_chips = n_samp // 2
    total, *messages = call(
        chips_kernel,
        [(part.shape, F32)] + [((2 * rhs, rows + LANES), BF16)] * (n_chips - 1),
        [VMEM] * 2,
        (part, part_other),
        moved=1 * MIB,
    )
    arrived = [swap(messages[k], "samp", 2 * (k + 1) + 1) for k in reversed(range(n_chips - 1))]
    (cross,) = call(
        dosage_kernel,
        [((2 * rhs + 8, imputed), F32)],
        [VMEM] * 5,
        (sample_order, sol, dire, dosage, total),
        flops=2 * 80 * own * (own + imputed),
        moved=4 * own * imputed,
    )
    cross_other = swap(cross, "samp", 1)

    wide = own + LANES
    scaled, sums, *messages = call(
        functools.partial(back_kernel, variants, len(arrived)),
        [((2 * rhs, rows), BF16), ((8, LANES), F32)] + [((rhs, wide), BF16)] * (n_var - 1),
        [VMEM] * (4 + len(arrived)),
        (total, coded, called_a, called_b, *arrived),
        flops=2 * rows * shard * 256,
        moved=2 * rows * shard,
    )
    backs = [swap(messages[k], "var", k + 1) for k in reversed(range(n_var - 1))]
    mine_back, both = call(
        functools.partial(own_kernel, variants),
        [((rhs, wide), F32), (cross.shape, F32)],
        [VMEM] * 7,
        (scaled, sums, coded, called_a, called_b, cross, cross_other),
        flops=rows * shard * 256,
        moved=rows * shard,
    )
    backs = [mine_back] + backs


    n_all = n_var * n_samp
    outgoing, res_keep = call(
        functools.partial(norm_kernel, variants, width),
        [((n_all, 1, 3 * LANES), F32), ((rhs, own), F32)],
        [VMEM] * (4 + n_var),
        (noise, dire, res, both, *backs),
        moved=4 * 3 * n_all * LANES,
    )
    came = lax.all_to_all(outgoing, ("var", "samp"), split_axis=0, concat_axis=0)
    sol_new, res_new, stats = call(
        functools.partial(new_kernel, variants),
        [((rhs, own), F32), ((rhs, own), F32), ((rhs, LANES), F32)],
        [VMEM] * (4 + n_var),
        (noise, dire, res, sol, *backs),
        moved=1 * MIB,
    )
    dir_new, scores = call(
        functools.partial(last_kernel, samples, width),
        [((rhs, own), F32), ((rhs, width), F32)],
        [VMEM] * 4,
        (came, stats, res_keep, dire),
    )
    return (sol_new.T, res_new.T, dir_new.T, scores.T)


def solution(mesh):
    placed = (
        P("var", "samp"),
        P("var", "samp"),
        P(("samp", "var"), None),
        P(("samp", "var"), None),
        P(),
        P(("samp", "var"), None),
        P(("samp", "var"), None),
        P(("samp", "var"), None),
    )
    return jax.shard_map(
        body,
        mesh=mesh,
        in_specs=placed,
        out_specs=(
            P(("samp", "var"), None),
            P(("samp", "var"), None),
            P(("samp", "var"), None),
            P(("var", "samp"), None),
        ),
        check_vma=False,
    )
```

```python
import functools
import math

import jax
import jax.numpy as jnp
from jax import lax
from jax.experimental import pallas as pl
from jax.experimental.pallas import tpu as pltpu
from jax.sharding import PartitionSpec as P

BF16 = jnp.bfloat16
F32 = jnp.float32
LANES = 128
NT = (((1,), (1,)), ((), ()))
VMEM = pl.BlockSpec(memory_space=pltpu.VMEM)
HBM = pl.BlockSpec(memory_space=pltpu.HBM)
MIB = 1 << 20


def swap(values, axis, distance):
    size = lax.axis_size(axis)
    return lax.ppermute(values, axis, [(i, i ^ distance) for i in range(size)])


def halves(values):
    high = values.astype(BF16)
    return high, (values - high.astype(F32)).astype(BF16)


def thirds(values):
    high = values.astype(BF16)
    rest = values - high.astype(F32)
    middle = rest.astype(BF16)
    return high, middle, (rest - middle.astype(F32)).astype(BF16)


def lane_of(shape):
    return lax.broadcasted_iota(jnp.int32, shape, len(shape) - 1)


def spot(q):
    shape = (16, LANES)
    return lane_of(shape) == 16 * q + lax.broadcasted_iota(jnp.int32, shape, 0)


def as_row(values):
    block = jnp.zeros((16, LANES), F32)
    for q, column in values.items():
        block = jnp.where(spot(q), column, block)
    return jnp.sum(block, axis=0, keepdims=True)


def as_column(row, q):
    return jnp.sum(jnp.where(spot(q), row, 0.0), axis=1, keepdims=True)


def to_column(row):
    shape = (16, row.shape[1])
    same = lax.broadcasted_iota(jnp.int32, shape, 0) == lane_of(shape)
    return jnp.sum(jnp.where(same, row, 0.0), axis=1, keepdims=True)


BLOCK = 512
CHUNK = 256


def blocks(rows, samples):
    return [
        (pl.ds(row, 16), pl.ds(sample, BLOCK)) for row in range(0, rows, 16) for sample in range(0, samples, BLOCK)
    ]


def row_copies(source, target, first, chunk, sems):
    return [
        pltpu.make_async_copy(source.at[pl.ds(first + i, chunk)], target.at[pl.ds(i, chunk)], sems.at[i // chunk])
        for i in range(0, target.shape[0], chunk)
    ]


def called_kernel(chunk, sol_hbm, dir_hbm, res_hbm, call_hbm, out_ref, sums_ref,
                  sol_ref, dir_ref, res_ref, cbuf, small_sems, sems):
    small = [
        pltpu.make_async_copy(source, target, small_sems.at[i])
        for i, (source, target) in enumerate(((sol_hbm, sol_ref), (dir_hbm, dir_ref), (res_hbm, res_ref)))
    ]
    for copy in small:
        copy.start()
    parts = row_copies(call_hbm, cbuf, 0, chunk, sems)
    for copy in parts:
        copy.start()
    for copy in small:
        copy.wait()
    sol, dire, res = sol_ref[...], dir_ref[...], res_ref[...]
    products = (res * res, dire * dire, sol, sol * sol, sol * dire, dire)
    row = as_row({q: jnp.sum(x, axis=1, keepdims=True) for q, x in enumerate(products)})
    sums_ref[...] = jnp.broadcast_to(row, sums_ref.shape)
    for i, copy in enumerate(parts):
        copy.wait()
        source, target = cbuf.at[pl.ds(i * chunk, chunk)], out_ref.at[pl.ds(i * chunk, chunk)]
        for here in blocks(chunk, source.shape[1]):
            target[here] = source[here].astype(F32).astype(BF16)


def pair_kernel(own_ref, other_ref, out_ref):
    upper = lax.axis_index("var") % 2
    rhs = own_ref.shape[0]
    own, other = own_ref[...], other_ref[...]
    out_ref[:rhs] = jnp.where(upper == 0, own, other).astype(BF16)
    out_ref[rhs:] = jnp.where(upper == 0, other, own).astype(BF16)


def weights(pair_ref, w):
    own = pair_ref.shape[1]
    row = lax.broadcasted_iota(jnp.int32, (16, 2 * own), 0)
    w[16:32] = jnp.where(row == 0, 1.0, 0.0).astype(BF16)
    for i in range(2):
        w[0:16, i * own : (i + 1) * own] = pair_ref[16 * i : 16 * i + 16]


def product(w, matrix, first, rows, samples):
    return lax.dot_general(w[...], matrix[pl.ds(first, rows), samples], NT, preferred_element_type=F32)


def split_product(w, head, tail, first, rows, samples):
    if first < head.shape[0]:
        return product(w, head, first, rows, samples)
    return product(w, tail, first - head.shape[0], rows, samples)


def rows_of(coded, called):
    counts = jnp.concatenate([coded[16:17], called[16:17], jnp.zeros((6, coded.shape[1]), F32)], axis=0)
    return jnp.concatenate([coded[0:16], called[0:16], counts], axis=0)


def pair_samples(pair, own):
    return pl.ds(pl.multiple_of(pair * 2 * own, LANES), 2 * own)


def called_product_kernel(pair_ref, called_first, out_ref, w):
    own = pair_ref.shape[1]
    samples = pair_samples(lax.axis_index("var") // 2, own)
    weights(pair_ref, w)
    for place in range(0, called_first.shape[0], CHUNK):
        out_ref[:, place : place + CHUNK] = product(w, called_first, place, CHUNK, samples)


def mask_kernel(pair_ref, called_first, done_ref, gen_ref, call_hbm, coded_ref, called_ref, out_ref, cbuf, w, sems):
    own = pair_ref.shape[1]
    rows, shard = gen_ref.shape
    first = called_first.shape[0]
    copies = row_copies(call_hbm, cbuf, first, LANES, sems)
    for copy in copies:
        copy.start()
    samples = pair_samples(lax.axis_index("var") // 2, own)
    weights(pair_ref, w)

    def convert(place):
        here, after = pl.ds(place, LANES), place - first
        gen, coded = gen_ref.at[here], coded_ref.at[here]
        if after >= 0:
            copies[after // LANES].wait()
            call, called = cbuf.at[pl.ds(after, LANES)], called_ref.at[pl.ds(after, LANES)]
        else:
            mask_ref = called_first.at[here]

        def store(block, value, mask):
            coded[block] = value
            if after >= 0:
                called[block] = mask

        held = []
        for block in blocks(LANES, shard):
            mask = call[block].astype(F32).astype(BF16) if after >= 0 else mask_ref[block]
            held.append((block, gen[block].astype(F32).astype(BF16) * mask, mask))
            if len(held) > 6:
                store(*held.pop(0))
        for item in held:
            store(*item)

    for place in range(0, rows + CHUNK, CHUNK):
        if place:
            before = place - CHUNK
            coded = product(w, coded_ref, before, CHUNK, samples)
            if before < first:
                called = done_ref[:, before:place]
            else:
                called = product(w, called_ref, before - first, CHUNK, samples)
            out_ref[:, before:place] = rows_of(coded, called)
        for part in range(place, min(place + CHUNK, rows), LANES):
            convert(part)


def forward_kernel(pair_ref, coded_ref, called_first, called_ref, half_ref, sums_ref, out_ref, w):
    own = pair_ref.shape[1]
    rows = coded_ref.shape[0]
    samples = pair_samples((lax.axis_index("var") // 2) ^ 1, own)
    weights(pair_ref, w)
    for place in range(0, rows, CHUNK):
        here = slice(place, place + CHUNK)
        coded = product(w, coded_ref, place, CHUNK, samples)
        called = split_product(w, called_first, called_ref, place, CHUNK, samples)
        out_ref[:, here] = half_ref[:, here] + rows_of(coded, called)
    out_ref[:, rows:] = jnp.zeros((out_ref.shape[0], LANES), F32)
    out_ref[0:8, rows:] = sums_ref[...]


def chips_kernel(own_ref, other_ref, total_ref, *messages):
    rows = own_ref.shape[1] - LANES
    total = own_ref[...] + other_ref[...]
    total_ref[...] = total
    pieces = []
    for part in halves(total[32:34, :rows]):
        part = part.astype(F32)
        for which in range(2):
            for j in range(rows // LANES):
                pieces.append(part[which : which + 1, j * LANES : (j + 1) * LANES])
    pieces += [part.astype(F32) for part in thirds(total[0:1, rows:])]
    pieces.append(jnp.zeros((32 - len(pieces), LANES), F32))
    extra = jnp.concatenate(pieces, axis=0).astype(BF16)
    for message in messages:
        message[:, :rows] = total[0:32, :rows].astype(BF16)
        message[:, rows:] = extra


def dosage_kernel(order_ref, sol_ref, dir_ref, dose_ref, after_ref, cross_ref):
    rhs = sol_ref.shape[0]
    sol_high, sol_low = halves(sol_ref[...])
    dir_high, dir_low = halves(dir_ref[...])
    stack = jnp.concatenate([sol_high, dir_high, sol_low, dir_low], axis=0)
    own = stack.shape[1]
    hot = lax.broadcasted_iota(jnp.int32, (own, own), 0) == order_ref[...]
    hot = jnp.where(hot, 1.0, 0.0).astype(BF16)
    picked = jnp.dot(stack, hot, preferred_element_type=F32).astype(BF16)
    picked = jnp.concatenate([picked, jnp.ones((16, own), BF16)], axis=0)
    dose = dose_ref[...].astype(F32).astype(BF16)
    cross = jnp.dot(picked, dose, preferred_element_type=F32)
    cross_ref[: 2 * rhs] = cross[: 2 * rhs] + cross[2 * rhs : 4 * rhs]
    cross_ref[2 * rhs :] = cross[4 * rhs : 4 * rhs + 8]


def term(scaled_ref, coded_ref, called_first, called_ref, p, own, variants):
    part = pl.ds(pl.multiple_of(p * own, LANES), own)
    first = called_first.shape[0]
    got = jnp.dot(scaled_ref[0:16], coded_ref[:, part], preferred_element_type=F32)
    got = got + jnp.dot(scaled_ref[16:32, :first], called_first[:, part], preferred_element_type=F32)
    got = got + jnp.dot(scaled_ref[16:32, first:], called_ref[:, part], preferred_element_type=F32)
    return got / variants


def sums_block(sums):
    parts = [part.astype(F32) for part in thirds(sums)]
    return jnp.concatenate(parts + [jnp.zeros((13, LANES), F32)], axis=0).astype(BF16)


def back_kernel(variants, n_arrived, total_ref, coded_ref, called_first, called_ref, *rest):
    arrived = rest[:n_arrived]
    scaled_ref, sums_ref, *messages = rest[n_arrived:]
    var = lax.axis_index("var")
    rows = total_ref.shape[1] - LANES

    main = total_ref[0:32, :rows]
    allele, count = total_ref[32:33, :rows], total_ref[33:34, :rows]
    extra = jnp.zeros((32, LANES), F32)
    for ref in arrived:
        main = main + ref[:, :rows].astype(F32)
        extra = extra + ref[:, rows:].astype(F32)
    tiles = rows // LANES
    pick = lambda first: jnp.concatenate(
        [extra[first + j : first + j + 1] + extra[first + 2 * tiles + j : first + 2 * tiles + j + 1]
         for j in range(tiles)], axis=1
    )
    allele = allele + pick(0)
    count = count + pick(tiles)
    last = 4 * tiles
    sums = total_ref[0:1, rows:] + extra[last : last + 1] + extra[last + 1 : last + 2] + extra[last + 2 : last + 3]

    frequency = (allele + 1.0) / (2.0 * count + 2.0)
    spread = jnp.sqrt(2.0 * frequency * (1.0 - frequency))
    loading = (main[0:16] - 2.0 * frequency * main[16:32]) / spread
    scaled = loading / spread
    scaled_ref[0:16] = scaled.astype(BF16)
    scaled_ref[16:32] = (-2.0 * frequency * scaled).astype(BF16)
    square = as_row({6: jnp.sum(loading * loading, axis=1, keepdims=True)})
    sums = jnp.where(lane_of((1, LANES)) < 96, sums, square)

    sums_ref[...] = jnp.broadcast_to(sums, sums_ref.shape)

    for k, ref in enumerate(messages):
        own = ref.shape[1] - LANES
        ref[:, :own] = term(scaled_ref, coded_ref, called_first, called_ref, var ^ (k + 1), own, variants).astype(BF16)
        ref[:, own:] = sums_block(sums)


def own_kernel(variants, scaled_ref, sums_ref, coded_ref, called_first, called_ref,
               cross_ref, other_ref, own_ref, both_ref):
    both_ref[...] = cross_ref[...] + other_ref[...]
    own = own_ref.shape[1] - LANES
    p = lax.axis_index("var")
    own_ref[:, :own] = term(scaled_ref, coded_ref, called_first, called_ref, p, own, variants)
    own_ref[:, own:] = jnp.concatenate([sums_ref[0:1], jnp.zeros((15, LANES), F32)], axis=0)


def step_of(refs, noise_row, variants):
    got = refs[0][...]
    for ref in refs[1:]:
        got = got + ref[...].astype(F32)
    own = got.shape[1] - LANES
    back, last = got[:, :own], got[:, own:]
    sums = last[0:1] + last[1:2] + last[2:3]
    column = functools.partial(as_column, sums)
    noise = to_column(noise_row)
    curvature = noise * column(1) + column(6) / variants
    step = column(0) / (curvature + 1e-06)
    return back, column, noise, step


def norm_kernel(variants, width, noise_ref, dir_ref, res_ref, both_ref, *rest):
    refs, (out_ref, new_ref) = rest[:-2], rest[-2:]
    back, _, noise, step = step_of(refs, noise_ref[...], variants)
    new = res_ref[...] - step * (noise * dir_ref[...] + back)
    new_ref[...] = new
    norm = as_row({6: jnp.sum(new * new, axis=1, keepdims=True)})
    both = both_ref[...]
    core = lax.axis_index("samp") % 2
    half = lambda x: jnp.where(core == 0, x[0:8], x[8:16])
    cross = half(both[0:16]) + half(step) * half(both[16:32])
    dose = both[32:40]
    lane = lane_of((8, LANES))
    row = lax.broadcasted_iota(jnp.int32, (8, LANES), 0)
    turned = {}

    def turn(values, name, tile, by):
        if (name, tile, by) not in turned:
            piece = values[:, tile : tile + LANES]
            turned[name, tile, by] = pltpu.roll(piece, by, 1) if by else piece
        return turned[name, tile, by]

    for j in range(out_ref.shape[0]):
        tile, inside = (j * width) // LANES * LANES, (j * width) % LANES
        block = jnp.zeros((8, LANES), F32)
        for m in range(4):
            here = (row // 2 == m) & (lane >= 32 * m) & (lane < 32 * m + width)
            block = jnp.where(here, turn(cross, "cross", tile, (32 * m - inside) % LANES), block)
        block = block[0:4] + block[4:8]
        block = block[0:2] + block[2:4]
        last = jnp.where(lane[0:1] < width, turn(dose, "dose", tile, -inside % LANES)[0:1], norm)
        for k in range(2):
            out_ref[j, :, k * LANES : (k + 1) * LANES] = block[k : k + 1]
        out_ref[j, :, 2 * LANES :] = last


def new_kernel(variants, noise_ref, dir_ref, res_ref, sol_ref, *rest):
    refs, (sol_out, res_out, stats_out) = rest[:-3], rest[-3:]
    back, column, noise, step = step_of(refs, noise_ref[...], variants)
    dire = dir_ref[...]
    sol_out[...] = sol_ref[...] + step * dire
    res_out[...] = res_ref[...] - step * (noise * dire + back)
    sol_sum = column(2) + step * column(5)
    sol_square = column(3) + 2.0 * step * column(4) + step * (step * column(1))
    lane = lane_of(stats_out.shape)
    stats_out[...] = jnp.where(lane == 0, column(0), jnp.where(lane == 1, sol_sum, sol_square))


def last_kernel(samples, width, came_ref, stats_ref, res_ref, dir_ref, out_ref, score_out):
    row = lax.broadcasted_iota(jnp.int32, (8, LANES), 0)
    halves_of, lasts = [], []
    for core in range(2):
        total = came_ref[core]
        for i in range(core + 2, came_ref.shape[0], 2):
            total = total + came_ref[i]
        spread = jnp.where(row % 2 == 0, total[:, :LANES], total[:, LANES : 2 * LANES])
        part = spread
        for m in range(1, 4):
            part = jnp.where(row // 2 == m, pltpu.roll(spread, LANES - 32 * m, 1), part)
        halves_of.append(part)
        lasts.append(total[:, 2 * LANES :])
    new_norm = as_column(lasts[0] + lasts[1], 6)
    out_ref[...] = res_ref[...] + (new_norm / (stats_ref[:, 0:1] + 1e-06)) * dir_ref[...]
    cross = jnp.concatenate(halves_of, axis=0)
    dose = lasts[0]
    sol_sum, sol_square = stats_ref[:, 1:2], stats_ref[:, 2:3]
    dose_freq = (dose / 100.0 + 1.0) / (2.0 * samples + 2.0)
    dose_spread = jnp.sqrt(2.0 * dose_freq * (1.0 - dose_freq))
    scale = math.sqrt(samples) * jnp.sqrt(sol_square / samples + 1e-06)
    scores = (cross / 100.0 - 2.0 * dose_freq * sol_sum) / (dose_spread * scale)
    score_out[...] = scores[:, :width]


def call(kernel, out, ins, args, scratch=(), limit=16, flops=0, moved=0):
    return pl.pallas_call(
        kernel,
        out_shape=[jax.ShapeDtypeStruct(*o) if len(o) == 2 else o[2](*o[:2]) for o in out],
        in_specs=list(ins),
        out_specs=[VMEM] * len(out),
        scratch_shapes=list(scratch),
        compiler_params=pltpu.CompilerParams(vmem_limit_bytes=limit * MIB),
        cost_estimate=pl.CostEstimate(flops=flops, bytes_accessed=moved, transcendentals=0),
    )(*[pltpu.with_memory_space_constraint(x, pltpu.HBM) if spec is HBM else x for spec, x in zip(ins, args)])


def body(genotypes, called, dosage, sample_order, noise_ratio, solution, residual, direction):
    n_var = lax.axis_size("var")
    n_samp = lax.axis_size("samp")
    own, rhs = direction.shape
    rows, shard = genotypes.shape
    variants = rows * n_var
    samples = own * n_samp * n_var
    imputed = dosage.shape[1]
    width = imputed // (n_var * n_samp)
    noise = noise_ratio[None]

    dire, res, sol = direction.T, residual.T, solution.T
    first, chunk = rows // 3 * 2, 64
    matrix = lambda n: ((n, shard), BF16, pltpu.VMEM)

    neighbour = swap(dire, "var", 1)
    called_a, sums = call(
        functools.partial(called_kernel, chunk),
        [matrix(first), ((8, LANES), F32)],
        [HBM] * 4,
        (sol, dire, res, called),
        scratch=[
            pltpu.VMEM((rhs, own), F32),
            pltpu.VMEM((rhs, own), F32),
            pltpu.VMEM((rhs, own), F32),
            pltpu.VMEM((first, shard), jnp.int32),
            pltpu.SemaphoreType.DMA((3,)),
            pltpu.SemaphoreType.DMA((first // chunk,)),
        ],
        limit=10,
        moved=4 * first * shard,
    )
    (pair,) = call(pair_kernel, [((2 * rhs, own), BF16)], [VMEM] * 2, (dire, neighbour), limit=4)
    pair_other = swap(pair, "var", 2)
    row_weights = pltpu.VMEM((2 * rhs, 2 * own), BF16)
    (done,) = call(
        called_product_kernel,
        [((2 * rhs, first), F32)],
        [VMEM] * 2,
        (pair, called_a),
        scratch=[row_weights],
        limit=4,
        flops=first * shard * 256,
        moved=first * shard,
    )
    coded, called_b, half = call(
        mask_kernel,
        [matrix(rows), matrix(rows - first), ((2 * rhs + 8, rows), F32)],
        [VMEM] * 4 + [HBM],
        (pair, called_a, done, genotypes, called),
        scratch=[
            pltpu.VMEM((rows - first, shard), jnp.int32),
            row_weights,
            pltpu.SemaphoreType.DMA(((rows - first) // LANES,)),
        ],
        limit=12,
        flops=2 * rows * shard * 256,
        moved=4 * rows * shard,
    )
    (part,) = call(
        forward_kernel,
        [((2 * rhs + 8, rows + LANES), F32)],
        [VMEM] * 6,
        (pair_other, coded, called_a, called_b, half, sums),
        scratch=[row_weights],
        flops=2 * rows * shard * 256,
        moved=2 * rows * shard,
    )
    part_other = swap(part, "samp", 1)

    n_chips = n_samp // 2
    total, *messages = call(
        chips_kernel,
        [(part.shape, F32)] + [((2 * rhs, rows + LANES), BF16)] * (n_chips - 1),
        [VMEM] * 2,
        (part, part_other),
        moved=1 * MIB,
    )
    arrived = [swap(messages[k], "samp", 2 * (k + 1) + 1) for k in reversed(range(n_chips - 1))]
    (cross,) = call(
        dosage_kernel,
        [((2 * rhs + 8, imputed), F32)],
        [VMEM] * 5,
        (sample_order, sol, dire, dosage, total),
        flops=2 * 80 * own * (own + imputed),
        moved=4 * own * imputed,
    )
    cross_other = swap(cross, "samp", 1)

    wide = own + LANES
    scaled, sums, *messages = call(
        functools.partial(back_kernel, variants, len(arrived)),
        [((2 * rhs, rows), BF16), ((8, LANES), F32)] + [((rhs, wide), BF16)] * (n_var - 1),
        [VMEM] * (4 + len(arrived)),
        (total, coded, called_a, called_b, *arrived),
        flops=2 * rows * shard * 256,
        moved=2 * rows * shard,
    )
    backs = [swap(messages[k], "var", k + 1) for k in reversed(range(n_var - 1))]
    mine_back, both = call(
        functools.partial(own_kernel, variants),
        [((rhs, wide), F32), (cross.shape, F32)],
        [VMEM] * 7,
        (scaled, sums, coded, called_a, called_b, cross, cross_other),
        flops=rows * shard * 256,
        moved=rows * shard,
    )
    backs = [mine_back] + backs


    n_all = n_var * n_samp
    outgoing, res_keep = call(
        functools.partial(norm_kernel, variants, width),
        [((n_all, 1, 3 * LANES), F32), ((rhs, own), F32)],
        [VMEM] * (4 + n_var),
        (noise, dire, res, both, *backs),
        moved=4 * 3 * n_all * LANES,
    )
    came = lax.all_to_all(outgoing, ("var", "samp"), split_axis=0, concat_axis=0)
    sol_new, res_new, stats = call(
        functools.partial(new_kernel, variants),
        [((rhs, own), F32), ((rhs, own), F32), ((rhs, LANES), F32)],
        [VMEM] * (4 + n_var),
        (noise, dire, res, sol, *backs),
        moved=1 * MIB,
    )
    dir_new, scores = call(
        functools.partial(last_kernel, samples, width),
        [((rhs, own), F32), ((rhs, width), F32)],
        [VMEM] * 4,
        (came, stats, res_keep, dire),
    )
    return (sol_new.T, res_new.T, dir_new.T, scores.T)


def solution(mesh):
    placed = (
        P("var", "samp"),
        P("var", "samp"),
        P(("samp", "var"), None),
        P(("samp", "var"), None),
        P(),
        P(("samp", "var"), None),
        P(("samp", "var"), None),
        P(("samp", "var"), None),
    )
    return jax.shard_map(
        body,
        mesh=mesh,
        in_specs=placed,
        out_specs=(
            P(("samp", "var"), None),
            P(("samp", "var"), None),
            P(("samp", "var"), None),
            P(("var", "samp"), None),
        ),
        check_vma=False,
    )
```
